32 devices in a mesh: dp: 8 (over z, y), seq: 4 (over x, core).
Axes of the slice: x: 2, y: 2, z: 4, core: 2. Of those that a mesh axis runs over, the one named last changes fastest.
Arguments:
- tokens: bfloat16 [32, 512, 768], P('dp', 'seq'), may hold values from -6 to 6
- doc_lengths: int32 [32], P('dp'), may hold values from 40 to 512, as said below
- query_weight: bfloat16 [768, 768], P('seq'), may hold values from -0.109375 to 0.109375
- key_weight: bfloat16 [768, 768], P('seq'), may hold values from -0.109375 to 0.109375
- value_weight: bfloat16 [768, 768], P('seq'), may hold values from -0.21875 to 0.21875
- out_weight: bfloat16 [768, 768], P('seq'), may hold values from -0.4375 to 0.4375
- gate_weight: bfloat16 [768, 2048], P('seq'), may hold values from -0.21875 to 0.21875
- up_weight: bfloat16 [768, 2048], P('seq'), may hold values from -0.21875 to 0.21875
- down_weight: bfloat16 [2048, 768], P('seq'), may hold values from -0.1875 to 0.1875
- proj_weight: bfloat16 [768, 128], P('seq'), may hold values from -0.21875 to 0.21875
- attn_gain: float32 [768], replicated, may hold values from 0.5 to 1.5
- ffn_gain: float32 [768], replicated, may hold values from 0.5 to 1.5
- final_gain: float32 [768], replicated, may hold values from 0.5 to 1.5
- bucket_bias_rows: float32 [32, 12], replicated, may hold values from -6 to 6
- embed_cotangent: bfloat16 [32, 512, 128], P('dp', 'seq'), may hold values from -6 to 6
Outputs:
- embedded: bfloat16 [32, 512, 128], P('dp', 'seq')
- tokens_grad: float32 [32, 512, 768], P('dp', 'seq')
- query_weight_grad: float32 [768, 768], P('seq')
- key_weight_grad: float32 [768, 768], P('seq')
- value_weight_grad: float32 [768, 768], P('seq')
- out_weight_grad: float32 [768, 768], P('seq')
- gate_weight_grad: float32 [768, 2048], P('seq')
- up_weight_grad: float32 [768, 2048], P('seq')
- down_weight_grad: float32 [2048, 768], P('seq')
- proj_weight_grad: float32 [768, 128], P('seq')
- attn_gain_grad: float32 [768], P('seq')
- ffn_gain_grad: float32 [768], P('seq')
- final_gain_grad: float32 [768], P('seq')
- bias_table_grad: float32 [32, 12], P('seq')
The draws below stay inside these ranges and needn't reach their ends.
Inputs may be any that keep to these rules, and one draw needn't show every extreme that they name: doc_lengths[d] counts the real tokens of document d; keys at later positions of its slot are padding. In each aligned group of 4 documents (those of one index of dp) one document, chosen by the seed, fills its slot with 512 tokens.
All inputs are finite; a program needn't handle non-finite values.
Results may differ from the reference program's by a relative error of at most 0.02.
Values may be sent and summed in bfloat16 or wider, within the bound.
No kernel may reach another device: no remote copies, remote signals or barrier semaphores. Data moves between devices by JAX's collectives and lax.ppermute only.
A program may use at most 192 MiB of HBM per device.

```python
import jax
import jax.numpy as jnp
import numpy as np
from jax import lax

D = 768
H = 12
HEAD = 64
FF = 2048
PROJ = 128
BUCKETS = 32
SLOT = 512
LMIN = 40
DOCS_DEV = 4
DOCS = 32


def draw_doc_lengths(key, part):
    key = jax.random.fold_in(key, 11)
    first_key, second_key, third_key = jax.random.split(key, 3)
    length_span = SLOT - LMIN
    left_side = jax.random.randint(first_key, (DOCS,), 0, length_span + 1, dtype=jnp.int32)
    right_side = jax.random.randint(second_key, (DOCS,), 0, length_span + 1, dtype=jnp.int32)
    lengths = SLOT - left_side * right_side // length_span
    chosen = jax.random.randint(third_key, (DOCS // DOCS_DEV,), 0, DOCS_DEV, dtype=jnp.int32)
    doc_index = jnp.arange(DOCS, dtype=jnp.int32)
    full_doc = chosen[doc_index // DOCS_DEV] == doc_index % DOCS_DEV
    return jnp.where(full_doc, SLOT, lengths).astype(jnp.int32)


def level_of(own_key, extent, pieces, low, top_value):
    def one(dim, shards_of):
        steps = jax.random.uniform(jax.random.fold_in(jax.random.fold_in(own_key, 6), dim), (shards_of,), jnp.float32, low / len(pieces), top_value / len(pieces))
        return jnp.repeat(jnp.exp(steps), extent[dim] // shards_of).reshape((-1,) + (1,) * (len(extent) - dim - 1))

    level = one(*pieces[0])
    for cut in pieces[1:]:
        level = level * one(*cut)
    return level


def normal_values(own_key, extent, width, bound, cuts=(), kind=jnp.bfloat16):
    gain = level_of(own_key, extent, cuts, -0.22, 0.18) if cuts else 1.0
    drawn = jax.random.normal(own_key, extent, jnp.float32) * width * gain
    return jnp.minimum(jnp.maximum(drawn, -bound), bound).astype(kind)


def setup_inputs(seed: int = 0) -> dict:
    streams_of = jax.random.split(jax.random.key(seed), 16)
    tokens = normal_values(streams_of[0], (DOCS, SLOT, D), 1.0, 6.0, ((0, 8), (1, 4)))
    doc_lengths = draw_doc_lengths(jax.random.fold_in(streams_of[15], 71), 0)
    query_weight = normal_values(streams_of[2], (D, D), (4 * D) ** -0.5, 0.109375, ((0, 4),))
    key_weight = normal_values(streams_of[3], (D, D), (4 * D) ** -0.5, 0.109375, ((0, 4),))
    value_weight = normal_values(streams_of[4], (D, D), D ** -0.5, 0.21875, ((0, 4),))
    out_weight = normal_values(streams_of[5], (D, D), (D // 4) ** -0.5, 0.4375, ((0, 4),))
    gate_weight = normal_values(streams_of[6], (D, FF), D ** -0.5, 0.21875, ((0, 4),))
    up_weight = normal_values(streams_of[7], (D, FF), D ** -0.5, 0.21875, ((0, 4),))
    down_weight = normal_values(streams_of[8], (FF, D), (FF // 2) ** -0.5, 0.1875, ((0, 4),))
    proj_weight = normal_values(streams_of[9], (D, PROJ), D ** -0.5, 0.21875, ((0, 4),))
    attn_gain = jnp.clip(1.0 + 0.1 * jax.random.normal(streams_of[10], (D,), jnp.float32), 0.5, 1.5)
    ffn_gain = jnp.clip(1.0 + 0.1 * jax.random.normal(streams_of[11], (D,), jnp.float32), 0.5, 1.5)
    final_gain = jnp.clip(1.0 + 0.1 * jax.random.normal(streams_of[12], (D,), jnp.float32), 0.5, 1.5)
    bucket_bias_rows = normal_values(streams_of[13], (BUCKETS, H), 1.0, 6.0, (), jnp.float32)
    embed_cotangent = normal_values(streams_of[14], (DOCS, SLOT, PROJ), 1.0, 6.0, ((0, 8), (1, 4)))
    return dict(tokens=tokens, doc_lengths=doc_lengths, query_weight=query_weight, key_weight=key_weight, value_weight=value_weight, out_weight=out_weight, gate_weight=gate_weight, up_weight=up_weight, down_weight=down_weight, proj_weight=proj_weight, attn_gain=attn_gain, ffn_gain=ffn_gain, final_gain=final_gain, bucket_bias_rows=bucket_bias_rows, embed_cotangent=embed_cotangent)


epsilon = 1e-06
highest_precision = lax.Precision.HIGHEST

@jax.custom_vjp
def low(v):
    return lax.optimization_barrier(v.astype(jnp.bfloat16)).astype(jnp.float32)

@jax.custom_vjp
def low_back(v):
    return v

def low_keep(v):
    return (low(v), None)

def low_pass(kept, grad):
    return (grad,)

def back_keep(v):
    return (v, None)

def back_low(kept, grad):
    return (low(grad),)
low.defvjp(low_keep, low_pass)
low_back.defvjp(back_keep, back_low)

def bucket_table(length):
    relative = np.arange(length)[None, :] - np.arange(length)[:, None]
    upper_half = (relative > 0).astype(np.int64) * 16
    distance = np.abs(relative)
    scaled = np.log(np.maximum(distance, 1) / 8.0) / np.log(16.0) * 8.0
    far_bucket = np.minimum(8 + scaled.astype(np.int64), 15)
    return (upper_half + np.where(distance < 8, distance, far_bucket)).astype(np.int32)

def rms_scale(values, scale_gain):
    return values * lax.rsqrt(lax.optimization_barrier(jnp.mean(values * values, axis=-1, keepdims=True)) + epsilon) * scale_gain

def matmul(left_side, right_side):
    return jnp.dot(left_side, right_side, precision=highest_precision, preferred_element_type=jnp.float32)

def layer_block(block_tokens, block_lengths, params):
    query_weight, key_weight, value_weight, out_weight, gate_weight, up_weight, down_weight, proj_weight, attn_gain, ffn_gain, final_gain, bucket_bias_rows = params
    doc_count = block_tokens.shape[0]
    token_rows = block_tokens.reshape(-1, D)
    normed_one = low(rms_scale(token_rows, attn_gain))
    queries = low(low_back(matmul(normed_one, query_weight))).reshape(doc_count, SLOT, H, HEAD)
    keys = low(low_back(matmul(normed_one, key_weight))).reshape(doc_count, SLOT, H, HEAD)
    values = low(low_back(matmul(normed_one, value_weight))).reshape(doc_count, SLOT, H, HEAD)
    buckets = jnp.asarray(bucket_table(SLOT))
    relative_position_bias = jnp.transpose(bucket_bias_rows[buckets], (2, 0, 1))
    scores = jnp.einsum('bqhe,bkhe->bhqk', queries, keys, precision=highest_precision) + relative_position_bias[None]
    scores = low_back(scores)
    key_valid = jnp.arange(SLOT)[None, :] < block_lengths[:, None]
    scores = jnp.where(key_valid[:, None, None, :], scores, -1e+30)
    row_top = lax.optimization_barrier(jnp.max(scores, axis=-1, keepdims=True))
    exponent = jnp.exp(scores - row_top)
    probs = exponent / lax.optimization_barrier(jnp.sum(exponent, axis=-1, keepdims=True))
    mixed_heads = jnp.einsum('bhqk,bkhe->bqhe', low(probs), values, precision=highest_precision)
    mixed_heads = low(low_back(mixed_heads.reshape(-1, D)))
    hidden_state = token_rows + low_back(matmul(mixed_heads, out_weight))
    normed_two = low(rms_scale(hidden_state, ffn_gain))
    gate_value = low_back(matmul(normed_two, gate_weight))
    upward = low_back(matmul(normed_two, up_weight))
    inner_value = low(jax.nn.gelu(gate_value, approximate=True) * upward)
    after_ffn = hidden_state + low_back(matmul(inner_value, down_weight))
    final_normed = low(rms_scale(after_ffn, final_gain))
    return matmul(final_normed, proj_weight).reshape(doc_count, SLOT, PROJ)

def reference(tokens, doc_lengths, query_weight, key_weight, value_weight, out_weight, gate_weight, up_weight, down_weight, proj_weight, attn_gain, ffn_gain, final_gain, bucket_bias_rows, embed_cotangent):
    params = (query_weight.astype(jnp.float32), key_weight.astype(jnp.float32), value_weight.astype(jnp.float32), out_weight.astype(jnp.float32), gate_weight.astype(jnp.float32), up_weight.astype(jnp.float32), down_weight.astype(jnp.float32), proj_weight.astype(jnp.float32), attn_gain.astype(jnp.float32), ffn_gain.astype(jnp.float32), final_gain.astype(jnp.float32), bucket_bias_rows.astype(jnp.float32))
    token_rows = tokens.astype(jnp.float32)
    lengths = doc_lengths.reshape(DOCS // 8, 8)
    checked = jax.checkpoint(layer_block)

    def forward_pass(all_tokens, all_params):
        blocks = all_tokens.reshape(DOCS // 8, 8, SLOT, D)
        result = lax.map(lambda block_pair: checked(block_pair[0], block_pair[1], all_params), (blocks, lengths))
        return result.reshape(DOCS, SLOT, PROJ)
    embedded, pullback = jax.vjp(forward_pass, token_rows, params)
    tokens_grad, grads = pullback(embed_cotangent.astype(jnp.float32))
    return (embedded.astype(jnp.bfloat16), tokens_grad, grads[0], grads[1], grads[2], grads[3], grads[4], grads[5], grads[6], grads[7], grads[8], grads[9], grads[10], grads[11])
```

```python
import functools

import jax
import jax.numpy as jnp
import numpy as np
from jax import lax
from jax.experimental import pallas as pl
from jax.experimental.pallas import tpu as pltpu
from jax.sharding import PartitionSpec as P

D = 768
H = 12
HEAD = 64
FF = 2048
PROJ = 128
BUCKETS = 32
SLOT = 512
BLOCK = 128
SEQ = 4
SHARD = D // SEQ
EPSILON = 1e-06
BIG_NEGATIVE = -1e30
GELU_A = 0.7978845608028654
GELU_B = 0.044715

F32 = jnp.float32
BF16 = jnp.bfloat16
VMEM = pl.BlockSpec(memory_space=pltpu.VMEM)
SMEM = pl.BlockSpec(memory_space=pltpu.SMEM)
ANY = pl.BlockSpec(memory_space=pl.ANY)
MIB = 1 << 20


def shape(dims, kind):
    return jax.ShapeDtypeStruct(dims, kind)


def params(mib):
    return pltpu.CompilerParams(vmem_limit_bytes=mib * MIB)


def cost(flops, data):
    return pl.CostEstimate(flops=int(flops), bytes_accessed=int(data), transcendentals=0)


def bucket_of(relative):
    distance = np.abs(relative)
    scaled = np.log(np.maximum(distance, 1) / 8.0) / np.log(16.0) * 8.0
    far_bucket = np.minimum(8 + scaled.astype(np.int64), 15)
    return (relative > 0) * 16 + np.where(distance < 8, distance, far_bucket)


def skew_buckets():
    lanes = (np.arange(SLOT) + SLOT // 2) % SLOT - SLOT // 2
    relative = np.arange(8)[:, None] - lanes[None, :]
    return bucket_of(relative).astype(np.int32)


def dot(left, right):
    return jnp.dot(left, right, preferred_element_type=F32)


def dot_t(left, right):
    return lax.dot_general(left, right, (((1,), (1,)), ((), ())), preferred_element_type=F32)


def start_all(copies):
    for copy in copies:
        copy.start()


def wait_all(copies):
    for copy in copies:
        copy.wait()


def weight_copies(ids, pieces, target, sems, first, columns, target_columns):
    me, y = ids[0], ids[1]
    rows = pieces[0].shape[0]
    half = rows // 2
    starts = (
        me * rows,
        (me ^ 1) * rows,
        (me ^ 2) * rows + y * half,
        (me ^ 2) * rows + (1 - y) * half,
        (me ^ 3) * rows + y * half,
        (me ^ 3) * rows + (1 - y) * half,
    )
    sizes = (rows, rows, half, half, half, half)
    copies = []
    for number, (piece, begin, size) in enumerate(zip(pieces, starts, sizes)):
        begin = pl.multiple_of(begin, 16)
        column = columns[0] if number < 2 else columns[1]
        width = target_columns[1]
        copies.append(
            pltpu.make_async_copy(
                piece.at[:, pl.ds(column, width)],
                target.at[pl.ds(begin, size), pl.ds(target_columns[0], width)],
                sems.at[first + number],
            )
        )
    return copies


def relative_copies(ids, source, target, sems, half):
    me, y = ids[0], ids[1]
    x, core = me >> 1, me & 1
    copies = []
    for number in range(8):
        core_own, x_own, y_own = number >> 2, (number >> 1) & 1, number & 1
        from_core = core if core_own else 1 - core
        from_x = x if x_own else 1 - x
        from_y = y if y_own else 1 - y
        begin = pl.multiple_of(((from_x * 2 + from_core) * 2 + from_y) * half, 16)
        copies.append(
            pltpu.make_async_copy(
                source.at[pl.ds(begin, half), :],
                target.at[pl.ds(number * half, half), :],
                sems.at[number],
            )
        )
    return copies


def inverse_rms(values):
    return lax.rsqrt(jnp.mean(values * values, axis=-1, keepdims=True) + EPSILON)


def norm_backward(values, gain, incoming):
    r = inverse_rms(values)
    weighted = gain * incoming
    inner = jnp.mean(weighted * values, axis=-1, keepdims=True)
    gradient = r * weighted - values * (r * r * r * inner)
    gain_part = jnp.sum(incoming * values * r, axis=0, keepdims=True)
    return gradient, gain_part


def first_norm_kernel(ids, own, from_x, from_core, from_far, gain, tok, cot, n1, n1t, held, sems):
    me = ids[0]
    copies = [
        pltpu.make_async_copy(
            piece, held.at[pl.ds(pl.multiple_of((me ^ flip) * BLOCK, BLOCK), BLOCK), :], sems.at[i]
        )
        for i, (piece, flip) in enumerate(
            ((own.at[me], 0), (from_x, 2), (from_core, 1), (from_far, 3))
        )
    ]
    start_all(copies)
    wait_all(copies)
    for block in range(SLOT // BLOCK):
        rows = pl.ds(block * BLOCK, BLOCK)
        here = held[rows, 0:D]
        tok[rows, :] = here
        cot[rows, :] = held[rows, D : D + PROJ]
        values = here.astype(F32)
        normed = (values * inverse_rms(values) * gain[...]).astype(BF16)
        n1[rows, :] = normed
        n1t[:, rows] = normed.T


def first_norm(ids, own, from_x, from_core, from_far, gain):
    return pl.pallas_call(
        first_norm_kernel,
        out_shape=(
            shape((SLOT, D), BF16),
            shape((SLOT, PROJ), BF16),
            shape((SLOT, D), BF16),
            shape((D, SLOT), BF16),
        ),
        in_specs=[SMEM, ANY, ANY, ANY, ANY, VMEM],
        out_specs=(VMEM,) * 4,
        scratch_shapes=[pltpu.VMEM((SLOT, D + PROJ), BF16), pltpu.SemaphoreType.DMA((4,))],
        compiler_params=params(32),
        cost_estimate=cost(0, 4e6),
        name="first_norm",
    )(ids, own, from_x, from_core, from_far, gain)


def qkv_kernel(ids, n1, *refs):
    pieces, (out, weight, sems) = refs[:6], refs[6:]
    copies = weight_copies(ids, pieces, weight, sems, 0, (0, 0), (0, 3 * D))
    start_all(copies)
    wait_all(copies)

    def step(tile, carry):
        columns = pl.ds(pl.multiple_of(tile * 256, 256), 256)
        out[:, columns] = dot(n1[...], weight[:, columns]).astype(BF16)
        return carry

    lax.fori_loop(0, 3 * D // 256, step, 0)


def qkv_project(ids, n1, pieces):
    return pl.pallas_call(
        qkv_kernel,
        out_shape=shape((SLOT, 3 * D), BF16),
        in_specs=[SMEM, VMEM] + [ANY] * 6,
        out_specs=VMEM,
        scratch_shapes=[pltpu.VMEM((D, 3 * D), BF16), pltpu.SemaphoreType.DMA((6,))],
        compiler_params=params(32),
        cost_estimate=cost(2 * SLOT * D * 3 * D, 8e6),
        name="qkv_project",
    )(ids, n1, *pieces)


HALF_Q = 256


def attention_kernel(ids, q, k, v, skew, et, linv, ot, o, bias):
    length = ids[2]
    k_pair = k[...]
    vt = v[...].T
    qt = q[...].T
    row_in_pair = lax.broadcasted_iota(jnp.int32, (2 * HEAD, SLOT), 0)
    key_index = lax.broadcasted_iota(jnp.int32, (SLOT, HALF_Q), 0)
    for head in range(2):
        base = skew[head]
        for group in range(BLOCK // 8):
            bias[pl.ds(group * 8, 8), :] = pltpu.roll(base, 8 * group, 1) if group else base
        below = base[0:1, 255:256]
        above = base[0:1, 256:257]
        in_head = (row_in_pair >= HEAD * head) & (row_in_pair < HEAD * (head + 1))
        qt_head = jnp.where(in_head, qt, jnp.zeros_like(qt))
        for part in range(SLOT // HALF_Q):
            raw = dot(k_pair, qt_head[:, part * HALF_Q : (part + 1) * HALF_Q])
            rows = []
            for key_block in range(4):
                cells = []
                for sub in range(HALF_Q // BLOCK):
                    query_block = part * (HALF_Q // BLOCK) + sub
                    cell = raw[
                        key_block * BLOCK : (key_block + 1) * BLOCK,
                        sub * BLOCK : (sub + 1) * BLOCK,
                    ]
                    apart = key_block - query_block
                    if apart >= 2:
                        cell = cell + above
                    elif apart <= -2:
                        cell = cell + below
                    else:
                        lane = (-apart * BLOCK) % SLOT
                        cell = cell + bias[:, lane : lane + BLOCK]
                    cells.append(cell)
                rows.append(jnp.concatenate(cells, axis=1))
            scores = jnp.concatenate(rows, axis=0)
            scores = jnp.where(key_index < length, scores, BIG_NEGATIVE)
            top = jnp.max(scores, axis=0, keepdims=True)
            weights = jnp.exp(scores - top)
            inverse = 1.0 / jnp.sum(weights, axis=0, keepdims=True)
            low = weights.astype(BF16)
            columns = pl.ds(part * HALF_Q, HALF_Q)
            et[head, :, columns] = low
            linv[head, :, columns] = inverse
            mixed = dot(vt[head * HEAD : (head + 1) * HEAD, :], low) * inverse
            ot[pl.ds(head * HEAD, HEAD), columns] = mixed.astype(BF16)
    o[...] = ot[...].T


def attention(ids, qkv, skew):
    pair = 2 * HEAD
    pairs = H // 2
    return pl.pallas_call(
        attention_kernel,
        grid=(pairs,),
        out_shape=(
            shape((H, SLOT, SLOT), BF16),
            shape((H, 1, SLOT), F32),
            shape((D, SLOT), BF16),
            shape((SLOT, D), BF16),
        ),
        in_specs=[
            SMEM,
            pl.BlockSpec((SLOT, pair), lambda i: (0, i)),
            pl.BlockSpec((SLOT, pair), lambda i: (0, pairs + i)),
            pl.BlockSpec((SLOT, pair), lambda i: (0, 2 * pairs + i)),
            pl.BlockSpec((2, 8, SLOT), lambda i: (i, 0, 0)),
        ],
        out_specs=(
            pl.BlockSpec((2, SLOT, SLOT), lambda i: (i, 0, 0)),
            pl.BlockSpec((2, 1, SLOT), lambda i: (i, 0, 0)),
            pl.BlockSpec((pair, SLOT), lambda i: (i, 0)),
            pl.BlockSpec((SLOT, pair), lambda i: (0, i)),
        ),
        scratch_shapes=[pltpu.VMEM((BLOCK, SLOT), F32)],
        compiler_params=params(32),
        cost_estimate=cost(4 * H * SLOT * SLOT * 256, 10e6),
        name="attention",
    )(ids, qkv, qkv, qkv, skew)


def hidden_kernel(ids, tok, mixed, gain, *refs):
    pieces, (hidden, n2, n2t, weight, sems) = refs[:6], refs[6:]
    copies = weight_copies(ids, pieces, weight, sems, 0, (0, 0), (0, D))
    start_all(copies)
    wait_all(copies)
    for block in range(2):
        rows = pl.ds(block * 256, 256)
        values = tok[rows, :].astype(F32) + dot(mixed[rows, :], weight[...])
        hidden[rows, :] = values
        normed = (values * inverse_rms(values) * gain[...]).astype(BF16)
        n2[rows, :] = normed
        n2t[:, rows] = normed.T


def hidden_project(ids, tok, mixed, gain, pieces):
    return pl.pallas_call(
        hidden_kernel,
        out_shape=(shape((SLOT, D), F32), shape((SLOT, D), BF16), shape((D, SLOT), BF16)),
        in_specs=[SMEM, VMEM, VMEM, VMEM] + [ANY] * 6,
        out_specs=(VMEM,) * 3,
        scratch_shapes=[pltpu.VMEM((D, D), BF16), pltpu.SemaphoreType.DMA((6,))],
        compiler_params=params(32),
        cost_estimate=cost(2 * SLOT * D * D, 6e6),
        name="hidden_project",
    )(ids, tok, mixed, gain, *pieces)


def gated_kernel(own_columns, ids, n2, *refs):
    gate_pieces, up_pieces = refs[:6], refs[6:12]
    inner, innert, slope, level, gate, up, sems = refs[12:]
    copies = weight_copies(ids, gate_pieces, gate, sems, 0, (own_columns[0], 0), (0, FF))
    copies += weight_copies(ids, up_pieces, up, sems, 6, (own_columns[1], 0), (0, FF))
    start_all(copies)
    wait_all(copies)

    def step(tile, carry):
        columns = pl.ds(pl.multiple_of(tile * 256, 256), 256)
        g = dot(n2[...], gate[:, columns])
        u = dot(n2[...], up[:, columns])
        square = g * g
        t = jnp.tanh(GELU_A * g * (1.0 + GELU_B * square))
        half_up = 0.5 * (1.0 + t)
        activated = g * half_up
        derivative = half_up + 0.5 * g * (1.0 - t * t) * (GELU_A * (1.0 + 3 * GELU_B * square))
        value = (activated * u).astype(BF16)
        inner[:, columns] = value
        innert[columns, :] = value.T
        slope[:, columns] = (derivative * u).astype(BF16)
        level[:, columns] = activated.astype(BF16)
        return carry

    lax.fori_loop(0, FF // 256, step, 0)


def gated(ids, n2, gate_pieces, up_pieces, own_columns):
    return pl.pallas_call(
        functools.partial(gated_kernel, own_columns),
        out_shape=(
            shape((SLOT, FF), BF16),
            shape((FF, SLOT), BF16),
            shape((SLOT, FF), BF16),
            shape((SLOT, FF), BF16),
        ),
        in_specs=[SMEM, VMEM] + [ANY] * 12,
        out_specs=(VMEM,) * 4,
        scratch_shapes=[
            pltpu.VMEM((D, FF), BF16),
            pltpu.VMEM((D, FF), BF16),
            pltpu.SemaphoreType.DMA((12,)),
        ],
        compiler_params=params(40),
        cost_estimate=cost(4 * SLOT * D * FF, 16e6),
        name="gated",
    )(ids, n2, *gate_pieces, *up_pieces)


def final_kernel(own_proj, ids, hidden, inner, cot, gain, *refs):
    down_pieces, proj_pieces = refs[:6], refs[6:12]
    embedded, after_grad, down_in, fnt, gain_grad, down, proj, sems = refs[12:]
    copies = weight_copies(ids, down_pieces, down, sems, 0, (0, 0), (0, D))
    copies += weight_copies(ids, proj_pieces, proj, sems, 6, own_proj, (0, PROJ))
    start_all(copies)
    wait_all(copies)
    total = jnp.zeros((1, D), F32)
    for block in range(2):
        rows = pl.ds(block * 256, 256)
        values = hidden[rows, :] + dot(inner[rows, :], down[...])
        normed = (values * inverse_rms(values) * gain[...]).astype(BF16)
        fnt[:, rows] = normed.T
        embedded[rows, :] = dot(normed, proj[...]).astype(BF16)
        gradient, part = norm_backward(values, gain[...], dot_t(cot[rows, :], proj[...]))
        after_grad[rows, :] = gradient
        down_in[rows, :] = gradient.astype(BF16)
        total = total + part
    gain_grad[...] = total


def final_stage(ids, hidden, inner, cot, gain, down_pieces, proj_pieces, own_proj):
    return pl.pallas_call(
        functools.partial(final_kernel, own_proj),
        out_shape=(
            shape((SLOT, PROJ), BF16),
            shape((SLOT, D), F32),
            shape((SLOT, D), BF16),
            shape((D, SLOT), BF16),
            shape((1, D), F32),
        ),
        in_specs=[SMEM, VMEM, VMEM, VMEM, VMEM] + [ANY] * 12,
        out_specs=(VMEM,) * 5,
        scratch_shapes=[
            pltpu.VMEM((FF, D), BF16),
            pltpu.VMEM((D, PROJ), BF16),
            pltpu.SemaphoreType.DMA((12,)),
        ],
        compiler_params=params(40),
        cost_estimate=cost(2 * SLOT * D * (FF + 2 * PROJ), 12e6),
        name="final_stage",
    )(ids, hidden, inner, cot, gain, *down_pieces, *proj_pieces)


def weight_grad_kernel(half, ids, source, right, send, keep, left, sems):
    @pl.when(pl.program_id(0) == 0)
    def load():
        copies = relative_copies(ids, source, left, sems, half)
        start_all(copies)
        wait_all(copies)

    send[...] = dot(left[0 : 4 * half, :], right[...]).astype(BF16)
    keep[...] = dot(left[4 * half :, :], right[...]).astype(BF16)


def weight_grad(ids, source, right, name):
    rows, width = source.shape[0], right.shape[1]
    tile = 512 if width % 512 == 0 else (256 if width % 256 == 0 else 128)
    half = rows // 8
    return pl.pallas_call(
        functools.partial(weight_grad_kernel, half),
        grid=(width // tile,),
        out_shape=(shape((rows // 2, width), BF16),) * 2,
        in_specs=[SMEM, ANY, pl.BlockSpec((SLOT, tile), lambda i: (0, i))],
        out_specs=(pl.BlockSpec((rows // 2, tile), lambda i: (0, i)),) * 2,
        scratch_shapes=[pltpu.VMEM((rows, SLOT), BF16), pltpu.SemaphoreType.DMA((8,))],
        compiler_params=params(32),
        cost_estimate=cost(2 * SLOT * rows * width, 2 * rows * (width + SLOT)),
        name=name,
    )(ids, source, right)


def inner_grad_kernel(ids, down_in, slope, level, *refs):
    pieces, (gate_grad, up_grad, down, sems) = refs[:6], refs[6:]
    copies = weight_copies(ids, pieces, down, sems, 0, (0, 0), (0, D))
    start_all(copies)
    wait_all(copies)

    def step(tile, carry):
        columns = pl.ds(pl.multiple_of(tile * 256, 256), 256)
        incoming = dot_t(down_in[...], down[columns, :])
        gate_grad[:, columns] = (incoming * slope[:, columns].astype(F32)).astype(BF16)
        up_grad[:, columns] = (incoming * level[:, columns].astype(F32)).astype(BF16)
        return carry

    lax.fori_loop(0, FF // 256, step, 0)


def inner_grads(ids, down_in, slope, level, pieces):
    return pl.pallas_call(
        inner_grad_kernel,
        out_shape=(shape((SLOT, FF), BF16),) * 2,
        in_specs=[SMEM, VMEM, VMEM, VMEM] + [ANY] * 6,
        out_specs=(VMEM,) * 2,
        scratch_shapes=[pltpu.VMEM((FF, D), BF16), pltpu.SemaphoreType.DMA((6,))],
        compiler_params=params(40),
        cost_estimate=cost(2 * SLOT * D * FF, 12e6),
        name="inner_grads",
    )(ids, down_in, slope, level, *pieces)


def hidden_grad_kernel(own_columns, ids, gate_grad, up_grad, hidden, after_grad, gain, *refs):
    gate_pieces, up_pieces = refs[:6], refs[6:12]
    hidden_grad, attn_in, gain_grad, gate, up, sems = refs[12:]
    copies = weight_copies(ids, gate_pieces, gate, sems, 0, (own_columns[0], 0), (0, FF))
    copies += weight_copies(ids, up_pieces, up, sems, 6, (own_columns[1], 0), (0, FF))
    start_all(copies)
    wait_all(copies)
    total = jnp.zeros((1, D), F32)
    for block in range(2):
        rows = pl.ds(block * 256, 256)
        incoming = dot_t(gate_grad[rows, :], gate[...]) + dot_t(up_grad[rows, :], up[...])
        gradient, part = norm_backward(hidden[rows, :], gain[...], incoming)
        gradient = gradient + after_grad[rows, :]
        hidden_grad[rows, :] = gradient
        attn_in[rows, :] = gradient.astype(BF16)
        total = total + part
    gain_grad[...] = total


def hidden_grads(ids, gate_grad, up_grad, hidden, after_grad, gain, gate_pieces, up_pieces, own):
    return pl.pallas_call(
        functools.partial(hidden_grad_kernel, own),
        out_shape=(shape((SLOT, D), F32), shape((SLOT, D), BF16), shape((1, D), F32)),
        in_specs=[SMEM, VMEM, VMEM, VMEM, VMEM, VMEM] + [ANY] * 12,
        out_specs=(VMEM,) * 3,
        scratch_shapes=[
            pltpu.VMEM((D, FF), BF16),
            pltpu.VMEM((D, FF), BF16),
            pltpu.SemaphoreType.DMA((12,)),
        ],
        compiler_params=params(40),
        cost_estimate=cost(4 * SLOT * D * FF, 16e6),
        name="hidden_grads",
    )(ids, gate_grad, up_grad, hidden, after_grad, gain, *gate_pieces, *up_pieces)


def mixed_grad_kernel(ids, attn_in, *refs):
    pieces, (out, weight, sems) = refs[:6], refs[6:]
    copies = weight_copies(ids, pieces, weight, sems, 0, (0, 0), (0, D))
    start_all(copies)
    wait_all(copies)
    out[...] = dot_t(attn_in[...], weight[...]).astype(BF16)


def mixed_grads(ids, attn_in, pieces):
    return pl.pallas_call(
        mixed_grad_kernel,
        out_shape=shape((SLOT, D), BF16),
        in_specs=[SMEM, VMEM] + [ANY] * 6,
        out_specs=VMEM,
        scratch_shapes=[pltpu.VMEM((D, D), BF16), pltpu.SemaphoreType.DMA((6,))],
        compiler_params=params(32),
        cost_estimate=cost(2 * SLOT * D * D, 4e6),
        name="mixed_grads",
    )(ids, attn_in, *pieces)


def attention_back_kernel(q, k, v, et, linv, ot, do, dq, dk, dv, bias_grad, dqt, near):
    lane_in_pair = lax.broadcasted_iota(jnp.int32, (SLOT, 2 * HEAD), 1)
    q_pair, v_pair = q[...], v[...]
    kt = k[...].T
    out_gradt = do[...].astype(F32).T
    scaled = []
    deltas = []
    for head in range(2):
        rows = slice(head * HEAD, (head + 1) * HEAD)
        low = (out_gradt[rows, :] * linv[head]).astype(BF16)
        scaled.append(low)
        deltas.append(
            jnp.sum(low.astype(F32) * ot[rows, :].astype(F32), axis=0, keepdims=True)
        )
    scaled_t = jnp.concatenate(scaled, axis=0)
    scaled_pair = scaled_t.T
    zeros = jnp.zeros((HEAD, SLOT), BF16)
    key_total = jnp.zeros((SLOT, 2 * HEAD), F32)
    value_total = jnp.zeros((SLOT, 2 * HEAD), F32)
    for head in range(2):
        in_head = (lane_in_pair >= head * HEAD) & (lane_in_pair < (head + 1) * HEAD)
        q_head = jnp.where(in_head, q_pair, jnp.zeros_like(q_pair))
        do_head = jnp.where(in_head, scaled_pair, jnp.zeros_like(scaled_pair))
        dot_head = jnp.concatenate(
            [scaled[head], zeros] if head == 0 else [zeros, scaled[head]], axis=0
        )
        near_sums = {-1: None, 0: None, 1: None}
        far_sums = {-1: None, 1: None}
        for part in range(SLOT // HALF_Q):
            columns = slice(part * HALF_Q, (part + 1) * HALF_Q)
            prob_grad = dot(v_pair, dot_head[:, columns])
            low_weights = et[head, :, columns]
            score_grad = low_weights.astype(F32) * (prob_grad - deltas[head][:, columns])
            low = score_grad.astype(BF16)
            key_total = key_total + dot(low, q_head[columns, :])
            value_total = value_total + dot(low_weights, do_head[columns, :])
            dqt[pl.ds(head * HEAD, HEAD), columns] = dot(
                kt[head * HEAD : (head + 1) * HEAD, :], low
            ).astype(BF16)
            for key_block in range(4):
                for sub in range(HALF_Q // BLOCK):
                    apart = key_block - part * (HALF_Q // BLOCK) - sub
                    cell = score_grad[
                        key_block * BLOCK : (key_block + 1) * BLOCK,
                        sub * BLOCK : (sub + 1) * BLOCK,
                    ]
                    if abs(apart) >= 2:
                        side = 1 if apart > 0 else -1
                        folded = jnp.sum(cell.reshape(BLOCK // 8, 8, BLOCK), axis=0)
                        old = far_sums[side]
                        far_sums[side] = folded if old is None else old + folded
                    else:
                        old = near_sums[apart]
                        near_sums[apart] = cell if old is None else old + cell
        near[...] = jnp.zeros_like(near)
        for apart in (-1, 0, 1):
            lane = (-apart * BLOCK) % SLOT
            near[:, lane : lane + BLOCK] = near_sums[apart]
        folded = near[0:8, :]
        for group in range(1, BLOCK // 8):
            folded = folded + pltpu.roll(near[group * 8 : group * 8 + 8, :], SLOT - 8 * group, 1)
        bias_grad[head, :, 0:SLOT] = folded
        bias_grad[head, :, SLOT : SLOT + BLOCK] = far_sums[-1]
        bias_grad[head, :, SLOT + BLOCK : SLOT + 2 * BLOCK] = far_sums[1]
    dk[...] = key_total.astype(BF16)
    dv[...] = value_total.astype(BF16)
    dq[...] = dqt[...].T


def attention_back(qkv, et, linv, ot, do):
    pair = 2 * HEAD
    pairs = H // 2
    wide = pl.BlockSpec((SLOT, pair), lambda i: (0, i))
    return pl.pallas_call(
        attention_back_kernel,
        grid=(pairs,),
        out_shape=(shape((SLOT, D), BF16),) * 3 + (shape((H, 8, SLOT + 2 * BLOCK), F32),),
        in_specs=[
            pl.BlockSpec((SLOT, pair), lambda i: (0, i)),
            pl.BlockSpec((SLOT, pair), lambda i: (0, pairs + i)),
            pl.BlockSpec((SLOT, pair), lambda i: (0, 2 * pairs + i)),
            pl.BlockSpec((2, SLOT, SLOT), lambda i: (i, 0, 0)),
            pl.BlockSpec((2, 1, SLOT), lambda i: (i, 0, 0)),
            pl.BlockSpec((pair, SLOT), lambda i: (i, 0)),
            wide,
        ],
        out_specs=(wide,) * 3 + (pl.BlockSpec((2, 8, SLOT + 2 * BLOCK), lambda i: (i, 0, 0)),),
        scratch_shapes=[pltpu.VMEM((pair, SLOT), BF16), pltpu.VMEM((BLOCK, SLOT), F32)],
        compiler_params=params(32),
        cost_estimate=cost(8 * H * SLOT * SLOT * 256, 12e6),
        name="attention_back",
    )(qkv, qkv, qkv, et, linv, ot, do)


def token_grad_kernel(ids, dq, dk, dv, hidden_grad, tok, gain, *refs):
    pieces, (out, gain_grad, weight, sems) = refs[:6], refs[6:]
    copies = weight_copies(ids, pieces, weight, sems, 0, (0, 0), (0, 3 * D))
    start_all(copies)
    wait_all(copies)
    total = jnp.zeros((1, D), F32)
    for block in range(4):
        rows = pl.ds(block * BLOCK, BLOCK)
        incoming = (
            dot_t(dq[rows, :], weight[:, 0:D])
            + dot_t(dk[rows, :], weight[:, D : 2 * D])
            + dot_t(dv[rows, :], weight[:, 2 * D : 3 * D])
        )
        gradient, part = norm_backward(tok[rows, :].astype(F32), gain[...], incoming)
        out[block] = (hidden_grad[rows, :] + gradient).astype(BF16)
        total = total + part
    gain_grad[...] = total


def token_grads(ids, dq, dk, dv, hidden_grad, tok, gain, pieces):
    return pl.pallas_call(
        token_grad_kernel,
        out_shape=(shape((SEQ, BLOCK, D), BF16), shape((1, D), F32)),
        in_specs=[SMEM, VMEM, VMEM, VMEM, VMEM, VMEM, VMEM] + [ANY] * 6,
        out_specs=(VMEM,) * 2,
        scratch_shapes=[pltpu.VMEM((D, 3 * D), BF16), pltpu.SemaphoreType.DMA((6,))],
        compiler_params=params(40),
        cost_estimate=cost(6 * SLOT * D * D, 10e6),
        name="token_grads",
    )(ids, dq, dk, dv, hidden_grad, tok, gain, *pieces)


def exchange(value, axis, flip, size):
    return lax.ppermute(value, axis, [(i, i ^ flip) for i in range(size)])


def after(value, *others):
    return lax.optimization_barrier((value,) + others)[0]


def reduce_chunk(send, keep, groups):
    half = send.shape[0] // 4
    from_core = exchange(send, "seq", 1, SEQ)

    def add(*terms):
        total = terms[0].astype(F32)
        for term in terms[1:]:
            total = total + term.astype(F32)
        return total.astype(BF16)

    to_x = add(keep[: 2 * half], from_core[: 2 * half])
    from_x = exchange(to_x, "seq", 2, SEQ)
    to_y = add(keep[2 * half : 3 * half], from_core[2 * half : 3 * half], from_x[:half])
    from_y = exchange(to_y, "dp", 1, groups)
    total = add(keep[3 * half :], from_core[3 * half :], from_x[half:], from_y)
    step = 2
    while step < groups:
        total = add(total, exchange(total, "dp", step, groups))
        step *= 2
    return total, exchange(total, "dp", 1, groups)


def per_device(
    groups,
    tokens,
    doc_lengths,
    query_weight,
    key_weight,
    value_weight,
    out_weight,
    gate_weight,
    up_weight,
    down_weight,
    proj_weight,
    attn_gain,
    ffn_gain,
    final_gain,
    bucket_bias_rows,
    embed_cotangent,
):
    me = lax.axis_index("seq")
    y = lax.axis_index("dp") % 2
    ids = jnp.stack([me, y, doc_lengths[me]]).astype(jnp.int32)
    attn_gain, ffn_gain, final_gain = (
        gain.reshape(1, D) for gain in (attn_gain, ffn_gain, final_gain)
    )

    packed = jnp.concatenate([tokens, embed_cotangent], axis=-1)

    def block_for(device):
        return lax.dynamic_index_in_dim(packed, device, 0, keepdims=False)

    def half_rows(*weights):
        half = weights[0].shape[0] // 2
        return jnp.concatenate(
            [lax.dynamic_slice_in_dim(w, y * half, half, 0) for w in weights], axis=1
        )

    def gather(mine, previous):
        if previous is not None:
            mine = after(mine, previous)
        from_x = exchange(mine, "seq", 2, SEQ)
        from_y = exchange(from_x, "dp", 1, groups)
        return from_x, from_y, exchange(from_x, "seq", 1, SEQ), exchange(from_y, "seq", 1, SEQ)

    qkv_half = half_rows(query_weight, key_weight, value_weight)
    qkv_parts = gather(qkv_half, None)
    tok_x = exchange(after(block_for(me ^ 2), qkv_parts[0]), "seq", 2, SEQ)
    tok_far = exchange(after(block_for(me ^ 3), qkv_parts[0]), "seq", 3, SEQ)
    tok_core = exchange(block_for(me ^ 1), "seq", 1, SEQ)
    qkv_own = jnp.concatenate([query_weight, key_weight, value_weight], axis=1)
    qkv_sibling = exchange(qkv_own, "seq", 1, SEQ)
    rest_own = jnp.concatenate([out_weight, proj_weight, gate_weight, up_weight], axis=1)
    rest_sibling = exchange(rest_own, "seq", 1, SEQ)
    down_sibling = exchange(down_weight, "seq", 1, SEQ)
    out_parts = gather(half_rows(out_weight, proj_weight), tok_x)
    gate_parts = gather(half_rows(gate_weight), out_parts[0])
    up_parts = gather(half_rows(up_weight), gate_parts[0])
    down_parts = gather(half_rows(down_weight), up_parts[0])

    qkv_pieces = (qkv_own, qkv_sibling) + qkv_parts
    out_pieces = (rest_own, rest_sibling) + out_parts
    gate_pieces = (rest_own, rest_sibling) + gate_parts
    up_pieces = (rest_own, rest_sibling) + up_parts
    down_pieces = (down_weight, down_sibling) + down_parts
    own_proj = (D, D)
    own_gated = (D + PROJ, D + PROJ + FF)

    skew_table = skew_buckets().reshape(-1)
    indicator = jnp.asarray(
        (skew_table[None, :] == np.arange(BUCKETS)[:, None]).astype(np.float32)
    )
    skew = lax.dot_general(
        bucket_bias_rows,
        indicator,
        (((0,), (0,)), ((), ())),
        precision=lax.Precision.HIGHEST,
    ).reshape(H, 8, SLOT)

    tok, cot, n1, n1t = first_norm(ids, packed, tok_x, tok_core, tok_far, attn_gain)
    qkv = qkv_project(ids, n1, qkv_pieces)
    et, linv, ot, mixed = attention(ids, qkv, skew)
    hidden, n2, n2t = hidden_project(ids, tok, mixed, ffn_gain, out_pieces)
    inner, innert, slope, level = gated(ids, n2, gate_pieces, up_pieces, own_gated)
    embedded, after_grad, down_in, fnt, final_part = final_stage(
        ids, hidden, inner, cot, final_gain, down_pieces, out_pieces, own_proj
    )

    down_sum = reduce_chunk(*weight_grad(ids, innert, down_in, "down_weight_grad"), groups)
    gate_grad, up_grad = inner_grads(ids, down_in, slope, level, down_pieces)
    gate_sum = reduce_chunk(*weight_grad(ids, n2t, gate_grad, "gate_weight_grad"), groups)
    up_sum = reduce_chunk(*weight_grad(ids, n2t, up_grad, "up_weight_grad"), groups)
    hidden_grad, attn_in, ffn_part = hidden_grads(
        ids, gate_grad, up_grad, hidden, after_grad, ffn_gain, gate_pieces, up_pieces, own_gated
    )
    proj_pair = weight_grad(ids, fnt, cot, "proj_weight_grad")
    out_pair = weight_grad(ids, ot, attn_in, "out_weight_grad")
    out_sum = reduce_chunk(
        *(jnp.concatenate(both, axis=1) for both in zip(out_pair, proj_pair)), groups
    )
    mixed_grad = mixed_grads(ids, attn_in, out_pieces)
    dq, dk, dv, bias_part = attention_back(qkv, et, linv, ot, mixed_grad)
    query_pair = weight_grad(ids, n1t, dq, "query_weight_grad")
    key_pair = weight_grad(ids, n1t, dk, "key_weight_grad")
    query_sum = reduce_chunk(*query_pair, groups)
    key_sum = reduce_chunk(*key_pair, groups)
    tokens_part, attn_part = token_grads(
        ids, dq, dk, dv, hidden_grad, tok, attn_gain, qkv_pieces
    )

    far = np.concatenate(
        [np.full((8, BLOCK), 15, np.int32), np.full((8, BLOCK), 31, np.int32)], axis=1
    )
    cells = np.concatenate([skew_buckets(), far], axis=1).reshape(-1)
    table_part = lax.dot_general(
        jnp.asarray((np.arange(BUCKETS)[:, None] == cells[None, :]).astype(np.float32)),
        bias_part.reshape(H, -1),
        (((1,), (1,)), ((), ())),
        precision=lax.Precision.HIGHEST,
    )
    gains = jnp.concatenate([attn_part, ffn_part, final_part], axis=0).T
    small = jnp.concatenate(
        [
            jnp.pad(gains, ((0, 0), (0, 13))),
            jnp.pad(
                table_part.reshape(SEQ, BUCKETS // SEQ, H),
                ((0, 0), (0, SHARD - BUCKETS // SEQ), (0, PROJ - 16 - H)),
            ).reshape(D, PROJ - 16),
        ],
        axis=1,
    )
    small = small.reshape(2, 2, 2, SHARD // 2, PROJ)
    x, core = me // 2, me % 2

    def from_flip(value, dim, own):
        return jnp.where(own == 1, value, jnp.flip(value, dim))

    small = from_flip(from_flip(from_flip(small, 0, x), 1, core), 2, y)
    small = jnp.transpose(small, (1, 0, 2, 3, 4)).reshape(2, D // 2, PROJ).astype(BF16)
    value_pair = weight_grad(ids, n1t, dv, "value_weight_grad")
    value_sum = reduce_chunk(
        *(jnp.concatenate([value_pair[i], small[i]], axis=1) for i in range(2)), groups
    )

    def whole(halves):
        mine, other = halves
        return jnp.where(
            y == 0,
            jnp.concatenate([mine, other], axis=0),
            jnp.concatenate([other, mine], axis=0),
        ).astype(F32)

    def documents(value, kind):
        parts = [lax.dynamic_index_in_dim(value, me, 0, keepdims=False)]
        for flip in (1, 2, 3):
            mine = lax.dynamic_index_in_dim(value, me ^ flip, 0, keepdims=False)
            parts.append(exchange(mine, "seq", flip, SEQ))
        by_flip = jnp.stack(parts)
        ordered = [lax.dynamic_index_in_dim(by_flip, me ^ d, 0) for d in range(SEQ)]
        return jnp.concatenate(ordered, axis=0).astype(kind)

    embedded = documents(embedded.reshape(SEQ, BLOCK, PROJ), BF16)
    tokens_grad = documents(tokens_part, F32)
    out_whole, value_whole = whole(out_sum), whole(value_sum)
    small_whole = value_whole[:, D:]
    return (
        embedded,
        tokens_grad,
        whole(query_sum),
        whole(key_sum),
        value_whole[:, :D],
        out_whole[:, :D],
        whole(gate_sum),
        whole(up_sum),
        whole(down_sum),
        out_whole[:, D:],
        small_whole[:, 0],
        small_whole[:, 1],
        small_whole[:, 2],
        small_whole[: BUCKETS // SEQ, 16 : 16 + H],
    )


def solution(mesh):
    placed = (
        P("dp", "seq", None),
        P("dp"),
        P("seq", None),
        P("seq", None),
        P("seq", None),
        P("seq", None),
        P("seq", None),
        P("seq", None),
        P("seq", None),
        P("seq", None),
        P(),
        P(),
        P(),
        P(),
        P("dp", "seq", None),
    )
    return jax.shard_map(
        functools.partial(per_device, mesh.shape["dp"]),
        mesh=mesh,
        in_specs=placed,
        out_specs=(
            P("dp", "seq", None),
            P("dp", "seq", None),
            P("seq", None),
            P("seq", None),
            P("seq", None),
            P("seq", None),
            P("seq", None),
            P("seq", None),
            P("seq", None),
            P("seq", None),
            P("seq"),
            P("seq"),
            P("seq"),
            P("seq", None),
        ),
        check_vma=False,
    )
```

```python
import functools

import jax
import jax.numpy as jnp
import numpy as np
from jax import lax
from jax.experimental import pallas as pl
from jax.experimental.pallas import tpu as pltpu
from jax.sharding import PartitionSpec as P

D = 768
H = 12
HEAD = 64
FF = 2048
PROJ = 128
BUCKETS = 32
SLOT = 512
BLOCK = 128
SEQ = 4
SHARD = D // SEQ
HALF_FF = FF // 2
WIDE = D + PROJ
TABLE_COLUMN = 16
EPSILON = 1e-06
BIG_NEGATIVE = -1e30
GELU_A = 0.7978845608028654
GELU_B = 0.044715

F32 = jnp.float32
BF16 = jnp.bfloat16
VMEM = pl.BlockSpec(memory_space=pltpu.VMEM)
SMEM = pl.BlockSpec(memory_space=pltpu.SMEM)
ANY = pl.BlockSpec(memory_space=pl.ANY)
MIB = 1 << 20


def shape(dims, kind):
    return jax.ShapeDtypeStruct(dims, kind)


def params():
    return pltpu.CompilerParams(vmem_limit_bytes=20 * MIB)


def bucket_of(relative):
    distance = np.abs(relative)
    scaled = np.log(np.maximum(distance, 1) / 8.0) / np.log(16.0) * 8.0
    far_bucket = np.minimum(8 + scaled.astype(np.int64), 15)
    return (relative > 0) * 16 + np.where(distance < 8, distance, far_bucket)


def skew_buckets():
    lanes = (np.arange(SLOT) + SLOT // 2) % SLOT - SLOT // 2
    relative = np.arange(8)[:, None] - lanes[None, :]
    return bucket_of(relative).astype(np.int32)


def table_indicator():
    lanes = (np.arange(SLOT) + SLOT // 2) % SLOT - SLOT // 2
    buckets = np.concatenate([bucket_of(-lanes), np.full(BLOCK, 15), np.full(BLOCK, 31)])
    here = BUCKETS // SEQ
    place = (buckets // here) * SHARD + buckets % here
    return (place[:, None] == np.arange(D)[None, :]).astype(np.float32)


def dot(left, right):
    return jnp.dot(left, right, preferred_element_type=F32)


def dot_t(left, right):
    return lax.dot_general(left, right, (((1,), (1,)), ((), ())), preferred_element_type=F32)


def place():
    return lax.axis_index("seq"), lax.rem(lax.axis_index("dp"), 2)


def relative_starts(rows):
    me, y = place()
    z = lax.rem(lax.axis_index("dp") // 2, 2)
    bits = (me & 1, me >> 1, y, z)
    block = rows // 16
    starts = []
    for number in range(16):
        own = [(number >> shift) & 1 for shift in (3, 2, 1, 0)]
        core, x, first, second = (b if o else 1 - b for b, o in zip(bits, own))
        place_of = ((x * 2 + core) * 2 + first) * 2 + second
        starts.append(pl.multiple_of(place_of * block, 16))
    return block, starts


def run_all(copies):
    for copy in copies:
        copy.start()
    for copy in copies:
        copy.wait()


def pieces_of(rows, plan, refs, target, sems):
    me, y = place()
    half = rows // 2
    starts = (
        me * rows,
        (me ^ 1) * rows,
        (me ^ 2) * rows + y * half,
        (me ^ 2) * rows + (1 - y) * half,
        (me ^ 3) * rows + y * half,
        (me ^ 3) * rows + (1 - y) * half,
        (me ^ 2) * rows,
        (me ^ 3) * rows,
    )
    return [
        pltpu.make_async_copy(
            refs[ref].at[:, pl.ds(source, width)],
            target.at[
                pl.ds(pl.multiple_of(starts[piece], 16), half if 2 <= piece < 6 else rows),
                pl.ds(to, width),
            ],
            sems.at[number],
        )
        for number, (ref, piece, source, to, width) in enumerate(plan)
    ]


QKV_PLAN = ((0, 0, 0, 0, D), (1, 0, 0, D, D), (2, 0, 0, 2 * D, D)) + tuple(
    (2 + piece, piece, 0, 0, 3 * D) for piece in range(1, 6)
)
OUT_PLAN = tuple((ref, piece, 0, 0, D) for ref, piece in enumerate((0, 1, 6, 7)))
PROJ_PLAN = tuple((ref, piece, D, 0, PROJ) for ref, piece in enumerate((0, 1, 6, 7)))
DOWN_PLAN = tuple((piece, piece, 0, 0, D) for piece in range(6))


def gated_plan(part, refs=(0, 1, 2, 3, 4, 5, 6, 7), base=0):
    column = part * HALF_FF
    return (
        (refs[0], 0, column, base, HALF_FF),
        (refs[1], 0, column, base + HALF_FF, HALF_FF),
        (refs[2], 1, column, base, HALF_FF),
        (refs[3], 1, column, base + HALF_FF, HALF_FF),
    ) + tuple((refs[2 + piece], piece, 0, base, FF) for piece in range(2, 6))


def relative_copies(source, target, sems):
    block, starts = relative_starts(source.shape[0])
    return [
        pltpu.make_async_copy(
            source.at[pl.ds(begin, block), :],
            target.at[pl.ds(number * block, block), :],
            sems.at[number],
        )
        for number, begin in enumerate(starts)
    ]


def inverse_rms(values):
    return lax.rsqrt(jnp.mean(values * values, axis=-1, keepdims=True) + EPSILON)


def norm_backward(values, gain, incoming):
    r = inverse_rms(values)
    weighted = gain * incoming
    inner = jnp.mean(weighted * values, axis=-1, keepdims=True)
    gradient = r * weighted - values * (r * r * r * inner)
    gain_part = jnp.sum(incoming * values * r, axis=0, keepdims=True)
    return gradient, gain_part


def pack_first_kernel(
    lens, q, k, v, tokens, cot, qkv_half, block_0, block_1, block_2, block_3, sems
):
    me, y = place()
    half = SHARD // 2
    rows = pl.ds(pl.multiple_of(y * half, 16), half)
    pairs = [
        (weight.at[rows, :], qkv_half.at[:, pl.ds(number * D, D)])
        for number, weight in enumerate((q, k, v))
    ]
    for flip, block in enumerate((block_0, block_1, block_2, block_3)):
        pairs.append((tokens.at[me ^ flip], block.at[:, pl.ds(0, D)]))
        pairs.append((cot.at[me ^ flip], block.at[:, pl.ds(D, PROJ)]))
    run_all([pltpu.make_async_copy(a, b, sems.at[i]) for i, (a, b) in enumerate(pairs)])


def pack_first(lens, q, k, v, tokens, cot):
    return pl.pallas_call(
        pack_first_kernel,
        out_shape=(shape((SHARD // 2, 3 * D), BF16),) + (shape((BLOCK, WIDE), BF16),) * 4,
        in_specs=[SMEM] + [ANY] * 5,
        out_specs=(VMEM,) * 5,
        scratch_shapes=[pltpu.SemaphoreType.DMA((11,))],
        compiler_params=params(),
        cost_estimate=pl.CostEstimate(flops=30000000000, bytes_accessed=100000000, transcendentals=0),
        name="pack_first",
    )(lens, q, k, v, tokens, cot)


def pack_rest_kernel(
    lens, q, k, v, out, proj, gate, up, down, qkv, out_own, part_0, part_1, down_half, sems
):
    _, y = place()
    half = SHARD // 2
    rows = pl.ds(pl.multiple_of(y * half, 16), half)
    down_rows = pl.ds(pl.multiple_of(y * (FF // SEQ // 2), 16), FF // SEQ // 2)
    pairs = [
        (q, qkv.at[:, pl.ds(0, D)]),
        (k, qkv.at[:, pl.ds(D, D)]),
        (v, qkv.at[:, pl.ds(2 * D, D)]),
        (out, out_own.at[:, pl.ds(0, D)]),
        (proj, out_own.at[:, pl.ds(D, PROJ)]),
        (down.at[down_rows, :], down_half),
    ]
    for number, part in enumerate((part_0, part_1)):
        columns = pl.ds(number * HALF_FF, HALF_FF)
        pairs.append((gate.at[rows, columns], part.at[:, pl.ds(0, HALF_FF)]))
        pairs.append((up.at[rows, columns], part.at[:, pl.ds(HALF_FF, HALF_FF)]))
    run_all([pltpu.make_async_copy(a, b, sems.at[i]) for i, (a, b) in enumerate(pairs)])


def pack_rest(lens, q, k, v, out, proj, gate, up, down):
    half = SHARD // 2
    return pl.pallas_call(
        pack_rest_kernel,
        out_shape=(
            shape((SHARD, 3 * D), BF16),
            shape((SHARD, WIDE), BF16),
            shape((half, FF), BF16),
            shape((half, FF), BF16),
            shape((FF // SEQ // 2, D), BF16),
        ),
        in_specs=[SMEM] + [ANY] * 8,
        out_specs=(VMEM,) * 5,
        scratch_shapes=[pltpu.SemaphoreType.DMA((10,))],
        compiler_params=params(),
        cost_estimate=pl.CostEstimate(flops=30000000000, bytes_accessed=100000000, transcendentals=0),
        name="pack_rest",
    )(lens, q, k, v, out, proj, gate, up, down)


def first_norm_kernel(lens, own, from_core, from_x, from_far, gain, tok, cot, n1, n1t, held, sems):
    me, _ = place()
    run_all(
        [
            pltpu.make_async_copy(
                piece,
                held.at[pl.ds(pl.multiple_of((me ^ flip) * BLOCK, BLOCK), BLOCK), :],
                sems.at[flip],
            )
            for flip, piece in enumerate((own, from_core, from_x, from_far))
        ]
    )
    scale = gain[...].reshape(1, D)
    for block in range(SLOT // BLOCK):
        rows = pl.ds(block * BLOCK, BLOCK)
        here = held[rows, 0:D]
        tok[rows, :] = here
        cot[rows, :] = held[rows, D : D + PROJ]
        values = here.astype(F32)
        normed = (values * inverse_rms(values) * scale).astype(BF16)
        n1[rows, :] = normed
        n1t[:, rows] = normed.T


def first_norm(lens, blocks, gain):
    return pl.pallas_call(
        first_norm_kernel,
        out_shape=(
            shape((SLOT, D), BF16),
            shape((SLOT, PROJ), BF16),
            shape((SLOT, D), BF16),
            shape((D, SLOT), BF16),
        ),
        in_specs=[SMEM, ANY, ANY, ANY, ANY, VMEM],
        out_specs=(VMEM,) * 4,
        scratch_shapes=[pltpu.VMEM((SLOT, WIDE), BF16), pltpu.SemaphoreType.DMA((4,))],
        compiler_params=params(),
        cost_estimate=pl.CostEstimate(flops=30000000000, bytes_accessed=100000000, transcendentals=0),
        name="first_norm",
    )(lens, *blocks, gain)


def qkv_kernel(lens, n1, *refs):
    pieces, (out, weight, sems) = refs[:8], refs[8:]
    run_all(pieces_of(SHARD, QKV_PLAN, pieces, weight, sems))

    def step(tile, carry):
        columns = pl.ds(pl.multiple_of(tile * 256, 256), 256)
        out[:, columns] = dot(n1[...], weight[:, columns]).astype(BF16)
        return carry

    lax.fori_loop(0, 3 * D // 256, step, 0)


def qkv_project(lens, n1, pieces):
    return pl.pallas_call(
        qkv_kernel,
        out_shape=shape((SLOT, 3 * D), BF16),
        in_specs=[SMEM, VMEM] + [ANY] * 8,
        out_specs=VMEM,
        scratch_shapes=[pltpu.VMEM((D, 3 * D), BF16), pltpu.SemaphoreType.DMA((8,))],
        compiler_params=params(),
        cost_estimate=pl.CostEstimate(flops=30000000000, bytes_accessed=100000000, transcendentals=0),
        name="qkv_project",
    )(lens, n1, *pieces)


HALF_Q = 256


def attention_kernel(first, lens, q, k, v, rows_of_bias, buckets, *refs):
    et, linv, ot, o, bias = refs[-5:]
    me, _ = place()
    length = lens[me]
    pair = pl.program_id(0) + first
    k_pair = k[...]
    vt = v[...].T
    qt = q[...].T
    row_in_pair = lax.broadcasted_iota(jnp.int32, (2 * HEAD, SLOT), 0)
    key_index = lax.broadcasted_iota(jnp.int32, (SLOT, HALF_Q), 0)
    for head in range(2):
        base = jnp.zeros((8, SLOT), F32)
        for bucket in range(BUCKETS):
            base = jnp.where(buckets[...] == bucket, rows_of_bias[bucket, 2 * pair + head], base)
        for group in range(BLOCK // 8):
            bias[pl.ds(group * 8, 8), :] = pltpu.roll(base, 8 * group, 1) if group else base
        below = rows_of_bias[15, 2 * pair + head]
        above = rows_of_bias[31, 2 * pair + head]
        in_head = (row_in_pair >= HEAD * head) & (row_in_pair < HEAD * (head + 1))
        qt_head = jnp.where(in_head, qt, jnp.zeros_like(qt))
        for part in range(SLOT // HALF_Q):
            raw = dot(k_pair, qt_head[:, part * HALF_Q : (part + 1) * HALF_Q])
            rows = []
            for key_block in range(4):
                cells = []
                for sub in range(HALF_Q // BLOCK):
                    query_block = part * (HALF_Q // BLOCK) + sub
                    cell = raw[
                        key_block * BLOCK : (key_block + 1) * BLOCK,
                        sub * BLOCK : (sub + 1) * BLOCK,
                    ]
                    apart = key_block - query_block
                    if apart >= 2:
                        cell = cell + above
                    elif apart <= -2:
                        cell = cell + below
                    else:
                        lane = (-apart * BLOCK) % SLOT
                        cell = cell + bias[:, lane : lane + BLOCK]
                    cells.append(cell)
                rows.append(jnp.concatenate(cells, axis=1))
            scores = jnp.concatenate(rows, axis=0)
            scores = jnp.where(key_index < length, scores, BIG_NEGATIVE)
            top = jnp.max(scores, axis=0, keepdims=True)
            weights = jnp.exp(scores - top)
            inverse = 1.0 / jnp.sum(weights, axis=0, keepdims=True)
            low = weights.astype(BF16)
            columns = pl.ds(part * HALF_Q, HALF_Q)
            et[head, :, columns] = low
            linv[head, :, columns] = inverse
            mixed = dot(vt[head * HEAD : (head + 1) * HEAD, :], low) * inverse
            ot[pl.ds(head * HEAD, HEAD), columns] = mixed.astype(BF16)
    o[...] = ot[...].T


def attention(lens, qkv, rows_of_bias, first, count, held):
    pair = 2 * HEAD
    pairs = H // 2
    return pl.pallas_call(
        functools.partial(attention_kernel, first),
        grid=(count,),
        out_shape=(
            shape((H, SLOT, SLOT), BF16),
            shape((H, 1, SLOT), F32),
            shape((D, SLOT), BF16),
            shape((SLOT, D), BF16),
        ),
        in_specs=[
            SMEM,
            pl.BlockSpec((SLOT, pair), lambda i: (0, first + i)),
            pl.BlockSpec((SLOT, pair), lambda i: (0, pairs + first + i)),
            pl.BlockSpec((SLOT, pair), lambda i: (0, 2 * pairs + first + i)),
            SMEM,
            pl.BlockSpec((8, SLOT), lambda i: (0, 0)),
        ]
        + [ANY] * len(held),
        out_specs=(
            pl.BlockSpec((2, SLOT, SLOT), lambda i: (first + i, 0, 0)),
            pl.BlockSpec((2, 1, SLOT), lambda i: (first + i, 0, 0)),
            pl.BlockSpec((pair, SLOT), lambda i: (first + i, 0)),
            pl.BlockSpec((SLOT, pair), lambda i: (0, first + i)),
        ),
        input_output_aliases={6 + i: i for i in range(len(held))},
        scratch_shapes=[pltpu.VMEM((BLOCK, SLOT), F32)],
        compiler_params=params(),
        cost_estimate=pl.CostEstimate(flops=30000000000, bytes_accessed=100000000, transcendentals=0),
        name="attention",
    )(lens, qkv, qkv, qkv, rows_of_bias, jnp.asarray(skew_buckets()), *held)


def hidden_kernel(lens, tok, mixed, gain, *refs):
    pieces, (hidden, n2, n2t, weight, sems) = refs[:4], refs[4:]
    run_all(pieces_of(SHARD, OUT_PLAN, pieces, weight, sems))
    scale = gain[...].reshape(1, D)
    for block in range(2):
        rows = pl.ds(block * 256, 256)
        values = tok[rows, :].astype(F32) + dot(mixed[rows, :], weight[...])
        hidden[rows, :] = values
        normed = (values * inverse_rms(values) * scale).astype(BF16)
        n2[rows, :] = normed
        n2t[:, rows] = normed.T


def hidden_project(lens, tok, mixed, gain, pieces):
    return pl.pallas_call(
        hidden_kernel,
        out_shape=(shape((SLOT, D), F32), shape((SLOT, D), BF16), shape((D, SLOT), BF16)),
        in_specs=[SMEM, VMEM, VMEM, VMEM] + [ANY] * 4,
        out_specs=(VMEM,) * 3,
        scratch_shapes=[pltpu.VMEM((D, D), BF16), pltpu.SemaphoreType.DMA((4,))],
        compiler_params=params(),
        cost_estimate=pl.CostEstimate(flops=30000000000, bytes_accessed=100000000, transcendentals=0),
        name="hidden_project",
    )(lens, tok, mixed, gain, *pieces)


def gated_kernel(part, lens, n2, *refs):
    pieces, (inner, innert, slope, level, weight, sems) = refs[:8], refs[-6:]
    tile = pl.program_id(0)

    @pl.when(tile == 0)
    def load():
        run_all(pieces_of(SHARD, gated_plan(part), pieces, weight, sems))

    columns = pl.ds(pl.multiple_of(tile * 256, 256), 256)
    up_columns = pl.ds(pl.multiple_of(HALF_FF + tile * 256, 256), 256)
    g = dot(n2[...], weight[:, columns])
    u = dot(n2[...], weight[:, up_columns])
    square = g * g
    t = jnp.tanh(GELU_A * g * (1.0 + GELU_B * square))
    half_up = 0.5 * (1.0 + t)
    activated = g * half_up
    derivative = half_up + 0.5 * g * (1.0 - t * t) * (GELU_A * (1.0 + 3 * GELU_B * square))
    value = (activated * u).astype(BF16)
    inner[...] = value
    innert[...] = value.T
    slope[...] = (derivative * u).astype(BF16)
    level[...] = activated.astype(BF16)


def gated(lens, n2, pieces, part, held):
    tiles = HALF_FF // 256
    wide = pl.BlockSpec((SLOT, 256), lambda i: (0, part * tiles + i))
    tall = pl.BlockSpec((256, SLOT), lambda i: (part * tiles + i, 0))
    return pl.pallas_call(
        functools.partial(gated_kernel, part),
        grid=(tiles,),
        out_shape=(
            shape((SLOT, FF), BF16),
            shape((FF, SLOT), BF16),
            shape((SLOT, FF), BF16),
            shape((SLOT, FF), BF16),
        ),
        in_specs=[SMEM, VMEM] + [ANY] * (8 + len(held)),
        out_specs=(wide, tall, wide, wide),
        input_output_aliases={10 + i: i for i in range(len(held))},
        scratch_shapes=[pltpu.VMEM((D, FF), BF16), pltpu.SemaphoreType.DMA((8,))],
        compiler_params=params(),
        cost_estimate=pl.CostEstimate(flops=30000000000, bytes_accessed=100000000, transcendentals=0),
        name="gated",
    )(lens, n2, *pieces, *held)


def final_kernel(lens, hidden, inner, cot, gain, *refs):
    down_pieces, proj_pieces = refs[:6], refs[6:10]
    embedded, after_grad, down_in, fnt, gain_grad, down, proj, down_sems, proj_sems = refs[10:]
    run_all(
        pieces_of(FF // SEQ, DOWN_PLAN, down_pieces, down, down_sems)
        + pieces_of(SHARD, PROJ_PLAN, proj_pieces, proj, proj_sems)
    )
    scale = gain[...].reshape(1, D)
    total = jnp.zeros((1, D), F32)
    for block in range(2):
        rows = pl.ds(block * 256, 256)
        values = hidden[rows, :] + dot(inner[rows, :], down[...])
        normed = (values * inverse_rms(values) * scale).astype(BF16)
        fnt[:, rows] = normed.T
        embedded[rows, :] = dot(normed, proj[...]).astype(BF16)
        gradient, part = norm_backward(values, scale, dot_t(cot[rows, :], proj[...]))
        after_grad[rows, :] = gradient
        down_in[rows, :] = gradient.astype(BF16)
        total = total + part
    gain_grad[...] = total


def final_stage(lens, hidden, inner, cot, gain, down_pieces, proj_pieces):
    return pl.pallas_call(
        final_kernel,
        out_shape=(
            shape((SLOT, PROJ), BF16),
            shape((SLOT, D), F32),
            shape((SLOT, D), BF16),
            shape((D, SLOT), BF16),
            shape((1, D), F32),
        ),
        in_specs=[SMEM, VMEM, VMEM, VMEM, VMEM] + [ANY] * 10,
        out_specs=(VMEM,) * 5,
        scratch_shapes=[
            pltpu.VMEM((FF, D), BF16),
            pltpu.VMEM((D, PROJ), BF16),
            pltpu.SemaphoreType.DMA((6,)),
            pltpu.SemaphoreType.DMA((4,)),
        ],
        compiler_params=params(),
        cost_estimate=pl.CostEstimate(flops=30000000000, bytes_accessed=100000000, transcendentals=0),
        name="final_stage",
    )(lens, hidden, inner, cot, gain, *down_pieces, *proj_pieces)


def weight_grad_kernel(lens, source, right, send, keep, left, sems):
    half = source.shape[0] // 2

    @pl.when(pl.program_id(0) == 0)
    def load():
        run_all(relative_copies(source, left, sems))

    send[...] = dot(left[0:half, :], right[...]).astype(BF16)
    keep[...] = dot(left[half:, :], right[...]).astype(BF16)


def weight_grad(lens, source, right, name):
    rows, width = source.shape[0], right.shape[1]
    tile = 512 if width % 512 == 0 else 256
    return pl.pallas_call(
        weight_grad_kernel,
        grid=(width // tile,),
        out_shape=(shape((rows // 2, width), BF16),) * 2,
        in_specs=[SMEM, ANY, pl.BlockSpec((SLOT, tile), lambda i: (0, i))],
        out_specs=(pl.BlockSpec((rows // 2, tile), lambda i: (0, i)),) * 2,
        scratch_shapes=[pltpu.VMEM((rows, SLOT), BF16), pltpu.SemaphoreType.DMA((16,))],
        compiler_params=params(),
        cost_estimate=pl.CostEstimate(flops=30000000000, bytes_accessed=100000000, transcendentals=0),
        name=name,
    )(lens, source, right)


def out_grad_kernel(lens, ot, fnt, attn_in, cot, send, keep, left, proj_left, sems, proj_sems):
    run_all(relative_copies(ot, left, sems) + relative_copies(fnt, proj_left, proj_sems))
    for number, target in enumerate((send, keep)):
        rows = slice(number * D // 2, (number + 1) * D // 2)
        target[:, 0:D] = dot(left[rows, :], attn_in[...]).astype(BF16)
        target[:, D:WIDE] = dot(proj_left[rows, :], cot[...]).astype(BF16)


def out_grads(lens, ot, fnt, attn_in, cot):
    return pl.pallas_call(
        out_grad_kernel,
        out_shape=(shape((D // 2, WIDE), BF16),) * 2,
        in_specs=[SMEM, ANY, ANY, VMEM, VMEM],
        out_specs=(VMEM,) * 2,
        scratch_shapes=[
            pltpu.VMEM((D, SLOT), BF16),
            pltpu.VMEM((D, SLOT), BF16),
            pltpu.SemaphoreType.DMA((16,)),
            pltpu.SemaphoreType.DMA((16,)),
        ],
        compiler_params=params(),
        cost_estimate=pl.CostEstimate(flops=30000000000, bytes_accessed=100000000, transcendentals=0),
        name="out_grads",
    )(lens, ot, fnt, attn_in, cot)


def query_key_grad_kernel(lens, n1t, dq, dk, send, keep, left, sems):
    run_all(relative_copies(n1t, left, sems))
    for number, target in enumerate((send, keep)):
        rows = slice(number * D // 2, (number + 1) * D // 2)
        target[:, 0:D] = dot(left[rows, :], dq[...]).astype(BF16)
        target[:, D : 2 * D] = dot(left[rows, :], dk[...]).astype(BF16)


def query_key_grads(lens, n1t, dq, dk):
    return pl.pallas_call(
        query_key_grad_kernel,
        out_shape=(shape((D // 2, 2 * D), BF16),) * 2,
        in_specs=[SMEM, ANY, VMEM, VMEM],
        out_specs=(VMEM,) * 2,
        scratch_shapes=[pltpu.VMEM((D, SLOT), BF16), pltpu.SemaphoreType.DMA((16,))],
        compiler_params=params(),
        cost_estimate=pl.CostEstimate(flops=30000000000, bytes_accessed=100000000, transcendentals=0),
        name="query_key_grads",
    )(lens, n1t, dq, dk)


def value_grad_kernel(
    lens, n1t, dv, table, indicator, attn_part, ffn_part, final_part, send, keep, left, small, sems
):
    copies = relative_copies(n1t, left, sems)
    for copy in copies:
        copy.start()
    high = table[...].astype(BF16)
    low = (table[...] - high.astype(F32)).astype(BF16)
    by_bucket = dot(high, indicator[...]) + dot(low, indicator[...])
    stacked = jnp.concatenate(
        [
            attn_part[...],
            ffn_part[...],
            final_part[...],
            jnp.zeros((TABLE_COLUMN - 3, D), F32),
            by_bucket,
            jnp.zeros((PROJ - TABLE_COLUMN - H, D), F32),
        ],
        axis=0,
    )
    small[...] = stacked.T
    for copy in copies:
        copy.wait()
    block, starts = relative_starts(D)
    for number, begin in enumerate(starts):
        target = keep if number >= 8 else send
        target[pl.ds((number & 7) * block, block), D:WIDE] = small[pl.ds(begin, block), :].astype(
            BF16
        )
    for number, target in enumerate((send, keep)):
        rows = slice(number * D // 2, (number + 1) * D // 2)
        target[:, 0:D] = dot(left[rows, :], dv[...]).astype(BF16)


def value_grads(lens, n1t, dv, table, attn_part, ffn_part, final_part):
    return pl.pallas_call(
        value_grad_kernel,
        out_shape=(shape((D // 2, WIDE), BF16),) * 2,
        in_specs=[SMEM, ANY] + [VMEM] * 6,
        out_specs=(VMEM,) * 2,
        scratch_shapes=[
            pltpu.VMEM((D, SLOT), BF16),
            pltpu.VMEM((D, PROJ), F32),
            pltpu.SemaphoreType.DMA((16,)),
        ],
        compiler_params=params(),
        cost_estimate=pl.CostEstimate(flops=30000000000, bytes_accessed=100000000, transcendentals=0),
        name="value_grads",
    )(
        lens,
        n1t,
        dv,
        table,
        jnp.asarray(table_indicator(), dtype=BF16),
        attn_part,
        ffn_part,
        final_part,
    )


def inner_grad_kernel(lens, down_in, slope, level, *refs):
    pieces, (gate_grad, up_grad, down, sems) = refs[:6], refs[6:]
    run_all(pieces_of(FF // SEQ, DOWN_PLAN, pieces, down, sems))

    def step(tile, carry):
        columns = pl.ds(pl.multiple_of(tile * 256, 256), 256)
        incoming = dot_t(down_in[...], down[columns, :])
        gate_grad[:, columns] = (incoming * slope[:, columns].astype(F32)).astype(BF16)
        up_grad[:, columns] = (incoming * level[:, columns].astype(F32)).astype(BF16)
        return carry

    lax.fori_loop(0, FF // 256, step, 0)


def inner_grads(lens, down_in, slope, level, pieces):
    return pl.pallas_call(
        inner_grad_kernel,
        out_shape=(shape((SLOT, FF), BF16),) * 2,
        in_specs=[SMEM, VMEM, VMEM, VMEM] + [ANY] * 6,
        out_specs=(VMEM,) * 2,
        scratch_shapes=[pltpu.VMEM((FF, D), BF16), pltpu.SemaphoreType.DMA((6,))],
        compiler_params=params(),
        cost_estimate=pl.CostEstimate(flops=30000000000, bytes_accessed=100000000, transcendentals=0),
        name="inner_grads",
    )(lens, down_in, slope, level, *pieces)


def hidden_grad_kernel(lens, gate_grad, up_grad, hidden, after_grad, gain, *refs):
    pieces, (hidden_grad, attn_in, gain_grad, weight, sems) = refs[:12], refs[12:]
    plan = gated_plan(0) + gated_plan(1, (0, 1, 2, 3, 8, 9, 10, 11), FF)
    run_all(pieces_of(SHARD, plan, pieces, weight, sems))
    scale = gain[...].reshape(1, D)
    total = jnp.zeros((1, D), F32)
    for block in range(2):
        rows = pl.ds(block * 256, 256)
        incoming = None
        for number, source in enumerate((gate_grad, up_grad)):
            for part in range(2):
                column = part * FF + number * HALF_FF
                term = dot_t(
                    source[rows, part * HALF_FF : (part + 1) * HALF_FF],
                    weight[:, column : column + HALF_FF],
                )
                incoming = term if incoming is None else incoming + term
        gradient, part = norm_backward(hidden[rows, :], scale, incoming)
        gradient = gradient + after_grad[rows, :]
        hidden_grad[rows, :] = gradient
        attn_in[rows, :] = gradient.astype(BF16)
        total = total + part
    gain_grad[...] = total


def hidden_grads(lens, gate_grad, up_grad, hidden, after_grad, gain, pieces):
    return pl.pallas_call(
        hidden_grad_kernel,
        out_shape=(shape((SLOT, D), F32), shape((SLOT, D), BF16), shape((1, D), F32)),
        in_specs=[SMEM, VMEM, VMEM, VMEM, VMEM, VMEM] + [ANY] * 12,
        out_specs=(VMEM,) * 3,
        scratch_shapes=[pltpu.VMEM((D, 2 * FF), BF16), pltpu.SemaphoreType.DMA((16,))],
        compiler_params=params(),
        cost_estimate=pl.CostEstimate(flops=30000000000, bytes_accessed=100000000, transcendentals=0),
        name="hidden_grads",
    )(lens, gate_grad, up_grad, hidden, after_grad, gain, *pieces)


def mixed_grad_kernel(lens, attn_in, *refs):
    pieces, (out, weight, sems) = refs[:4], refs[4:]
    run_all(pieces_of(SHARD, OUT_PLAN, pieces, weight, sems))
    out[...] = dot_t(attn_in[...], weight[...]).astype(BF16)


def mixed_grads(lens, attn_in, pieces):
    return pl.pallas_call(
        mixed_grad_kernel,
        out_shape=shape((SLOT, D), BF16),
        in_specs=[SMEM, VMEM] + [ANY] * 4,
        out_specs=VMEM,
        scratch_shapes=[pltpu.VMEM((D, D), BF16), pltpu.SemaphoreType.DMA((4,))],
        compiler_params=params(),
        cost_estimate=pl.CostEstimate(flops=30000000000, bytes_accessed=100000000, transcendentals=0),
        name="mixed_grads",
    )(lens, attn_in, *pieces)


def attention_back_kernel(lens, q, k, v, et, linv, ot, do, *refs):
    dq, dk, dv, bias_grad, dqt, near = refs[-6:]
    lane_in_pair = lax.broadcasted_iota(jnp.int32, (SLOT, 2 * HEAD), 1)
    q_pair, v_pair = q[...], v[...]
    kt = k[...].T
    out_gradt = do[...].astype(F32).T
    scaled = []
    deltas = []
    for head in range(2):
        rows = slice(head * HEAD, (head + 1) * HEAD)
        low = (out_gradt[rows, :] * linv[head]).astype(BF16)
        scaled.append(low)
        deltas.append(
            jnp.sum(low.astype(F32) * ot[rows, :].astype(F32), axis=0, keepdims=True)
        )
    scaled_pair = jnp.concatenate(scaled, axis=0).T
    zeros = jnp.zeros((HEAD, SLOT), BF16)
    key_total = jnp.zeros((SLOT, 2 * HEAD), F32)
    value_total = jnp.zeros((SLOT, 2 * HEAD), F32)
    row_of_eight = lax.broadcasted_iota(jnp.int32, (8, SLOT), 0)
    for head in range(2):
        in_head = (lane_in_pair >= head * HEAD) & (lane_in_pair < (head + 1) * HEAD)
        q_head = jnp.where(in_head, q_pair, jnp.zeros_like(q_pair))
        do_head = jnp.where(in_head, scaled_pair, jnp.zeros_like(scaled_pair))
        dot_head = jnp.concatenate(
            [scaled[head], zeros] if head == 0 else [zeros, scaled[head]], axis=0
        )
        near_sums = {-1: None, 0: None, 1: None}
        far_sums = {-1: None, 1: None}
        for part in range(SLOT // HALF_Q):
            columns = slice(part * HALF_Q, (part + 1) * HALF_Q)
            prob_grad = dot(v_pair, dot_head[:, columns])
            low_weights = et[head, :, columns]
            score_grad = low_weights.astype(F32) * (prob_grad - deltas[head][:, columns])
            low = score_grad.astype(BF16)
            key_total = key_total + dot(low, q_head[columns, :])
            value_total = value_total + dot(low_weights, do_head[columns, :])
            dqt[pl.ds(head * HEAD, HEAD), columns] = dot(
                kt[head * HEAD : (head + 1) * HEAD, :], low
            ).astype(BF16)
            for key_block in range(4):
                for sub in range(HALF_Q // BLOCK):
                    apart = key_block - part * (HALF_Q // BLOCK) - sub
                    cell = score_grad[
                        key_block * BLOCK : (key_block + 1) * BLOCK,
                        sub * BLOCK : (sub + 1) * BLOCK,
                    ]
                    if abs(apart) >= 2:
                        side = 1 if apart > 0 else -1
                        folded = jnp.sum(cell.reshape(BLOCK // 8, 8, BLOCK), axis=0)
                        old = far_sums[side]
                        far_sums[side] = folded if old is None else old + folded
                    else:
                        old = near_sums[apart]
                        near_sums[apart] = cell if old is None else old + cell
        near[...] = jnp.zeros_like(near)
        for apart in (-1, 0, 1):
            lane = (-apart * BLOCK) % SLOT
            near[:, lane : lane + BLOCK] = near_sums[apart]
        folded = near[0:8, :]
        for group in range(1, BLOCK // 8):
            folded = folded + pltpu.roll(near[group * 8 : group * 8 + 8, :], SLOT - 8 * group, 1)
        for bit in (1, 2, 4):
            folded = jnp.where(
                (row_of_eight & bit) != 0, pltpu.roll(folded, SLOT - bit, 1), folded
            )
        here = slice(head, head + 1)
        bias_grad[0, here, 0:SLOT] = jnp.sum(folded, axis=0, keepdims=True)
        for number, side in enumerate((-1, 1)):
            lane = SLOT + number * BLOCK
            bias_grad[0, here, lane : lane + BLOCK] = jnp.sum(
                far_sums[side], axis=0, keepdims=True
            )
    dk[...] = key_total.astype(BF16)
    dv[...] = value_total.astype(BF16)
    dq[...] = dqt[...].T


def attention_back(lens, qkv, et, linv, ot, do, first, count, held):
    pair = 2 * HEAD
    pairs = H // 2
    wide = pl.BlockSpec((SLOT, pair), lambda i: (0, first + i))
    return pl.pallas_call(
        attention_back_kernel,
        grid=(count,),
        out_shape=(shape((SLOT, D), BF16),) * 3 + (shape((pairs, 2, D), F32),),
        in_specs=[
            SMEM,
            wide,
            pl.BlockSpec((SLOT, pair), lambda i: (0, pairs + first + i)),
            pl.BlockSpec((SLOT, pair), lambda i: (0, 2 * pairs + first + i)),
            pl.BlockSpec((2, SLOT, SLOT), lambda i: (first + i, 0, 0)),
            pl.BlockSpec((2, 1, SLOT), lambda i: (first + i, 0, 0)),
            pl.BlockSpec((pair, SLOT), lambda i: (first + i, 0)),
            wide,
        ]
        + [ANY] * len(held),
        out_specs=(wide,) * 3 + (pl.BlockSpec((1, 2, D), lambda i: (first + i, 0, 0)),),
        input_output_aliases={8 + i: i for i in range(len(held))},
        scratch_shapes=[pltpu.VMEM((pair, SLOT), BF16), pltpu.VMEM((BLOCK, SLOT), F32)],
        compiler_params=params(),
        cost_estimate=pl.CostEstimate(flops=30000000000, bytes_accessed=100000000, transcendentals=0),
        name="attention_back",
    )(lens, qkv, qkv, qkv, et, linv, ot, do, *held)


def token_grad_kernel(lens, dq, dk, dv, hidden_grad, tok, embedded, gain, *refs):
    pieces, (block_0, block_1, block_2, block_3, gain_grad, weight, sems) = refs[:8], refs[8:]
    me, _ = place()
    run_all(pieces_of(SHARD, QKV_PLAN, pieces, weight, sems))
    scale = gain[...].reshape(1, D)
    total = jnp.zeros((1, D), F32)
    for flip, target in enumerate((block_0, block_1, block_2, block_3)):
        rows = pl.ds(pl.multiple_of((me ^ flip) * BLOCK, BLOCK), BLOCK)
        incoming = (
            dot_t(dq[rows, :], weight[:, 0:D])
            + dot_t(dk[rows, :], weight[:, D : 2 * D])
            + dot_t(dv[rows, :], weight[:, 2 * D : 3 * D])
        )
        gradient, part = norm_backward(tok[rows, :].astype(F32), scale, incoming)
        target[:, 0:D] = (hidden_grad[rows, :] + gradient).astype(BF16)
        target[:, D:WIDE] = embedded[rows, :]
        total = total + part
    gain_grad[...] = total


def token_grads(lens, dq, dk, dv, hidden_grad, tok, embedded, gain, pieces):
    return pl.pallas_call(
        token_grad_kernel,
        out_shape=(shape((BLOCK, WIDE), BF16),) * 4 + (shape((1, D), F32),),
        in_specs=[SMEM] + [VMEM] * 7 + [ANY] * 8,
        out_specs=(VMEM,) * 5,
        scratch_shapes=[pltpu.VMEM((D, 3 * D), BF16), pltpu.SemaphoreType.DMA((8,))],
        compiler_params=params(),
        cost_estimate=pl.CostEstimate(flops=30000000000, bytes_accessed=100000000, transcendentals=0),
        name="token_grads",
    )(lens, dq, dk, dv, hidden_grad, tok, embedded, gain, *pieces)


def unpack_kernel(block_0, block_1, block_2, block_3, embedded, tokens_grad):
    me, _ = place()
    for flip, block in enumerate((block_0, block_1, block_2, block_3)):
        tokens_grad[me ^ flip] = block[:, 0:D].astype(F32)
        embedded[me ^ flip] = block[:, D:WIDE]


def unpack(blocks):
    return pl.pallas_call(
        unpack_kernel,
        out_shape=(shape((SEQ, BLOCK, PROJ), BF16), shape((SEQ, BLOCK, D), F32)),
        in_specs=[VMEM] * 4,
        out_specs=(VMEM,) * 2,
        compiler_params=params(),
        cost_estimate=pl.CostEstimate(flops=30000000000, bytes_accessed=100000000, transcendentals=0),
        name="unpack",
    )(*blocks)


def exchange(value, axis, flip, size):
    return lax.ppermute(value, axis, [(i, i ^ flip) for i in range(size)])


def after(value, *others):
    return lax.optimization_barrier((value,) + others)[0]


def add(*terms):
    total = terms[0].astype(F32)
    for term in terms[1:]:
        total = total + term.astype(F32)
    return total.astype(BF16)


class Chunk:
    def __init__(self, groups, pair, scatter):
        self.groups, self.scatter = groups, scatter
        self.send, self.keep = pair
        self.rows = self.send.shape[0] // 4
        self.step = 4

    def core(self, tick):
        self.send = after(self.send, tick)
        self.from_core = exchange(self.send, "seq", 1, SEQ)
        return self.from_core

    def x(self, tick):
        both = 2 * self.rows
        self.from_core = after(self.from_core, tick)
        mine = add(self.keep[:both], self.from_core[:both])
        self.from_x = exchange(mine, "seq", 2, SEQ)
        return self.from_x

    def y(self, tick):
        rows = self.rows
        self.from_x = after(self.from_x, tick)
        mine = add(
            self.keep[2 * rows : 3 * rows], self.from_core[2 * rows : 3 * rows], self.from_x[:rows]
        )
        self.from_y = exchange(mine, "dp", 1, self.groups)
        return self.from_y

    def _summed(self, begin, end):
        rows = self.rows
        return add(
            self.keep[3 * rows + begin : 3 * rows + end],
            self.from_core[3 * rows + begin : 3 * rows + end],
            self.from_x[rows + begin : rows + end],
            self.from_y[begin:end],
        )

    def z(self, tick):
        half = self.rows // 2
        self.from_y = after(self.from_y, tick)
        self.total = self._summed(0, half if self.scatter else self.rows)
        self.from_z = exchange(self.total, "dp", 2, self.groups)
        return self.from_z

    def z_next(self, tick):
        self.from_z = after(self.from_z, tick)
        if self.scatter and self.step == 4:
            self.total = add(self._summed(self.rows // 2, self.rows), self.from_z)
        elif self.step == 4:
            half = self.rows // 2
            turned = jnp.concatenate([self.from_z[half:], self.from_z[:half]], axis=0)
            self.total = add(self.total, turned)
        else:
            self.total = add(self.total, self.from_z)
        if self.step < self.groups:
            self.from_z = exchange(self.total, "dp", self.step, self.groups)
        self.step *= 2
        while self.step < self.groups:
            self.z_next(tick)
        return self.from_z

    def z_last(self, tick):
        self.from_z = after(self.from_z, tick)
        self.total = add(self.total, self.from_z)
        self.from_z = exchange(self.total, "dp", 2, self.groups)
        return self.from_z

    def last(self, tick):
        self.from_z = after(self.from_z, tick)
        if self.scatter:
            self.total = jnp.concatenate([self.from_z, self.total], axis=0)
        else:
            self.total = add(self.total, self.from_z)
        self.other = exchange(self.total, "dp", 1, self.groups)
        return self.other


def assemble_kernel(widths, rows, total, other, *outs):
    _, y = place()
    z = lax.rem(lax.axis_index("dp") // 2, 2)
    half = rows // 2
    column = 0
    for width, out in zip(widths, outs):
        columns = slice(column, column + width)
        for source, whose in ((total, y), (other, 1 - y)):
            for own in range(2):
                which = z if own else 1 - z
                begin = pl.multiple_of(whose * rows + which * half, 16)
                out[pl.ds(begin, half), :] = source[
                    own * half : (own + 1) * half, columns
                ].astype(F32)
        column += width


def assemble(chunk, *widths):
    rows = chunk.rows
    return pl.pallas_call(
        functools.partial(assemble_kernel, widths, rows),
        out_shape=tuple(shape((2 * rows, width), F32) for width in widths),
        in_specs=[VMEM] * 2,
        out_specs=(VMEM,) * len(widths),
        compiler_params=params(),
        cost_estimate=pl.CostEstimate(flops=30000000000, bytes_accessed=100000000, transcendentals=0),
        name="assemble",
    )(chunk.total, chunk.other)


def per_device(
    groups,
    tokens,
    doc_lengths,
    query_weight,
    key_weight,
    value_weight,
    out_weight,
    gate_weight,
    up_weight,
    down_weight,
    proj_weight,
    attn_gain,
    ffn_gain,
    final_gain,
    bucket_bias_rows,
    embed_cotangent,
):
    tick = doc_lengths

    def across_x(mine):
        return exchange(after(mine, tick), "seq", 2, SEQ)

    def across_y(mine):
        return exchange(after(mine, tick), "dp", 1, groups)

    def across_core(mine):
        return exchange(after(mine, tick), "seq", 1, SEQ)

    def across_far(mine):
        return exchange(after(mine, tick), "seq", 3, SEQ)

    qkv_half, *blocks = pack_first(
        tick, query_weight, key_weight, value_weight, tokens, embed_cotangent
    )
    qkv_x = across_x(qkv_half)
    block_x = across_x(blocks[2])
    block_far = across_far(blocks[3])
    block_core = across_core(blocks[1])
    tick = after(tick, qkv_half)
    qkv_own, out_own, gated_half_0, gated_half_1, down_half = pack_rest(
        tick,
        query_weight,
        key_weight,
        value_weight,
        out_weight,
        proj_weight,
        gate_weight,
        up_weight,
        down_weight,
    )
    qkv_core = across_core(qkv_own)

    tick = after(tick, qkv_x, qkv_core, block_core)
    qkv_y = across_y(qkv_x)
    qkv_cx = across_core(qkv_x)
    out_x = across_x(out_own)
    tick = after(tick, block_x, block_far, qkv_cx)
    out_core = across_core(out_own)
    gated_x_0 = across_x(gated_half_0)
    gate_core = across_core(gate_weight)
    tok, cot, n1, n1t = first_norm(tick, (blocks[0], block_core, block_x, block_far), attn_gain)
    tick = after(tick, n1, qkv_y, out_core, gate_core)
    qkv_cy = across_core(qkv_y)
    up_core = across_core(up_weight)
    tick = after(tick, qkv_cy, up_core)
    gated_x_1 = across_x(gated_half_1)
    down_core = across_core(down_weight)
    qkv_pieces = (
        query_weight, key_weight, value_weight, qkv_core, qkv_x, qkv_y, qkv_cx, qkv_cy
    )
    qkv = qkv_project(tick, n1, qkv_pieces)
    pairs = H // 2
    tick = after(tick, qkv, out_x, down_core)
    out_cx = across_core(out_x)
    down_x = across_x(down_half)
    held = attention(tick, qkv, bucket_bias_rows, 0, pairs // 2, ())
    tick = after(tick, held[0], gated_x_0, out_cx)
    gated_y_0 = across_y(gated_x_0)
    gated_cx_0 = across_core(gated_x_0)
    et, linv, ot, mixed = attention(
        tick, qkv, bucket_bias_rows, pairs // 2, pairs - pairs // 2, held
    )
    tick = after(tick, mixed, gated_x_1, gated_cx_0)
    gated_y_1 = across_y(gated_x_1)
    gated_cx_1 = across_core(gated_x_1)
    out_pieces = (out_own, out_core, out_x, out_cx)
    hidden, n2, n2t = hidden_project(tick, tok, mixed, ffn_gain, out_pieces)
    tick = after(tick, n2, gated_y_0, gated_cx_1)
    gated_cy_0 = across_core(gated_y_0)
    tick = after(tick, gated_cy_0)
    own = (gate_weight, up_weight, gate_core, up_core)
    gated_0 = (gated_x_0, gated_y_0, gated_cx_0, gated_cy_0)
    held = gated(tick, n2, own + gated_0, 0, ())
    tick = after(tick, held[0], gated_y_1, down_x)
    gated_cy_1 = across_core(gated_y_1)
    down_y = across_y(down_x)
    down_cx = across_core(down_x)
    tick = after(tick, gated_cy_1)
    gated_1 = (gated_x_1, gated_y_1, gated_cx_1, gated_cy_1)
    inner, innert, slope, level = gated(tick, n2, own + gated_1, 1, held)
    tick = after(tick, inner, down_y, down_cx)
    down_cy = across_core(down_y)
    tick = after(tick, down_cy)
    down_pieces = (down_weight, down_core, down_x, down_y, down_cx, down_cy)
    embedded, after_grad, down_in, fnt, final_part = final_stage(
        tick, hidden, inner, cot, final_gain, down_pieces, out_pieces
    )

    big = functools.partial(Chunk, groups, scatter=True)
    thin = functools.partial(Chunk, groups, scatter=False)
    tick = after(tick, down_in)
    down_sum = big(weight_grad(tick, innert, down_in, "down_weight_grad"))
    tick = after(tick, down_sum.keep)
    down_sum.core(tick)
    gate_grad, up_grad = inner_grads(tick, down_in, slope, level, down_pieces)
    tick = after(tick, gate_grad, down_sum.from_core)
    down_sum.x(tick)
    gate_sum = big(weight_grad(tick, n2t, gate_grad, "gate_weight_grad"))
    tick = after(tick, gate_sum.keep)
    gate_sum.core(tick)
    up_sum = big(weight_grad(tick, n2t, up_grad, "up_weight_grad"))
    tick = after(tick, up_sum.keep, gate_sum.from_core)
    gate_sum.x(tick)
    up_sum.core(tick)
    hidden_grad, attn_in, ffn_part = hidden_grads(
        tick, gate_grad, up_grad, hidden, after_grad, ffn_gain, own + gated_0 + gated_1
    )
    tick = after(tick, attn_in, up_sum.from_core)
    up_sum.x(tick)
    out_sum = thin(out_grads(tick, ot, fnt, attn_in, cot))
    tick = after(tick, out_sum.keep, down_sum.from_x)
    out_sum.core(tick)
    down_sum.y(tick)
    mixed_grad = mixed_grads(tick, attn_in, out_pieces)
    tick = after(tick, mixed_grad, out_sum.from_core)
    out_sum.x(tick)
    held = attention_back(tick, qkv, et, linv, ot, mixed_grad, 0, pairs // 2, ())
    tick = after(tick, held[0], gate_sum.from_x, down_sum.from_y)
    gate_sum.y(tick)
    down_sum.z(tick)
    dq, dk, dv, bias_part = attention_back(
        tick, qkv, et, linv, ot, mixed_grad, pairs // 2, pairs - pairs // 2, held
    )
    tick = after(tick, dq, down_sum.from_z)
    down_sum.z_next(tick)
    first_sum = thin(query_key_grads(tick, n1t, dq, dk))
    tick = after(tick, first_sum.keep, gate_sum.from_y)
    first_sum.core(tick)
    gate_sum.z(tick)
    *blocks, attn_part = token_grads(
        tick, dq, dk, dv, hidden_grad, tok, embedded, attn_gain, qkv_pieces
    )
    tick = after(tick, attn_part, first_sum.from_core, up_sum.from_x, down_sum.from_z)
    first_sum.x(tick)
    up_sum.y(tick)
    down_sum.z_last(tick)
    value_sum = thin(
        value_grads(tick, n1t, dv, bias_part.reshape(H, D), attn_part, ffn_part, final_part)
    )
    tick = after(tick, value_sum.keep, gate_sum.from_z)
    value_sum.core(tick)
    gate_sum.z_next(tick)
    tick = after(tick, value_sum.from_core, down_sum.from_z, out_sum.from_x)
    value_sum.x(tick)
    out_sum.y(tick)
    tick = after(tick, up_sum.from_y)
    up_sum.z(tick)
    down_sum.last(tick)
    tick = after(tick, out_sum.from_y, first_sum.from_x)
    first_sum.y(tick)
    out_sum.z(tick)
    tick = after(tick, gate_sum.from_z)
    gate_sum.z_last(tick)
    tick = after(tick, up_sum.from_z, value_sum.from_x)
    value_sum.y(tick)
    up_sum.z_next(tick)
    tick = after(tick, first_sum.from_y, out_sum.from_z, down_sum.other)
    first_sum.z(tick)
    out_sum.z_next(tick)
    block_x = across_x(blocks[2])
    tick = after(tick, value_sum.from_y, gate_sum.from_z)
    value_sum.z(tick)
    gate_sum.last(tick)
    tick = after(tick, first_sum.from_z, up_sum.from_z)
    first_sum.z_next(tick)
    up_sum.z_last(tick)
    tick = after(tick, value_sum.from_z, out_sum.from_z, block_x)
    value_sum.z_next(tick)
    out_sum.last(tick)
    block_far = across_far(blocks[3])
    tick = after(tick, gate_sum.other, up_sum.from_z)
    up_sum.last(tick)
    tick = after(tick, first_sum.from_z, out_sum.other)
    first_sum.last(tick)
    block_core = across_core(blocks[1])
    tick = after(tick, value_sum.from_z)
    value_sum.last(tick)

    embedded, tokens_grad = unpack((blocks[0], block_core, block_x, block_far))
    value_grad, small = assemble(value_sum, D, PROJ)
    query_grad, key_grad = assemble(first_sum, D, D)
    out_grad, proj_grad = assemble(out_sum, D, PROJ)
    return (
        embedded,
        tokens_grad,
        query_grad,
        key_grad,
        value_grad,
        out_grad,
        assemble(gate_sum, FF)[0],
        assemble(up_sum, FF)[0],
        assemble(down_sum, D)[0],
        proj_grad,
        small[:, 0],
        small[:, 1],
        small[:, 2],
        small[: BUCKETS // SEQ, TABLE_COLUMN : TABLE_COLUMN + H],
    )


def solution(mesh):
    placed = (
        P("dp", "seq", None),
        P("dp"),
        P("seq", None),
        P("seq", None),
        P("seq", None),
        P("seq", None),
        P("seq", None),
        P("seq", None),
        P("seq", None),
        P("seq", None),
        P(),
        P(),
        P(),
        P(),
        P("dp", "seq", None),
    )
    return jax.shard_map(
        functools.partial(per_device, mesh.shape["dp"]),
        mesh=mesh,
        in_specs=placed,
        out_specs=(
            P("dp", "seq", None),
            P("dp", "seq", None),
            P("seq", None),
            P("seq", None),
            P("seq", None),
            P("seq", None),
            P("seq", None),
            P("seq", None),
            P("seq", None),
            P("seq", None),
            P("seq"),
            P("seq"),
            P("seq"),
            P("seq", None),
        ),
        check_vma=False,
    )
```

```python
import functools

import jax
import jax.numpy as jnp
import numpy as np
from jax import lax
from jax.experimental import pallas as pl
from jax.experimental.pallas import tpu as pltpu
from jax.sharding import PartitionSpec as P

D = 768
H = 12
HEAD = 64
FF = 2048
PROJ = 128
BUCKETS = 32
SLOT = 512
BLOCK = 128
SEQ = 4
SHARD = D // SEQ
HALF_FF = FF // 2
WIDE = D + PROJ
EPSILON = 1e-06
BIG_NEGATIVE = -1e30
GELU_A = 0.7978845608028654
GELU_B = 0.044715

F32 = jnp.float32
BF16 = jnp.bfloat16
VMEM = pl.BlockSpec(memory_space=pltpu.VMEM)
SMEM = pl.BlockSpec(memory_space=pltpu.SMEM)
ANY = pl.BlockSpec(memory_space=pl.ANY)
MIB = 1 << 20


def shape(dims, kind):
    return jax.ShapeDtypeStruct(dims, kind)


def params(wide=False):
    return pltpu.CompilerParams(vmem_limit_bytes=(58 if wide else 20) * MIB)


COST = pl.CostEstimate(flops=30000000000, bytes_accessed=100000000, transcendentals=0)
SMALL_COST = pl.CostEstimate(flops=1, bytes_accessed=1, transcendentals=0)


def bucket_of(relative):
    distance = np.abs(relative)
    scaled = np.log(np.maximum(distance, 1) / 8.0) / np.log(16.0) * 8.0
    far_bucket = np.minimum(8 + scaled.astype(np.int64), 15)
    return (relative > 0) * 16 + np.where(distance < 8, distance, far_bucket)


def skew_buckets():
    lanes = (np.arange(SLOT) + SLOT // 2) % SLOT - SLOT // 2
    relative = np.arange(8)[:, None] - lanes[None, :]
    return bucket_of(relative).astype(np.int32)


def table_indicator():
    lanes = (np.arange(SLOT) + SLOT // 2) % SLOT - SLOT // 2
    buckets = np.concatenate([bucket_of(-lanes), np.full(BLOCK, 15), np.full(BLOCK, 31)])
    here = BUCKETS // SEQ
    place = (buckets // here) * SHARD + buckets % here
    return (place[:, None] == np.arange(D)[None, :]).astype(np.float32)


def dot(left, right):
    return jnp.dot(left, right, preferred_element_type=F32)


def dot_t(left, right):
    return lax.dot_general(left, right, (((1,), (1,)), ((), ())), preferred_element_type=F32)


def place():
    return lax.axis_index("seq"), lax.rem(lax.axis_index("dp"), 2)


def relative_starts(rows, natural=False):
    me, y = place()
    z = lax.rem(lax.axis_index("dp") // 2, 2)
    bits = (me & 1, me >> 1, y, z)
    block = rows // 16
    starts = []
    for number in range(16):
        own = [(number >> shift) & 1 for shift in (3, 2, 1, 0)]
        core, x, first, second = (b if o else 1 - b for b, o in zip(bits, own))
        if natural:
            second = own[3]
        place_of = ((x * 2 + core) * 2 + first) * 2 + second
        starts.append(pl.multiple_of(place_of * block, 16))
    return block, starts


def begin(copies):
    for copy in copies:
        copy.start()
    return copies


def finish(copies):
    for copy in copies:
        copy.wait()


def run_all(copies):
    finish(begin(copies))


class Copies:
    def __init__(self, sems):
        self.sems, self.used = sems, 0

    def __call__(self, source, target):
        copy = pltpu.make_async_copy(source, target, self.sems.at[self.used])
        self.used += 1
        copy.start()
        return copy


def pieces_of(rows, plan, refs, target, sems, first=0):
    me, y = place()
    half = rows // 2
    starts = (
        me * rows,
        (me ^ 1) * rows,
        (me ^ 2) * rows + y * half,
        (me ^ 2) * rows + (1 - y) * half,
        (me ^ 3) * rows + y * half,
        (me ^ 3) * rows + (1 - y) * half,
        (me ^ 2) * rows,
        (me ^ 3) * rows,
    )
    return [
        pltpu.make_async_copy(
            refs[ref].at[:, pl.ds(source, width)],
            target.at[
                pl.ds(pl.multiple_of(starts[piece], 16), half if 2 <= piece < 6 else rows),
                pl.ds(to, width),
            ],
            sems.at[first + number],
        )
        for number, (ref, piece, source, to, width) in enumerate(plan)
    ]


QKV_PLANS = tuple(
    ((number, 0, 0, number * D, D),)
    + tuple((2 + piece, piece, number * D, number * D, D) for piece in range(1, 6))
    for number in range(3)
)
OUT_PLAN = tuple((ref, piece, 0, 0, WIDE) for ref, piece in enumerate((0, 1, 6, 7)))
DOWN_PLAN = tuple((ref, piece, 0, 0, D) for ref, piece in enumerate((0, 1, 6, 7)))


def gated_plan(part):
    column = part * HALF_FF
    parts = [(4 + 4 * part + number, piece) for number, piece in enumerate((2, 3, 4, 5))]
    return (
        (0, 0, column, column, HALF_FF),
        (1, 0, column, FF + column, HALF_FF),
        (2, 1, column, column, HALF_FF),
        (3, 1, column, FF + column, HALF_FF),
    ) + tuple(
        (ref, piece, number * HALF_FF, number * FF + column, HALF_FF)
        for ref, piece in parts
        for number in range(2)
    )


GATED_PLANS = (gated_plan(0), gated_plan(1))


def relative_copies(source, target, sems, natural=False):
    block, starts = relative_starts(source.shape[0], natural)
    return [
        pltpu.make_async_copy(
            source.at[pl.ds(begin, block), :],
            target.at[pl.ds(number * block, block), :],
            sems.at[number],
        )
        for number, begin in enumerate(starts)
    ]


def inverse_rms(values):
    return lax.rsqrt(jnp.mean(values * values, axis=-1, keepdims=True) + EPSILON)


def norm_backward(values, gain, incoming):
    r = inverse_rms(values)
    weighted = gain * incoming
    inner = jnp.mean(weighted * values, axis=-1, keepdims=True)
    return r * weighted - values * (r * r * r * inner)


def pack_first_kernel(lens, q, k, v, qkv_half, sems):
    _, y = place()
    half = SHARD // 2
    rows = pl.ds(pl.multiple_of(y * half, 16), half)
    run_all(
        [
            pltpu.make_async_copy(
                weight.at[rows, :], qkv_half.at[:, pl.ds(number * D, D)], sems.at[number]
            )
            for number, weight in enumerate((q, k, v))
        ]
    )


def pack_first(lens, q, k, v):
    return pl.pallas_call(
        pack_first_kernel,
        out_shape=shape((SHARD // 2, 3 * D), BF16),
        in_specs=[SMEM] + [ANY] * 3,
        out_specs=VMEM,
        scratch_shapes=[pltpu.SemaphoreType.DMA((3,))],
        compiler_params=params(wide=True),
        cost_estimate=COST,
        name="pack_first",
    )(lens, q, k, v)


def pack_tokens_kernel(lens, tokens, cot, *refs):
    blocks, sems = refs[:4], refs[4]
    me, _ = place()
    pairs = []
    for flip, block in enumerate(blocks):
        pairs.append((tokens.at[me ^ flip], block.at[:, pl.ds(0, D)]))
        pairs.append((cot.at[me ^ flip], block.at[:, pl.ds(D, PROJ)]))
    run_all([pltpu.make_async_copy(a, b, sems.at[i]) for i, (a, b) in enumerate(pairs)])


def pack_tokens(lens, tokens, cot):
    return pl.pallas_call(
        pack_tokens_kernel,
        out_shape=(shape((BLOCK, WIDE), BF16),) * 4,
        in_specs=[SMEM] + [ANY] * 2,
        out_specs=(VMEM,) * 4,
        scratch_shapes=[pltpu.SemaphoreType.DMA((8,))],
        compiler_params=params(wide=True),
        cost_estimate=COST,
        name="pack_tokens",
    )(lens, tokens, cot)


def pack_rest_kernel(lens, q, k, v, out, proj, gate, up, qkv, out_own, part_0, part_1, sems):
    _, y = place()
    half = SHARD // 2
    rows = pl.ds(pl.multiple_of(y * half, 16), half)
    pairs = [(w, qkv.at[:, pl.ds(number * D, D)]) for number, w in enumerate((q, k, v))]
    pairs.append((out, out_own.at[:, pl.ds(0, D)]))
    pairs.append((proj, out_own.at[:, pl.ds(D, PROJ)]))
    for number, part in enumerate((part_0, part_1)):
        columns = pl.ds(number * HALF_FF, HALF_FF)
        pairs.append((gate.at[rows, columns], part.at[:, pl.ds(0, HALF_FF)]))
        pairs.append((up.at[rows, columns], part.at[:, pl.ds(HALF_FF, HALF_FF)]))
    run_all([pltpu.make_async_copy(a, b, sems.at[i]) for i, (a, b) in enumerate(pairs)])


def pack_rest(lens, q, k, v, out, proj, gate, up):
    half = SHARD // 2
    return pl.pallas_call(
        pack_rest_kernel,
        out_shape=(shape((SHARD, 3 * D), BF16), shape((SHARD, WIDE), BF16))
        + (shape((half, FF), BF16),) * 2,
        in_specs=[SMEM] + [ANY] * 7,
        out_specs=(VMEM,) * 4,
        scratch_shapes=[pltpu.SemaphoreType.DMA((9,))],
        compiler_params=params(wide=True),
        cost_estimate=COST,
        name="pack_rest",
    )(lens, q, k, v, out, proj, gate, up)


def qkv_kernel(lens, gain, own, from_core, from_x, from_far, *refs):
    pieces, outs, refs = refs[:8], refs[8:12], refs[12:]
    held, n1, n1t, weight, out, block_sems, sems, done_sems = refs
    me, _ = place()
    store = Copies(done_sems)
    blocks = begin(
        [
            pltpu.make_async_copy(
                piece,
                held.at[pl.ds(pl.multiple_of((me ^ flip) * BLOCK, BLOCK), BLOCK), :],
                block_sems.at[flip],
            )
            for flip, piece in enumerate((own, from_core, from_x, from_far))
        ]
    )
    loads = [
        begin(pieces_of(SHARD, plan, pieces, weight, sems, 6 * number))
        for number, plan in enumerate(QKV_PLANS)
    ]
    finish(blocks)
    stores = [store(held.at[:, pl.ds(0, D)], outs[0]), store(held.at[:, pl.ds(D, PROJ)], outs[1])]
    scale = gain[...].reshape(1, D)
    for block in range(SLOT // BLOCK):
        rows = pl.ds(block * BLOCK, BLOCK)
        values = held[rows, 0:D].astype(F32)
        normed = (values * inverse_rms(values) * scale).astype(BF16)
        n1[rows, :] = normed
        n1t[:, rows] = normed.T
    stores.append(store(n1t, outs[2]))
    for number in range(3):
        finish(loads[number])
        columns = slice(number * D, (number + 1) * D)
        out[:, columns] = dot(n1[...], weight[:, columns]).astype(BF16)
        stores.append(store(out.at[:, columns], outs[3].at[:, columns]))
    finish(stores)


def qkv_project(lens, gain, blocks, pieces):
    wide, tall = (SLOT, D), (D, SLOT)
    return pl.pallas_call(
        qkv_kernel,
        out_shape=(
            shape(wide, BF16),
            shape((SLOT, PROJ), BF16),
            shape(tall, BF16),
            shape((SLOT, 3 * D), BF16),
        ),
        in_specs=[SMEM, VMEM] + [ANY] * 12,
        out_specs=(ANY,) * 4,
        scratch_shapes=[
            pltpu.VMEM((SLOT, WIDE), BF16),
            pltpu.VMEM(wide, BF16),
            pltpu.VMEM(tall, BF16),
            pltpu.VMEM((D, 3 * D), BF16),
            pltpu.VMEM((SLOT, 3 * D), BF16),
            pltpu.SemaphoreType.DMA((4,)),
            pltpu.SemaphoreType.DMA((18,)),
            pltpu.SemaphoreType.DMA((6,)),
        ],
        compiler_params=params(wide=True),
        cost_estimate=COST,
        name="qkv_project",
    )(lens, gain, *blocks, *pieces)


HALF_Q = 256


def attention_kernel(first, lens, q, k, v, rows_of_bias, buckets, *refs):
    et, linv, ot, o, bias = refs[-5:]
    me, _ = place()
    length = lens[me]
    pair = pl.program_id(0) + first
    k_pair = k[...]
    vt = v[...].T
    qt = q[...].T
    row_in_pair = lax.broadcasted_iota(jnp.int32, (2 * HEAD, SLOT), 0)
    key_index = lax.broadcasted_iota(jnp.int32, (SLOT, HALF_Q), 0)
    for head in range(2):
        base = jnp.zeros((8, SLOT), F32)
        for bucket in range(BUCKETS):
            base = jnp.where(buckets[...] == bucket, rows_of_bias[bucket, 2 * pair + head], base)
        for group in range(BLOCK // 8):
            bias[pl.ds(group * 8, 8), :] = pltpu.roll(base, 8 * group, 1) if group else base
        below = rows_of_bias[15, 2 * pair + head]
        above = rows_of_bias[31, 2 * pair + head]
        in_head = (row_in_pair >= HEAD * head) & (row_in_pair < HEAD * (head + 1))
        qt_head = jnp.where(in_head, qt, jnp.zeros_like(qt))
        for part in range(SLOT // HALF_Q):
            raw = dot(k_pair, qt_head[:, part * HALF_Q : (part + 1) * HALF_Q])
            rows = []
            for key_block in range(4):
                cells = []
                for sub in range(HALF_Q // BLOCK):
                    query_block = part * (HALF_Q // BLOCK) + sub
                    cell = raw[
                        key_block * BLOCK : (key_block + 1) * BLOCK,
                        sub * BLOCK : (sub + 1) * BLOCK,
                    ]
                    apart = key_block - query_block
                    if apart >= 2:
                        cell = cell + above
                    elif apart <= -2:
                        cell = cell + below
                    else:
                        lane = (-apart * BLOCK) % SLOT
                        cell = cell + bias[:, lane : lane + BLOCK]
                    cells.append(cell)
                rows.append(jnp.concatenate(cells, axis=1))
            scores = jnp.concatenate(rows, axis=0)
            scores = jnp.where(key_index < length, scores, BIG_NEGATIVE)
            top = jnp.max(scores, axis=0, keepdims=True)
            weights = jnp.exp(scores - top)
            inverse = 1.0 / jnp.sum(weights, axis=0, keepdims=True)
            low = weights.astype(BF16)
            columns = pl.ds(part * HALF_Q, HALF_Q)
            et[head, :, columns] = low
            linv[head, :, columns] = inverse
            mixed = dot(vt[head * HEAD : (head + 1) * HEAD, :], low) * inverse
            ot[pl.ds(head * HEAD, HEAD), columns] = mixed.astype(BF16)
    o[...] = ot[...].T


def attention(lens, qkv, rows_of_bias, first, count, held):
    pair = 2 * HEAD
    pairs = H // 2
    return pl.pallas_call(
        functools.partial(attention_kernel, first),
        grid=(count,),
        out_shape=(
            shape((H, SLOT, SLOT), BF16),
            shape((H, 1, SLOT), F32),
            shape((D, SLOT), BF16),
            shape((SLOT, D), BF16),
        ),
        in_specs=[
            SMEM,
            pl.BlockSpec((SLOT, pair), lambda i: (0, first + i)),
            pl.BlockSpec((SLOT, pair), lambda i: (0, pairs + first + i)),
            pl.BlockSpec((SLOT, pair), lambda i: (0, 2 * pairs + first + i)),
            SMEM,
            pl.BlockSpec((8, SLOT), lambda i: (0, 0)),
        ]
        + [ANY] * len(held),
        out_specs=(
            pl.BlockSpec((2, SLOT, SLOT), lambda i: (first + i, 0, 0)),
            pl.BlockSpec((2, 1, SLOT), lambda i: (first + i, 0, 0)),
            pl.BlockSpec((pair, SLOT), lambda i: (first + i, 0)),
            pl.BlockSpec((SLOT, pair), lambda i: (0, first + i)),
        ),
        input_output_aliases={6 + i: i for i in range(len(held))},
        scratch_shapes=[pltpu.VMEM((BLOCK, SLOT), F32)],
        compiler_params=params(wide=True),
        cost_estimate=COST,
        name="attention",
    )(lens, qkv, qkv, qkv, rows_of_bias, jnp.asarray(skew_buckets()), *held)


def feed_forward_kernel(lens, ffn_gain, final_gain, tok, mixed, cot, *refs):
    out_pieces, gated_pieces, down_pieces, refs = refs[:4], refs[4:16], refs[16:20], refs[20:]
    hidden_out, n2t_out, gate_out, up_out, embedded_out, after_out, fnt_out = refs[:7]
    send_out, keep_out = refs[7:9]
    w_out, w_gated, w_down, tok_v, mixed_v, cot_v, hidden, n2, n2t, inner, innert = refs[9:20]
    slope, level, embedded, after_grad, down_in, fnt, send, keep = refs[20:28]
    out_sems, gated_sems, down_sems, in_sems, done_sems = refs[28:]
    load, store = Copies(in_sems), Copies(done_sems)

    loads = begin(pieces_of(SHARD, OUT_PLAN, out_pieces, w_out, out_sems))
    loads += [load(mixed, mixed_v), load(tok, tok_v), load(cot, cot_v)]
    gated_loads = [
        begin(pieces_of(SHARD, plan, gated_pieces, w_gated, gated_sems, 12 * number))
        for number, plan in enumerate(GATED_PLANS)
    ]
    down_loads = begin(pieces_of(FF // SEQ, DOWN_PLAN, down_pieces, w_down, down_sems))
    stores = []

    finish(loads)
    scale = ffn_gain[...].reshape(1, D)
    for block in range(2):
        rows = pl.ds(block * 256, 256)
        values = tok_v[rows, :].astype(F32) + dot(mixed_v[rows, :], w_out[:, 0:D])
        hidden[rows, :] = values
        normed = (values * inverse_rms(values) * scale).astype(BF16)
        n2[rows, :] = normed
        n2t[:, rows] = normed.T
    stores.append(store(hidden, hidden_out))
    size, starts = relative_starts(D)
    for number, begin_row in enumerate(starts):
        stores.append(
            store(n2t.at[pl.ds(begin_row, size), :], n2t_out.at[pl.ds(number * size, size), :])
        )

    me, y = place()
    z = lax.rem(lax.axis_index("dp") // 2, 2)

    def step(tile, carry):
        columns = pl.ds(pl.multiple_of(tile * 512, 512), 512)
        g = dot(n2[...], w_gated[:, columns])
        u = dot(n2[...], w_gated[:, pl.ds(pl.multiple_of(FF + tile * 512, 512), 512)])
        square = g * g
        t = jnp.tanh(GELU_A * g * (1.0 + GELU_B * square))
        half_up = 0.5 * (1.0 + t)
        activated = g * half_up
        derivative = half_up + 0.5 * g * (1.0 - t * t) * (GELU_A * (1.0 + 3 * GELU_B * square))
        value = (activated * u).astype(BF16)
        inner[:, columns] = value
        slope[:, columns] = (derivative * u).astype(BF16)
        level[:, columns] = activated.astype(BF16)
        core_own = (lax.rem(tile, 2) == lax.rem(me, 2)).astype(jnp.int32)
        x_own = (tile // 2 == me // 2).astype(jnp.int32)
        target = (core_own * 2 + x_own) * 512
        turned = value.T
        for number in range(4):
            y_own = (number >> 1 == y).astype(jnp.int32)
            z_own = ((number & 1) == z).astype(jnp.int32)
            row = pl.multiple_of(target + y_own * 256 + z_own * BLOCK, BLOCK)
            innert[pl.ds(row, BLOCK), :] = turned[number * BLOCK : (number + 1) * BLOCK, :]
        return carry

    for part in range(2):
        finish(gated_loads[part])
        lax.fori_loop(2 * part, 2 * part + 2, step, 0)

    finish(down_loads)
    scale = final_gain[...].reshape(1, D)
    for block in range(2):
        rows = pl.ds(block * 256, 256)
        values = hidden[rows, :] + dot(inner[rows, :], w_down[...])
        normed = (values * inverse_rms(values) * scale).astype(BF16)
        fnt[:, rows] = normed.T
        embedded[rows, :] = dot(normed, w_out[:, D:WIDE]).astype(BF16)
        gradient = norm_backward(values, scale, dot_t(cot_v[rows, :], w_out[:, D:WIDE]))
        after_grad[rows, :] = gradient
        down_in[rows, :] = gradient.astype(BF16)
    for source, target in ((after_grad, after_out), (embedded, embedded_out), (fnt, fnt_out)):
        stores.append(store(source, target))

    for number, (part, target) in enumerate(((send, send_out), (keep, keep_out))):

        def grad(tile, carry):
            rows = pl.ds(pl.multiple_of(tile * 256, 256), 256)
            source = pl.ds(pl.multiple_of(number * (FF // 2) + tile * 256, 256), 256)
            part[rows, :] = dot(innert[source, :], down_in[...]).astype(BF16)
            return carry

        lax.fori_loop(0, FF // 2 // 256, grad, 0)
        stores.append(store(part, target))

    def back(tile, carry):
        columns = pl.ds(pl.multiple_of(tile * 512, 512), 512)
        incoming = dot_t(down_in[...], w_down[columns, :])
        slope[:, columns] = (incoming * slope[:, columns].astype(F32)).astype(BF16)
        level[:, columns] = (incoming * level[:, columns].astype(F32)).astype(BF16)
        return carry

    lax.fori_loop(0, FF // 512, back, 0)
    stores += [store(slope, gate_out), store(level, up_out)]
    finish(stores)


def feed_forward(lens, tok, mixed, cot, ffn_gain, final_gain, out_pieces, gated_pieces, down_pieces):
    wide, tall, full = (SLOT, D), (D, SLOT), (SLOT, FF)
    pieces = tuple(out_pieces) + tuple(gated_pieces) + tuple(down_pieces)
    return pl.pallas_call(
        feed_forward_kernel,
        out_shape=(
            shape(wide, F32),
            shape(tall, BF16),
            shape(full, BF16),
            shape(full, BF16),
            shape((SLOT, PROJ), BF16),
            shape(wide, F32),
            shape(tall, BF16),
            shape((FF // 2, D), BF16),
            shape((FF // 2, D), BF16),
        ),
        in_specs=[SMEM, VMEM, VMEM] + [ANY] * (3 + len(pieces)),
        out_specs=(ANY,) * 9,
        scratch_shapes=[
            pltpu.VMEM((D, WIDE), BF16),
            pltpu.VMEM((D, 2 * FF), BF16),
            pltpu.VMEM((FF, D), BF16),
            pltpu.VMEM(wide, BF16),
            pltpu.VMEM(wide, BF16),
            pltpu.VMEM((SLOT, PROJ), BF16),
            pltpu.VMEM(wide, F32),
            pltpu.VMEM(wide, BF16),
            pltpu.VMEM(tall, BF16),
            pltpu.VMEM(full, BF16),
            pltpu.VMEM((FF, SLOT), BF16),
            pltpu.VMEM(full, BF16),
            pltpu.VMEM(full, BF16),
            pltpu.VMEM((SLOT, PROJ), BF16),
            pltpu.VMEM(wide, F32),
            pltpu.VMEM(wide, BF16),
            pltpu.VMEM(tall, BF16),
            pltpu.VMEM((FF // 2, D), BF16),
            pltpu.VMEM((FF // 2, D), BF16),
            pltpu.SemaphoreType.DMA((4,)),
            pltpu.SemaphoreType.DMA((24,)),
            pltpu.SemaphoreType.DMA((4,)),
            pltpu.SemaphoreType.DMA((3,)),
            pltpu.SemaphoreType.DMA((24,)),
        ],
        compiler_params=params(wide=True),
        cost_estimate=COST,
        name="feed_forward",
    )(lens, ffn_gain, final_gain, tok, mixed, cot, *pieces)


def row_grads(left, right, halves, column=0, loads=(), store=None, outs=()):
    half = left.shape[0] // 2
    width = right.shape[1]
    size = 1024 if width % 1024 == 0 else width
    stores = []
    for tile in range(width // size):
        if loads:
            loads[tile].wait()
        target = slice(column + tile * size, column + (tile + 1) * size)
        both = dot(left[...], right[:, tile * size : (tile + 1) * size]).astype(BF16)
        for number, part in enumerate(halves):
            part[:, target] = both[number * half : (number + 1) * half, :]
            stores.append(store(part.at[:, target], outs[number].at[:, target]))
    return stores


def tile_loads(load, source, target, size=1024):
    return [
        load(source.at[:, pl.ds(begin_at, size)], target.at[:, pl.ds(begin_at, size)])
        for begin_at in range(0, source.shape[1], size)
    ]


def gate_grad_kernel(lens, n2t, gate_grad, send_out, keep_out, n2t_v, gate_v, send, keep, *sems):
    load, store = Copies(sems[0]), Copies(sems[1])
    first = load(n2t, n2t_v)
    loads = tile_loads(load, gate_grad, gate_v)
    first.wait()
    finish(row_grads(n2t_v, gate_v, (send, keep), 0, loads, store, (send_out, keep_out)))


def gate_grads(lens, n2t, gate_grad):
    part = (D // 2, FF)
    return pl.pallas_call(
        gate_grad_kernel,
        out_shape=(shape(part, BF16),) * 2,
        in_specs=[SMEM] + [ANY] * 2,
        out_specs=(ANY,) * 2,
        scratch_shapes=[
            pltpu.VMEM((D, SLOT), BF16),
            pltpu.VMEM((SLOT, FF), BF16),
            pltpu.VMEM(part, BF16),
            pltpu.VMEM(part, BF16),
            pltpu.SemaphoreType.DMA((3,)),
            pltpu.SemaphoreType.DMA((4,)),
        ],
        compiler_params=params(wide=True),
        cost_estimate=COST,
        name="gate_grads",
    )(lens, n2t, gate_grad)


def up_grad_kernel(lens, gain, n2t, gate_grad, up_grad, hidden, after_grad, *refs):
    pieces, outs, refs = refs[:12], refs[12:16], refs[16:]
    weight, n2t_v, gate_v, up_v, hidden_v, after_v, send, keep, grad, attn_in = refs[:10]
    sems, in_sems, done_sems = refs[10:]
    load, store = Copies(in_sems), Copies(done_sems)
    first = load(n2t, n2t_v)
    loads = tile_loads(load, up_grad, up_v)
    gate_load = load(gate_grad, gate_v)
    plan = sum(GATED_PLANS, ())
    gate_plan = tuple(entry for entry in plan if entry[3] < FF)
    up_plan = tuple(entry for entry in plan if entry[3] >= FF)
    gate_pieces = begin(pieces_of(SHARD, gate_plan, pieces, weight, sems))
    up_pieces = begin(pieces_of(SHARD, up_plan, pieces, weight, sems, len(gate_plan)))
    later = [load(hidden, hidden_v), load(after_grad, after_v)]
    first.wait()
    stores = row_grads(n2t_v, up_v, (send, keep), 0, loads, store, outs[0:2])
    gate_load.wait()
    finish(gate_pieces)
    for block in range(2):
        rows = pl.ds(block * 256, 256)
        grad[rows, :] = dot_t(gate_v[rows, :], weight[:, 0:FF])
    finish(up_pieces)
    finish(later)
    scale = gain[...].reshape(1, D)
    for block in range(2):
        rows = pl.ds(block * 256, 256)
        incoming = grad[rows, :] + dot_t(up_v[rows, :], weight[:, FF:])
        gradient = norm_backward(hidden_v[rows, :], scale, incoming) + after_v[rows, :]
        grad[rows, :] = gradient
        attn_in[rows, :] = gradient.astype(BF16)
    stores += [store(attn_in, outs[3]), store(grad, outs[2])]
    finish(stores)


def up_grads(lens, gain, n2t, gate_grad, up_grad, hidden, after_grad, pieces):
    full, part, wide = (SLOT, FF), (D // 2, FF), (SLOT, D)
    return pl.pallas_call(
        up_grad_kernel,
        out_shape=(shape(part, BF16),) * 2 + (shape(wide, F32), shape(wide, BF16)),
        in_specs=[SMEM, VMEM] + [ANY] * 17,
        out_specs=(ANY,) * 4,
        scratch_shapes=[
            pltpu.VMEM((D, 2 * FF), BF16),
            pltpu.VMEM((D, SLOT), BF16),
            pltpu.VMEM(full, BF16),
            pltpu.VMEM(full, BF16),
            pltpu.VMEM(wide, F32),
            pltpu.VMEM(wide, F32),
            pltpu.VMEM(part, BF16),
            pltpu.VMEM(part, BF16),
            pltpu.VMEM(wide, F32),
            pltpu.VMEM(wide, BF16),
            pltpu.SemaphoreType.DMA((24,)),
            pltpu.SemaphoreType.DMA((6,)),
            pltpu.SemaphoreType.DMA((6,)),
        ],
        compiler_params=params(wide=True),
        cost_estimate=COST,
        name="up_grads",
    )(lens, gain, n2t, gate_grad, up_grad, hidden, after_grad, *pieces)


def out_grad_kernel(lens, ot, fnt, attn_in, cot, *refs):
    pieces, outs, refs = refs[:4], refs[4:7], refs[7:]
    weight, left, proj_left, attn_v, cot_v, send, keep, mixed = refs[:8]
    sems, left_sems, proj_sems, in_sems, done_sems = refs[8:]
    load, store = Copies(in_sems), Copies(done_sems)
    loads = [load(attn_in, attn_v)]
    loads += begin(relative_copies(ot, left, left_sems))
    pieces = begin(pieces_of(SHARD, OUT_PLAN, pieces, weight, sems))
    later = [load(cot, cot_v)]
    later += begin(relative_copies(fnt, proj_left, proj_sems))
    finish(loads)
    stores = row_grads(left, attn_v, (send, keep), 0, (), store, outs[0:2])
    finish(later)
    stores += row_grads(proj_left, cot_v, (send, keep), D, (), store, outs[0:2])
    finish(pieces)
    mixed[...] = dot_t(attn_v[...], weight[:, 0:D]).astype(BF16)
    stores.append(store(mixed, outs[2]))
    finish(stores)


def out_grads(lens, ot, fnt, attn_in, cot, pieces):
    return pl.pallas_call(
        out_grad_kernel,
        out_shape=(shape((D // 2, WIDE), BF16),) * 2 + (shape((SLOT, D), BF16),),
        in_specs=[SMEM] + [ANY] * 8,
        out_specs=(ANY,) * 3,
        scratch_shapes=[
            pltpu.VMEM((D, WIDE), BF16),
            pltpu.VMEM((D, SLOT), BF16),
            pltpu.VMEM((D, SLOT), BF16),
            pltpu.VMEM((SLOT, D), BF16),
            pltpu.VMEM((SLOT, PROJ), BF16),
            pltpu.VMEM((D // 2, WIDE), BF16),
            pltpu.VMEM((D // 2, WIDE), BF16),
            pltpu.VMEM((SLOT, D), BF16),
            pltpu.SemaphoreType.DMA((4,)),
            pltpu.SemaphoreType.DMA((16,)),
            pltpu.SemaphoreType.DMA((16,)),
            pltpu.SemaphoreType.DMA((2,)),
            pltpu.SemaphoreType.DMA((5,)),
        ],
        compiler_params=params(wide=True),
        cost_estimate=COST,
        name="out_grads",
    )(lens, ot, fnt, attn_in, cot, *pieces)


def qkv_grad_kernel(lens, table, indicator, n1t, dq, dk, dv, *refs):
    outs, left, dq_v, dk_v, dv_v = refs[:4], refs[4], refs[5], refs[6], refs[7]
    send, keep, value_send, value_keep, small, left_sems, in_sems, done_sems = refs[8:]
    load, store = Copies(in_sems), Copies(done_sems)
    first = [load(dq, dq_v)] + begin(relative_copies(n1t, left, left_sems))
    second, third = load(dk, dk_v), load(dv, dv_v)
    finish(first)
    stores = row_grads(left, dq_v, (send, keep), 0, (), store, outs[0:2])
    stores += row_grads(left, dk_v, (send, keep), D, (second,), store, outs[0:2])
    by_lane = jnp.concatenate([table[pair] for pair in range(H // 2)], axis=0)
    high = by_lane.astype(BF16)
    low = (by_lane - high.astype(F32)).astype(BF16)
    by_bucket = dot(high, indicator[...]) + dot(low, indicator[...])
    small[...] = jnp.concatenate([by_bucket, jnp.zeros((PROJ - H, D), F32)], axis=0).T
    block, starts = relative_starts(D)
    for number, row in enumerate(starts):
        target = value_keep if number >= 8 else value_send
        target[pl.ds((number & 7) * block, block), D:WIDE] = small[pl.ds(row, block), :].astype(
            BF16
        )
    columns = pl.ds(D, PROJ)
    for number, part in enumerate((value_send, value_keep)):
        stores.append(store(part.at[:, columns], outs[2 + number].at[:, columns]))
    stores += row_grads(left, dv_v, (value_send, value_keep), 0, (third,), store, outs[2:4])
    finish(stores)


def qkv_grads(lens, table, n1t, dq, dk, dv):
    pair, single = (D // 2, 2 * D), (D // 2, WIDE)
    return pl.pallas_call(
        qkv_grad_kernel,
        out_shape=(shape(pair, BF16),) * 2 + (shape(single, BF16),) * 2,
        in_specs=[SMEM, VMEM, VMEM] + [ANY] * 4,
        out_specs=(ANY,) * 4,
        scratch_shapes=[pltpu.VMEM((D, SLOT), BF16)]
        + [pltpu.VMEM((SLOT, D), BF16)] * 3
        + [pltpu.VMEM(pair, BF16)] * 2
        + [pltpu.VMEM(single, BF16)] * 2
        + [
            pltpu.VMEM((D, PROJ), F32),
            pltpu.SemaphoreType.DMA((16,)),
            pltpu.SemaphoreType.DMA((3,)),
            pltpu.SemaphoreType.DMA((8,)),
        ],
        compiler_params=params(wide=True),
        cost_estimate=COST,
        name="qkv_grads",
    )(lens, table, jnp.asarray(table_indicator(), dtype=BF16), n1t, dq, dk, dv)


def attention_back_kernel(lens, q, k, v, et, linv, ot, do, *refs):
    dq, dk, dv, bias_grad, dqt, near = refs[-6:]
    lane_in_pair = lax.broadcasted_iota(jnp.int32, (SLOT, 2 * HEAD), 1)
    q_pair, v_pair = q[...], v[...]
    kt = k[...].T
    out_gradt = do[...].astype(F32).T
    scaled = []
    deltas = []
    for head in range(2):
        rows = slice(head * HEAD, (head + 1) * HEAD)
        low = (out_gradt[rows, :] * linv[head]).astype(BF16)
        scaled.append(low)
        deltas.append(
            jnp.sum(low.astype(F32) * ot[rows, :].astype(F32), axis=0, keepdims=True)
        )
    scaled_pair = jnp.concatenate(scaled, axis=0).T
    zeros = jnp.zeros((HEAD, SLOT), BF16)
    key_total = jnp.zeros((SLOT, 2 * HEAD), F32)
    value_total = jnp.zeros((SLOT, 2 * HEAD), F32)
    row_of_eight = lax.broadcasted_iota(jnp.int32, (8, SLOT), 0)
    for head in range(2):
        in_head = (lane_in_pair >= head * HEAD) & (lane_in_pair < (head + 1) * HEAD)
        q_head = jnp.where(in_head, q_pair, jnp.zeros_like(q_pair))
        do_head = jnp.where(in_head, scaled_pair, jnp.zeros_like(scaled_pair))
        dot_head = jnp.concatenate(
            [scaled[head], zeros] if head == 0 else [zeros, scaled[head]], axis=0
        )
        near_sums = {-1: None, 0: None, 1: None}
        far_sums = {-1: None, 1: None}
        for part in range(SLOT // HALF_Q):
            columns = slice(part * HALF_Q, (part + 1) * HALF_Q)
            prob_grad = dot(v_pair, dot_head[:, columns])
            low_weights = et[head, :, columns]
            score_grad = low_weights.astype(F32) * (prob_grad - deltas[head][:, columns])
            low = score_grad.astype(BF16)
            key_total = key_total + dot(low, q_head[columns, :])
            value_total = value_total + dot(low_weights, do_head[columns, :])
            dqt[pl.ds(head * HEAD, HEAD), columns] = dot(
                kt[head * HEAD : (head + 1) * HEAD, :], low
            ).astype(BF16)
            for key_block in range(4):
                for sub in range(HALF_Q // BLOCK):
                    apart = key_block - part * (HALF_Q // BLOCK) - sub
                    cell = score_grad[
                        key_block * BLOCK : (key_block + 1) * BLOCK,
                        sub * BLOCK : (sub + 1) * BLOCK,
                    ]
                    if abs(apart) >= 2:
                        side = 1 if apart > 0 else -1
                        folded = jnp.sum(cell.reshape(BLOCK // 8, 8, BLOCK), axis=0)
                        old = far_sums[side]
                        far_sums[side] = folded if old is None else old + folded
                    else:
                        old = near_sums[apart]
                        near_sums[apart] = cell if old is None else old + cell
        near[...] = jnp.zeros_like(near)
        for apart in (-1, 0, 1):
            lane = (-apart * BLOCK) % SLOT
            near[:, lane : lane + BLOCK] = near_sums[apart]
        folded = near[0:8, :]
        for group in range(1, BLOCK // 8):
            folded = folded + pltpu.roll(near[group * 8 : group * 8 + 8, :], SLOT - 8 * group, 1)
        for bit in (1, 2, 4):
            folded = jnp.where(
                (row_of_eight & bit) != 0, pltpu.roll(folded, SLOT - bit, 1), folded
            )
        here = slice(head, head + 1)
        bias_grad[0, here, 0:SLOT] = jnp.sum(folded, axis=0, keepdims=True)
        for number, side in enumerate((-1, 1)):
            lane = SLOT + number * BLOCK
            bias_grad[0, here, lane : lane + BLOCK] = jnp.sum(
                far_sums[side], axis=0, keepdims=True
            )
    dk[...] = key_total.astype(BF16)
    dv[...] = value_total.astype(BF16)
    dq[...] = dqt[...].T


def attention_back(lens, qkv, et, linv, ot, do, first, count, held):
    pair = 2 * HEAD
    pairs = H // 2
    wide = pl.BlockSpec((SLOT, pair), lambda i: (0, first + i))
    return pl.pallas_call(
        attention_back_kernel,
        grid=(count,),
        out_shape=(shape((SLOT, D), BF16),) * 3 + (shape((pairs, 2, D), F32),),
        in_specs=[
            SMEM,
            wide,
            pl.BlockSpec((SLOT, pair), lambda i: (0, pairs + first + i)),
            pl.BlockSpec((SLOT, pair), lambda i: (0, 2 * pairs + first + i)),
            pl.BlockSpec((2, SLOT, SLOT), lambda i: (first + i, 0, 0)),
            pl.BlockSpec((2, 1, SLOT), lambda i: (first + i, 0, 0)),
            pl.BlockSpec((pair, SLOT), lambda i: (first + i, 0)),
            wide,
        ]
        + [ANY] * len(held),
        out_specs=(wide,) * 3 + (pl.BlockSpec((1, 2, D), lambda i: (first + i, 0, 0)),),
        input_output_aliases={8 + i: i for i in range(len(held))},
        scratch_shapes=[pltpu.VMEM((pair, SLOT), BF16), pltpu.VMEM((BLOCK, SLOT), F32)],
        compiler_params=params(wide=True),
        cost_estimate=COST,
        name="attention_back",
    )(lens, qkv, qkv, qkv, et, linv, ot, do, *held)


def token_grad_kernel(lens, gain, embedded, dq, dk, dv, hidden_grad, tok, *refs):
    pieces, outs, refs = refs[:8], refs[8:12], refs[12:]
    weight, embedded_v, dq_v, dk_v, dv_v, hidden_v, tok_v, total = refs[:8]
    packed, (sems, in_sems, done_sems) = refs[8:12], refs[12:]
    load, store = Copies(in_sems), Copies(done_sems)
    me, _ = place()
    loads = []
    for number, (source, target) in enumerate(((dq, dq_v), (dk, dk_v), (dv, dv_v))):
        plan = QKV_PLANS[number]
        loads.append(
            [load(source, target)]
            + begin(pieces_of(SHARD, plan, pieces, weight, sems, 6 * number))
        )
    later = [load(hidden_grad, hidden_v), load(tok, tok_v), load(embedded, embedded_v)]
    for number, source in enumerate((dq_v, dk_v, dv_v)):
        finish(loads[number])
        for block in range(2):
            rows = pl.ds(block * 256, 256)
            term = dot_t(source[rows, :], weight[:, number * D : (number + 1) * D])
            total[rows, :] = term if number == 0 else total[rows, :] + term
    finish(later)
    scale = gain[...].reshape(1, D)
    stores = []
    for flip, target in enumerate(packed):
        rows = pl.ds(pl.multiple_of((me ^ flip) * BLOCK, BLOCK), BLOCK)
        gradient = norm_backward(tok_v[rows, :].astype(F32), scale, total[rows, :])
        target[:, 0:D] = (hidden_v[rows, :] + gradient).astype(BF16)
        target[:, D:WIDE] = embedded_v[rows, :]
        stores.append(store(target, outs[flip]))
    finish(stores)


def token_grads(lens, gain, embedded, dq, dk, dv, hidden_grad, tok, pieces):
    wide = (SLOT, D)
    return pl.pallas_call(
        token_grad_kernel,
        out_shape=(shape((BLOCK, WIDE), BF16),) * 4,
        in_specs=[SMEM, VMEM] + [ANY] * 14,
        out_specs=(ANY,) * 4,
        scratch_shapes=[
            pltpu.VMEM((D, 3 * D), BF16),
            pltpu.VMEM((SLOT, PROJ), BF16),
            pltpu.VMEM(wide, BF16),
            pltpu.VMEM(wide, BF16),
            pltpu.VMEM(wide, BF16),
            pltpu.VMEM(wide, F32),
            pltpu.VMEM(wide, BF16),
            pltpu.VMEM(wide, F32),
        ]
        + [pltpu.VMEM((BLOCK, WIDE), BF16)] * 4
        + [
            pltpu.SemaphoreType.DMA((18,)),
            pltpu.SemaphoreType.DMA((6,)),
            pltpu.SemaphoreType.DMA((4,)),
        ],
        compiler_params=params(wide=True),
        cost_estimate=COST,
        name="token_grads",
    )(lens, gain, embedded, dq, dk, dv, hidden_grad, tok, *pieces)


def unpack_kernel(block_0, block_1, block_2, block_3, embedded, tokens_grad):
    me, _ = place()
    for flip, block in enumerate((block_0, block_1, block_2, block_3)):
        tokens_grad[me ^ flip] = block[:, 0:D].astype(F32)
        embedded[me ^ flip] = block[:, D:WIDE]


def unpack(blocks):
    return pl.pallas_call(
        unpack_kernel,
        out_shape=(shape((SEQ, BLOCK, PROJ), BF16), shape((SEQ, BLOCK, D), F32)),
        in_specs=[VMEM] * 4,
        out_specs=(VMEM,) * 2,
        compiler_params=params(),
        cost_estimate=SMALL_COST,
        name="unpack",
    )(*blocks)


def exchange(value, axis, flip, size):
    return lax.ppermute(value, axis, [(i, i ^ flip) for i in range(size)])


def after(value, *others):
    return lax.optimization_barrier((value,) + others)[0]


def add(*terms):
    total = terms[0].astype(F32)
    for term in terms[1:]:
        total = total + term.astype(F32)
    return total.astype(BF16)


def marker_kernel(tick, mark):
    pass


def marker(tick):
    return pl.pallas_call(
        marker_kernel,
        out_shape=shape((8, 128), F32),
        in_specs=[ANY],
        out_specs=ANY,
        compiler_params=params(),
        cost_estimate=COST,
        name="marker",
    )(tick)


class Chunk:
    def __init__(self, groups, pair, thin=False):
        self.groups, self.thin = groups, thin
        self.send, self.keep = pair
        self.rows = self.send.shape[0] // 4

    def along(self, flip, value):
        return exchange(value, "dp", flip, self.groups)

    def core(self, tick):
        self.send = after(self.send, tick)
        self.from_core = exchange(self.send, "seq", 1, SEQ)

    def x(self, tick):
        both = 2 * self.rows
        self.from_core = after(self.from_core, tick)
        mine = add(self.keep[:both], self.from_core[:both])
        self.from_x = exchange(mine, "seq", 2, SEQ)

    def first(self, tick):
        rows = self.rows
        self.from_x = after(self.from_x, tick)
        mine = add(
            self.keep[2 * rows : 3 * rows], self.from_core[2 * rows : 3 * rows], self.from_x[:rows]
        )
        self.from_first = self.along(1, mine)

    def _summed(self, begin, end):
        rows = self.rows
        return add(
            self.keep[3 * rows + begin : 3 * rows + end],
            self.from_core[3 * rows + begin : 3 * rows + end],
            self.from_x[rows + begin : rows + end],
            self.from_first[begin:end],
        )

    def second(self, tick):
        self.from_first = after(self.from_first, tick)
        self.total = self._summed(0, self.rows if self.thin else self.rows // 2)
        self.from_second = self.along(2, self.total)

    def rest(self, tick):
        self.from_second = after(self.from_second, tick)
        if not self.thin:
            self.total = self._summed(self.rows // 2, self.rows)
        self.total = add(self.total, self.from_second)
        step = 4
        while step < self.groups:
            if step > 4:
                self.total = add(self.total, self.from_rest)
            self.from_rest = self.along(step, self.total)
            step *= 2

    def back_second(self, tick):
        self.from_rest = after(self.from_rest, tick)
        self.total = add(self.total, self.from_rest)
        self.other_second = self.along(2, self.total)

    def back_first(self, tick):
        if self.thin:
            self.from_rest = after(self.from_rest, tick)
            self.total = add(self.total, self.from_rest)
        else:
            self.other_second = after(self.other_second, tick)
            self.total = jnp.concatenate([self.other_second, self.total], axis=0)
        self.other = self.along(1, self.total)


def assemble_kernel(rows, widths, count, carried, gained, table, natural, total, other, *refs):
    weights, refs = refs[:count], refs[count:]
    before, refs = refs[:carried], refs[carried:]
    gain, outs = refs[:gained], refs[gained:]
    me, y = place()
    z = lax.rem(lax.axis_index("dp") // 2, 2)
    half = rows // 2
    column = 0
    summed = None

    def blocks():
        for source, first in ((total, 1), (other, 0)):
            for second in range(2):
                y_of = y if first else 1 - y
                z_of = second if natural else (z if second else 1 - z)
                yield source, second * half, y_of, z_of

    for number, width in enumerate(widths):
        columns = slice(column, column + width)
        out = outs[number]
        for source, row, y_of, z_of in blocks():
            begin_row = pl.multiple_of(y_of * rows + z_of * half, 16)
            out[pl.ds(begin_row, half), :] = source[row : row + half, columns].astype(F32)
        column += width
        first = len(widths) - count
        if number >= first:
            part = jnp.sum(
                weights[number - first][...].astype(F32) * out[...], axis=1, keepdims=True
            )
            summed = part if summed is None else summed + part
    if count:
        total_rows = jnp.broadcast_to(summed, (2 * rows, BLOCK)).T[0:1, :]
        if carried:
            total_rows = total_rows + before[0][...]
        if gained:
            whole = gain[0][...].reshape(1, D)
            mine = whole[:, 0:SHARD]
            for shard in range(1, SEQ):
                mine = jnp.where(me == shard, whole[:, shard * SHARD : (shard + 1) * SHARD], mine)
            outs[len(widths)][...] = (total_rows / mine).reshape(2 * rows)
        else:
            outs[len(widths)][...] = total_rows
    if table:
        for source, row, y_of, z_of in blocks():

            if natural and z_of:
                continue

            @pl.when((y_of == 0) if natural else (y_of == 0) & (z_of == 0))
            def store():
                outs[-1][...] = source[
                    row : row + BUCKETS // SEQ, column : column + H
                ].astype(F32)


def assemble(chunk, widths, weights=(), before=(), gain=(), table=False):
    rows = chunk.rows
    out_shape = [shape((2 * rows, width), F32) for width in widths]
    if weights:
        out_shape.append(shape((2 * rows,) if gain else (1, 2 * rows), F32))
    if table:
        out_shape.append(shape((BUCKETS // SEQ, H), F32))
    operands = tuple(weights) + tuple(before) + tuple(gain)
    return pl.pallas_call(
        functools.partial(
            assemble_kernel,
            rows,
            widths,
            len(weights),
            len(before),
            len(gain),
            table,
            chunk.thin,
        ),
        out_shape=tuple(out_shape),
        in_specs=[VMEM] * (2 + len(operands)),
        out_specs=(VMEM,) * len(out_shape),
        compiler_params=params(),
        cost_estimate=SMALL_COST,
        name="assemble",
    )(chunk.total, chunk.other, *operands)


def per_device(
    groups,
    tokens,
    doc_lengths,
    query_weight,
    key_weight,
    value_weight,
    out_weight,
    gate_weight,
    up_weight,
    down_weight,
    proj_weight,
    attn_gain,
    ffn_gain,
    final_gain,
    bucket_bias_rows,
    embed_cotangent,
):
    tick = doc_lengths

    def across_x(mine):
        return exchange(after(mine, tick), "seq", 2, SEQ)

    def across_y(mine):
        return exchange(after(mine, tick), "dp", 1, groups)

    def across_core(mine):
        return exchange(after(mine, tick), "seq", 1, SEQ)

    def across_far(mine):
        return exchange(after(mine, tick), "seq", 3, SEQ)

    qkv_half = pack_first(tick, query_weight, key_weight, value_weight)
    qkv_x = across_x(qkv_half)
    tick = after(tick, qkv_half)
    blocks = pack_tokens(tick, tokens, embed_cotangent)
    block_x = across_x(blocks[2])
    block_far = across_far(blocks[3])
    block_core = across_core(blocks[1])
    tick = after(tick, blocks[0])
    qkv_own, out_own, gated_half_0, gated_half_1 = pack_rest(
        tick,
        query_weight,
        key_weight,
        value_weight,
        out_weight,
        proj_weight,
        gate_weight,
        up_weight,
    )
    tick = after(tick, qkv_x, gated_half_0, block_core)
    qkv_y = across_y(qkv_x)
    qkv_cx = across_core(qkv_x)
    out_x = across_x(out_own)
    tick = after(tick, block_x, block_far, qkv_y, qkv_cx)
    qkv_cy = across_core(qkv_y)
    gated_x_0 = across_x(gated_half_0)
    qkv_core = across_core(qkv_own)
    tick = after(tick, out_x, qkv_cy, qkv_core)
    gated_x_1 = across_x(gated_half_1)
    gate_core = across_core(gate_weight)
    out_core = across_core(out_own)
    qkv_pieces = (
        query_weight, key_weight, value_weight, qkv_core, qkv_x, qkv_y, qkv_cx, qkv_cy
    )
    tok, cot, n1t, qkv = qkv_project(
        tick, attn_gain, (blocks[0], block_core, block_x, block_far), qkv_pieces
    )
    pairs = H // 2
    third = pairs // 3
    tick = after(tick, qkv, gated_x_0, gate_core, out_core)
    gated_y_0 = across_y(gated_x_0)
    gated_cx_0 = across_core(gated_x_0)
    out_cx = across_core(out_x)
    down_x = across_x(down_weight)
    held = attention(tick, qkv, bucket_bias_rows, 0, third, ())
    tick = after(tick, held[0], gated_x_1, gated_cx_0, out_cx)
    gated_y_1 = across_y(gated_x_1)
    gated_cx_1 = across_core(gated_x_1)
    up_core = across_core(up_weight)
    held = attention(tick, qkv, bucket_bias_rows, third, third, held)
    tick = after(tick, held[0], gated_y_0, gated_cx_1, up_core)
    gated_cy_0 = across_core(gated_y_0)
    down_core = across_core(down_weight)
    et, linv, ot, mixed = attention(
        tick, qkv, bucket_bias_rows, 2 * third, pairs - 2 * third, held
    )
    tick = after(tick, mixed, gated_y_1, gated_cy_0, down_core)
    gated_cy_1 = across_core(gated_y_1)
    tick = after(tick, down_x)
    down_cx = across_core(down_x)
    tick = after(tick, gated_cy_1, down_cx)
    out_pieces = (out_own, out_core, out_x, out_cx)
    down_pieces = (down_weight, down_core, down_x, down_cx)
    gated_pieces = (
        gate_weight, up_weight, gate_core, up_core,
        gated_x_0, gated_y_0, gated_cx_0, gated_cy_0,
        gated_x_1, gated_y_1, gated_cx_1, gated_cy_1,
    )
    hidden, n2t, gate_grad, up_grad, embedded, after_grad, fnt, *pair = feed_forward(
        tick, tok, mixed, cot, ffn_gain, final_gain, out_pieces, gated_pieces, down_pieces
    )

    chunk = functools.partial(Chunk, groups)
    down_sum = chunk(pair)
    tick = after(tick, down_sum.keep)
    down_sum.core(tick)
    gate_sum = chunk(gate_grads(tick, n2t, gate_grad))
    tick = after(tick, gate_sum.keep, down_sum.from_core)
    down_sum.x(tick)
    gate_sum.core(tick)
    *pair, hidden_grad, attn_in = up_grads(
        tick, ffn_gain, n2t, gate_grad, up_grad, hidden, after_grad, gated_pieces
    )
    up_sum = chunk(pair)
    tick = after(tick, up_sum.keep, gate_sum.from_core)
    gate_sum.x(tick)
    up_sum.core(tick)
    *pair, mixed_grad = out_grads(tick, ot, fnt, attn_in, cot, out_pieces)
    out_sum = chunk(pair)
    tick = after(tick, out_sum.keep, up_sum.from_core, down_sum.from_x)
    down_sum.first(tick)
    up_sum.x(tick)
    out_sum.core(tick)
    held = attention_back(tick, qkv, et, linv, ot, mixed_grad, 0, pairs // 2, ())
    tick = after(tick, held[0], out_sum.from_core, down_sum.from_first)
    down_sum.second(tick)
    out_sum.x(tick)
    dq, dk, dv, bias_part = attention_back(
        tick, qkv, et, linv, ot, mixed_grad, pairs // 2, pairs - pairs // 2, held
    )
    tick = after(tick, dq, gate_sum.from_x, down_sum.from_second)
    gate_sum.first(tick)
    down_sum.rest(tick)
    *pair, value_send, value_keep = qkv_grads(tick, bias_part, n1t, dq, dk, dv)
    first_sum, value_sum = chunk(pair), chunk((value_send, value_keep))
    tick = after(
        tick,
        first_sum.keep,
        gate_sum.from_first,
        up_sum.from_x,
        down_sum.from_rest,
        out_sum.from_x,
    )
    first_sum.core(tick)
    value_sum.core(tick)
    gate_sum.second(tick)
    up_sum.first(tick)
    down_sum.back_second(tick)
    blocks = token_grads(
        tick, attn_gain, embedded, dq, dk, dv, hidden_grad, tok, qkv_pieces
    )
    tick = after(
        tick,
        blocks[0],
        first_sum.from_core,
        value_sum.from_core,
        gate_sum.from_second,
        up_sum.from_first,
        down_sum.other_second,
    )
    first_sum.x(tick)
    value_sum.x(tick)
    down_sum.back_first(tick)
    gate_sum.rest(tick)
    up_sum.second(tick)
    tick = after(tick, marker(tick), down_sum.other, up_sum.from_second)
    up_sum.rest(tick)
    out_sum.first(tick)
    tick = after(tick, marker(tick), gate_sum.from_rest)
    gate_sum.back_second(tick)
    tick = after(tick, marker(tick), first_sum.from_x)
    first_sum.first(tick)
    tick = after(tick, marker(tick), out_sum.from_first, gate_sum.other_second)
    gate_sum.back_first(tick)
    out_sum.second(tick)
    tick = after(tick, marker(tick), value_sum.from_x)
    value_sum.first(tick)
    tick = after(tick, marker(tick), up_sum.from_rest)
    up_sum.back_second(tick)
    tick = after(tick, marker(tick), first_sum.from_first)
    first_sum.second(tick)
    tick = after(tick, marker(tick), gate_sum.other, out_sum.from_second)
    out_sum.rest(tick)
    tick = after(tick, marker(tick), value_sum.from_first, up_sum.other_second)
    value_sum.second(tick)
    up_sum.back_first(tick)
    tick = after(tick, marker(tick), first_sum.from_second)
    first_sum.rest(tick)
    tick = after(tick, marker(tick), value_sum.from_second)
    value_sum.rest(tick)
    block_x = across_x(blocks[2])
    block_far = across_far(blocks[3])
    tick = after(tick, marker(tick), out_sum.from_rest)
    out_sum.back_second(tick)
    tick = after(tick, marker(tick), first_sum.from_rest)
    first_sum.back_second(tick)
    tick = after(tick, marker(tick), value_sum.from_rest, up_sum.other, out_sum.other_second)
    value_sum.back_second(tick)
    out_sum.back_first(tick)
    tick = after(tick, marker(tick), first_sum.other_second, block_x, block_far)
    first_sum.back_first(tick)
    block_core = across_core(blocks[1])
    tick = after(tick, marker(tick), value_sum.other_second)
    value_sum.back_first(tick)
    down_grad, = assemble(down_sum, (D,))
    gate_weight_grad, gate_rows = assemble(gate_sum, (FF,), (gate_weight,))
    up_weight_grad, ffn_gain_grad = assemble(
        up_sum, (FF,), (up_weight,), (gate_rows,), (ffn_gain,)
    )
    embedded, tokens_grad = unpack((blocks[0], block_core, block_x, block_far))
    query_grad, key_grad, first_rows = assemble(first_sum, (D, D), (query_weight, key_weight))
    value_grad, attn_gain_grad, table_grad = assemble(
        value_sum, (D,), (value_weight,), (first_rows,), (attn_gain,), table=True
    )
    out_grad, proj_grad, final_gain_grad = assemble(
        out_sum, (D, PROJ), (proj_weight,), (), (final_gain,)
    )
    return (
        embedded,
        tokens_grad,
        query_grad,
        key_grad,
        value_grad,
        out_grad,
        gate_weight_grad,
        up_weight_grad,
        down_grad,
        proj_grad,
        attn_gain_grad,
        ffn_gain_grad,
        final_gain_grad,
        table_grad,
    )


def solution(mesh):
    placed = (
        P("dp", "seq", None),
        P("dp"),
        P("seq", None),
        P("seq", None),
        P("seq", None),
        P("seq", None),
        P("seq", None),
        P("seq", None),
        P("seq", None),
        P("seq", None),
        P(),
        P(),
        P(),
        P(),
        P("dp", "seq", None),
    )
    return jax.shard_map(
        functools.partial(per_device, mesh.shape["dp"]),
        mesh=mesh,
        in_specs=placed,
        out_specs=(
            P("dp", "seq", None),
            P("dp", "seq", None),
            P("seq", None),
            P("seq", None),
            P("seq", None),
            P("seq", None),
            P("seq", None),
            P("seq", None),
            P("seq", None),
            P("seq", None),
            P("seq"),
            P("seq"),
            P("seq"),
            P("seq", None),
        ),
        check_vma=False,
    )
```

```python
import functools

import jax
import jax.numpy as jnp
import numpy as np
from jax import lax
from jax.experimental import pallas as pl
from jax.experimental.pallas import tpu as pltpu
from jax.sharding import PartitionSpec as P

D = 768
H = 12
HEAD = 64
FF = 2048
PROJ = 128
BUCKETS = 32
SLOT = 512
BLOCK = 128
SEQ = 4
SHARD = D // SEQ
HALF_FF = FF // 2
WIDE = D + PROJ
EPSILON = 1e-06
BIG_NEGATIVE = -1e30
GELU_A = 0.7978845608028654
GELU_B = 0.044715

F32 = jnp.float32
BF16 = jnp.bfloat16
VMEM = pl.BlockSpec(memory_space=pltpu.VMEM)
SMEM = pl.BlockSpec(memory_space=pltpu.SMEM)
ANY = pl.BlockSpec(memory_space=pl.ANY)
MIB = 1 << 20


def shape(dims, kind):
    return jax.ShapeDtypeStruct(dims, kind)


def params(wide=False):
    return pltpu.CompilerParams(vmem_limit_bytes=(58 if wide else 20) * MIB)


COST = pl.CostEstimate(flops=30000000000, bytes_accessed=100000000, transcendentals=0)
SMALL_COST = pl.CostEstimate(flops=1, bytes_accessed=1, transcendentals=0)


def bucket_of(relative):
    distance = np.abs(relative)
    scaled = np.log(np.maximum(distance, 1) / 8.0) / np.log(16.0) * 8.0
    far_bucket = np.minimum(8 + scaled.astype(np.int64), 15)
    return (relative > 0) * 16 + np.where(distance < 8, distance, far_bucket)


def skew_buckets():
    lanes = (np.arange(SLOT) + SLOT // 2) % SLOT - SLOT // 2
    relative = np.arange(8)[:, None] - lanes[None, :]
    return bucket_of(relative).astype(np.int32)


def table_indicator():
    lanes = (np.arange(SLOT) + SLOT // 2) % SLOT - SLOT // 2
    buckets = np.concatenate([bucket_of(-lanes), np.full(BLOCK, 15), np.full(BLOCK, 31)])
    here = BUCKETS // SEQ
    place = (buckets // here) * SHARD + buckets % here
    return (place[:, None] == np.arange(D)[None, :]).astype(np.float32)


def dot(left, right):
    return jnp.dot(left, right, preferred_element_type=F32)


def dot_t(left, right):
    return lax.dot_general(left, right, (((1,), (1,)), ((), ())), preferred_element_type=F32)


def place():
    return lax.axis_index("seq"), lax.rem(lax.axis_index("dp"), 2)


def relative_starts(rows, natural=False):
    me, y = place()
    z = lax.rem(lax.axis_index("dp") // 2, 2)
    bits = (me & 1, me >> 1, y, z)
    block = rows // 16
    starts = []
    for number in range(16):
        own = [(number >> shift) & 1 for shift in (3, 2, 1, 0)]
        core, x, first, second = (b if o else 1 - b for b, o in zip(bits, own))
        if natural:
            second = own[3]
        place_of = ((x * 2 + core) * 2 + first) * 2 + second
        starts.append(pl.multiple_of(place_of * block, 16))
    return block, starts


def begin(copies):
    for copy in copies:
        copy.start()
    return copies


def finish(copies):
    for copy in copies:
        copy.wait()


def run_all(copies):
    finish(begin(copies))


class Copies:
    def __init__(self, sems):
        self.sems, self.used = sems, 0

    def __call__(self, source, target):
        copy = pltpu.make_async_copy(source, target, self.sems.at[self.used])
        self.used += 1
        copy.start()
        return copy


def pieces_of(rows, plan, refs, target, sems, first=0):
    me, y = place()
    half = rows // 2
    starts = (
        me * rows,
        (me ^ 1) * rows,
        (me ^ 2) * rows + y * half,
        (me ^ 2) * rows + (1 - y) * half,
        (me ^ 3) * rows + y * half,
        (me ^ 3) * rows + (1 - y) * half,
        (me ^ 2) * rows,
        (me ^ 3) * rows,
    )
    copies = []
    for number, (ref, piece, source, to, width, *some) in enumerate(plan):
        first_row, skip, size = some or (0, 0, half if 2 <= piece < 6 else rows)
        copies.append(
            pltpu.make_async_copy(
                refs[ref].at[pl.ds(first_row, size), pl.ds(source, width)],
                target.at[
                    pl.ds(pl.multiple_of(starts[piece] + skip, 16), size), pl.ds(to, width)
                ],
                sems.at[first + number],
            )
        )
    return copies


QKV_PLANS = tuple(
    ((number, 0, 0, number * D, D),)
    + tuple((2 + piece, piece, number * D, number * D, D) for piece in range(1, 6))
    for number in range(3)
)
OUT_PLAN = tuple((ref, piece, 0, 0, WIDE) for ref, piece in enumerate((0, 1, 6, 7)))
DOWN_SHARD = FF // SEQ
EARLY = 64
DOWN_PLAN = (
    (0, 0, 0, 0, D),
    (1, 1, 0, 0, D),
    (2, 6, 0, 0, D, SHARD, 0, EARLY),
    (3, 6, 0, 0, D, 0, EARLY, DOWN_SHARD - EARLY),
    (4, 7, 0, 0, D, SHARD, 0, EARLY),
    (5, 7, 0, 0, D, 0, EARLY, DOWN_SHARD - EARLY),
)


def gated_plan(part):
    column = part * HALF_FF
    parts = [(4 + 4 * part + number, piece) for number, piece in enumerate((2, 3, 4, 5))]
    return (
        (0, 0, column, column, HALF_FF),
        (1, 0, column, FF + column, HALF_FF),
        (2, 1, column, column, HALF_FF),
        (3, 1, column, FF + column, HALF_FF),
    ) + tuple(
        (ref, piece, number * HALF_FF, number * FF + column, HALF_FF)
        for ref, piece in parts
        for number in range(2)
    )


GATED_PLANS = (gated_plan(0), gated_plan(1))


def relative_copies(source, target, sems, natural=False):
    block, starts = relative_starts(source.shape[0], natural)
    return [
        pltpu.make_async_copy(
            source.at[pl.ds(begin, block), :],
            target.at[pl.ds(number * block, block), :],
            sems.at[number],
        )
        for number, begin in enumerate(starts)
    ]


def inverse_rms(values):
    return lax.rsqrt(jnp.mean(values * values, axis=-1, keepdims=True) + EPSILON)


def norm_backward(values, gain, incoming):
    r = inverse_rms(values)
    weighted = gain * incoming
    inner = jnp.mean(weighted * values, axis=-1, keepdims=True)
    return r * weighted - values * (r * r * r * inner)


def pack_first_kernel(lens, q, k, v, qkv_half, sems):
    _, y = place()
    half = SHARD // 2
    rows = pl.ds(pl.multiple_of(y * half, 16), half)
    run_all(
        [
            pltpu.make_async_copy(
                weight.at[rows, :], qkv_half.at[:, pl.ds(number * D, D)], sems.at[number]
            )
            for number, weight in enumerate((q, k, v))
        ]
    )


def pack_first(lens, q, k, v):
    return pl.pallas_call(
        pack_first_kernel,
        out_shape=shape((SHARD // 2, 3 * D), BF16),
        in_specs=[SMEM] + [ANY] * 3,
        out_specs=VMEM,
        scratch_shapes=[pltpu.SemaphoreType.DMA((3,))],
        compiler_params=params(wide=True),
        cost_estimate=COST,
        name="pack_first",
    )(lens, q, k, v)


def pack_tokens_kernel(lens, tokens, cot, *refs):
    blocks, sems = refs[:4], refs[4]
    me, _ = place()
    pairs = []
    for flip, block in enumerate(blocks):
        pairs.append((tokens.at[me ^ flip], block.at[:, pl.ds(0, D)]))
        pairs.append((cot.at[me ^ flip], block.at[:, pl.ds(D, PROJ)]))
    run_all([pltpu.make_async_copy(a, b, sems.at[i]) for i, (a, b) in enumerate(pairs)])


def pack_tokens(lens, tokens, cot):
    return pl.pallas_call(
        pack_tokens_kernel,
        out_shape=(shape((BLOCK, WIDE), BF16),) * 4,
        in_specs=[SMEM] + [ANY] * 2,
        out_specs=(VMEM,) * 4,
        scratch_shapes=[pltpu.SemaphoreType.DMA((8,))],
        compiler_params=params(wide=True),
        cost_estimate=COST,
        name="pack_tokens",
    )(lens, tokens, cot)


def pack_rest_kernel(
    lens, q, k, v, out, proj, gate, up, down, qkv, out_own, part_0, part_1, down_rest, sems
):
    _, y = place()
    half = SHARD // 2
    rows = pl.ds(pl.multiple_of(y * half, 16), half)
    pairs = [(w, qkv.at[:, pl.ds(number * D, D)]) for number, w in enumerate((q, k, v))]
    pairs.append((out, out_own.at[pl.ds(0, SHARD), pl.ds(0, D)]))
    pairs.append((proj, out_own.at[pl.ds(0, SHARD), pl.ds(D, PROJ)]))
    pairs.append((down.at[pl.ds(0, EARLY), :], out_own.at[pl.ds(SHARD, EARLY), pl.ds(0, D)]))
    pairs.append((down.at[pl.ds(EARLY, DOWN_SHARD - EARLY), :], down_rest))
    for number, part in enumerate((part_0, part_1)):
        columns = pl.ds(number * HALF_FF, HALF_FF)
        pairs.append((gate.at[rows, columns], part.at[:, pl.ds(0, HALF_FF)]))
        pairs.append((up.at[rows, columns], part.at[:, pl.ds(HALF_FF, HALF_FF)]))
    run_all([pltpu.make_async_copy(a, b, sems.at[i]) for i, (a, b) in enumerate(pairs)])


def pack_rest(lens, q, k, v, out, proj, gate, up, down):
    half = SHARD // 2
    return pl.pallas_call(
        pack_rest_kernel,
        out_shape=(shape((SHARD, 3 * D), BF16), shape((SHARD + EARLY, WIDE), BF16))
        + (shape((half, FF), BF16),) * 2
        + (shape((DOWN_SHARD - EARLY, D), BF16),),
        in_specs=[SMEM] + [ANY] * 8,
        out_specs=(VMEM,) * 5,
        scratch_shapes=[pltpu.SemaphoreType.DMA((11,))],
        compiler_params=params(wide=True),
        cost_estimate=COST,
        name="pack_rest",
    )(lens, q, k, v, out, proj, gate, up, down)


def first_norm_kernel(lens, own, from_core, from_x, from_far, gain, tok, cot, n1, n1t, held, sems):
    me, _ = place()
    run_all(
        [
            pltpu.make_async_copy(
                piece,
                held.at[pl.ds(pl.multiple_of((me ^ flip) * BLOCK, BLOCK), BLOCK), :],
                sems.at[flip],
            )
            for flip, piece in enumerate((own, from_core, from_x, from_far))
        ]
    )
    scale = gain[...].reshape(1, D)
    for block in range(SLOT // BLOCK):
        rows = pl.ds(block * BLOCK, BLOCK)
        here = held[rows, 0:D]
        tok[rows, :] = here
        cot[rows, :] = held[rows, D : D + PROJ]
        values = here.astype(F32)
        normed = (values * inverse_rms(values) * scale).astype(BF16)
        n1[rows, :] = normed
        n1t[:, rows] = normed.T


def first_norm(lens, blocks, gain):
    return pl.pallas_call(
        first_norm_kernel,
        out_shape=(
            shape((SLOT, D), BF16),
            shape((SLOT, PROJ), BF16),
            shape((SLOT, D), BF16),
            shape((D, SLOT), BF16),
        ),
        in_specs=[SMEM, ANY, ANY, ANY, ANY, VMEM],
        out_specs=(VMEM,) * 4,
        scratch_shapes=[pltpu.VMEM((SLOT, WIDE), BF16), pltpu.SemaphoreType.DMA((4,))],
        compiler_params=params(wide=True),
        cost_estimate=COST,
        name="first_norm",
    )(lens, *blocks, gain)


def qkv_kernel(lens, n1, *refs):
    pieces, (out, weight, sems) = refs[:8], refs[8:]
    group = pl.program_id(0)

    def copies(number):
        return pieces_of(SHARD, QKV_PLANS[number], pieces, weight, sems, 6 * number)

    @pl.when(group == 0)
    def start():
        for number in range(3):
            begin(copies(number))

    for number in range(3):

        @pl.when(group == number)
        def ready():
            finish(copies(number))

    for tile in range(D // 256):
        columns = pl.ds(pl.multiple_of(group * D + tile * 256, 256), 256)
        out[:, tile * 256 : (tile + 1) * 256] = dot(n1[...], weight[:, columns]).astype(BF16)


def qkv_project(lens, n1, pieces):
    return pl.pallas_call(
        qkv_kernel,
        grid=(3,),
        out_shape=shape((SLOT, 3 * D), BF16),
        in_specs=[SMEM, VMEM] + [ANY] * 8,
        out_specs=pl.BlockSpec((SLOT, D), lambda i: (0, i)),
        scratch_shapes=[pltpu.VMEM((D, 3 * D), BF16), pltpu.SemaphoreType.DMA((18,))],
        compiler_params=params(wide=True),
        cost_estimate=COST,
        name="qkv_project",
    )(lens, n1, *pieces)


HALF_Q = 512


def attention_kernel(first, lens, q, k, v, rows_of_bias, buckets, *refs):
    et, linv, ot, o, bias = refs[-5:]
    me, _ = place()
    length = lens[me]
    pair = pl.program_id(0) + first
    k_pair = k[...]
    vt = v[...].T
    qt = q[...].T
    row_in_pair = lax.broadcasted_iota(jnp.int32, (2 * HEAD, SLOT), 0)
    key_index = lax.broadcasted_iota(jnp.int32, (SLOT, HALF_Q), 0)
    for head in range(2):
        base = jnp.zeros((8, SLOT), F32)
        for bucket in range(BUCKETS):
            base = jnp.where(buckets[...] == bucket, rows_of_bias[bucket, 2 * pair + head], base)
        for group in range(BLOCK // 8):
            bias[pl.ds(group * 8, 8), :] = pltpu.roll(base, 8 * group, 1) if group else base
        below = rows_of_bias[15, 2 * pair + head]
        above = rows_of_bias[31, 2 * pair + head]
        in_head = (row_in_pair >= HEAD * head) & (row_in_pair < HEAD * (head + 1))
        qt_head = jnp.where(in_head, qt, jnp.zeros_like(qt))
        for part in range(SLOT // HALF_Q):
            raw = dot(k_pair, qt_head[:, part * HALF_Q : (part + 1) * HALF_Q])
            rows = []
            for key_block in range(4):
                cells = []
                for sub in range(HALF_Q // BLOCK):
                    query_block = part * (HALF_Q // BLOCK) + sub
                    cell = raw[
                        key_block * BLOCK : (key_block + 1) * BLOCK,
                        sub * BLOCK : (sub + 1) * BLOCK,
                    ]
                    apart = key_block - query_block
                    if apart >= 2:
                        cell = cell + above
                    elif apart <= -2:
                        cell = cell + below
                    else:
                        lane = (-apart * BLOCK) % SLOT
                        cell = cell + bias[:, lane : lane + BLOCK]
                    cells.append(cell)
                rows.append(jnp.concatenate(cells, axis=1))
            scores = jnp.concatenate(rows, axis=0)
            scores = jnp.where(key_index < length, scores, BIG_NEGATIVE)
            top = jnp.max(scores, axis=0, keepdims=True)
            weights = jnp.exp(scores - top)
            inverse = 1.0 / jnp.sum(weights, axis=0, keepdims=True)
            low = weights.astype(BF16)
            columns = pl.ds(part * HALF_Q, HALF_Q)
            et[head, :, columns] = low
            linv[head, :, columns] = inverse
            mixed = dot(vt[head * HEAD : (head + 1) * HEAD, :], low) * inverse
            ot[pl.ds(head * HEAD, HEAD), columns] = mixed.astype(BF16)
    o[...] = ot[...].T


def attention(lens, qkv, rows_of_bias, first, count, held):
    pair = 2 * HEAD
    pairs = H // 2
    return pl.pallas_call(
        functools.partial(attention_kernel, first),
        grid=(count,),
        out_shape=(
            shape((H, SLOT, SLOT), BF16),
            shape((H, 1, SLOT), F32),
            shape((D, SLOT), BF16),
            shape((SLOT, D), BF16),
        ),
        in_specs=[
            SMEM,
            pl.BlockSpec((SLOT, pair), lambda i: (0, first + i)),
            pl.BlockSpec((SLOT, pair), lambda i: (0, pairs + first + i)),
            pl.BlockSpec((SLOT, pair), lambda i: (0, 2 * pairs + first + i)),
            SMEM,
            pl.BlockSpec((8, SLOT), lambda i: (0, 0)),
        ]
        + [ANY] * len(held),
        out_specs=(
            pl.BlockSpec((2, SLOT, SLOT), lambda i: (first + i, 0, 0)),
            pl.BlockSpec((2, 1, SLOT), lambda i: (first + i, 0, 0)),
            pl.BlockSpec((pair, SLOT), lambda i: (first + i, 0)),
            pl.BlockSpec((SLOT, pair), lambda i: (0, first + i)),
        ),
        input_output_aliases={6 + i: i for i in range(len(held))},
        scratch_shapes=[pltpu.VMEM((BLOCK, SLOT), F32)],
        compiler_params=params(wide=True),
        cost_estimate=COST,
        name="attention",
    )(lens, qkv, qkv, qkv, rows_of_bias, jnp.asarray(skew_buckets()), *held)


def feed_forward_kernel(lens, ffn_gain, final_gain, tok, mixed, cot, *refs):
    out_pieces, gated_pieces, down_pieces, refs = refs[:4], refs[4:16], refs[16:22], refs[22:]
    hidden_out, n2t_out, gate_out, up_out, embedded_out, after_out, fnt_out = refs[:7]
    send_out, keep_out = refs[7:9]
    w_out, w_gated, w_down, tok_v, mixed_v, cot_v, hidden, n2, n2t, inner, innert = refs[9:20]
    slope, level, embedded, after_grad, down_in, fnt, send, keep = refs[20:28]
    out_sems, gated_sems, down_sems, in_sems, done_sems = refs[28:]
    load, store = Copies(in_sems), Copies(done_sems)

    loads = begin(pieces_of(SHARD, OUT_PLAN, out_pieces, w_out, out_sems))
    loads += [load(mixed, mixed_v), load(tok, tok_v), load(cot, cot_v)]
    gated_loads = [
        begin(pieces_of(SHARD, plan, gated_pieces, w_gated, gated_sems, 12 * number))
        for number, plan in enumerate(GATED_PLANS)
    ]
    down_loads = begin(pieces_of(FF // SEQ, DOWN_PLAN, down_pieces, w_down, down_sems))
    stores = []

    finish(loads)
    scale = ffn_gain[...].reshape(1, D)
    for block in range(2):
        rows = pl.ds(block * 256, 256)
        values = tok_v[rows, :].astype(F32) + dot(mixed_v[rows, :], w_out[:, 0:D])
        hidden[rows, :] = values
        normed = (values * inverse_rms(values) * scale).astype(BF16)
        n2[rows, :] = normed
        n2t[:, rows] = normed.T
    stores.append(store(hidden, hidden_out))
    size, starts = relative_starts(D)
    for number, begin_row in enumerate(starts):
        stores.append(
            store(n2t.at[pl.ds(begin_row, size), :], n2t_out.at[pl.ds(number * size, size), :])
        )

    me, y = place()
    z = lax.rem(lax.axis_index("dp") // 2, 2)

    def step(tile, carry):
        columns = pl.ds(pl.multiple_of(tile * 512, 512), 512)
        g = dot(n2[...], w_gated[:, columns])
        u = dot(n2[...], w_gated[:, pl.ds(pl.multiple_of(FF + tile * 512, 512), 512)])
        square = g * g
        t = jnp.tanh(GELU_A * g * (1.0 + GELU_B * square))
        half_up = 0.5 * (1.0 + t)
        activated = g * half_up
        derivative = half_up + 0.5 * g * (1.0 - t * t) * (GELU_A * (1.0 + 3 * GELU_B * square))
        value = (activated * u).astype(BF16)
        inner[:, columns] = value
        slope[:, columns] = (derivative * u).astype(BF16)
        level[:, columns] = activated.astype(BF16)
        core_own = (lax.rem(tile, 2) == lax.rem(me, 2)).astype(jnp.int32)
        x_own = (tile // 2 == me // 2).astype(jnp.int32)
        target = (core_own * 2 + x_own) * 512
        turned = value.T
        for number in range(4):
            y_own = (number >> 1 == y).astype(jnp.int32)
            z_own = ((number & 1) == z).astype(jnp.int32)
            row = pl.multiple_of(target + y_own * 256 + z_own * BLOCK, BLOCK)
            innert[pl.ds(row, BLOCK), :] = turned[number * BLOCK : (number + 1) * BLOCK, :]
        return carry

    for part in range(2):
        finish(gated_loads[part])
        lax.fori_loop(2 * part, 2 * part + 2, step, 0)

    finish(down_loads)
    scale = final_gain[...].reshape(1, D)
    for block in range(2):
        rows = pl.ds(block * 256, 256)
        values = hidden[rows, :] + dot(inner[rows, :], w_down[...])
        normed = (values * inverse_rms(values) * scale).astype(BF16)
        fnt[:, rows] = normed.T
        embedded[rows, :] = dot(normed, w_out[:, D:WIDE]).astype(BF16)
        gradient = norm_backward(values, scale, dot_t(cot_v[rows, :], w_out[:, D:WIDE]))
        after_grad[rows, :] = gradient
        down_in[rows, :] = gradient.astype(BF16)
    for source, target in ((after_grad, after_out), (embedded, embedded_out), (fnt, fnt_out)):
        stores.append(store(source, target))

    for number, (part, target) in enumerate(((send, send_out), (keep, keep_out))):

        def grad(tile, carry):
            rows = pl.ds(pl.multiple_of(tile * 256, 256), 256)
            source = pl.ds(pl.multiple_of(number * (FF // 2) + tile * 256, 256), 256)
            part[rows, :] = dot(innert[source, :], down_in[...]).astype(BF16)
            return carry

        lax.fori_loop(0, FF // 2 // 256, grad, 0)
        stores.append(store(part, target))

    def back(tile, carry):
        columns = pl.ds(pl.multiple_of(tile * 512, 512), 512)
        incoming = dot_t(down_in[...], w_down[columns, :])
        slope[:, columns] = (incoming * slope[:, columns].astype(F32)).astype(BF16)
        level[:, columns] = (incoming * level[:, columns].astype(F32)).astype(BF16)
        return carry

    lax.fori_loop(0, FF // 512, back, 0)
    stores += [store(slope, gate_out), store(level, up_out)]
    finish(stores)


def feed_forward(lens, tok, mixed, cot, ffn_gain, final_gain, out_pieces, gated_pieces, down_pieces):
    wide, tall, full = (SLOT, D), (D, SLOT), (SLOT, FF)
    pieces = tuple(out_pieces) + tuple(gated_pieces) + tuple(down_pieces)
    return pl.pallas_call(
        feed_forward_kernel,
        out_shape=(
            shape(wide, F32),
            shape(tall, BF16),
            shape(full, BF16),
            shape(full, BF16),
            shape((SLOT, PROJ), BF16),
            shape(wide, F32),
            shape(tall, BF16),
            shape((FF // 2, D), BF16),
            shape((FF // 2, D), BF16),
        ),
        in_specs=[SMEM, VMEM, VMEM] + [ANY] * (3 + len(pieces)),
        out_specs=(ANY,) * 9,
        scratch_shapes=[
            pltpu.VMEM((D, WIDE), BF16),
            pltpu.VMEM((D, 2 * FF), BF16),
            pltpu.VMEM((FF, D), BF16),
            pltpu.VMEM(wide, BF16),
            pltpu.VMEM(wide, BF16),
            pltpu.VMEM((SLOT, PROJ), BF16),
            pltpu.VMEM(wide, F32),
            pltpu.VMEM(wide, BF16),
            pltpu.VMEM(tall, BF16),
            pltpu.VMEM(full, BF16),
            pltpu.VMEM((FF, SLOT), BF16),
            pltpu.VMEM(full, BF16),
            pltpu.VMEM(full, BF16),
            pltpu.VMEM((SLOT, PROJ), BF16),
            pltpu.VMEM(wide, F32),
            pltpu.VMEM(wide, BF16),
            pltpu.VMEM(tall, BF16),
            pltpu.VMEM((FF // 2, D), BF16),
            pltpu.VMEM((FF // 2, D), BF16),
            pltpu.SemaphoreType.DMA((4,)),
            pltpu.SemaphoreType.DMA((24,)),
            pltpu.SemaphoreType.DMA((6,)),
            pltpu.SemaphoreType.DMA((3,)),
            pltpu.SemaphoreType.DMA((24,)),
        ],
        compiler_params=params(wide=True),
        cost_estimate=COST,
        name="feed_forward",
    )(lens, ffn_gain, final_gain, tok, mixed, cot, *pieces)


def row_grads(left, right, halves, column=0, loads=(), store=None, outs=()):
    half = left.shape[0] // 2
    width = right.shape[1]
    size = 1024 if width % 1024 == 0 else width
    stores = []
    for tile in range(width // size):
        if loads:
            loads[tile].wait()
        target = slice(column + tile * size, column + (tile + 1) * size)
        both = dot(left[...], right[:, tile * size : (tile + 1) * size]).astype(BF16)
        for number, part in enumerate(halves):
            part[:, target] = both[number * half : (number + 1) * half, :]
            stores.append(store(part.at[:, target], outs[number].at[:, target]))
    return stores


def tile_loads(load, source, target, size=1024):
    return [
        load(source.at[:, pl.ds(begin_at, size)], target.at[:, pl.ds(begin_at, size)])
        for begin_at in range(0, source.shape[1], size)
    ]


def gate_grad_kernel(lens, n2t, gate_grad, send_out, keep_out, n2t_v, gate_v, send, keep, *sems):
    load, store = Copies(sems[0]), Copies(sems[1])
    first = load(n2t, n2t_v)
    loads = tile_loads(load, gate_grad, gate_v)
    first.wait()
    finish(row_grads(n2t_v, gate_v, (send, keep), 0, loads, store, (send_out, keep_out)))


def gate_grads(lens, n2t, gate_grad):
    part = (D // 2, FF)
    return pl.pallas_call(
        gate_grad_kernel,
        out_shape=(shape(part, BF16),) * 2,
        in_specs=[SMEM] + [ANY] * 2,
        out_specs=(ANY,) * 2,
        scratch_shapes=[
            pltpu.VMEM((D, SLOT), BF16),
            pltpu.VMEM((SLOT, FF), BF16),
            pltpu.VMEM(part, BF16),
            pltpu.VMEM(part, BF16),
            pltpu.SemaphoreType.DMA((3,)),
            pltpu.SemaphoreType.DMA((4,)),
        ],
        compiler_params=params(wide=True),
        cost_estimate=COST,
        name="gate_grads",
    )(lens, n2t, gate_grad)


def up_grad_kernel(lens, gain, n2t, gate_grad, up_grad, hidden, after_grad, *refs):
    pieces, outs, refs = refs[:12], refs[12:16], refs[16:]
    weight, n2t_v, gate_v, up_v, hidden_v, after_v, send, keep, grad, attn_in = refs[:10]
    sems, in_sems, done_sems = refs[10:]
    load, store = Copies(in_sems), Copies(done_sems)
    first = load(n2t, n2t_v)
    loads = tile_loads(load, up_grad, up_v)
    gate_load = load(gate_grad, gate_v)
    plan = sum(GATED_PLANS, ())
    gate_plan = tuple(entry for entry in plan if entry[3] < FF)
    up_plan = tuple(entry for entry in plan if entry[3] >= FF)
    gate_pieces = begin(pieces_of(SHARD, gate_plan, pieces, weight, sems))
    up_pieces = begin(pieces_of(SHARD, up_plan, pieces, weight, sems, len(gate_plan)))
    later = [load(hidden, hidden_v), load(after_grad, after_v)]
    first.wait()
    stores = row_grads(n2t_v, up_v, (send, keep), 0, loads, store, outs[0:2])
    gate_load.wait()
    finish(gate_pieces)
    for block in range(2):
        rows = pl.ds(block * 256, 256)
        grad[rows, :] = dot_t(gate_v[rows, :], weight[:, 0:FF])
    finish(up_pieces)
    finish(later)
    scale = gain[...].reshape(1, D)
    for block in range(2):
        rows = pl.ds(block * 256, 256)
        incoming = grad[rows, :] + dot_t(up_v[rows, :], weight[:, FF:])
        gradient = norm_backward(hidden_v[rows, :], scale, incoming) + after_v[rows, :]
        grad[rows, :] = gradient
        attn_in[rows, :] = gradient.astype(BF16)
    stores += [store(attn_in, outs[3]), store(grad, outs[2])]
    finish(stores)


def up_grads(lens, gain, n2t, gate_grad, up_grad, hidden, after_grad, pieces):
    full, part, wide = (SLOT, FF), (D // 2, FF), (SLOT, D)
    return pl.pallas_call(
        up_grad_kernel,
        out_shape=(shape(part, BF16),) * 2 + (shape(wide, F32), shape(wide, BF16)),
        in_specs=[SMEM, VMEM] + [ANY] * 17,
        out_specs=(ANY,) * 4,
        scratch_shapes=[
            pltpu.VMEM((D, 2 * FF), BF16),
            pltpu.VMEM((D, SLOT), BF16),
            pltpu.VMEM(full, BF16),
            pltpu.VMEM(full, BF16),
            pltpu.VMEM(wide, F32),
            pltpu.VMEM(wide, F32),
            pltpu.VMEM(part, BF16),
            pltpu.VMEM(part, BF16),
            pltpu.VMEM(wide, F32),
            pltpu.VMEM(wide, BF16),
            pltpu.SemaphoreType.DMA((24,)),
            pltpu.SemaphoreType.DMA((6,)),
            pltpu.SemaphoreType.DMA((6,)),
        ],
        compiler_params=params(wide=True),
        cost_estimate=COST,
        name="up_grads",
    )(lens, gain, n2t, gate_grad, up_grad, hidden, after_grad, *pieces)


def out_grad_kernel(lens, ot, fnt, attn_in, cot, *refs):
    pieces, outs, refs = refs[:4], refs[4:7], refs[7:]
    weight, left, proj_left, attn_v, cot_v, send, keep, mixed = refs[:8]
    sems, left_sems, proj_sems, in_sems, done_sems = refs[8:]
    load, store = Copies(in_sems), Copies(done_sems)
    loads = [load(attn_in, attn_v)]
    loads += begin(relative_copies(ot, left, left_sems))
    pieces = begin(pieces_of(SHARD, OUT_PLAN, pieces, weight, sems))
    later = [load(cot, cot_v)]
    later += begin(relative_copies(fnt, proj_left, proj_sems))
    finish(loads)
    stores = row_grads(left, attn_v, (send, keep), 0, (), store, outs[0:2])
    finish(later)
    stores += row_grads(proj_left, cot_v, (send, keep), D, (), store, outs[0:2])
    finish(pieces)
    mixed[...] = dot_t(attn_v[...], weight[:, 0:D]).astype(BF16)
    stores.append(store(mixed, outs[2]))
    finish(stores)


def out_grads(lens, ot, fnt, attn_in, cot, pieces):
    return pl.pallas_call(
        out_grad_kernel,
        out_shape=(shape((D // 2, WIDE), BF16),) * 2 + (shape((SLOT, D), BF16),),
        in_specs=[SMEM] + [ANY] * 8,
        out_specs=(ANY,) * 3,
        scratch_shapes=[
            pltpu.VMEM((D, WIDE), BF16),
            pltpu.VMEM((D, SLOT), BF16),
            pltpu.VMEM((D, SLOT), BF16),
            pltpu.VMEM((SLOT, D), BF16),
            pltpu.VMEM((SLOT, PROJ), BF16),
            pltpu.VMEM((D // 2, WIDE), BF16),
            pltpu.VMEM((D // 2, WIDE), BF16),
            pltpu.VMEM((SLOT, D), BF16),
            pltpu.SemaphoreType.DMA((4,)),
            pltpu.SemaphoreType.DMA((16,)),
            pltpu.SemaphoreType.DMA((16,)),
            pltpu.SemaphoreType.DMA((2,)),
            pltpu.SemaphoreType.DMA((5,)),
        ],
        compiler_params=params(wide=True),
        cost_estimate=COST,
        name="out_grads",
    )(lens, ot, fnt, attn_in, cot, *pieces)


def qkv_grad_kernel(lens, table, indicator, n1t, dq, dk, dv, *refs):
    outs, left, dq_v, dk_v, dv_v = refs[:4], refs[4], refs[5], refs[6], refs[7]
    send, keep, value_send, value_keep, small, left_sems, in_sems, done_sems = refs[8:]
    load, store = Copies(in_sems), Copies(done_sems)
    first = [load(dq, dq_v)] + begin(relative_copies(n1t, left, left_sems))
    second, third = load(dk, dk_v), load(dv, dv_v)
    finish(first)
    stores = row_grads(left, dq_v, (send, keep), 0, (), store, outs[0:2])
    stores += row_grads(left, dk_v, (send, keep), D, (second,), store, outs[0:2])
    by_lane = jnp.concatenate([table[pair] for pair in range(H // 2)], axis=0)
    high = by_lane.astype(BF16)
    low = (by_lane - high.astype(F32)).astype(BF16)
    by_bucket = dot(high, indicator[...]) + dot(low, indicator[...])
    small[...] = jnp.concatenate([by_bucket, jnp.zeros((PROJ - H, D), F32)], axis=0).T
    block, starts = relative_starts(D)
    for number, row in enumerate(starts):
        target = value_keep if number >= 8 else value_send
        target[pl.ds((number & 7) * block, block), D:WIDE] = small[pl.ds(row, block), :].astype(
            BF16
        )
    columns = pl.ds(D, PROJ)
    for number, part in enumerate((value_send, value_keep)):
        stores.append(store(part.at[:, columns], outs[2 + number].at[:, columns]))
    stores += row_grads(left, dv_v, (value_send, value_keep), 0, (third,), store, outs[2:4])
    finish(stores)


def qkv_grads(lens, table, n1t, dq, dk, dv):
    pair, single = (D // 2, 2 * D), (D // 2, WIDE)
    return pl.pallas_call(
        qkv_grad_kernel,
        out_shape=(shape(pair, BF16),) * 2 + (shape(single, BF16),) * 2,
        in_specs=[SMEM, VMEM, VMEM] + [ANY] * 4,
        out_specs=(ANY,) * 4,
        scratch_shapes=[pltpu.VMEM((D, SLOT), BF16)]
        + [pltpu.VMEM((SLOT, D), BF16)] * 3
        + [pltpu.VMEM(pair, BF16)] * 2
        + [pltpu.VMEM(single, BF16)] * 2
        + [
            pltpu.VMEM((D, PROJ), F32),
            pltpu.SemaphoreType.DMA((16,)),
            pltpu.SemaphoreType.DMA((3,)),
            pltpu.SemaphoreType.DMA((8,)),
        ],
        compiler_params=params(wide=True),
        cost_estimate=COST,
        name="qkv_grads",
    )(lens, table, jnp.asarray(table_indicator(), dtype=BF16), n1t, dq, dk, dv)


def attention_back_kernel(lens, q, k, v, et, linv, ot, do, *refs):
    dq, dk, dv, bias_grad, dqt, near = refs[-6:]
    lane_in_pair = lax.broadcasted_iota(jnp.int32, (SLOT, 2 * HEAD), 1)
    q_pair, v_pair = q[...], v[...]
    kt = k[...].T
    out_gradt = do[...].astype(F32).T
    scaled = []
    deltas = []
    for head in range(2):
        rows = slice(head * HEAD, (head + 1) * HEAD)
        low = (out_gradt[rows, :] * linv[head]).astype(BF16)
        scaled.append(low)
        deltas.append(
            jnp.sum(low.astype(F32) * ot[rows, :].astype(F32), axis=0, keepdims=True)
        )
    scaled_pair = jnp.concatenate(scaled, axis=0).T
    zeros = jnp.zeros((HEAD, SLOT), BF16)
    key_total = jnp.zeros((SLOT, 2 * HEAD), F32)
    value_total = jnp.zeros((SLOT, 2 * HEAD), F32)
    row_of_eight = lax.broadcasted_iota(jnp.int32, (8, SLOT), 0)
    for head in range(2):
        in_head = (lane_in_pair >= head * HEAD) & (lane_in_pair < (head + 1) * HEAD)
        q_head = jnp.where(in_head, q_pair, jnp.zeros_like(q_pair))
        do_head = jnp.where(in_head, scaled_pair, jnp.zeros_like(scaled_pair))
        dot_head = jnp.concatenate(
            [scaled[head], zeros] if head == 0 else [zeros, scaled[head]], axis=0
        )
        near_sums = {-1: None, 0: None, 1: None}
        far_sums = {-1: None, 1: None}
        for part in range(SLOT // HALF_Q):
            columns = slice(part * HALF_Q, (part + 1) * HALF_Q)
            prob_grad = dot(v_pair, dot_head[:, columns])
            low_weights = et[head, :, columns]
            score_grad = low_weights.astype(F32) * (prob_grad - deltas[head][:, columns])
            low = score_grad.astype(BF16)
            key_total = key_total + dot(low, q_head[columns, :])
            value_total = value_total + dot(low_weights, do_head[columns, :])
            dqt[pl.ds(head * HEAD, HEAD), columns] = dot(
                kt[head * HEAD : (head + 1) * HEAD, :], low
            ).astype(BF16)
            for key_block in range(4):
                for sub in range(HALF_Q // BLOCK):
                    apart = key_block - part * (HALF_Q // BLOCK) - sub
                    cell = score_grad[
                        key_block * BLOCK : (key_block + 1) * BLOCK,
                        sub * BLOCK : (sub + 1) * BLOCK,
                    ]
                    if abs(apart) >= 2:
                        side = 1 if apart > 0 else -1
                        folded = jnp.sum(cell.reshape(BLOCK // 8, 8, BLOCK), axis=0)
                        old = far_sums[side]
                        far_sums[side] = folded if old is None else old + folded
                    else:
                        old = near_sums[apart]
                        near_sums[apart] = cell if old is None else old + cell
        near[...] = jnp.zeros_like(near)
        for apart in (-1, 0, 1):
            lane = (-apart * BLOCK) % SLOT
            near[:, lane : lane + BLOCK] = near_sums[apart]
        folded = near[0:8, :]
        for group in range(1, BLOCK // 8):
            folded = folded + pltpu.roll(near[group * 8 : group * 8 + 8, :], SLOT - 8 * group, 1)
        for bit in (1, 2, 4):
            folded = jnp.where(
                (row_of_eight & bit) != 0, pltpu.roll(folded, SLOT - bit, 1), folded
            )
        here = slice(head, head + 1)
        bias_grad[0, here, 0:SLOT] = jnp.sum(folded, axis=0, keepdims=True)
        for number, side in enumerate((-1, 1)):
            lane = SLOT + number * BLOCK
            bias_grad[0, here, lane : lane + BLOCK] = jnp.sum(
                far_sums[side], axis=0, keepdims=True
            )
    dk[...] = key_total.astype(BF16)
    dv[...] = value_total.astype(BF16)
    dq[...] = dqt[...].T


def attention_back(lens, qkv, et, linv, ot, do, first, count, held):
    pair = 2 * HEAD
    pairs = H // 2
    wide = pl.BlockSpec((SLOT, pair), lambda i: (0, first + i))
    return pl.pallas_call(
        attention_back_kernel,
        grid=(count,),
        out_shape=(shape((SLOT, D), BF16),) * 3 + (shape((pairs, 2, D), F32),),
        in_specs=[
            SMEM,
            wide,
            pl.BlockSpec((SLOT, pair), lambda i: (0, pairs + first + i)),
            pl.BlockSpec((SLOT, pair), lambda i: (0, 2 * pairs + first + i)),
            pl.BlockSpec((2, SLOT, SLOT), lambda i: (first + i, 0, 0)),
            pl.BlockSpec((2, 1, SLOT), lambda i: (first + i, 0, 0)),
            pl.BlockSpec((pair, SLOT), lambda i: (first + i, 0)),
            wide,
        ]
        + [ANY] * len(held),
        out_specs=(wide,) * 3 + (pl.BlockSpec((1, 2, D), lambda i: (first + i, 0, 0)),),
        input_output_aliases={8 + i: i for i in range(len(held))},
        scratch_shapes=[pltpu.VMEM((pair, SLOT), BF16), pltpu.VMEM((BLOCK, SLOT), F32)],
        compiler_params=params(wide=True),
        cost_estimate=COST,
        name="attention_back",
    )(lens, qkv, qkv, qkv, et, linv, ot, do, *held)


def token_grad_kernel(lens, gain, embedded, dq, dk, dv, hidden_grad, tok, *refs):
    pieces, outs, refs = refs[:8], refs[8:12], refs[12:]
    weight, embedded_v, dq_v, dk_v, dv_v, hidden_v, tok_v, total = refs[:8]
    packed, (sems, in_sems, done_sems) = refs[8:12], refs[12:]
    load, store = Copies(in_sems), Copies(done_sems)
    me, _ = place()
    loads = []
    for number, (source, target) in enumerate(((dq, dq_v), (dk, dk_v), (dv, dv_v))):
        plan = QKV_PLANS[number]
        loads.append(
            [load(source, target)]
            + begin(pieces_of(SHARD, plan, pieces, weight, sems, 6 * number))
        )
    later = [load(hidden_grad, hidden_v), load(tok, tok_v), load(embedded, embedded_v)]
    for number, source in enumerate((dq_v, dk_v, dv_v)):
        finish(loads[number])
        for block in range(2):
            rows = pl.ds(block * 256, 256)
            term = dot_t(source[rows, :], weight[:, number * D : (number + 1) * D])
            total[rows, :] = term if number == 0 else total[rows, :] + term
    finish(later)
    scale = gain[...].reshape(1, D)
    stores = []
    for flip, target in enumerate(packed):
        rows = pl.ds(pl.multiple_of((me ^ flip) * BLOCK, BLOCK), BLOCK)
        gradient = norm_backward(tok_v[rows, :].astype(F32), scale, total[rows, :])
        target[:, 0:D] = (hidden_v[rows, :] + gradient).astype(BF16)
        target[:, D:WIDE] = embedded_v[rows, :]
        stores.append(store(target, outs[flip]))
    finish(stores)


def token_grads(lens, gain, embedded, dq, dk, dv, hidden_grad, tok, pieces):
    wide = (SLOT, D)
    return pl.pallas_call(
        token_grad_kernel,
        out_shape=(shape((BLOCK, WIDE), BF16),) * 4,
        in_specs=[SMEM, VMEM] + [ANY] * 14,
        out_specs=(ANY,) * 4,
        scratch_shapes=[
            pltpu.VMEM((D, 3 * D), BF16),
            pltpu.VMEM((SLOT, PROJ), BF16),
            pltpu.VMEM(wide, BF16),
            pltpu.VMEM(wide, BF16),
            pltpu.VMEM(wide, BF16),
            pltpu.VMEM(wide, F32),
            pltpu.VMEM(wide, BF16),
            pltpu.VMEM(wide, F32),
        ]
        + [pltpu.VMEM((BLOCK, WIDE), BF16)] * 4
        + [
            pltpu.SemaphoreType.DMA((18,)),
            pltpu.SemaphoreType.DMA((6,)),
            pltpu.SemaphoreType.DMA((4,)),
        ],
        compiler_params=params(wide=True),
        cost_estimate=COST,
        name="token_grads",
    )(lens, gain, embedded, dq, dk, dv, hidden_grad, tok, *pieces)


def unpack_kernel(block_0, block_1, block_2, block_3, embedded, tokens_grad):
    me, _ = place()
    for flip, block in enumerate((block_0, block_1, block_2, block_3)):
        tokens_grad[me ^ flip] = block[:, 0:D].astype(F32)
        embedded[me ^ flip] = block[:, D:WIDE]


def unpack(blocks):
    return pl.pallas_call(
        unpack_kernel,
        out_shape=(shape((SEQ, BLOCK, PROJ), BF16), shape((SEQ, BLOCK, D), F32)),
        in_specs=[VMEM] * 4,
        out_specs=(VMEM,) * 2,
        compiler_params=params(),
        cost_estimate=SMALL_COST,
        name="unpack",
    )(*blocks)


def exchange(value, axis, flip, size):
    return lax.ppermute(value, axis, [(i, i ^ flip) for i in range(size)])


def after(value, *others):
    return lax.optimization_barrier((value,) + others)[0]


def add(*terms):
    total = terms[0].astype(F32)
    for term in terms[1:]:
        total = total + term.astype(F32)
    return total.astype(BF16)


def marker_kernel(tick, mark):
    pass


def marker(tick):
    return pl.pallas_call(
        marker_kernel,
        out_shape=shape((8, 128), F32),
        in_specs=[ANY],
        out_specs=ANY,
        compiler_params=params(),
        cost_estimate=COST,
        name="marker",
    )(tick)


class Chunk:
    def __init__(self, groups, pair, thin=False):
        self.groups, self.thin = groups, thin
        self.send, self.keep = pair
        self.rows = self.send.shape[0] // 4

    def along(self, flip, value):
        return exchange(value, "dp", flip, self.groups)

    def core(self, tick):
        self.send = after(self.send, tick)
        self.from_core = exchange(self.send, "seq", 1, SEQ)

    def x(self, tick):
        both = 2 * self.rows
        self.from_core = after(self.from_core, tick)
        mine = add(self.keep[:both], self.from_core[:both])
        self.from_x = exchange(mine, "seq", 2, SEQ)

    def first(self, tick):
        rows = self.rows
        self.from_x = after(self.from_x, tick)
        mine = add(
            self.keep[2 * rows : 3 * rows], self.from_core[2 * rows : 3 * rows], self.from_x[:rows]
        )
        self.from_first = self.along(1, mine)

    def _summed(self, begin, end):
        rows = self.rows
        return add(
            self.keep[3 * rows + begin : 3 * rows + end],
            self.from_core[3 * rows + begin : 3 * rows + end],
            self.from_x[rows + begin : rows + end],
            self.from_first[begin:end],
        )

    def second(self, tick):
        self.from_first = after(self.from_first, tick)
        self.total = self._summed(0, self.rows if self.thin else self.rows // 2)
        self.from_second = self.along(2, self.total)

    def rest(self, tick):
        self.from_second = after(self.from_second, tick)
        if not self.thin:
            self.total = self._summed(self.rows // 2, self.rows)
        self.total = add(self.total, self.from_second)
        step = 4
        while step < self.groups:
            if step > 4:
                self.total = add(self.total, self.from_rest)
            self.from_rest = self.along(step, self.total)
            step *= 2

    def back_second(self, tick):
        self.from_rest = after(self.from_rest, tick)
        self.total = add(self.total, self.from_rest)
        self.other_second = self.along(2, self.total)

    def back_first(self, tick):
        if self.thin:
            self.from_rest = after(self.from_rest, tick)
            self.total = add(self.total, self.from_rest)
        else:
            self.other_second = after(self.other_second, tick)
            self.total = jnp.concatenate([self.other_second, self.total], axis=0)
        self.other = self.along(1, self.total)


def join_kernel(*refs):
    terms, out = refs[:-1], refs[-1]
    column = 0
    for left, right in zip(terms[0::2], terms[1::2]):
        width = left.shape[1]
        out[:, column : column + width] = (
            left[...].astype(F32) + right[...].astype(F32)
        ).astype(BF16)
        column += width


class Group:
    thin = False

    def __init__(self, *chunks):
        self.chunks, self.rows, self.along = chunks, chunks[0].rows, chunks[0].along

    def back_second(self, tick):
        terms = []
        for chunk in self.chunks:
            terms += [chunk.total, after(chunk.from_rest, tick)]
        width = sum(chunk.total.shape[1] for chunk in self.chunks)
        self.total = pl.pallas_call(
            join_kernel,
            out_shape=shape((self.rows // 2, width), BF16),
            in_specs=[VMEM] * len(terms),
            out_specs=VMEM,
            compiler_params=params(),
            cost_estimate=SMALL_COST,
            name="join",
        )(*terms)
        self.other_second = self.along(2, self.total)

    def back_first(self, tick):
        self.other_second = after(self.other_second, tick)
        self.total = jnp.concatenate([self.other_second, self.total], axis=0)
        self.other = self.along(1, self.total)


def assemble_kernel(rows, widths, marks, counts, table, natural, total, other, *refs):
    weights, refs = refs[: counts[0]], refs[counts[0] :]
    gains, outs = refs[: counts[1]], refs[counts[1] :]
    me, y = place()
    z = lax.rem(lax.axis_index("dp") // 2, 2)
    half = rows // 2
    column = 0
    sums = [None] * counts[1]

    def blocks():
        for source, first in ((total, 1), (other, 0)):
            for second in range(2):
                y_of = y if first else 1 - y
                z_of = second if natural else (z if second else 1 - z)
                yield source, second * half, y_of, z_of

    for number, width in enumerate(widths):
        columns = slice(column, column + width)
        out = outs[number]
        for source, row, y_of, z_of in blocks():
            begin_row = pl.multiple_of(y_of * rows + z_of * half, 16)
            out[pl.ds(begin_row, half), :] = source[row : row + half, columns].astype(F32)
        column += width
        for which, weight, target in marks:
            if which == number:
                part = jnp.sum(
                    weights[weight][...].astype(F32) * out[...], axis=1, keepdims=True
                )
                sums[target] = part if sums[target] is None else sums[target] + part
    for number, (summed, gain) in enumerate(zip(sums, gains)):
        total_rows = jnp.broadcast_to(summed, (2 * rows, BLOCK)).T[0:1, :]
        whole = gain[...].reshape(1, D)
        mine = whole[:, 0:SHARD]
        for shard in range(1, SEQ):
            mine = jnp.where(me == shard, whole[:, shard * SHARD : (shard + 1) * SHARD], mine)
        outs[len(widths) + number][...] = (total_rows / mine).reshape(2 * rows)
    if table:
        for source, row, y_of, z_of in blocks():
            if natural and z_of:
                continue

            @pl.when((y_of == 0) if natural else (y_of == 0) & (z_of == 0))
            def store():
                outs[-1][...] = source[
                    row : row + BUCKETS // SEQ, column : column + H
                ].astype(F32)


def assemble(chunk, widths, marks=(), weights=(), gains=(), table=False):
    rows = chunk.rows
    out_shape = [shape((2 * rows, width), F32) for width in widths]
    out_shape += [shape((2 * rows,), F32) for _ in gains]
    if table:
        out_shape.append(shape((BUCKETS // SEQ, H), F32))
    operands = tuple(weights) + tuple(gains)
    return pl.pallas_call(
        functools.partial(
            assemble_kernel,
            rows,
            widths,
            marks,
            (len(weights), len(gains)),
            table,
            chunk.thin,
        ),
        out_shape=tuple(out_shape),
        in_specs=[VMEM] * (2 + len(operands)),
        out_specs=(VMEM,) * len(out_shape),
        compiler_params=params(),
        cost_estimate=SMALL_COST,
        name="assemble",
    )(chunk.total, chunk.other, *operands)


def per_device(
    groups,
    tokens,
    doc_lengths,
    query_weight,
    key_weight,
    value_weight,
    out_weight,
    gate_weight,
    up_weight,
    down_weight,
    proj_weight,
    attn_gain,
    ffn_gain,
    final_gain,
    bucket_bias_rows,
    embed_cotangent,
):
    tick = doc_lengths

    def across_x(mine):
        return exchange(after(mine, tick), "seq", 2, SEQ)

    def across_y(mine):
        return exchange(after(mine, tick), "dp", 1, groups)

    def across_core(mine):
        return exchange(after(mine, tick), "seq", 1, SEQ)

    def across_far(mine):
        return exchange(after(mine, tick), "seq", 3, SEQ)

    qkv_half = pack_first(tick, query_weight, key_weight, value_weight)
    qkv_x = across_x(qkv_half)
    tick = after(tick, qkv_half)
    blocks = pack_tokens(tick, tokens, embed_cotangent)
    block_x = across_x(blocks[2])
    block_far = across_far(blocks[3])
    block_core = across_core(blocks[1])
    tick = after(tick, blocks[0])
    qkv_own, out_own, gated_half_0, gated_half_1, down_rest = pack_rest(
        tick,
        query_weight,
        key_weight,
        value_weight,
        out_weight,
        proj_weight,
        gate_weight,
        up_weight,
        down_weight,
    )
    tick = after(tick, qkv_x, gated_half_0)
    qkv_y = across_y(qkv_x)
    qkv_cx = across_core(qkv_x)
    tick = after(tick, block_x, block_far, block_core)
    qkv_core = across_core(qkv_own)
    out_x = across_x(out_own)
    tok, cot, n1, n1t = first_norm(tick, (blocks[0], block_core, block_x, block_far), attn_gain)
    tick = after(tick, n1, qkv_y, qkv_cx)
    qkv_cy = across_core(qkv_y)
    tick = after(tick, qkv_cy, qkv_core, out_x)
    out_core = across_core(out_own)
    gated_x_0 = across_x(gated_half_0)
    gated_x_1 = across_x(gated_half_1)
    gate_core = across_core(gate_weight)
    qkv_pieces = (
        query_weight, key_weight, value_weight, qkv_core, qkv_x, qkv_y, qkv_cx, qkv_cy
    )
    qkv = qkv_project(tick, n1, qkv_pieces)
    pairs = H // 2
    third = pairs // 3
    tick = after(tick, qkv, gated_x_0, out_core, gate_core)
    gated_y_0 = across_y(gated_x_0)
    gated_cx_0 = across_core(gated_x_0)
    out_cx = across_core(out_x)
    down_x = across_x(down_rest)
    held = attention(tick, qkv, bucket_bias_rows, 0, third, ())
    tick = after(tick, held[0], gated_x_1, gated_cx_0, out_cx)
    gated_y_1 = across_y(gated_x_1)
    gated_cx_1 = across_core(gated_x_1)
    up_core = across_core(up_weight)
    held = attention(tick, qkv, bucket_bias_rows, third, third, held)
    tick = after(tick, held[0], gated_y_0, gated_cx_1, up_core)
    gated_cy_0 = across_core(gated_y_0)
    down_core = across_core(down_weight)
    et, linv, ot, mixed = attention(
        tick, qkv, bucket_bias_rows, 2 * third, pairs - 2 * third, held
    )
    tick = after(tick, mixed, gated_y_1, gated_cy_0, down_core)
    gated_cy_1 = across_core(gated_y_1)
    tick = after(tick, down_x)
    down_cx = across_core(down_x)
    tick = after(tick, gated_cy_1, down_cx)
    out_pieces = (out_own, out_core, out_x, out_cx)
    down_pieces = (down_weight, down_core, out_x, down_x, out_cx, down_cx)
    gated_pieces = (
        gate_weight, up_weight, gate_core, up_core,
        gated_x_0, gated_y_0, gated_cx_0, gated_cy_0,
        gated_x_1, gated_y_1, gated_cx_1, gated_cy_1,
    )
    hidden, n2t, gate_grad, up_grad, embedded, after_grad, fnt, *pair = feed_forward(
        tick, tok, mixed, cot, ffn_gain, final_gain, out_pieces, gated_pieces, down_pieces
    )

    chunk = functools.partial(Chunk, groups)
    down_sum = chunk(pair)
    tick = after(tick, down_sum.keep)
    down_sum.core(tick)
    gate_sum = chunk(gate_grads(tick, n2t, gate_grad))
    tick = after(tick, gate_sum.keep, down_sum.from_core)
    down_sum.x(tick)
    gate_sum.core(tick)
    *pair, hidden_grad, attn_in = up_grads(
        tick, ffn_gain, n2t, gate_grad, up_grad, hidden, after_grad, gated_pieces
    )
    up_sum = chunk(pair)
    tick = after(tick, up_sum.keep, gate_sum.from_core)
    gate_sum.x(tick)
    up_sum.core(tick)
    *pair, mixed_grad = out_grads(tick, ot, fnt, attn_in, cot, out_pieces)
    out_sum = chunk(pair)
    tick = after(tick, out_sum.keep, up_sum.from_core, down_sum.from_x)
    down_sum.first(tick)
    up_sum.x(tick)
    out_sum.core(tick)
    held = attention_back(tick, qkv, et, linv, ot, mixed_grad, 0, pairs // 2, ())
    tick = after(tick, held[0], out_sum.from_core, down_sum.from_first)
    down_sum.second(tick)
    out_sum.x(tick)
    dq, dk, dv, bias_part = attention_back(
        tick, qkv, et, linv, ot, mixed_grad, pairs // 2, pairs - pairs // 2, held
    )
    tick = after(tick, dq, gate_sum.from_x, down_sum.from_second)
    gate_sum.first(tick)
    down_sum.rest(tick)
    *pair, value_send, value_keep = qkv_grads(tick, bias_part, n1t, dq, dk, dv)
    first_sum, value_sum = chunk(pair), chunk((value_send, value_keep))
    tick = after(
        tick,
        first_sum.keep,
        gate_sum.from_first,
        up_sum.from_x,
        down_sum.from_rest,
        out_sum.from_x,
    )
    first_sum.core(tick)
    value_sum.core(tick)
    gate_sum.second(tick)
    up_sum.first(tick)
    down_sum.back_second(tick)
    blocks = token_grads(
        tick, attn_gain, embedded, dq, dk, dv, hidden_grad, tok, qkv_pieces
    )
    tick = after(
        tick,
        blocks[0],
        first_sum.from_core,
        value_sum.from_core,
        gate_sum.from_second,
        up_sum.from_first,
        down_sum.other_second,
    )
    first_sum.x(tick)
    gate_sum.rest(tick)
    up_sum.second(tick)
    down_sum.back_first(tick)
    tick = after(tick, marker(tick), up_sum.from_second)
    up_sum.rest(tick)
    value_sum.x(tick)
    tick = after(tick, marker(tick), gate_sum.from_rest, down_sum.other)
    out_sum.first(tick)
    tick = after(tick, marker(tick), first_sum.from_x)
    first_sum.first(tick)
    tick = after(tick, marker(tick), up_sum.from_rest)
    gated_sum = Group(gate_sum, up_sum)
    gated_sum.back_second(tick)
    tick = after(tick, marker(tick), out_sum.from_first, value_sum.from_x)
    value_sum.first(tick)
    out_sum.second(tick)
    tick = after(tick, marker(tick), first_sum.from_first, gated_sum.other_second)
    first_sum.second(tick)
    gated_sum.back_first(tick)
    tick = after(tick, marker(tick), value_sum.from_first, out_sum.from_second)
    value_sum.second(tick)
    out_sum.rest(tick)
    tick = after(tick, marker(tick), first_sum.from_second)
    first_sum.rest(tick)
    block_x = across_x(blocks[2])
    block_far = across_far(blocks[3])
    tick = after(tick, marker(tick), value_sum.from_second)
    value_sum.rest(tick)
    tick = after(
        tick, marker(tick), first_sum.from_rest, value_sum.from_rest, out_sum.from_rest, gated_sum.other, block_x, block_far
    )
    attn_sum = Group(out_sum, first_sum, value_sum)
    attn_sum.back_second(tick)
    block_core = across_core(blocks[1])
    tick = after(tick, marker(tick), attn_sum.other_second, block_core)
    attn_sum.back_first(tick)
    down_grad, = assemble(down_sum, (D,))
    gate_weight_grad, up_weight_grad, ffn_gain_grad = assemble(
        gated_sum, (FF, FF), ((0, 0, 0), (1, 1, 0)), (gate_weight, up_weight), (ffn_gain,)
    )
    embedded, tokens_grad = unpack((blocks[0], block_core, block_x, block_far))
    (
        out_grad,
        proj_grad,
        query_grad,
        key_grad,
        value_grad,
        final_gain_grad,
        attn_gain_grad,
        table_grad,
    ) = assemble(
        attn_sum,
        (D, PROJ, D, D, D),
        ((1, 0, 0), (2, 1, 1), (3, 2, 1), (4, 3, 1)),
        (proj_weight, query_weight, key_weight, value_weight),
        (final_gain, attn_gain),
        table=True,
    )
    return (
        embedded,
        tokens_grad,
        query_grad,
        key_grad,
        value_grad,
        out_grad,
        gate_weight_grad,
        up_weight_grad,
        down_grad,
        proj_grad,
        attn_gain_grad,
        ffn_gain_grad,
        final_gain_grad,
        table_grad,
    )


def solution(mesh):
    placed = (
        P("dp", "seq", None),
        P("dp"),
        P("seq", None),
        P("seq", None),
        P("seq", None),
        P("seq", None),
        P("seq", None),
        P("seq", None),
        P("seq", None),
        P("seq", None),
        P(),
        P(),
        P(),
        P(),
        P("dp", "seq", None),
    )
    return jax.shard_map(
        functools.partial(per_device, mesh.shape["dp"]),
        mesh=mesh,
        in_specs=placed,
        out_specs=(
            P("dp", "seq", None),
            P("dp", "seq", None),
            P("seq", None),
            P("seq", None),
            P("seq", None),
            P("seq", None),
            P("seq", None),
            P("seq", None),
            P("seq", None),
            P("seq", None),
            P("seq"),
            P("seq"),
            P("seq"),
            P("seq", None),
        ),
        check_vma=False,
    )
```

```python
import functools

import jax
import jax.numpy as jnp
import numpy as np
from jax import lax
from jax.experimental import pallas as pl
from jax.experimental.pallas import tpu as pltpu
from jax.sharding import PartitionSpec as P

D = 768
H = 12
HEAD = 64
FF = 2048
PROJ = 128
BUCKETS = 32
SLOT = 512
BLOCK = 128
SEQ = 4
SHARD = D // SEQ
HALF_FF = FF // 2
WIDE = D + PROJ
EPSILON = 1e-06
BIG_NEGATIVE = -1e30
GELU_A = 0.7978845608028654
GELU_B = 0.044715

F32 = jnp.float32
BF16 = jnp.bfloat16
VMEM = pl.BlockSpec(memory_space=pltpu.VMEM)
SMEM = pl.BlockSpec(memory_space=pltpu.SMEM)
ANY = pl.BlockSpec(memory_space=pl.ANY)
MIB = 1 << 20


def shape(dims, kind):
    return jax.ShapeDtypeStruct(dims, kind)


def params(wide=False):
    return pltpu.CompilerParams(vmem_limit_bytes=(58 if wide else 20) * MIB)


COST = pl.CostEstimate(flops=30000000000, bytes_accessed=100000000, transcendentals=0)
SMALL_COST = pl.CostEstimate(flops=1, bytes_accessed=1, transcendentals=0)


def bucket_of(relative):
    distance = np.abs(relative)
    scaled = np.log(np.maximum(distance, 1) / 8.0) / np.log(16.0) * 8.0
    far_bucket = np.minimum(8 + scaled.astype(np.int64), 15)
    return (relative > 0) * 16 + np.where(distance < 8, distance, far_bucket)


def skew_buckets():
    lanes = (np.arange(SLOT) + SLOT // 2) % SLOT - SLOT // 2
    relative = np.arange(8)[:, None] - lanes[None, :]
    return bucket_of(relative).astype(np.int32)


def table_indicator():
    lanes = (np.arange(SLOT) + SLOT // 2) % SLOT - SLOT // 2
    buckets = np.concatenate([bucket_of(-lanes), np.full(BLOCK, 15), np.full(BLOCK, 31)])
    here = BUCKETS // SEQ
    place = (buckets // here) * SHARD + buckets % here
    return (place[:, None] == np.arange(D)[None, :]).astype(np.float32)


def dot(left, right):
    return jnp.dot(left, right, preferred_element_type=F32)


def dot_t(left, right):
    return lax.dot_general(left, right, (((1,), (1,)), ((), ())), preferred_element_type=F32)


def place():
    return lax.axis_index("seq"), lax.rem(lax.axis_index("dp"), 2)


def relative_starts(rows, natural=False):
    me, y = place()
    z = lax.rem(lax.axis_index("dp") // 2, 2)
    bits = (me & 1, me >> 1, y, z)
    block = rows // 16
    starts = []
    for number in range(16):
        own = [(number >> shift) & 1 for shift in (3, 2, 1, 0)]
        core, x, first, second = (b if o else 1 - b for b, o in zip(bits, own))
        if natural:
            second = own[3]
        place_of = ((x * 2 + core) * 2 + first) * 2 + second
        starts.append(pl.multiple_of(place_of * block, 16))
    return block, starts


def begin(copies):
    for copy in copies:
        copy.start()
    return copies


def finish(copies):
    for copy in copies:
        copy.wait()


def run_all(copies):
    finish(begin(copies))


class Copies:
    def __init__(self, sems):
        self.sems, self.used = sems, 0

    def __call__(self, source, target):
        copy = pltpu.make_async_copy(source, target, self.sems.at[self.used])
        self.used += 1
        copy.start()
        return copy


def pieces_of(rows, plan, refs, target, sems, first=0):
    me, y = place()
    half = rows // 2
    starts = (
        me * rows,
        (me ^ 1) * rows,
        (me ^ 2) * rows + y * half,
        (me ^ 2) * rows + (1 - y) * half,
        (me ^ 3) * rows + y * half,
        (me ^ 3) * rows + (1 - y) * half,
        (me ^ 2) * rows,
        (me ^ 3) * rows,
    )
    copies = []
    for number, (ref, piece, source, to, width, *some) in enumerate(plan):
        first_row, skip, size = some or (0, 0, half if 2 <= piece < 6 else rows)
        copies.append(
            pltpu.make_async_copy(
                refs[ref].at[pl.ds(first_row, size), pl.ds(source, width)],
                target.at[
                    pl.ds(pl.multiple_of(starts[piece] + skip, 16), size), pl.ds(to, width)
                ],
                sems.at[first + number],
            )
        )
    return copies


QKV_PLANS = tuple(
    ((number, 0, 0, number * D, D),)
    + tuple((2 + piece, piece, number * D, number * D, D) for piece in range(1, 6))
    for number in range(3)
)
OUT_PLAN = tuple((ref, piece, 0, 0, WIDE) for ref, piece in enumerate((0, 1, 6, 7)))
DOWN_SHARD = FF // SEQ
EARLY = 64
DOWN_PLAN = (
    (0, 0, 0, 0, D),
    (1, 1, 0, 0, D),
    (2, 6, 0, 0, D, SHARD, 0, EARLY),
    (3, 6, 0, 0, D, 0, EARLY, DOWN_SHARD - EARLY),
    (4, 7, 0, 0, D, SHARD, 0, EARLY),
    (5, 7, 0, 0, D, 0, EARLY, DOWN_SHARD - EARLY),
)


def gated_plan(part):
    column = part * HALF_FF
    parts = [(4 + 4 * part + number, piece) for number, piece in enumerate((2, 3, 4, 5))]
    return (
        (0, 0, column, column, HALF_FF),
        (1, 0, column, FF + column, HALF_FF),
        (2, 1, column, column, HALF_FF),
        (3, 1, column, FF + column, HALF_FF),
    ) + tuple(
        (ref, piece, number * HALF_FF, number * FF + column, HALF_FF)
        for ref, piece in parts
        for number in range(2)
    )


GATED_PLANS = (gated_plan(0), gated_plan(1))


def relative_copies(source, target, sems, natural=False):
    block, starts = relative_starts(source.shape[0], natural)
    return [
        pltpu.make_async_copy(
            source.at[pl.ds(begin, block), :],
            target.at[pl.ds(number * block, block), :],
            sems.at[number],
        )
        for number, begin in enumerate(starts)
    ]


def inverse_rms(values):
    return lax.rsqrt(jnp.mean(values * values, axis=-1, keepdims=True) + EPSILON)


def norm_backward(values, gain, incoming):
    r = inverse_rms(values)
    weighted = gain * incoming
    inner = jnp.mean(weighted * values, axis=-1, keepdims=True)
    return r * weighted - values * (r * r * r * inner)


def pack_first_kernel(lens, q, k, v, qkv_half, sems):
    _, y = place()
    half = SHARD // 2
    rows = pl.ds(pl.multiple_of(y * half, 16), half)
    run_all(
        [
            pltpu.make_async_copy(
                weight.at[rows, :], qkv_half.at[:, pl.ds(number * D, D)], sems.at[number]
            )
            for number, weight in enumerate((q, k, v))
        ]
    )


def pack_first(lens, q, k, v):
    return pl.pallas_call(
        pack_first_kernel,
        out_shape=shape((SHARD // 2, 3 * D), BF16),
        in_specs=[SMEM] + [ANY] * 3,
        out_specs=VMEM,
        scratch_shapes=[pltpu.SemaphoreType.DMA((3,))],
        compiler_params=params(wide=True),
        cost_estimate=COST,
        name="pack_first",
    )(lens, q, k, v)


def pack_tokens_kernel(lens, tokens, cot, *refs):
    blocks, sems = refs[:4], refs[4]
    me, _ = place()
    pairs = []
    for flip, block in enumerate(blocks):
        pairs.append((tokens.at[me ^ flip], block.at[:, pl.ds(0, D)]))
        pairs.append((cot.at[me ^ flip], block.at[:, pl.ds(D, PROJ)]))
    run_all([pltpu.make_async_copy(a, b, sems.at[i]) for i, (a, b) in enumerate(pairs)])


def pack_tokens(lens, tokens, cot):
    return pl.pallas_call(
        pack_tokens_kernel,
        out_shape=(shape((BLOCK, WIDE), BF16),) * 4,
        in_specs=[SMEM] + [ANY] * 2,
        out_specs=(VMEM,) * 4,
        scratch_shapes=[pltpu.SemaphoreType.DMA((8,))],
        compiler_params=params(wide=True),
        cost_estimate=COST,
        name="pack_tokens",
    )(lens, tokens, cot)


def pack_rest_kernel(
    lens, q, k, v, out, proj, gate, up, down, qkv, out_own, part_0, part_1, down_rest, sems
):
    _, y = place()
    half = SHARD // 2
    rows = pl.ds(pl.multiple_of(y * half, 16), half)
    pairs = [(w, qkv.at[:, pl.ds(number * D, D)]) for number, w in enumerate((q, k, v))]
    pairs.append((out, out_own.at[pl.ds(0, SHARD), pl.ds(0, D)]))
    pairs.append((proj, out_own.at[pl.ds(0, SHARD), pl.ds(D, PROJ)]))
    pairs.append((down.at[pl.ds(0, EARLY), :], out_own.at[pl.ds(SHARD, EARLY), pl.ds(0, D)]))
    pairs.append((down.at[pl.ds(EARLY, DOWN_SHARD - EARLY), :], down_rest))
    for number, part in enumerate((part_0, part_1)):
        columns = pl.ds(number * HALF_FF, HALF_FF)
        pairs.append((gate.at[rows, columns], part.at[:, pl.ds(0, HALF_FF)]))
        pairs.append((up.at[rows, columns], part.at[:, pl.ds(HALF_FF, HALF_FF)]))
    run_all([pltpu.make_async_copy(a, b, sems.at[i]) for i, (a, b) in enumerate(pairs)])


def pack_rest(lens, q, k, v, out, proj, gate, up, down):
    half = SHARD // 2
    return pl.pallas_call(
        pack_rest_kernel,
        out_shape=(shape((SHARD, 3 * D), BF16), shape((SHARD + EARLY, WIDE), BF16))
        + (shape((half, FF), BF16),) * 2
        + (shape((DOWN_SHARD - EARLY, D), BF16),),
        in_specs=[SMEM] + [ANY] * 8,
        out_specs=(VMEM,) * 5,
        scratch_shapes=[pltpu.SemaphoreType.DMA((11,))],
        compiler_params=params(wide=True),
        cost_estimate=COST,
        name="pack_rest",
    )(lens, q, k, v, out, proj, gate, up, down)


def first_norm_kernel(lens, own, from_core, from_x, from_far, gain, tok, cot, n1, n1t, held, sems):
    me, _ = place()
    run_all(
        [
            pltpu.make_async_copy(
                piece,
                held.at[pl.ds(pl.multiple_of((me ^ flip) * BLOCK, BLOCK), BLOCK), :],
                sems.at[flip],
            )
            for flip, piece in enumerate((own, from_core, from_x, from_far))
        ]
    )
    scale = gain[...].reshape(1, D)
    for block in range(SLOT // BLOCK):
        rows = pl.ds(block * BLOCK, BLOCK)
        here = held[rows, 0:D]
        tok[rows, :] = here
        cot[rows, :] = held[rows, D : D + PROJ]
        values = here.astype(F32)
        normed = (values * inverse_rms(values) * scale).astype(BF16)
        n1[rows, :] = normed
        n1t[:, rows] = normed.T


def first_norm(lens, blocks, gain):
    return pl.pallas_call(
        first_norm_kernel,
        out_shape=(
            shape((SLOT, D), BF16),
            shape((SLOT, PROJ), BF16),
            shape((SLOT, D), BF16),
            shape((D, SLOT), BF16),
        ),
        in_specs=[SMEM, ANY, ANY, ANY, ANY, VMEM],
        out_specs=(VMEM,) * 4,
        scratch_shapes=[pltpu.VMEM((SLOT, WIDE), BF16), pltpu.SemaphoreType.DMA((4,))],
        compiler_params=params(wide=True),
        cost_estimate=COST,
        name="first_norm",
    )(lens, *blocks, gain)


def qkv_kernel(lens, n1, *refs):
    pieces, (out, weight, sems) = refs[:8], refs[8:]
    group = pl.program_id(0)

    def copies(number):
        return pieces_of(SHARD, QKV_PLANS[number], pieces, weight, sems, 6 * number)

    @pl.when(group == 0)
    def start():
        for number in range(3):
            begin(copies(number))

    for number in range(3):

        @pl.when(group == number)
        def ready():
            finish(copies(number))

    for tile in range(D // 256):
        columns = pl.ds(pl.multiple_of(group * D + tile * 256, 256), 256)
        out[:, tile * 256 : (tile + 1) * 256] = dot(n1[...], weight[:, columns]).astype(BF16)


def qkv_project(lens, n1, pieces):
    return pl.pallas_call(
        qkv_kernel,
        grid=(3,),
        out_shape=shape((SLOT, 3 * D), BF16),
        in_specs=[SMEM, VMEM] + [ANY] * 8,
        out_specs=pl.BlockSpec((SLOT, D), lambda i: (0, i)),
        scratch_shapes=[pltpu.VMEM((D, 3 * D), BF16), pltpu.SemaphoreType.DMA((18,))],
        compiler_params=params(wide=True),
        cost_estimate=COST,
        name="qkv_project",
    )(lens, n1, *pieces)


HALF_Q = 512


def attention_kernel(first, lens, q, k, v, rows_of_bias, buckets, *refs):
    et, linv, ot, o, bias = refs[-5:]
    me, _ = place()
    length = lens[me]
    pair = pl.program_id(0) + first
    k_pair = k[...]
    vt = v[...].T
    qt = q[...].T
    row_in_pair = lax.broadcasted_iota(jnp.int32, (2 * HEAD, SLOT), 0)
    key_index = lax.broadcasted_iota(jnp.int32, (SLOT, HALF_Q), 0)
    for head in range(2):
        base = jnp.zeros((8, SLOT), F32)
        for bucket in range(BUCKETS):
            base = jnp.where(buckets[...] == bucket, rows_of_bias[bucket, 2 * pair + head], base)
        for group in range(BLOCK // 8):
            bias[pl.ds(group * 8, 8), :] = pltpu.roll(base, 8 * group, 1) if group else base
        below = rows_of_bias[15, 2 * pair + head]
        above = rows_of_bias[31, 2 * pair + head]
        in_head = (row_in_pair >= HEAD * head) & (row_in_pair < HEAD * (head + 1))
        qt_head = jnp.where(in_head, qt, jnp.zeros_like(qt))
        for part in range(SLOT // HALF_Q):
            raw = dot(k_pair, qt_head[:, part * HALF_Q : (part + 1) * HALF_Q])
            rows = []
            for key_block in range(4):
                cells = []
                for sub in range(HALF_Q // BLOCK):
                    query_block = part * (HALF_Q // BLOCK) + sub
                    cell = raw[
                        key_block * BLOCK : (key_block + 1) * BLOCK,
                        sub * BLOCK : (sub + 1) * BLOCK,
                    ]
                    apart = key_block - query_block
                    if apart >= 2:
                        cell = cell + above
                    elif apart <= -2:
                        cell = cell + below
                    else:
                        lane = (-apart * BLOCK) % SLOT
                        cell = cell + bias[:, lane : lane + BLOCK]
                    cells.append(cell)
                rows.append(jnp.concatenate(cells, axis=1))
            scores = jnp.concatenate(rows, axis=0)
            scores = jnp.where(key_index < length, scores, BIG_NEGATIVE)
            top = jnp.max(scores, axis=0, keepdims=True)
            weights = jnp.exp(scores - top)
            inverse = 1.0 / jnp.sum(weights, axis=0, keepdims=True)
            low = weights.astype(BF16)
            columns = pl.ds(part * HALF_Q, HALF_Q)
            et[head, :, columns] = low
            linv[head, :, columns] = inverse
            mixed = dot(vt[head * HEAD : (head + 1) * HEAD, :], low) * inverse
            ot[pl.ds(head * HEAD, HEAD), columns] = mixed.astype(BF16)
    o[...] = ot[...].T


def attention(lens, qkv, rows_of_bias, first, count, held):
    pair = 2 * HEAD
    pairs = H // 2
    return pl.pallas_call(
        functools.partial(attention_kernel, first),
        grid=(count,),
        out_shape=(
            shape((H, SLOT, SLOT), BF16),
            shape((H, 1, SLOT), F32),
            shape((D, SLOT), BF16),
            shape((SLOT, D), BF16),
        ),
        in_specs=[
            SMEM,
            pl.BlockSpec((SLOT, pair), lambda i: (0, first + i)),
            pl.BlockSpec((SLOT, pair), lambda i: (0, pairs + first + i)),
            pl.BlockSpec((SLOT, pair), lambda i: (0, 2 * pairs + first + i)),
            SMEM,
            pl.BlockSpec((8, SLOT), lambda i: (0, 0)),
        ]
        + [ANY] * len(held),
        out_specs=(
            pl.BlockSpec((2, SLOT, SLOT), lambda i: (first + i, 0, 0)),
            pl.BlockSpec((2, 1, SLOT), lambda i: (first + i, 0, 0)),
            pl.BlockSpec((pair, SLOT), lambda i: (first + i, 0)),
            pl.BlockSpec((SLOT, pair), lambda i: (0, first + i)),
        ),
        input_output_aliases={6 + i: i for i in range(len(held))},
        scratch_shapes=[pltpu.VMEM((BLOCK, SLOT), F32)],
        compiler_params=params(wide=True),
        cost_estimate=COST,
        name="attention",
    )(lens, qkv, qkv, qkv, rows_of_bias, jnp.asarray(skew_buckets()), *held)


def feed_forward_kernel(lens, ffn_gain, final_gain, tok, mixed, cot, *refs):
    out_pieces, gated_pieces, down_pieces, refs = refs[:4], refs[4:16], refs[16:22], refs[22:]
    hidden_out, n2t_out, gate_out, up_out, embedded_out, after_out, fnt_out = refs[:7]
    send_out, keep_out = refs[7:9]
    w_out, w_gated, w_down, tok_v, mixed_v, cot_v, hidden, n2, n2t, inner, innert = refs[9:20]
    slope, level, embedded, after_grad, down_in, fnt, send, keep = refs[20:28]
    out_sems, gated_sems, down_sems, in_sems, done_sems = refs[28:]
    load, store = Copies(in_sems), Copies(done_sems)

    loads = begin(pieces_of(SHARD, OUT_PLAN, out_pieces, w_out, out_sems))
    loads += [load(mixed, mixed_v), load(tok, tok_v), load(cot, cot_v)]
    gated_loads = [
        begin(pieces_of(SHARD, plan, gated_pieces, w_gated, gated_sems, 12 * number))
        for number, plan in enumerate(GATED_PLANS)
    ]
    down_loads = begin(pieces_of(FF // SEQ, DOWN_PLAN, down_pieces, w_down, down_sems))
    stores = []

    finish(loads)
    scale = ffn_gain[...].reshape(1, D)
    for block in range(2):
        rows = pl.ds(block * 256, 256)
        values = tok_v[rows, :].astype(F32) + dot(mixed_v[rows, :], w_out[:, 0:D])
        hidden[rows, :] = values
        normed = (values * inverse_rms(values) * scale).astype(BF16)
        n2[rows, :] = normed
        n2t[:, rows] = normed.T
    stores.append(store(hidden, hidden_out))
    size, starts = relative_starts(D)
    for number, begin_row in enumerate(starts):
        stores.append(
            store(n2t.at[pl.ds(begin_row, size), :], n2t_out.at[pl.ds(number * size, size), :])
        )

    me, y = place()
    z = lax.rem(lax.axis_index("dp") // 2, 2)

    def step(tile, carry):
        columns = pl.ds(pl.multiple_of(tile * 512, 512), 512)
        g = dot(n2[...], w_gated[:, columns])
        u = dot(n2[...], w_gated[:, pl.ds(pl.multiple_of(FF + tile * 512, 512), 512)])
        square = g * g
        t = jnp.tanh(GELU_A * g * (1.0 + GELU_B * square))
        half_up = 0.5 * (1.0 + t)
        activated = g * half_up
        derivative = half_up + 0.5 * g * (1.0 - t * t) * (GELU_A * (1.0 + 3 * GELU_B * square))
        value = (activated * u).astype(BF16)
        inner[:, columns] = value
        slope[:, columns] = (derivative * u).astype(BF16)
        level[:, columns] = activated.astype(BF16)
        core_own = (lax.rem(tile, 2) == lax.rem(me, 2)).astype(jnp.int32)
        x_own = (tile // 2 == me // 2).astype(jnp.int32)
        target = (core_own * 2 + x_own) * 512
        turned = value.T
        for number in range(4):
            y_own = (number >> 1 == y).astype(jnp.int32)
            z_own = ((number & 1) == z).astype(jnp.int32)
            row = pl.multiple_of(target + y_own * 256 + z_own * BLOCK, BLOCK)
            innert[pl.ds(row, BLOCK), :] = turned[number * BLOCK : (number + 1) * BLOCK, :]
        return carry

    for part in range(2):
        finish(gated_loads[part])
        lax.fori_loop(2 * part, 2 * part + 2, step, 0)

    finish(down_loads)
    scale = final_gain[...].reshape(1, D)
    for block in range(2):
        rows = pl.ds(block * 256, 256)
        values = hidden[rows, :] + dot(inner[rows, :], w_down[...])
        normed = (values * inverse_rms(values) * scale).astype(BF16)
        fnt[:, rows] = normed.T
        embedded[rows, :] = dot(normed, w_out[:, D:WIDE]).astype(BF16)
        gradient = norm_backward(values, scale, dot_t(cot_v[rows, :], w_out[:, D:WIDE]))
        after_grad[rows, :] = gradient
        down_in[rows, :] = gradient.astype(BF16)
    for source, target in ((after_grad, after_out), (embedded, embedded_out), (fnt, fnt_out)):
        stores.append(store(source, target))

    for number, (part, target) in enumerate(((send, send_out), (keep, keep_out))):

        def grad(tile, carry):
            rows = pl.ds(pl.multiple_of(tile * 256, 256), 256)
            source = pl.ds(pl.multiple_of(number * (FF // 2) + tile * 256, 256), 256)
            part[rows, :] = dot(innert[source, :], down_in[...]).astype(BF16)
            return carry

        lax.fori_loop(0, FF // 2 // 256, grad, 0)
        stores.append(store(part, target))

    def back(tile, carry):
        columns = pl.ds(pl.multiple_of(tile * 512, 512), 512)
        incoming = dot_t(down_in[...], w_down[columns, :])
        slope[:, columns] = (incoming * slope[:, columns].astype(F32)).astype(BF16)
        level[:, columns] = (incoming * level[:, columns].astype(F32)).astype(BF16)
        return carry

    lax.fori_loop(0, FF // 512, back, 0)
    stores += [store(slope, gate_out), store(level, up_out)]
    finish(stores)


def feed_forward(lens, tok, mixed, cot, ffn_gain, final_gain, out_pieces, gated_pieces, down_pieces):
    wide, tall, full = (SLOT, D), (D, SLOT), (SLOT, FF)
    pieces = tuple(out_pieces) + tuple(gated_pieces) + tuple(down_pieces)
    return pl.pallas_call(
        feed_forward_kernel,
        out_shape=(
            shape(wide, F32),
            shape(tall, BF16),
            shape(full, BF16),
            shape(full, BF16),
            shape((SLOT, PROJ), BF16),
            shape(wide, F32),
            shape(tall, BF16),
            shape((FF // 2, D), BF16),
            shape((FF // 2, D), BF16),
        ),
        in_specs=[SMEM, VMEM, VMEM] + [ANY] * (3 + len(pieces)),
        out_specs=(ANY,) * 9,
        scratch_shapes=[
            pltpu.VMEM((D, WIDE), BF16),
            pltpu.VMEM((D, 2 * FF), BF16),
            pltpu.VMEM((FF, D), BF16),
            pltpu.VMEM(wide, BF16),
            pltpu.VMEM(wide, BF16),
            pltpu.VMEM((SLOT, PROJ), BF16),
            pltpu.VMEM(wide, F32),
            pltpu.VMEM(wide, BF16),
            pltpu.VMEM(tall, BF16),
            pltpu.VMEM(full, BF16),
            pltpu.VMEM((FF, SLOT), BF16),
            pltpu.VMEM(full, BF16),
            pltpu.VMEM(full, BF16),
            pltpu.VMEM((SLOT, PROJ), BF16),
            pltpu.VMEM(wide, F32),
            pltpu.VMEM(wide, BF16),
            pltpu.VMEM(tall, BF16),
            pltpu.VMEM((FF // 2, D), BF16),
            pltpu.VMEM((FF // 2, D), BF16),
            pltpu.SemaphoreType.DMA((4,)),
            pltpu.SemaphoreType.DMA((24,)),
            pltpu.SemaphoreType.DMA((6,)),
            pltpu.SemaphoreType.DMA((3,)),
            pltpu.SemaphoreType.DMA((24,)),
        ],
        compiler_params=params(wide=True),
        cost_estimate=COST,
        name="feed_forward",
    )(lens, ffn_gain, final_gain, tok, mixed, cot, *pieces)


def row_grads(left, right, halves, column=0, loads=(), store=None, outs=()):
    half = left.shape[0] // 2
    width = right.shape[1]
    size = 1024 if width % 1024 == 0 else width
    stores = []
    for tile in range(width // size):
        if loads:
            loads[tile].wait()
        target = slice(column + tile * size, column + (tile + 1) * size)
        both = dot(left[...], right[:, tile * size : (tile + 1) * size]).astype(BF16)
        for number, part in enumerate(halves):
            part[:, target] = both[number * half : (number + 1) * half, :]
            stores.append(store(part.at[:, target], outs[number].at[:, target]))
    return stores


def tile_loads(load, source, target, size=1024):
    return [
        load(source.at[:, pl.ds(begin_at, size)], target.at[:, pl.ds(begin_at, size)])
        for begin_at in range(0, source.shape[1], size)
    ]


def gate_grad_kernel(lens, n2t, gate_grad, send_out, keep_out, n2t_v, gate_v, send, keep, *sems):
    load, store = Copies(sems[0]), Copies(sems[1])
    first = load(n2t, n2t_v)
    loads = tile_loads(load, gate_grad, gate_v)
    first.wait()
    finish(row_grads(n2t_v, gate_v, (send, keep), 0, loads, store, (send_out, keep_out)))


def gate_grads(lens, n2t, gate_grad):
    part = (D // 2, FF)
    return pl.pallas_call(
        gate_grad_kernel,
        out_shape=(shape(part, BF16),) * 2,
        in_specs=[SMEM] + [ANY] * 2,
        out_specs=(ANY,) * 2,
        scratch_shapes=[
            pltpu.VMEM((D, SLOT), BF16),
            pltpu.VMEM((SLOT, FF), BF16),
            pltpu.VMEM(part, BF16),
            pltpu.VMEM(part, BF16),
            pltpu.SemaphoreType.DMA((3,)),
            pltpu.SemaphoreType.DMA((4,)),
        ],
        compiler_params=params(wide=True),
        cost_estimate=COST,
        name="gate_grads",
    )(lens, n2t, gate_grad)


def up_grad_kernel(lens, gain, n2t, gate_grad, up_grad, hidden, after_grad, *refs):
    pieces, outs, refs = refs[:12], refs[12:16], refs[16:]
    weight, n2t_v, gate_v, up_v, hidden_v, after_v, send, keep, grad, attn_in = refs[:10]
    sems, in_sems, done_sems = refs[10:]
    load, store = Copies(in_sems), Copies(done_sems)
    first = load(n2t, n2t_v)
    loads = tile_loads(load, up_grad, up_v)
    gate_load = load(gate_grad, gate_v)
    plan = sum(GATED_PLANS, ())
    gate_plan = tuple(entry for entry in plan if entry[3] < FF)
    up_plan = tuple(entry for entry in plan if entry[3] >= FF)
    gate_pieces = begin(pieces_of(SHARD, gate_plan, pieces, weight, sems))
    up_pieces = begin(pieces_of(SHARD, up_plan, pieces, weight, sems, len(gate_plan)))
    later = [load(hidden, hidden_v), load(after_grad, after_v)]
    first.wait()
    stores = row_grads(n2t_v, up_v, (send, keep), 0, loads, store, outs[0:2])
    gate_load.wait()
    finish(gate_pieces)
    for block in range(2):
        rows = pl.ds(block * 256, 256)
        grad[rows, :] = dot_t(gate_v[rows, :], weight[:, 0:FF])
    finish(up_pieces)
    finish(later)
    scale = gain[...].reshape(1, D)
    for block in range(2):
        rows = pl.ds(block * 256, 256)
        incoming = grad[rows, :] + dot_t(up_v[rows, :], weight[:, FF:])
        gradient = norm_backward(hidden_v[rows, :], scale, incoming) + after_v[rows, :]
        grad[rows, :] = gradient
        attn_in[rows, :] = gradient.astype(BF16)
    stores += [store(attn_in, outs[3]), store(grad, outs[2])]
    finish(stores)


def up_grads(lens, gain, n2t, gate_grad, up_grad, hidden, after_grad, pieces):
    full, part, wide = (SLOT, FF), (D // 2, FF), (SLOT, D)
    return pl.pallas_call(
        up_grad_kernel,
        out_shape=(shape(part, BF16),) * 2 + (shape(wide, F32), shape(wide, BF16)),
        in_specs=[SMEM, VMEM] + [ANY] * 17,
        out_specs=(ANY,) * 4,
        scratch_shapes=[
            pltpu.VMEM((D, 2 * FF), BF16),
            pltpu.VMEM((D, SLOT), BF16),
            pltpu.VMEM(full, BF16),
            pltpu.VMEM(full, BF16),
            pltpu.VMEM(wide, F32),
            pltpu.VMEM(wide, F32),
            pltpu.VMEM(part, BF16),
            pltpu.VMEM(part, BF16),
            pltpu.VMEM(wide, F32),
            pltpu.VMEM(wide, BF16),
            pltpu.SemaphoreType.DMA((24,)),
            pltpu.SemaphoreType.DMA((6,)),
            pltpu.SemaphoreType.DMA((6,)),
        ],
        compiler_params=params(wide=True),
        cost_estimate=COST,
        name="up_grads",
    )(lens, gain, n2t, gate_grad, up_grad, hidden, after_grad, *pieces)


def out_grad_kernel(lens, ot, fnt, attn_in, cot, *refs):
    pieces, outs, refs = refs[:4], refs[4:7], refs[7:]
    weight, left, proj_left, attn_v, cot_v, send, keep, mixed = refs[:8]
    sems, left_sems, proj_sems, in_sems, done_sems = refs[8:]
    load, store = Copies(in_sems), Copies(done_sems)
    loads = [load(attn_in, attn_v)]
    loads += begin(relative_copies(ot, left, left_sems))
    pieces = begin(pieces_of(SHARD, OUT_PLAN, pieces, weight, sems))
    later = [load(cot, cot_v)]
    later += begin(relative_copies(fnt, proj_left, proj_sems))
    finish(loads)
    stores = row_grads(left, attn_v, (send, keep), 0, (), store, outs[0:2])
    finish(later)
    stores += row_grads(proj_left, cot_v, (send, keep), D, (), store, outs[0:2])
    finish(pieces)
    mixed[...] = dot_t(attn_v[...], weight[:, 0:D]).astype(BF16)
    stores.append(store(mixed, outs[2]))
    finish(stores)


def out_grads(lens, ot, fnt, attn_in, cot, pieces):
    return pl.pallas_call(
        out_grad_kernel,
        out_shape=(shape((D // 2, WIDE), BF16),) * 2 + (shape((SLOT, D), BF16),),
        in_specs=[SMEM] + [ANY] * 8,
        out_specs=(ANY,) * 3,
        scratch_shapes=[
            pltpu.VMEM((D, WIDE), BF16),
            pltpu.VMEM((D, SLOT), BF16),
            pltpu.VMEM((D, SLOT), BF16),
            pltpu.VMEM((SLOT, D), BF16),
            pltpu.VMEM((SLOT, PROJ), BF16),
            pltpu.VMEM((D // 2, WIDE), BF16),
            pltpu.VMEM((D // 2, WIDE), BF16),
            pltpu.VMEM((SLOT, D), BF16),
            pltpu.SemaphoreType.DMA((4,)),
            pltpu.SemaphoreType.DMA((16,)),
            pltpu.SemaphoreType.DMA((16,)),
            pltpu.SemaphoreType.DMA((2,)),
            pltpu.SemaphoreType.DMA((5,)),
        ],
        compiler_params=params(wide=True),
        cost_estimate=COST,
        name="out_grads",
    )(lens, ot, fnt, attn_in, cot, *pieces)


def qkv_grad_kernel(lens, table, indicator, n1t, dq, dk, dv, *refs):
    outs, left, dq_v, dk_v, dv_v = refs[:4], refs[4], refs[5], refs[6], refs[7]
    send, keep, value_send, value_keep, small, left_sems, in_sems, done_sems = refs[8:]
    load, store = Copies(in_sems), Copies(done_sems)
    first = [load(dq, dq_v)] + begin(relative_copies(n1t, left, left_sems))
    second, third = load(dk, dk_v), load(dv, dv_v)
    finish(first)
    stores = row_grads(left, dq_v, (send, keep), 0, (), store, outs[0:2])
    stores += row_grads(left, dk_v, (send, keep), D, (second,), store, outs[0:2])
    by_lane = jnp.concatenate([table[pair] for pair in range(H // 2)], axis=0)
    high = by_lane.astype(BF16)
    low = (by_lane - high.astype(F32)).astype(BF16)
    by_bucket = dot(high, indicator[...]) + dot(low, indicator[...])
    small[...] = jnp.concatenate([by_bucket, jnp.zeros((PROJ - H, D), F32)], axis=0).T
    block, starts = relative_starts(D)
    for number, row in enumerate(starts):
        target = value_keep if number >= 8 else value_send
        target[pl.ds((number & 7) * block, block), D:WIDE] = small[pl.ds(row, block), :].astype(
            BF16
        )
    columns = pl.ds(D, PROJ)
    for number, part in enumerate((value_send, value_keep)):
        stores.append(store(part.at[:, columns], outs[2 + number].at[:, columns]))
    stores += row_grads(left, dv_v, (value_send, value_keep), 0, (third,), store, outs[2:4])
    finish(stores)


def qkv_grads(lens, table, n1t, dq, dk, dv):
    pair, single = (D // 2, 2 * D), (D // 2, WIDE)
    return pl.pallas_call(
        qkv_grad_kernel,
        out_shape=(shape(pair, BF16),) * 2 + (shape(single, BF16),) * 2,
        in_specs=[SMEM, VMEM, VMEM] + [ANY] * 4,
        out_specs=(ANY,) * 4,
        scratch_shapes=[pltpu.VMEM((D, SLOT), BF16)]
        + [pltpu.VMEM((SLOT, D), BF16)] * 3
        + [pltpu.VMEM(pair, BF16)] * 2
        + [pltpu.VMEM(single, BF16)] * 2
        + [
            pltpu.VMEM((D, PROJ), F32),
            pltpu.SemaphoreType.DMA((16,)),
            pltpu.SemaphoreType.DMA((3,)),
            pltpu.SemaphoreType.DMA((8,)),
        ],
        compiler_params=params(wide=True),
        cost_estimate=COST,
        name="qkv_grads",
    )(lens, table, jnp.asarray(table_indicator(), dtype=BF16), n1t, dq, dk, dv)


def attention_back_kernel(lens, q, k, v, et, linv, ot, do, *refs):
    dq, dk, dv, bias_grad, dqt, near = refs[-6:]
    lane_in_pair = lax.broadcasted_iota(jnp.int32, (SLOT, 2 * HEAD), 1)
    q_pair, v_pair = q[...], v[...]
    kt = k[...].T
    out_gradt = do[...].astype(F32).T
    scaled = []
    deltas = []
    for head in range(2):
        rows = slice(head * HEAD, (head + 1) * HEAD)
        low = (out_gradt[rows, :] * linv[head]).astype(BF16)
        scaled.append(low)
        deltas.append(
            jnp.sum(low.astype(F32) * ot[rows, :].astype(F32), axis=0, keepdims=True)
        )
    scaled_pair = jnp.concatenate(scaled, axis=0).T
    zeros = jnp.zeros((HEAD, SLOT), BF16)
    key_total = jnp.zeros((SLOT, 2 * HEAD), F32)
    value_total = jnp.zeros((SLOT, 2 * HEAD), F32)
    row_of_eight = lax.broadcasted_iota(jnp.int32, (8, SLOT), 0)
    for head in range(2):
        in_head = (lane_in_pair >= head * HEAD) & (lane_in_pair < (head + 1) * HEAD)
        q_head = jnp.where(in_head, q_pair, jnp.zeros_like(q_pair))
        do_head = jnp.where(in_head, scaled_pair, jnp.zeros_like(scaled_pair))
        dot_head = jnp.concatenate(
            [scaled[head], zeros] if head == 0 else [zeros, scaled[head]], axis=0
        )
        near_sums = {-1: None, 0: None, 1: None}
        far_sums = {-1: None, 1: None}
        for part in range(SLOT // HALF_Q):
            columns = slice(part * HALF_Q, (part + 1) * HALF_Q)
            prob_grad = dot(v_pair, dot_head[:, columns])
            low_weights = et[head, :, columns]
            score_grad = low_weights.astype(F32) * (prob_grad - deltas[head][:, columns])
            low = score_grad.astype(BF16)
            key_total = key_total + dot(low, q_head[columns, :])
            value_total = value_total + dot(low_weights, do_head[columns, :])
            dqt[pl.ds(head * HEAD, HEAD), columns] = dot(
                kt[head * HEAD : (head + 1) * HEAD, :], low
            ).astype(BF16)
            for key_block in range(4):
                for sub in range(HALF_Q // BLOCK):
                    apart = key_block - part * (HALF_Q // BLOCK) - sub
                    cell = score_grad[
                        key_block * BLOCK : (key_block + 1) * BLOCK,
                        sub * BLOCK : (sub + 1) * BLOCK,
                    ]
                    if abs(apart) >= 2:
                        side = 1 if apart > 0 else -1
                        folded = jnp.sum(cell.reshape(BLOCK // 8, 8, BLOCK), axis=0)
                        old = far_sums[side]
                        far_sums[side] = folded if old is None else old + folded
                    else:
                        old = near_sums[apart]
                        near_sums[apart] = cell if old is None else old + cell
        near[...] = jnp.zeros_like(near)
        for apart in (-1, 0, 1):
            lane = (-apart * BLOCK) % SLOT
            near[:, lane : lane + BLOCK] = near_sums[apart]
        folded = near[0:8, :]
        for group in range(1, BLOCK // 8):
            folded = folded + pltpu.roll(near[group * 8 : group * 8 + 8, :], SLOT - 8 * group, 1)
        for bit in (1, 2, 4):
            folded = jnp.where(
                (row_of_eight & bit) != 0, pltpu.roll(folded, SLOT - bit, 1), folded
            )
        here = slice(head, head + 1)
        bias_grad[0, here, 0:SLOT] = jnp.sum(folded, axis=0, keepdims=True)
        for number, side in enumerate((-1, 1)):
            lane = SLOT + number * BLOCK
            bias_grad[0, here, lane : lane + BLOCK] = jnp.sum(
                far_sums[side], axis=0, keepdims=True
            )
    dk[...] = key_total.astype(BF16)
    dv[...] = value_total.astype(BF16)
    dq[...] = dqt[...].T


def attention_back(lens, qkv, et, linv, ot, do, first, count, held):
    pair = 2 * HEAD
    pairs = H // 2
    wide = pl.BlockSpec((SLOT, pair), lambda i: (0, first + i))
    return pl.pallas_call(
        attention_back_kernel,
        grid=(count,),
        out_shape=(shape((SLOT, D), BF16),) * 3 + (shape((pairs, 2, D), F32),),
        in_specs=[
            SMEM,
            wide,
            pl.BlockSpec((SLOT, pair), lambda i: (0, pairs + first + i)),
            pl.BlockSpec((SLOT, pair), lambda i: (0, 2 * pairs + first + i)),
            pl.BlockSpec((2, SLOT, SLOT), lambda i: (first + i, 0, 0)),
            pl.BlockSpec((2, 1, SLOT), lambda i: (first + i, 0, 0)),
            pl.BlockSpec((pair, SLOT), lambda i: (first + i, 0)),
            wide,
        ]
        + [ANY] * len(held),
        out_specs=(wide,) * 3 + (pl.BlockSpec((1, 2, D), lambda i: (first + i, 0, 0)),),
        input_output_aliases={8 + i: i for i in range(len(held))},
        scratch_shapes=[pltpu.VMEM((pair, SLOT), BF16), pltpu.VMEM((BLOCK, SLOT), F32)],
        compiler_params=params(wide=True),
        cost_estimate=COST,
        name="attention_back",
    )(lens, qkv, qkv, qkv, et, linv, ot, do, *held)


def token_grad_kernel(lens, gain, embedded, dq, dk, dv, hidden_grad, tok, *refs):
    pieces, outs, refs = refs[:8], refs[8:12], refs[12:]
    weight, embedded_v, dq_v, dk_v, dv_v, hidden_v, tok_v, total = refs[:8]
    packed, (sems, in_sems, done_sems) = refs[8:12], refs[12:]
    load, store = Copies(in_sems), Copies(done_sems)
    me, _ = place()
    loads = []
    for number, (source, target) in enumerate(((dq, dq_v), (dk, dk_v), (dv, dv_v))):
        plan = QKV_PLANS[number]
        loads.append(
            [load(source, target)]
            + begin(pieces_of(SHARD, plan, pieces, weight, sems, 6 * number))
        )
    later = [load(hidden_grad, hidden_v), load(tok, tok_v), load(embedded, embedded_v)]
    for number, source in enumerate((dq_v, dk_v, dv_v)):
        finish(loads[number])
        for block in range(2):
            rows = pl.ds(block * 256, 256)
            term = dot_t(source[rows, :], weight[:, number * D : (number + 1) * D])
            total[rows, :] = term if number == 0 else total[rows, :] + term
    finish(later)
    scale = gain[...].reshape(1, D)
    stores = []
    for flip, target in enumerate(packed):
        rows = pl.ds(pl.multiple_of((me ^ flip) * BLOCK, BLOCK), BLOCK)
        gradient = norm_backward(tok_v[rows, :].astype(F32), scale, total[rows, :])
        target[:, 0:D] = (hidden_v[rows, :] + gradient).astype(BF16)
        target[:, D:WIDE] = embedded_v[rows, :]
        stores.append(store(target, outs[flip]))
    finish(stores)


def token_grads(lens, gain, embedded, dq, dk, dv, hidden_grad, tok, pieces):
    wide = (SLOT, D)
    return pl.pallas_call(
        token_grad_kernel,
        out_shape=(shape((BLOCK, WIDE), BF16),) * 4,
        in_specs=[SMEM, VMEM] + [ANY] * 14,
        out_specs=(ANY,) * 4,
        scratch_shapes=[
            pltpu.VMEM((D, 3 * D), BF16),
            pltpu.VMEM((SLOT, PROJ), BF16),
            pltpu.VMEM(wide, BF16),
            pltpu.VMEM(wide, BF16),
            pltpu.VMEM(wide, BF16),
            pltpu.VMEM(wide, F32),
            pltpu.VMEM(wide, BF16),
            pltpu.VMEM(wide, F32),
        ]
        + [pltpu.VMEM((BLOCK, WIDE), BF16)] * 4
        + [
            pltpu.SemaphoreType.DMA((18,)),
            pltpu.SemaphoreType.DMA((6,)),
            pltpu.SemaphoreType.DMA((4,)),
        ],
        compiler_params=params(wide=True),
        cost_estimate=COST,
        name="token_grads",
    )(lens, gain, embedded, dq, dk, dv, hidden_grad, tok, *pieces)


def unpack_kernel(block_0, block_1, block_2, block_3, embedded, tokens_grad):
    me, _ = place()
    for flip, block in enumerate((block_0, block_1, block_2, block_3)):
        tokens_grad[me ^ flip] = block[:, 0:D].astype(F32)
        embedded[me ^ flip] = block[:, D:WIDE]


def unpack(blocks):
    return pl.pallas_call(
        unpack_kernel,
        out_shape=(shape((SEQ, BLOCK, PROJ), BF16), shape((SEQ, BLOCK, D), F32)),
        in_specs=[VMEM] * 4,
        out_specs=(VMEM,) * 2,
        compiler_params=params(),
        cost_estimate=SMALL_COST,
        name="unpack",
    )(*blocks)


def exchange(value, axis, flip, size):
    return lax.ppermute(value, axis, [(i, i ^ flip) for i in range(size)])


def after(value, *others):
    return lax.optimization_barrier((value,) + others)[0]


def add(*terms):
    total = terms[0].astype(F32)
    for term in terms[1:]:
        total = total + term.astype(F32)
    return total.astype(BF16)


def marker_kernel(tick, mark):
    pass


def marker(tick):
    return pl.pallas_call(
        marker_kernel,
        out_shape=shape((8, 128), F32),
        in_specs=[ANY],
        out_specs=ANY,
        compiler_params=params(),
        cost_estimate=COST,
        name="marker",
    )(tick)


class Chunk:
    def __init__(self, groups, pair, thin=False):
        self.groups, self.thin = groups, thin
        self.send, self.keep = pair
        self.rows = self.send.shape[0] // 4

    def along(self, flip, value):
        return exchange(value, "dp", flip, self.groups)

    def core(self, tick):
        self.send = after(self.send, tick)
        self.from_core = exchange(self.send, "seq", 1, SEQ)

    def x(self, tick):
        both = 2 * self.rows
        self.from_core = after(self.from_core, tick)
        mine = add(self.keep[:both], self.from_core[:both])
        self.from_x = exchange(mine, "seq", 2, SEQ)

    def first(self, tick):
        rows = self.rows
        self.from_x = after(self.from_x, tick)
        mine = add(
            self.keep[2 * rows : 3 * rows], self.from_core[2 * rows : 3 * rows], self.from_x[:rows]
        )
        self.from_first = self.along(1, mine)

    def _summed(self, begin, end):
        rows = self.rows
        return add(
            self.keep[3 * rows + begin : 3 * rows + end],
            self.from_core[3 * rows + begin : 3 * rows + end],
            self.from_x[rows + begin : rows + end],
            self.from_first[begin:end],
        )

    def second(self, tick):
        self.from_first = after(self.from_first, tick)
        self.total = self._summed(0, self.rows if self.thin else self.rows // 2)
        self.from_second = self.along(2, self.total)

    def rest(self, tick):
        self.from_second = after(self.from_second, tick)
        if not self.thin:
            self.total = self._summed(self.rows // 2, self.rows)
        self.total = add(self.total, self.from_second)
        step = 4
        while step < self.groups:
            if step > 4:
                self.total = add(self.total, self.from_rest)
            self.from_rest = self.along(step, self.total)
            step *= 2

    def back_second(self, tick):
        self.from_rest = after(self.from_rest, tick)
        self.total = add(self.total, self.from_rest)
        self.other_second = self.along(2, self.total)

    def back_first(self, tick):
        if self.thin:
            self.from_rest = after(self.from_rest, tick)
            self.total = add(self.total, self.from_rest)
        else:
            self.other_second = after(self.other_second, tick)
            self.total = jnp.concatenate([self.other_second, self.total], axis=0)
        self.other = self.along(1, self.total)


def join_kernel(*refs):
    terms, out = refs[:-1], refs[-1]
    column = 0
    for left, right in zip(terms[0::2], terms[1::2]):
        width = left.shape[1]
        out[:, column : column + width] = (
            left[...].astype(F32) + right[...].astype(F32)
        ).astype(BF16)
        column += width


class Group:
    thin = False

    def __init__(self, *chunks):
        self.chunks, self.rows, self.along = chunks, chunks[0].rows, chunks[0].along

    def back_second(self, tick):
        terms = []
        for chunk in self.chunks:
            terms += [chunk.total, after(chunk.from_rest, tick)]
        width = sum(chunk.total.shape[1] for chunk in self.chunks)
        self.total = pl.pallas_call(
            join_kernel,
            out_shape=shape((self.rows // 2, width), BF16),
            in_specs=[VMEM] * len(terms),
            out_specs=VMEM,
            compiler_params=params(),
            cost_estimate=SMALL_COST,
            name="join",
        )(*terms)
        self.other_second = self.along(2, self.total)

    def back_first(self, tick):
        self.other_second = after(self.other_second, tick)
        self.total = jnp.concatenate([self.other_second, self.total], axis=0)
        self.other = self.along(1, self.total)


def assemble_kernel(rows, widths, marks, counts, table, natural, total, other, *refs):
    weights, refs = refs[: counts[0]], refs[counts[0] :]
    gains, outs = refs[: counts[1]], refs[counts[1] :]
    me, y = place()
    z = lax.rem(lax.axis_index("dp") // 2, 2)
    half = rows // 2
    column = 0
    sums = [None] * counts[1]

    def blocks():
        for source, first in ((total, 1), (other, 0)):
            for second in range(2):
                y_of = y if first else 1 - y
                z_of = second if natural else (z if second else 1 - z)
                yield source, second * half, y_of, z_of

    for number, width in enumerate(widths):
        columns = slice(column, column + width)
        out = outs[number]
        for source, row, y_of, z_of in blocks():
            begin_row = pl.multiple_of(y_of * rows + z_of * half, 16)
            out[pl.ds(begin_row, half), :] = source[row : row + half, columns].astype(F32)
        column += width
        for which, weight, target in marks:
            if which == number:
                part = jnp.sum(
                    weights[weight][...].astype(F32) * out[...], axis=1, keepdims=True
                )
                sums[target] = part if sums[target] is None else sums[target] + part
    for number, (summed, gain) in enumerate(zip(sums, gains)):
        total_rows = jnp.broadcast_to(summed, (2 * rows, BLOCK)).T[0:1, :]
        whole = gain[...].reshape(1, D)
        mine = whole[:, 0:SHARD]
        for shard in range(1, SEQ):
            mine = jnp.where(me == shard, whole[:, shard * SHARD : (shard + 1) * SHARD], mine)
        outs[len(widths) + number][...] = (total_rows / mine).reshape(2 * rows)
    if table:
        for source, row, y_of, z_of in blocks():
            if natural and z_of:
                continue

            @pl.when((y_of == 0) if natural else (y_of == 0) & (z_of == 0))
            def store():
                outs[-1][...] = source[
                    row : row + BUCKETS // SEQ, column : column + H
                ].astype(F32)


def assemble(chunk, widths, marks=(), weights=(), gains=(), table=False):
    rows = chunk.rows
    out_shape = [shape((2 * rows, width), F32) for width in widths]
    out_shape += [shape((2 * rows,), F32) for _ in gains]
    if table:
        out_shape.append(shape((BUCKETS // SEQ, H), F32))
    operands = tuple(weights) + tuple(gains)
    return pl.pallas_call(
        functools.partial(
            assemble_kernel,
            rows,
            widths,
            marks,
            (len(weights), len(gains)),
            table,
            chunk.thin,
        ),
        out_shape=tuple(out_shape),
        in_specs=[VMEM] * (2 + len(operands)),
        out_specs=(VMEM,) * len(out_shape),
        compiler_params=params(),
        cost_estimate=SMALL_COST,
        name="assemble",
    )(chunk.total, chunk.other, *operands)


def per_device(
    groups,
    tokens,
    doc_lengths,
    query_weight,
    key_weight,
    value_weight,
    out_weight,
    gate_weight,
    up_weight,
    down_weight,
    proj_weight,
    attn_gain,
    ffn_gain,
    final_gain,
    bucket_bias_rows,
    embed_cotangent,
):
    tick = doc_lengths

    def across_x(mine):
        return exchange(after(mine, tick), "seq", 2, SEQ)

    def across_y(mine):
        return exchange(after(mine, tick), "dp", 1, groups)

    def across_core(mine):
        return exchange(after(mine, tick), "seq", 1, SEQ)

    def across_far(mine):
        return exchange(after(mine, tick), "seq", 3, SEQ)

    qkv_half = pack_first(tick, query_weight, key_weight, value_weight)
    qkv_x = across_x(qkv_half)
    tick = after(tick, qkv_half)
    blocks = pack_tokens(tick, tokens, embed_cotangent)
    block_x = across_x(blocks[2])
    block_far = across_far(blocks[3])
    block_core = across_core(blocks[1])
    tick = after(tick, blocks[0])
    qkv_own, out_own, gated_half_0, gated_half_1, down_rest = pack_rest(
        tick,
        query_weight,
        key_weight,
        value_weight,
        out_weight,
        proj_weight,
        gate_weight,
        up_weight,
        down_weight,
    )
    tick = after(tick, qkv_x, gated_half_0)
    qkv_y = across_y(qkv_x)
    qkv_cx = across_core(qkv_x)
    tick = after(tick, block_x, block_far, block_core)
    qkv_core = across_core(qkv_own)
    out_x = across_x(out_own)
    tok, cot, n1, n1t = first_norm(tick, (blocks[0], block_core, block_x, block_far), attn_gain)
    tick = after(tick, n1, qkv_y, qkv_cx)
    qkv_cy = across_core(qkv_y)
    tick = after(tick, qkv_cy, qkv_core, out_x)
    out_core = across_core(out_own)
    gated_x_0 = across_x(gated_half_0)
    gated_x_1 = across_x(gated_half_1)
    gate_core = across_core(gate_weight)
    qkv_pieces = (
        query_weight, key_weight, value_weight, qkv_core, qkv_x, qkv_y, qkv_cx, qkv_cy
    )
    qkv = qkv_project(tick, n1, qkv_pieces)
    pairs = H // 2
    third = pairs // 3
    tick = after(tick, qkv, gated_x_0, out_core, gate_core)
    gated_y_0 = across_y(gated_x_0)
    gated_cx_0 = across_core(gated_x_0)
    out_cx = across_core(out_x)
    down_x = across_x(down_rest)
    held = attention(tick, qkv, bucket_bias_rows, 0, third, ())
    tick = after(tick, held[0], gated_x_1, gated_cx_0, out_cx)
    gated_y_1 = across_y(gated_x_1)
    gated_cx_1 = across_core(gated_x_1)
    up_core = across_core(up_weight)
    held = attention(tick, qkv, bucket_bias_rows, third, third, held)
    tick = after(tick, held[0], gated_y_0, gated_cx_1, up_core)
    gated_cy_0 = across_core(gated_y_0)
    down_core = across_core(down_weight)
    et, linv, ot, mixed = attention(
        tick, qkv, bucket_bias_rows, 2 * third, pairs - 2 * third, held
    )
    tick = after(tick, mixed, gated_y_1, gated_cy_0, down_core)
    gated_cy_1 = across_core(gated_y_1)
    tick = after(tick, down_x)
    down_cx = across_core(down_x)
    tick = after(tick, gated_cy_1, down_cx)
    out_pieces = (out_own, out_core, out_x, out_cx)
    down_pieces = (down_weight, down_core, out_x, down_x, out_cx, down_cx)
    gated_pieces = (
        gate_weight, up_weight, gate_core, up_core,
        gated_x_0, gated_y_0, gated_cx_0, gated_cy_0,
        gated_x_1, gated_y_1, gated_cx_1, gated_cy_1,
    )
    hidden, n2t, gate_grad, up_grad, embedded, after_grad, fnt, *pair = feed_forward(
        tick, tok, mixed, cot, ffn_gain, final_gain, out_pieces, gated_pieces, down_pieces
    )

    chunk = functools.partial(Chunk, groups)
    down_sum = chunk(pair)
    tick = after(tick, down_sum.keep)
    down_sum.core(tick)
    gate_sum = chunk(gate_grads(tick, n2t, gate_grad))
    tick = after(tick, gate_sum.keep, down_sum.from_core)
    down_sum.x(tick)
    gate_sum.core(tick)
    *pair, hidden_grad, attn_in = up_grads(
        tick, ffn_gain, n2t, gate_grad, up_grad, hidden, after_grad, gated_pieces
    )
    up_sum = chunk(pair)
    tick = after(tick, up_sum.keep, gate_sum.from_core)
    gate_sum.x(tick)
    up_sum.core(tick)
    *pair, mixed_grad = out_grads(tick, ot, fnt, attn_in, cot, out_pieces)
    out_sum = chunk(pair)
    tick = after(tick, out_sum.keep, up_sum.from_core, down_sum.from_x)
    down_sum.first(tick)
    up_sum.x(tick)
    out_sum.core(tick)
    held = attention_back(tick, qkv, et, linv, ot, mixed_grad, 0, pairs // 2, ())
    tick = after(tick, held[0], out_sum.from_core, down_sum.from_first)
    down_sum.second(tick)
    out_sum.x(tick)
    dq, dk, dv, bias_part = attention_back(
        tick, qkv, et, linv, ot, mixed_grad, pairs // 2, pairs - pairs // 2, held
    )
    tick = after(tick, dq, gate_sum.from_x, down_sum.from_second)
    gate_sum.first(tick)
    down_sum.rest(tick)
    *pair, value_send, value_keep = qkv_grads(tick, bias_part, n1t, dq, dk, dv)
    first_sum, value_sum = chunk(pair), chunk((value_send, value_keep))
    tick = after(
        tick,
        first_sum.keep,
        gate_sum.from_first,
        up_sum.from_x,
        down_sum.from_rest,
        out_sum.from_x,
    )
    first_sum.core(tick)
    value_sum.core(tick)
    gate_sum.second(tick)
    up_sum.first(tick)
    down_sum.back_second(tick)
    blocks = token_grads(
        tick, attn_gain, embedded, dq, dk, dv, hidden_grad, tok, qkv_pieces
    )
    tick = after(
        tick,
        blocks[0],
        first_sum.from_core,
        value_sum.from_core,
        gate_sum.from_second,
        up_sum.from_first,
        down_sum.other_second,
    )
    first_sum.x(tick)
    gate_sum.rest(tick)
    up_sum.second(tick)
    down_sum.back_first(tick)
    tick = after(tick, marker(tick), up_sum.from_second)
    up_sum.rest(tick)
    value_sum.x(tick)
    tick = after(tick, marker(tick), gate_sum.from_rest, down_sum.other)
    out_sum.first(tick)
    tick = after(tick, marker(tick), up_sum.from_rest)
    gated_sum = Group(gate_sum, up_sum)
    gated_sum.back_second(tick)
    tick = after(tick, marker(tick), first_sum.from_x)
    first_sum.first(tick)
    block_x = across_x(blocks[2])
    block_far = across_far(blocks[3])
    tick = after(tick, marker(tick), out_sum.from_first, value_sum.from_x)
    value_sum.first(tick)
    out_sum.second(tick)
    tick = after(tick, marker(tick), first_sum.from_first, gated_sum.other_second)
    first_sum.second(tick)
    gated_sum.back_first(tick)
    tick = after(tick, marker(tick), value_sum.from_first, out_sum.from_second)
    value_sum.second(tick)
    out_sum.rest(tick)
    tick = after(tick, marker(tick), first_sum.from_second)
    first_sum.rest(tick)
    tick = after(tick, marker(tick), value_sum.from_second)
    value_sum.rest(tick)
    tick = after(
        tick, marker(tick), first_sum.from_rest, value_sum.from_rest, out_sum.from_rest, gated_sum.other, block_x, block_far
    )
    attn_sum = Group(out_sum, first_sum, value_sum)
    attn_sum.back_second(tick)
    block_core = across_core(blocks[1])
    tick = after(tick, marker(tick), attn_sum.other_second, block_core)
    attn_sum.back_first(tick)
    down_grad, = assemble(down_sum, (D,))
    gate_weight_grad, up_weight_grad, ffn_gain_grad = assemble(
        gated_sum, (FF, FF), ((0, 0, 0), (1, 1, 0)), (gate_weight, up_weight), (ffn_gain,)
    )
    embedded, tokens_grad = unpack((blocks[0], block_core, block_x, block_far))
    (
        out_grad,
        proj_grad,
        query_grad,
        key_grad,
        value_grad,
        final_gain_grad,
        attn_gain_grad,
        table_grad,
    ) = assemble(
        attn_sum,
        (D, PROJ, D, D, D),
        ((1, 0, 0), (2, 1, 1), (3, 2, 1), (4, 3, 1)),
        (proj_weight, query_weight, key_weight, value_weight),
        (final_gain, attn_gain),
        table=True,
    )
    return (
        embedded,
        tokens_grad,
        query_grad,
        key_grad,
        value_grad,
        out_grad,
        gate_weight_grad,
        up_weight_grad,
        down_grad,
        proj_grad,
        attn_gain_grad,
        ffn_gain_grad,
        final_gain_grad,
        table_grad,
    )


def solution(mesh):
    placed = (
        P("dp", "seq", None),
        P("dp"),
        P("seq", None),
        P("seq", None),
        P("seq", None),
        P("seq", None),
        P("seq", None),
        P("seq", None),
        P("seq", None),
        P("seq", None),
        P(),
        P(),
        P(),
        P(),
        P("dp", "seq", None),
    )
    return jax.shard_map(
        functools.partial(per_device, mesh.shape["dp"]),
        mesh=mesh,
        in_specs=placed,
        out_specs=(
            P("dp", "seq", None),
            P("dp", "seq", None),
            P("seq", None),
            P("seq", None),
            P("seq", None),
            P("seq", None),
            P("seq", None),
            P("seq", None),
            P("seq", None),
            P("seq", None),
            P("seq"),
            P("seq"),
            P("seq"),
            P("seq", None),
        ),
        check_vma=False,
    )
```

```python
import functools

import jax
import jax.numpy as jnp
import numpy as np
from jax import lax
from jax.experimental import pallas as pl
from jax.experimental.pallas import tpu as pltpu
from jax.sharding import PartitionSpec as P

D = 768
H = 12
HEAD = 64
FF = 2048
PROJ = 128
BUCKETS = 32
SLOT = 512
BLOCK = 128
SEQ = 4
SHARD = D // SEQ
HALF_FF = FF // 2
WIDE = D + PROJ
EPSILON = 1e-06
BIG_NEGATIVE = -1e30
GELU_A = 0.7978845608028654
GELU_B = 0.044715

F32 = jnp.float32
BF16 = jnp.bfloat16
VMEM = pl.BlockSpec(memory_space=pltpu.VMEM)
SMEM = pl.BlockSpec(memory_space=pltpu.SMEM)
ANY = pl.BlockSpec(memory_space=pl.ANY)
MIB = 1 << 20


def shape(dims, kind):
    return jax.ShapeDtypeStruct(dims, kind)


def params(wide=False):
    return pltpu.CompilerParams(vmem_limit_bytes=(58 if wide else 20) * MIB)


COST = pl.CostEstimate(flops=90000000000, bytes_accessed=300000000, transcendentals=0)
SMALL_COST = pl.CostEstimate(flops=1, bytes_accessed=1, transcendentals=0)


def bucket_of(relative):
    distance = np.abs(relative)
    scaled = np.log(np.maximum(distance, 1) / 8.0) / np.log(16.0) * 8.0
    far_bucket = np.minimum(8 + scaled.astype(np.int64), 15)
    return (relative > 0) * 16 + np.where(distance < 8, distance, far_bucket)


def skew_buckets():
    lanes = (np.arange(SLOT) + SLOT // 2) % SLOT - SLOT // 2
    relative = np.arange(8)[:, None] - lanes[None, :]
    return bucket_of(relative).astype(np.int32)


def table_indicator():
    lanes = (np.arange(SLOT) + SLOT // 2) % SLOT - SLOT // 2
    buckets = np.concatenate([bucket_of(-lanes), np.full(BLOCK, 15), np.full(BLOCK, 31)])
    here = BUCKETS // SEQ
    place = (buckets // here) * SHARD + buckets % here
    return (place[:, None] == np.arange(D)[None, :]).astype(np.float32)


def dot(left, right):
    return jnp.dot(left, right, preferred_element_type=F32)


def dot_t(left, right):
    return lax.dot_general(left, right, (((1,), (1,)), ((), ())), preferred_element_type=F32)


def place():
    return lax.axis_index("seq"), lax.rem(lax.axis_index("dp"), 2)


def relative_starts(rows, natural=False):
    me, y = place()
    z = lax.rem(lax.axis_index("dp") // 2, 2)
    bits = (me & 1, me >> 1, y, z)
    block = rows // 16
    starts = []
    for number in range(16):
        own = [(number >> shift) & 1 for shift in (3, 2, 1, 0)]
        core, x, first, second = (b if o else 1 - b for b, o in zip(bits, own))
        if natural:
            second = own[3]
        place_of = ((x * 2 + core) * 2 + first) * 2 + second
        starts.append(pl.multiple_of(place_of * block, 16))
    return block, starts


def begin(copies):
    for copy in copies:
        copy.start()
    return copies


def finish(copies):
    for copy in copies:
        copy.wait()


def run_all(copies):
    finish(begin(copies))


class Copies:
    def __init__(self, sems):
        self.sems, self.used = sems, 0

    def __call__(self, source, target):
        copy = pltpu.make_async_copy(source, target, self.sems.at[self.used])
        self.used += 1
        copy.start()
        return copy


def pieces_of(rows, plan, refs, target, sems, first=0):
    me, y = place()
    half = rows // 2
    starts = (
        me * rows,
        (me ^ 1) * rows,
        (me ^ 2) * rows + y * half,
        (me ^ 2) * rows + (1 - y) * half,
        (me ^ 3) * rows + y * half,
        (me ^ 3) * rows + (1 - y) * half,
        (me ^ 2) * rows,
        (me ^ 3) * rows,
    )
    copies = []
    for number, (ref, piece, source, to, width, *some) in enumerate(plan):
        first_row, skip, size = some or (0, 0, half if 2 <= piece < 6 else rows)
        copies.append(
            pltpu.make_async_copy(
                refs[ref].at[pl.ds(first_row, size), pl.ds(source, width)],
                target.at[
                    pl.ds(pl.multiple_of(starts[piece] + skip, 16), size), pl.ds(to, width)
                ],
                sems.at[first + number],
            )
        )
    return copies


QKV_PLANS = tuple(
    ((number, 0, 0, number * D, D),)
    + tuple((2 + piece, piece, number * D, number * D, D) for piece in range(1, 6))
    for number in range(3)
)
OUT_PLAN = tuple((ref, piece, 0, 0, WIDE) for ref, piece in enumerate((0, 1, 6, 7)))
DOWN_SHARD = FF // SEQ
EARLY = 64
DOWN_PLAN = (
    (0, 0, 0, 0, D),
    (1, 1, 0, 0, D),
    (2, 6, 0, 0, D, SHARD, 0, EARLY),
    (3, 6, 0, 0, D, 0, EARLY, DOWN_SHARD - EARLY),
    (4, 7, 0, 0, D, SHARD, 0, EARLY),
    (5, 7, 0, 0, D, 0, EARLY, DOWN_SHARD - EARLY),
)


def gated_plan(part):
    column = part * HALF_FF
    parts = [(4 + 4 * part + number, piece) for number, piece in enumerate((2, 3, 4, 5))]
    return (
        (0, 0, column, column, HALF_FF),
        (1, 0, column, FF + column, HALF_FF),
        (2, 1, column, column, HALF_FF),
        (3, 1, column, FF + column, HALF_FF),
    ) + tuple(
        (ref, piece, number * HALF_FF, number * FF + column, HALF_FF)
        for ref, piece in parts
        for number in range(2)
    )


GATED_PLANS = (gated_plan(0), gated_plan(1))


def relative_copies(source, target, sems, natural=False):
    block, starts = relative_starts(source.shape[0], natural)
    return [
        pltpu.make_async_copy(
            source.at[pl.ds(begin, block), :],
            target.at[pl.ds(number * block, block), :],
            sems.at[number],
        )
        for number, begin in enumerate(starts)
    ]


def inverse_rms(values):
    return lax.rsqrt(jnp.mean(values * values, axis=-1, keepdims=True) + EPSILON)


def norm_backward(values, gain, incoming):
    r = inverse_rms(values)
    weighted = gain * incoming
    inner = jnp.mean(weighted * values, axis=-1, keepdims=True)
    return r * weighted - values * (r * r * r * inner)


def pack_first_kernel(lens, q, k, v, qkv_half, sems):
    _, y = place()
    half = SHARD // 2
    rows = pl.ds(pl.multiple_of(y * half, 16), half)
    run_all(
        [
            pltpu.make_async_copy(
                weight.at[rows, :], qkv_half.at[:, pl.ds(number * D, D)], sems.at[number]
            )
            for number, weight in enumerate((q, k, v))
        ]
    )


def pack_first(lens, q, k, v):
    return pl.pallas_call(
        pack_first_kernel,
        out_shape=shape((SHARD // 2, 3 * D), BF16),
        in_specs=[SMEM] + [ANY] * 3,
        out_specs=VMEM,
        scratch_shapes=[pltpu.SemaphoreType.DMA((3,))],
        compiler_params=params(wide=True),
        cost_estimate=COST,
        name="pack_first",
    )(lens, q, k, v)


def pack_tokens_kernel(lens, tokens, cot, *refs):
    blocks, sems = refs[:4], refs[4]
    me, _ = place()
    pairs = []
    for flip, block in enumerate(blocks):
        pairs.append((tokens.at[me ^ flip], block.at[:, pl.ds(0, D)]))
        pairs.append((cot.at[me ^ flip], block.at[:, pl.ds(D, PROJ)]))
    run_all([pltpu.make_async_copy(a, b, sems.at[i]) for i, (a, b) in enumerate(pairs)])


def pack_tokens(lens, tokens, cot):
    return pl.pallas_call(
        pack_tokens_kernel,
        out_shape=(shape((BLOCK, WIDE), BF16),) * 4,
        in_specs=[SMEM] + [ANY] * 2,
        out_specs=(VMEM,) * 4,
        scratch_shapes=[pltpu.SemaphoreType.DMA((8,))],
        compiler_params=params(wide=True),
        cost_estimate=COST,
        name="pack_tokens",
    )(lens, tokens, cot)


def pack_rest_kernel(
    lens, q, k, v, out, proj, gate, up, down, qkv, out_own, part_0, part_1, down_rest, sems
):
    _, y = place()
    half = SHARD // 2
    rows = pl.ds(pl.multiple_of(y * half, 16), half)
    pairs = [(w, qkv.at[:, pl.ds(number * D, D)]) for number, w in enumerate((q, k, v))]
    pairs.append((out, out_own.at[pl.ds(0, SHARD), pl.ds(0, D)]))
    pairs.append((proj, out_own.at[pl.ds(0, SHARD), pl.ds(D, PROJ)]))
    pairs.append((down.at[pl.ds(0, EARLY), :], out_own.at[pl.ds(SHARD, EARLY), pl.ds(0, D)]))
    pairs.append((down.at[pl.ds(EARLY, DOWN_SHARD - EARLY), :], down_rest))
    for number, part in enumerate((part_0, part_1)):
        columns = pl.ds(number * HALF_FF, HALF_FF)
        pairs.append((gate.at[rows, columns], part.at[:, pl.ds(0, HALF_FF)]))
        pairs.append((up.at[rows, columns], part.at[:, pl.ds(HALF_FF, HALF_FF)]))
    run_all([pltpu.make_async_copy(a, b, sems.at[i]) for i, (a, b) in enumerate(pairs)])


def pack_rest(lens, q, k, v, out, proj, gate, up, down):
    half = SHARD // 2
    return pl.pallas_call(
        pack_rest_kernel,
        out_shape=(shape((SHARD, 3 * D), BF16), shape((SHARD + EARLY, WIDE), BF16))
        + (shape((half, FF), BF16),) * 2
        + (shape((DOWN_SHARD - EARLY, D), BF16),),
        in_specs=[SMEM] + [ANY] * 8,
        out_specs=(VMEM,) * 5,
        scratch_shapes=[pltpu.SemaphoreType.DMA((11,))],
        compiler_params=params(wide=True),
        cost_estimate=COST,
        name="pack_rest",
    )(lens, q, k, v, out, proj, gate, up, down)


def first_norm_kernel(lens, own, from_core, from_x, from_far, gain, tok, cot, n1, n1t, held, sems):
    me, _ = place()
    run_all(
        [
            pltpu.make_async_copy(
                piece,
                held.at[pl.ds(pl.multiple_of((me ^ flip) * BLOCK, BLOCK), BLOCK), :],
                sems.at[flip],
            )
            for flip, piece in enumerate((own, from_core, from_x, from_far))
        ]
    )
    scale = gain[...].reshape(1, D)
    for block in range(SLOT // BLOCK):
        rows = pl.ds(block * BLOCK, BLOCK)
        here = held[rows, 0:D]
        tok[rows, :] = here
        cot[rows, :] = held[rows, D : D + PROJ]
        values = here.astype(F32)
        normed = (values * inverse_rms(values) * scale).astype(BF16)
        n1[rows, :] = normed
        n1t[:, rows] = normed.T


def first_norm(lens, blocks, gain):
    return pl.pallas_call(
        first_norm_kernel,
        out_shape=(
            shape((SLOT, D), BF16),
            shape((SLOT, PROJ), BF16),
            shape((SLOT, D), BF16),
            shape((D, SLOT), BF16),
        ),
        in_specs=[SMEM, ANY, ANY, ANY, ANY, VMEM],
        out_specs=(VMEM,) * 4,
        scratch_shapes=[pltpu.VMEM((SLOT, WIDE), BF16), pltpu.SemaphoreType.DMA((4,))],
        compiler_params=params(wide=True),
        cost_estimate=COST,
        name="first_norm",
    )(lens, *blocks, gain)


def qkv_kernel(lens, n1, *refs):
    pieces, (out, weight, sems) = refs[:8], refs[8:]
    group = pl.program_id(0)

    def copies(number):
        return pieces_of(SHARD, QKV_PLANS[number], pieces, weight, sems, 6 * number)

    @pl.when(group == 0)
    def start():
        for number in range(3):
            begin(copies(number))

    for number in range(3):

        @pl.when(group == number)
        def ready():
            finish(copies(number))

    for tile in range(D // 256):
        columns = pl.ds(pl.multiple_of(group * D + tile * 256, 256), 256)
        out[:, tile * 256 : (tile + 1) * 256] = dot(n1[...], weight[:, columns]).astype(BF16)


def qkv_project(lens, n1, pieces):
    return pl.pallas_call(
        qkv_kernel,
        grid=(3,),
        out_shape=shape((SLOT, 3 * D), BF16),
        in_specs=[SMEM, VMEM] + [ANY] * 8,
        out_specs=pl.BlockSpec((SLOT, D), lambda i: (0, i)),
        scratch_shapes=[pltpu.VMEM((D, 3 * D), BF16), pltpu.SemaphoreType.DMA((18,))],
        compiler_params=params(wide=True),
        cost_estimate=COST,
        name="qkv_project",
    )(lens, n1, *pieces)


HALF_Q = 512


def attention_kernel(first, lens, q, k, v, rows_of_bias, buckets, *refs):
    et, linv, ot, o, bias = refs[-5:]
    me, _ = place()
    length = lens[me]
    pair = pl.program_id(0) + first
    k_pair = k[...]
    vt = v[...].T
    qt = q[...].T
    row_in_pair = lax.broadcasted_iota(jnp.int32, (2 * HEAD, SLOT), 0)
    key_index = lax.broadcasted_iota(jnp.int32, (SLOT, HALF_Q), 0)
    for head in range(2):
        base = jnp.zeros((8, SLOT), F32)
        for bucket in range(BUCKETS):
            base = jnp.where(buckets[...] == bucket, rows_of_bias[bucket, 2 * pair + head], base)
        for group in range(BLOCK // 8):
            bias[pl.ds(group * 8, 8), :] = pltpu.roll(base, 8 * group, 1) if group else base
        below = rows_of_bias[15, 2 * pair + head]
        above = rows_of_bias[31, 2 * pair + head]
        in_head = (row_in_pair >= HEAD * head) & (row_in_pair < HEAD * (head + 1))
        qt_head = jnp.where(in_head, qt, jnp.zeros_like(qt))
        for part in range(SLOT // HALF_Q):
            raw = dot(k_pair, qt_head[:, part * HALF_Q : (part + 1) * HALF_Q])
            rows = []
            for key_block in range(4):
                cells = []
                for sub in range(HALF_Q // BLOCK):
                    query_block = part * (HALF_Q // BLOCK) + sub
                    cell = raw[
                        key_block * BLOCK : (key_block + 1) * BLOCK,
                        sub * BLOCK : (sub + 1) * BLOCK,
                    ]
                    apart = key_block - query_block
                    if apart >= 2:
                        cell = cell + above
                    elif apart <= -2:
                        cell = cell + below
                    else:
                        lane = (-apart * BLOCK) % SLOT
                        cell = cell + bias[:, lane : lane + BLOCK]
                    cells.append(cell)
                rows.append(jnp.concatenate(cells, axis=1))
            scores = jnp.concatenate(rows, axis=0)
            scores = jnp.where(key_index < length, scores, BIG_NEGATIVE)
            top = jnp.max(scores, axis=0, keepdims=True)
            weights = jnp.exp(scores - top)
            inverse = 1.0 / jnp.sum(weights, axis=0, keepdims=True)
            low = weights.astype(BF16)
            columns = pl.ds(part * HALF_Q, HALF_Q)
            et[head, :, columns] = low
            linv[head, :, columns] = inverse
            mixed = dot(vt[head * HEAD : (head + 1) * HEAD, :], low) * inverse
            ot[pl.ds(head * HEAD, HEAD), columns] = mixed.astype(BF16)
    o[...] = ot[...].T


def attention(lens, qkv, rows_of_bias, first, count, held):
    pair = 2 * HEAD
    pairs = H // 2
    return pl.pallas_call(
        functools.partial(attention_kernel, first),
        grid=(count,),
        out_shape=(
            shape((H, SLOT, SLOT), BF16),
            shape((H, 1, SLOT), F32),
            shape((D, SLOT), BF16),
            shape((SLOT, D), BF16),
        ),
        in_specs=[
            SMEM,
            pl.BlockSpec((SLOT, pair), lambda i: (0, first + i)),
            pl.BlockSpec((SLOT, pair), lambda i: (0, pairs + first + i)),
            pl.BlockSpec((SLOT, pair), lambda i: (0, 2 * pairs + first + i)),
            SMEM,
            pl.BlockSpec((8, SLOT), lambda i: (0, 0)),
        ]
        + [ANY] * len(held),
        out_specs=(
            pl.BlockSpec((2, SLOT, SLOT), lambda i: (first + i, 0, 0)),
            pl.BlockSpec((2, 1, SLOT), lambda i: (first + i, 0, 0)),
            pl.BlockSpec((pair, SLOT), lambda i: (first + i, 0)),
            pl.BlockSpec((SLOT, pair), lambda i: (0, first + i)),
        ),
        input_output_aliases={6 + i: i for i in range(len(held))},
        scratch_shapes=[pltpu.VMEM((BLOCK, SLOT), F32)],
        compiler_params=params(wide=True),
        cost_estimate=COST,
        name="attention",
    )(lens, qkv, qkv, qkv, rows_of_bias, jnp.asarray(skew_buckets()), *held)


def feed_forward_kernel(lens, ffn_gain, final_gain, tok, mixed, cot, *refs):
    out_pieces, gated_pieces, down_pieces, refs = refs[:4], refs[4:16], refs[16:22], refs[22:]
    hidden_out, n2t_out, gate_out, up_out, embedded_out, after_out, fnt_out = refs[:7]
    send_out, keep_out = refs[7:9]
    w_out, w_gated, w_down, tok_v, mixed_v, cot_v, hidden, n2, n2t, inner, innert = refs[9:20]
    slope, level, embedded, after_grad, down_in, fnt, send, keep = refs[20:28]
    out_sems, gated_sems, down_sems, in_sems, done_sems = refs[28:]
    load, store = Copies(in_sems), Copies(done_sems)

    loads = begin(pieces_of(SHARD, OUT_PLAN, out_pieces, w_out, out_sems))
    loads += [load(mixed, mixed_v), load(tok, tok_v), load(cot, cot_v)]
    gated_loads = [
        begin(pieces_of(SHARD, plan, gated_pieces, w_gated, gated_sems, 12 * number))
        for number, plan in enumerate(GATED_PLANS)
    ]
    down_loads = begin(pieces_of(FF // SEQ, DOWN_PLAN, down_pieces, w_down, down_sems))
    stores = []

    finish(loads)
    scale = ffn_gain[...].reshape(1, D)
    for block in range(2):
        rows = pl.ds(block * 256, 256)
        values = tok_v[rows, :].astype(F32) + dot(mixed_v[rows, :], w_out[:, 0:D])
        hidden[rows, :] = values
        normed = (values * inverse_rms(values) * scale).astype(BF16)
        n2[rows, :] = normed
        n2t[:, rows] = normed.T
    stores.append(store(hidden, hidden_out))
    size, starts = relative_starts(D)
    for number, begin_row in enumerate(starts):
        stores.append(
            store(n2t.at[pl.ds(begin_row, size), :], n2t_out.at[pl.ds(number * size, size), :])
        )

    me, y = place()
    z = lax.rem(lax.axis_index("dp") // 2, 2)

    def step(tile, carry):
        columns = pl.ds(pl.multiple_of(tile * 512, 512), 512)
        g = dot(n2[...], w_gated[:, columns])
        u = dot(n2[...], w_gated[:, pl.ds(pl.multiple_of(FF + tile * 512, 512), 512)])
        square = g * g
        t = jnp.tanh(GELU_A * g * (1.0 + GELU_B * square))
        half_up = 0.5 * (1.0 + t)
        activated = g * half_up
        derivative = half_up + 0.5 * g * (1.0 - t * t) * (GELU_A * (1.0 + 3 * GELU_B * square))
        value = (activated * u).astype(BF16)
        inner[:, columns] = value
        slope[:, columns] = (derivative * u).astype(BF16)
        level[:, columns] = activated.astype(BF16)
        core_own = (lax.rem(tile, 2) == lax.rem(me, 2)).astype(jnp.int32)
        x_own = (tile // 2 == me // 2).astype(jnp.int32)
        target = (core_own * 2 + x_own) * 512
        turned = value.T
        for number in range(4):
            y_own = (number >> 1 == y).astype(jnp.int32)
            z_own = ((number & 1) == z).astype(jnp.int32)
            row = pl.multiple_of(target + y_own * 256 + z_own * BLOCK, BLOCK)
            innert[pl.ds(row, BLOCK), :] = turned[number * BLOCK : (number + 1) * BLOCK, :]
        return carry

    for part in range(2):
        finish(gated_loads[part])
        lax.fori_loop(2 * part, 2 * part + 2, step, 0)

    finish(down_loads)
    scale = final_gain[...].reshape(1, D)
    for block in range(2):
        rows = pl.ds(block * 256, 256)
        values = hidden[rows, :] + dot(inner[rows, :], w_down[...])
        normed = (values * inverse_rms(values) * scale).astype(BF16)
        fnt[:, rows] = normed.T
        embedded[rows, :] = dot(normed, w_out[:, D:WIDE]).astype(BF16)
        gradient = norm_backward(values, scale, dot_t(cot_v[rows, :], w_out[:, D:WIDE]))
        after_grad[rows, :] = gradient
        down_in[rows, :] = gradient.astype(BF16)
    for source, target in ((after_grad, after_out), (embedded, embedded_out), (fnt, fnt_out)):
        stores.append(store(source, target))

    for number, (part, target) in enumerate(((send, send_out), (keep, keep_out))):

        def grad(tile, carry):
            rows = pl.ds(pl.multiple_of(tile * 256, 256), 256)
            source = pl.ds(pl.multiple_of(number * (FF // 2) + tile * 256, 256), 256)
            part[rows, :] = dot(innert[source, :], down_in[...]).astype(BF16)
            return carry

        lax.fori_loop(0, FF // 2 // 256, grad, 0)
        stores.append(store(part, target))

    def back(tile, carry):
        columns = pl.ds(pl.multiple_of(tile * 512, 512), 512)
        incoming = dot_t(down_in[...], w_down[columns, :])
        slope[:, columns] = (incoming * slope[:, columns].astype(F32)).astype(BF16)
        level[:, columns] = (incoming * level[:, columns].astype(F32)).astype(BF16)
        return carry

    lax.fori_loop(0, FF // 512, back, 0)
    stores += [store(slope, gate_out), store(level, up_out)]
    finish(stores)


def feed_forward(lens, tok, mixed, cot, ffn_gain, final_gain, out_pieces, gated_pieces, down_pieces):
    wide, tall, full = (SLOT, D), (D, SLOT), (SLOT, FF)
    pieces = tuple(out_pieces) + tuple(gated_pieces) + tuple(down_pieces)
    return pl.pallas_call(
        feed_forward_kernel,
        out_shape=(
            shape(wide, F32),
            shape(tall, BF16),
            shape(full, BF16),
            shape(full, BF16),
            shape((SLOT, PROJ), BF16),
            shape(wide, F32),
            shape(tall, BF16),
            shape((FF // 2, D), BF16),
            shape((FF // 2, D), BF16),
        ),
        in_specs=[SMEM, VMEM, VMEM] + [ANY] * (3 + len(pieces)),
        out_specs=(ANY,) * 9,
        scratch_shapes=[
            pltpu.VMEM((D, WIDE), BF16),
            pltpu.VMEM((D, 2 * FF), BF16),
            pltpu.VMEM((FF, D), BF16),
            pltpu.VMEM(wide, BF16),
            pltpu.VMEM(wide, BF16),
            pltpu.VMEM((SLOT, PROJ), BF16),
            pltpu.VMEM(wide, F32),
            pltpu.VMEM(wide, BF16),
            pltpu.VMEM(tall, BF16),
            pltpu.VMEM(full, BF16),
            pltpu.VMEM((FF, SLOT), BF16),
            pltpu.VMEM(full, BF16),
            pltpu.VMEM(full, BF16),
            pltpu.VMEM((SLOT, PROJ), BF16),
            pltpu.VMEM(wide, F32),
            pltpu.VMEM(wide, BF16),
            pltpu.VMEM(tall, BF16),
            pltpu.VMEM((FF // 2, D), BF16),
            pltpu.VMEM((FF // 2, D), BF16),
            pltpu.SemaphoreType.DMA((4,)),
            pltpu.SemaphoreType.DMA((24,)),
            pltpu.SemaphoreType.DMA((6,)),
            pltpu.SemaphoreType.DMA((3,)),
            pltpu.SemaphoreType.DMA((24,)),
        ],
        compiler_params=params(wide=True),
        cost_estimate=COST,
        name="feed_forward",
    )(lens, ffn_gain, final_gain, tok, mixed, cot, *pieces)


def row_grads(left, right, halves, column=0, loads=(), store=None, outs=()):
    half = left.shape[0] // 2
    width = right.shape[1]
    size = 1024 if width % 1024 == 0 else width
    stores = []
    for tile in range(width // size):
        if loads:
            loads[tile].wait()
        target = slice(column + tile * size, column + (tile + 1) * size)
        both = dot(left[...], right[:, tile * size : (tile + 1) * size]).astype(BF16)
        for number, part in enumerate(halves):
            part[:, target] = both[number * half : (number + 1) * half, :]
            stores.append(store(part.at[:, target], outs[number].at[:, target]))
    return stores


def tile_loads(load, source, target, size=1024):
    return [
        load(source.at[:, pl.ds(begin_at, size)], target.at[:, pl.ds(begin_at, size)])
        for begin_at in range(0, source.shape[1], size)
    ]


def gate_grad_kernel(lens, n2t, gate_grad, send_out, keep_out, n2t_v, gate_v, send, keep, *sems):
    load, store = Copies(sems[0]), Copies(sems[1])
    first = load(n2t, n2t_v)
    loads = tile_loads(load, gate_grad, gate_v)
    first.wait()
    finish(row_grads(n2t_v, gate_v, (send, keep), 0, loads, store, (send_out, keep_out)))


def gate_grads(lens, n2t, gate_grad):
    part = (D // 2, FF)
    return pl.pallas_call(
        gate_grad_kernel,
        out_shape=(shape(part, BF16),) * 2,
        in_specs=[SMEM] + [ANY] * 2,
        out_specs=(ANY,) * 2,
        scratch_shapes=[
            pltpu.VMEM((D, SLOT), BF16),
            pltpu.VMEM((SLOT, FF), BF16),
            pltpu.VMEM(part, BF16),
            pltpu.VMEM(part, BF16),
            pltpu.SemaphoreType.DMA((3,)),
            pltpu.SemaphoreType.DMA((4,)),
        ],
        compiler_params=params(wide=True),
        cost_estimate=COST,
        name="gate_grads",
    )(lens, n2t, gate_grad)


def up_grad_kernel(lens, gain, n2t, gate_grad, up_grad, hidden, after_grad, *refs):
    pieces, outs, refs = refs[:12], refs[12:16], refs[16:]
    weight, n2t_v, gate_v, up_v, hidden_v, after_v, send, keep, grad, attn_in = refs[:10]
    sems, in_sems, done_sems = refs[10:]
    load, store = Copies(in_sems), Copies(done_sems)
    first = load(n2t, n2t_v)
    loads = tile_loads(load, up_grad, up_v)
    gate_load = load(gate_grad, gate_v)
    plan = sum(GATED_PLANS, ())
    gate_plan = tuple(entry for entry in plan if entry[3] < FF)
    up_plan = tuple(entry for entry in plan if entry[3] >= FF)
    gate_pieces = begin(pieces_of(SHARD, gate_plan, pieces, weight, sems))
    up_pieces = begin(pieces_of(SHARD, up_plan, pieces, weight, sems, len(gate_plan)))
    later = [load(hidden, hidden_v), load(after_grad, after_v)]
    first.wait()
    stores = row_grads(n2t_v, up_v, (send, keep), 0, loads, store, outs[0:2])
    gate_load.wait()
    finish(gate_pieces)
    for block in range(2):
        rows = pl.ds(block * 256, 256)
        grad[rows, :] = dot_t(gate_v[rows, :], weight[:, 0:FF])
    finish(up_pieces)
    finish(later)
    scale = gain[...].reshape(1, D)
    for block in range(2):
        rows = pl.ds(block * 256, 256)
        incoming = grad[rows, :] + dot_t(up_v[rows, :], weight[:, FF:])
        gradient = norm_backward(hidden_v[rows, :], scale, incoming) + after_v[rows, :]
        grad[rows, :] = gradient
        attn_in[rows, :] = gradient.astype(BF16)
    stores += [store(attn_in, outs[3]), store(grad, outs[2])]
    finish(stores)


def up_grads(lens, gain, n2t, gate_grad, up_grad, hidden, after_grad, pieces):
    full, part, wide = (SLOT, FF), (D // 2, FF), (SLOT, D)
    return pl.pallas_call(
        up_grad_kernel,
        out_shape=(shape(part, BF16),) * 2 + (shape(wide, F32), shape(wide, BF16)),
        in_specs=[SMEM, VMEM] + [ANY] * 17,
        out_specs=(ANY,) * 4,
        scratch_shapes=[
            pltpu.VMEM((D, 2 * FF), BF16),
            pltpu.VMEM((D, SLOT), BF16),
            pltpu.VMEM(full, BF16),
            pltpu.VMEM(full, BF16),
            pltpu.VMEM(wide, F32),
            pltpu.VMEM(wide, F32),
            pltpu.VMEM(part, BF16),
            pltpu.VMEM(part, BF16),
            pltpu.VMEM(wide, F32),
            pltpu.VMEM(wide, BF16),
            pltpu.SemaphoreType.DMA((24,)),
            pltpu.SemaphoreType.DMA((6,)),
            pltpu.SemaphoreType.DMA((6,)),
        ],
        compiler_params=params(wide=True),
        cost_estimate=COST,
        name="up_grads",
    )(lens, gain, n2t, gate_grad, up_grad, hidden, after_grad, *pieces)


def out_grad_kernel(lens, ot, fnt, attn_in, cot, *refs):
    pieces, outs, refs = refs[:4], refs[4:7], refs[7:]
    weight, left, proj_left, attn_v, cot_v, send, keep, mixed = refs[:8]
    sems, left_sems, proj_sems, in_sems, done_sems = refs[8:]
    load, store = Copies(in_sems), Copies(done_sems)
    loads = [load(attn_in, attn_v)]
    loads += begin(relative_copies(ot, left, left_sems))
    pieces = begin(pieces_of(SHARD, OUT_PLAN, pieces, weight, sems))
    later = [load(cot, cot_v)]
    later += begin(relative_copies(fnt, proj_left, proj_sems))
    finish(loads)
    stores = row_grads(left, attn_v, (send, keep), 0, (), store, outs[0:2])
    finish(later)
    stores += row_grads(proj_left, cot_v, (send, keep), D, (), store, outs[0:2])
    finish(pieces)
    mixed[...] = dot_t(attn_v[...], weight[:, 0:D]).astype(BF16)
    stores.append(store(mixed, outs[2]))
    finish(stores)


def out_grads(lens, ot, fnt, attn_in, cot, pieces):
    return pl.pallas_call(
        out_grad_kernel,
        out_shape=(shape((D // 2, WIDE), BF16),) * 2 + (shape((SLOT, D), BF16),),
        in_specs=[SMEM] + [ANY] * 8,
        out_specs=(ANY,) * 3,
        scratch_shapes=[
            pltpu.VMEM((D, WIDE), BF16),
            pltpu.VMEM((D, SLOT), BF16),
            pltpu.VMEM((D, SLOT), BF16),
            pltpu.VMEM((SLOT, D), BF16),
            pltpu.VMEM((SLOT, PROJ), BF16),
            pltpu.VMEM((D // 2, WIDE), BF16),
            pltpu.VMEM((D // 2, WIDE), BF16),
            pltpu.VMEM((SLOT, D), BF16),
            pltpu.SemaphoreType.DMA((4,)),
            pltpu.SemaphoreType.DMA((16,)),
            pltpu.SemaphoreType.DMA((16,)),
            pltpu.SemaphoreType.DMA((2,)),
            pltpu.SemaphoreType.DMA((5,)),
        ],
        compiler_params=params(wide=True),
        cost_estimate=COST,
        name="out_grads",
    )(lens, ot, fnt, attn_in, cot, *pieces)


def qkv_grad_kernel(lens, table, indicator, n1t, dq, dk, dv, *refs):
    outs, left, dq_v, dk_v, dv_v = refs[:4], refs[4], refs[5], refs[6], refs[7]
    send, keep, value_send, value_keep, small, left_sems, in_sems, done_sems = refs[8:]
    load, store = Copies(in_sems), Copies(done_sems)
    first = [load(dq, dq_v)] + begin(relative_copies(n1t, left, left_sems))
    second, third = load(dk, dk_v), load(dv, dv_v)
    finish(first)
    stores = row_grads(left, dq_v, (send, keep), 0, (), store, outs[0:2])
    stores += row_grads(left, dk_v, (send, keep), D, (second,), store, outs[0:2])
    by_lane = jnp.concatenate([table[pair] for pair in range(H // 2)], axis=0)
    high = by_lane.astype(BF16)
    low = (by_lane - high.astype(F32)).astype(BF16)
    by_bucket = dot(high, indicator[...]) + dot(low, indicator[...])
    small[...] = jnp.concatenate([by_bucket, jnp.zeros((PROJ - H, D), F32)], axis=0).T
    block, starts = relative_starts(D)
    for number, row in enumerate(starts):
        target = value_keep if number >= 8 else value_send
        target[pl.ds((number & 7) * block, block), D:WIDE] = small[pl.ds(row, block), :].astype(
            BF16
        )
    columns = pl.ds(D, PROJ)
    for number, part in enumerate((value_send, value_keep)):
        stores.append(store(part.at[:, columns], outs[2 + number].at[:, columns]))
    stores += row_grads(left, dv_v, (value_send, value_keep), 0, (third,), store, outs[2:4])
    finish(stores)


def qkv_grads(lens, table, n1t, dq, dk, dv):
    pair, single = (D // 2, 2 * D), (D // 2, WIDE)
    return pl.pallas_call(
        qkv_grad_kernel,
        out_shape=(shape(pair, BF16),) * 2 + (shape(single, BF16),) * 2,
        in_specs=[SMEM, VMEM, VMEM] + [ANY] * 4,
        out_specs=(ANY,) * 4,
        scratch_shapes=[pltpu.VMEM((D, SLOT), BF16)]
        + [pltpu.VMEM((SLOT, D), BF16)] * 3
        + [pltpu.VMEM(pair, BF16)] * 2
        + [pltpu.VMEM(single, BF16)] * 2
        + [
            pltpu.VMEM((D, PROJ), F32),
            pltpu.SemaphoreType.DMA((16,)),
            pltpu.SemaphoreType.DMA((3,)),
            pltpu.SemaphoreType.DMA((8,)),
        ],
        compiler_params=params(wide=True),
        cost_estimate=COST,
        name="qkv_grads",
    )(lens, table, jnp.asarray(table_indicator(), dtype=BF16), n1t, dq, dk, dv)


def attention_back_kernel(lens, q, k, v, et, linv, ot, do, *refs):
    dq, dk, dv, bias_grad, dqt, near = refs[-6:]
    lane_in_pair = lax.broadcasted_iota(jnp.int32, (SLOT, 2 * HEAD), 1)
    q_pair, v_pair = q[...], v[...]
    kt = k[...].T
    out_gradt = do[...].astype(F32).T
    scaled = []
    deltas = []
    for head in range(2):
        rows = slice(head * HEAD, (head + 1) * HEAD)
        low = (out_gradt[rows, :] * linv[head]).astype(BF16)
        scaled.append(low)
        deltas.append(
            jnp.sum(low.astype(F32) * ot[rows, :].astype(F32), axis=0, keepdims=True)
        )
    scaled_pair = jnp.concatenate(scaled, axis=0).T
    zeros = jnp.zeros((HEAD, SLOT), BF16)
    key_total = jnp.zeros((SLOT, 2 * HEAD), F32)
    value_total = jnp.zeros((SLOT, 2 * HEAD), F32)
    row_of_eight = lax.broadcasted_iota(jnp.int32, (8, SLOT), 0)
    for head in range(2):
        in_head = (lane_in_pair >= head * HEAD) & (lane_in_pair < (head + 1) * HEAD)
        q_head = jnp.where(in_head, q_pair, jnp.zeros_like(q_pair))
        do_head = jnp.where(in_head, scaled_pair, jnp.zeros_like(scaled_pair))
        dot_head = jnp.concatenate(
            [scaled[head], zeros] if head == 0 else [zeros, scaled[head]], axis=0
        )
        near_sums = {-1: None, 0: None, 1: None}
        far_sums = {-1: None, 1: None}
        for part in range(SLOT // HALF_Q):
            columns = slice(part * HALF_Q, (part + 1) * HALF_Q)
            prob_grad = dot(v_pair, dot_head[:, columns])
            low_weights = et[head, :, columns]
            score_grad = low_weights.astype(F32) * (prob_grad - deltas[head][:, columns])
            low = score_grad.astype(BF16)
            key_total = key_total + dot(low, q_head[columns, :])
            value_total = value_total + dot(low_weights, do_head[columns, :])
            dqt[pl.ds(head * HEAD, HEAD), columns] = dot(
                kt[head * HEAD : (head + 1) * HEAD, :], low
            ).astype(BF16)
            for key_block in range(4):
                for sub in range(HALF_Q // BLOCK):
                    apart = key_block - part * (HALF_Q // BLOCK) - sub
                    cell = score_grad[
                        key_block * BLOCK : (key_block + 1) * BLOCK,
                        sub * BLOCK : (sub + 1) * BLOCK,
                    ]
                    if abs(apart) >= 2:
                        side = 1 if apart > 0 else -1
                        folded = jnp.sum(cell.reshape(BLOCK // 8, 8, BLOCK), axis=0)
                        old = far_sums[side]
                        far_sums[side] = folded if old is None else old + folded
                    else:
                        old = near_sums[apart]
                        near_sums[apart] = cell if old is None else old + cell
        near[...] = jnp.zeros_like(near)
        for apart in (-1, 0, 1):
            lane = (-apart * BLOCK) % SLOT
            near[:, lane : lane + BLOCK] = near_sums[apart]
        folded = near[0:8, :]
        for group in range(1, BLOCK // 8):
            folded = folded + pltpu.roll(near[group * 8 : group * 8 + 8, :], SLOT - 8 * group, 1)
        for bit in (1, 2, 4):
            folded = jnp.where(
                (row_of_eight & bit) != 0, pltpu.roll(folded, SLOT - bit, 1), folded
            )
        here = slice(head, head + 1)
        bias_grad[0, here, 0:SLOT] = jnp.sum(folded, axis=0, keepdims=True)
        for number, side in enumerate((-1, 1)):
            lane = SLOT + number * BLOCK
            bias_grad[0, here, lane : lane + BLOCK] = jnp.sum(
                far_sums[side], axis=0, keepdims=True
            )
    dk[...] = key_total.astype(BF16)
    dv[...] = value_total.astype(BF16)
    dq[...] = dqt[...].T


def attention_back(lens, qkv, et, linv, ot, do, first, count, held):
    pair = 2 * HEAD
    pairs = H // 2
    wide = pl.BlockSpec((SLOT, pair), lambda i: (0, first + i))
    return pl.pallas_call(
        attention_back_kernel,
        grid=(count,),
        out_shape=(shape((SLOT, D), BF16),) * 3 + (shape((pairs, 2, D), F32),),
        in_specs=[
            SMEM,
            wide,
            pl.BlockSpec((SLOT, pair), lambda i: (0, pairs + first + i)),
            pl.BlockSpec((SLOT, pair), lambda i: (0, 2 * pairs + first + i)),
            pl.BlockSpec((2, SLOT, SLOT), lambda i: (first + i, 0, 0)),
            pl.BlockSpec((2, 1, SLOT), lambda i: (first + i, 0, 0)),
            pl.BlockSpec((pair, SLOT), lambda i: (first + i, 0)),
            wide,
        ]
        + [ANY] * len(held),
        out_specs=(wide,) * 3 + (pl.BlockSpec((1, 2, D), lambda i: (first + i, 0, 0)),),
        input_output_aliases={8 + i: i for i in range(len(held))},
        scratch_shapes=[pltpu.VMEM((pair, SLOT), BF16), pltpu.VMEM((BLOCK, SLOT), F32)],
        compiler_params=params(wide=True),
        cost_estimate=COST,
        name="attention_back",
    )(lens, qkv, qkv, qkv, et, linv, ot, do, *held)


def token_grad_kernel(lens, gain, embedded, dq, dk, dv, hidden_grad, tok, *refs):
    pieces, outs, refs = refs[:8], refs[8:12], refs[12:]
    weight, embedded_v, dq_v, dk_v, dv_v, hidden_v, tok_v, total = refs[:8]
    packed, (sems, in_sems, done_sems) = refs[8:12], refs[12:]
    load, store = Copies(in_sems), Copies(done_sems)
    me, _ = place()
    loads = []
    for number, (source, target) in enumerate(((dq, dq_v), (dk, dk_v), (dv, dv_v))):
        plan = QKV_PLANS[number]
        loads.append(
            [load(source, target)]
            + begin(pieces_of(SHARD, plan, pieces, weight, sems, 6 * number))
        )
    later = [load(hidden_grad, hidden_v), load(tok, tok_v), load(embedded, embedded_v)]
    for number, source in enumerate((dq_v, dk_v, dv_v)):
        finish(loads[number])
        for block in range(2):
            rows = pl.ds(block * 256, 256)
            term = dot_t(source[rows, :], weight[:, number * D : (number + 1) * D])
            total[rows, :] = term if number == 0 else total[rows, :] + term
    finish(later)
    scale = gain[...].reshape(1, D)
    stores = []
    for flip, target in enumerate(packed):
        rows = pl.ds(pl.multiple_of((me ^ flip) * BLOCK, BLOCK), BLOCK)
        gradient = norm_backward(tok_v[rows, :].astype(F32), scale, total[rows, :])
        target[:, 0:D] = (hidden_v[rows, :] + gradient).astype(BF16)
        target[:, D:WIDE] = embedded_v[rows, :]
        stores.append(store(target, outs[flip]))
    finish(stores)


def token_grads(lens, gain, embedded, dq, dk, dv, hidden_grad, tok, pieces):
    wide = (SLOT, D)
    return pl.pallas_call(
        token_grad_kernel,
        out_shape=(shape((BLOCK, WIDE), BF16),) * 4,
        in_specs=[SMEM, VMEM] + [ANY] * 14,
        out_specs=(ANY,) * 4,
        scratch_shapes=[
            pltpu.VMEM((D, 3 * D), BF16),
            pltpu.VMEM((SLOT, PROJ), BF16),
            pltpu.VMEM(wide, BF16),
            pltpu.VMEM(wide, BF16),
            pltpu.VMEM(wide, BF16),
            pltpu.VMEM(wide, F32),
            pltpu.VMEM(wide, BF16),
            pltpu.VMEM(wide, F32),
        ]
        + [pltpu.VMEM((BLOCK, WIDE), BF16)] * 4
        + [
            pltpu.SemaphoreType.DMA((18,)),
            pltpu.SemaphoreType.DMA((6,)),
            pltpu.SemaphoreType.DMA((4,)),
        ],
        compiler_params=params(wide=True),
        cost_estimate=COST,
        name="token_grads",
    )(lens, gain, embedded, dq, dk, dv, hidden_grad, tok, *pieces)


def unpack_kernel(block_0, block_1, block_2, block_3, embedded, tokens_grad):
    me, _ = place()
    for flip, block in enumerate((block_0, block_1, block_2, block_3)):
        tokens_grad[me ^ flip] = block[:, 0:D].astype(F32)
        embedded[me ^ flip] = block[:, D:WIDE]


def unpack(blocks):
    return pl.pallas_call(
        unpack_kernel,
        out_shape=(shape((SEQ, BLOCK, PROJ), BF16), shape((SEQ, BLOCK, D), F32)),
        in_specs=[VMEM] * 4,
        out_specs=(VMEM,) * 2,
        compiler_params=params(),
        cost_estimate=SMALL_COST,
        name="unpack",
    )(*blocks)


def exchange(value, axis, flip, size):
    return lax.ppermute(value, axis, [(i, i ^ flip) for i in range(size)])


def after(value, *others):
    return lax.optimization_barrier((value,) + others)[0]


def add(*terms):
    total = terms[0].astype(F32)
    for term in terms[1:]:
        total = total + term.astype(F32)
    return total.astype(BF16)


def marker_kernel(tick, mark):
    pass


def marker(tick):
    return pl.pallas_call(
        marker_kernel,
        out_shape=shape((8, 128), F32),
        in_specs=[ANY],
        out_specs=ANY,
        compiler_params=params(),
        cost_estimate=COST,
        name="marker",
    )(tick)


def halves_kernel(skip, *refs):
    terms, (to_send, own, held, sems) = refs[:-4], refs[-4:]
    rows = own.shape[0]
    finish(
        begin(
            [
                pltpu.make_async_copy(
                    source.at[pl.ds(first, 2 * rows), :], held.at[number], sems.at[number]
                )
                for number, (source, first) in enumerate(zip(terms, skip))
            ]
        )
    )
    for number, target in enumerate((to_send, own)):

        def body(index, carry):
            here = pl.ds(pl.multiple_of(number * rows + index * 16, 16), 16)
            total = held[0, here, :].astype(F32)
            for term in range(1, len(terms)):
                total = total + held[term, here, :].astype(F32)
            target[pl.ds(pl.multiple_of(index * 16, 16), 16), :] = total.astype(BF16)
            return carry

        lax.fori_loop(0, rows // 16, body, 0)


def halves(rows, *terms):
    width = terms[0][0].shape[1]
    return pl.pallas_call(
        functools.partial(halves_kernel, tuple(first for _, first in terms)),
        out_shape=(shape((rows, width), BF16),) * 2,
        in_specs=[ANY] * len(terms),
        out_specs=(VMEM,) * 2,
        scratch_shapes=[
            pltpu.VMEM((len(terms), 2 * rows, width), BF16),
            pltpu.SemaphoreType.DMA((len(terms),)),
        ],
        compiler_params=params(),
        cost_estimate=SMALL_COST,
        name="halves",
    )(*(term for term, _ in terms))


class Chunk:
    def __init__(self, groups, pair, thin=False):
        self.groups, self.thin = groups, thin
        self.send, self.keep = pair
        self.rows = self.send.shape[0] // 4

    def along(self, flip, value):
        return exchange(value, "dp", flip, self.groups)

    def core(self, tick):
        self.send = after(self.send, tick)
        self.from_core = exchange(self.send, "seq", 1, SEQ)

    def x(self, tick):
        both = 2 * self.rows
        self.from_core = after(self.from_core, tick)
        mine = add(self.keep[:both], self.from_core[:both])
        self.from_x = exchange(mine, "seq", 2, SEQ)

    def first(self, tick):
        self.from_x = after(self.from_x, tick)
        rows = self.rows
        mine, self.base = halves(
            rows, (self.keep, 2 * rows), (self.from_core, 2 * rows), (self.from_x, 0)
        )
        self.from_first = self.along(1, mine)

    def _summed(self, begin, end):
        return add(self.base[begin:end], self.from_first[begin:end])

    def second(self, tick):
        self.from_first = after(self.from_first, tick)
        self.total = self._summed(0, self.rows if self.thin else self.rows // 2)
        self.from_second = self.along(2, self.total)

    def rest(self, tick):
        self.from_second = after(self.from_second, tick)
        if not self.thin:
            self.total = self._summed(self.rows // 2, self.rows)
        self.total = add(self.total, self.from_second)
        step = 4
        while step < self.groups:
            if step > 4:
                self.total = add(self.total, self.from_rest)
            self.from_rest = self.along(step, self.total)
            step *= 2

    def back_second(self, tick):
        self.from_rest = after(self.from_rest, tick)
        self.total = add(self.total, self.from_rest)
        self.other_second = self.along(2, self.total)

    def back_first(self, tick):
        if self.thin:
            self.from_rest = after(self.from_rest, tick)
            self.total = add(self.total, self.from_rest)
        else:
            self.other_second = after(self.other_second, tick)
            self.total = jnp.concatenate([self.other_second, self.total], axis=0)
        self.other = self.along(1, self.total)


def join_kernel(*refs):
    terms, out = refs[:-1], refs[-1]
    column = 0
    for left, right in zip(terms[0::2], terms[1::2]):
        width = left.shape[1]
        out[:, column : column + width] = (
            left[...].astype(F32) + right[...].astype(F32)
        ).astype(BF16)
        column += width


class Group:
    thin = False

    def __init__(self, *chunks):
        self.chunks, self.rows, self.along = chunks, chunks[0].rows, chunks[0].along

    def back_second(self, tick):
        terms = []
        for chunk in self.chunks:
            terms += [chunk.total, after(chunk.from_rest, tick)]
        width = sum(chunk.total.shape[1] for chunk in self.chunks)
        self.total = pl.pallas_call(
            join_kernel,
            out_shape=shape((self.rows // 2, width), BF16),
            in_specs=[VMEM] * len(terms),
            out_specs=VMEM,
            compiler_params=params(),
            cost_estimate=SMALL_COST,
            name="join",
        )(*terms)
        self.other_second = self.along(2, self.total)

    def back_first(self, tick):
        self.other_second = after(self.other_second, tick)
        self.total = jnp.concatenate([self.other_second, self.total], axis=0)
        self.other = self.along(1, self.total)


def assemble_kernel(rows, widths, marks, counts, table, natural, total, other, *refs):
    weights, refs = refs[: counts[0]], refs[counts[0] :]
    gains, outs = refs[: counts[1]], refs[counts[1] :]
    me, y = place()
    z = lax.rem(lax.axis_index("dp") // 2, 2)
    half = rows // 2
    column = 0
    sums = [None] * counts[1]

    def blocks():
        for source, first in ((total, 1), (other, 0)):
            for second in range(2):
                y_of = y if first else 1 - y
                z_of = second if natural else (z if second else 1 - z)
                yield source, second * half, y_of, z_of

    for number, width in enumerate(widths):
        columns = slice(column, column + width)
        out = outs[number]
        for source, row, y_of, z_of in blocks():
            begin_row = pl.multiple_of(y_of * rows + z_of * half, 16)
            out[pl.ds(begin_row, half), :] = source[row : row + half, columns].astype(F32)
        column += width
        for which, weight, target in marks:
            if which == number:
                part = jnp.sum(
                    weights[weight][...].astype(F32) * out[...], axis=1, keepdims=True
                )
                sums[target] = part if sums[target] is None else sums[target] + part
    for number, (summed, gain) in enumerate(zip(sums, gains)):
        total_rows = jnp.broadcast_to(summed, (2 * rows, BLOCK)).T[0:1, :]
        whole = gain[...].reshape(1, D)
        mine = whole[:, 0:SHARD]
        for shard in range(1, SEQ):
            mine = jnp.where(me == shard, whole[:, shard * SHARD : (shard + 1) * SHARD], mine)
        outs[len(widths) + number][...] = (total_rows / mine).reshape(2 * rows)
    if table:
        for source, row, y_of, z_of in blocks():
            if natural and z_of:
                continue

            @pl.when((y_of == 0) if natural else (y_of == 0) & (z_of == 0))
            def store():
                outs[-1][...] = source[
                    row : row + BUCKETS // SEQ, column : column + H
                ].astype(F32)


def assemble(chunk, widths, marks=(), weights=(), gains=(), table=False):
    rows = chunk.rows
    out_shape = [shape((2 * rows, width), F32) for width in widths]
    out_shape += [shape((2 * rows,), F32) for _ in gains]
    if table:
        out_shape.append(shape((BUCKETS // SEQ, H), F32))
    operands = tuple(weights) + tuple(gains)
    return pl.pallas_call(
        functools.partial(
            assemble_kernel,
            rows,
            widths,
            marks,
            (len(weights), len(gains)),
            table,
            chunk.thin,
        ),
        out_shape=tuple(out_shape),
        in_specs=[VMEM] * (2 + len(operands)),
        out_specs=(VMEM,) * len(out_shape),
        compiler_params=params(),
        cost_estimate=SMALL_COST,
        name="assemble",
    )(chunk.total, chunk.other, *operands)


def per_device(
    groups,
    tokens,
    doc_lengths,
    query_weight,
    key_weight,
    value_weight,
    out_weight,
    gate_weight,
    up_weight,
    down_weight,
    proj_weight,
    attn_gain,
    ffn_gain,
    final_gain,
    bucket_bias_rows,
    embed_cotangent,
):
    tick = doc_lengths

    def across_x(mine):
        return exchange(after(mine, tick), "seq", 2, SEQ)

    def across_y(mine):
        return exchange(after(mine, tick), "dp", 1, groups)

    def across_core(mine):
        return exchange(after(mine, tick), "seq", 1, SEQ)

    def across_far(mine):
        return exchange(after(mine, tick), "seq", 3, SEQ)

    qkv_half = pack_first(tick, query_weight, key_weight, value_weight)
    qkv_x = across_x(qkv_half)
    tick = after(tick, qkv_half)
    blocks = pack_tokens(tick, tokens, embed_cotangent)
    block_x = across_x(blocks[2])
    block_far = across_far(blocks[3])
    block_core = across_core(blocks[1])
    tick = after(tick, blocks[0])
    qkv_own, out_own, gated_half_0, gated_half_1, down_rest = pack_rest(
        tick,
        query_weight,
        key_weight,
        value_weight,
        out_weight,
        proj_weight,
        gate_weight,
        up_weight,
        down_weight,
    )
    tick = after(tick, qkv_x, gated_half_0)
    qkv_y = across_y(qkv_x)
    qkv_cx = across_core(qkv_x)
    tick = after(tick, block_x, block_far, block_core)
    qkv_core = across_core(qkv_own)
    out_x = across_x(out_own)
    tok, cot, n1, n1t = first_norm(tick, (blocks[0], block_core, block_x, block_far), attn_gain)
    tick = after(tick, n1, qkv_y, qkv_cx)
    qkv_cy = across_core(qkv_y)
    tick = after(tick, qkv_cy, qkv_core, out_x)
    out_core = across_core(out_own)
    gated_x_0 = across_x(gated_half_0)
    gated_x_1 = across_x(gated_half_1)
    gate_core = across_core(gate_weight)
    qkv_pieces = (
        query_weight, key_weight, value_weight, qkv_core, qkv_x, qkv_y, qkv_cx, qkv_cy
    )
    qkv = qkv_project(tick, n1, qkv_pieces)
    pairs = H // 2
    third = pairs // 3
    tick = after(tick, qkv, gated_x_0, out_core, gate_core)
    gated_y_0 = across_y(gated_x_0)
    gated_cx_0 = across_core(gated_x_0)
    out_cx = across_core(out_x)
    down_x = across_x(down_rest)
    held = attention(tick, qkv, bucket_bias_rows, 0, third, ())
    tick = after(tick, held[0], gated_x_1, gated_cx_0, out_cx)
    gated_y_1 = across_y(gated_x_1)
    gated_cx_1 = across_core(gated_x_1)
    up_core = across_core(up_weight)
    held = attention(tick, qkv, bucket_bias_rows, third, third, held)
    tick = after(tick, held[0], gated_y_0, gated_cx_1, up_core)
    gated_cy_0 = across_core(gated_y_0)
    down_core = across_core(down_weight)
    et, linv, ot, mixed = attention(
        tick, qkv, bucket_bias_rows, 2 * third, pairs - 2 * third, held
    )
    tick = after(tick, mixed, gated_y_1, gated_cy_0, down_core)
    gated_cy_1 = across_core(gated_y_1)
    tick = after(tick, down_x)
    down_cx = across_core(down_x)
    tick = after(tick, gated_cy_1, down_cx)
    out_pieces = (out_own, out_core, out_x, out_cx)
    down_pieces = (down_weight, down_core, out_x, down_x, out_cx, down_cx)
    gated_pieces = (
        gate_weight, up_weight, gate_core, up_core,
        gated_x_0, gated_y_0, gated_cx_0, gated_cy_0,
        gated_x_1, gated_y_1, gated_cx_1, gated_cy_1,
    )
    hidden, n2t, gate_grad, up_grad, embedded, after_grad, fnt, *pair = feed_forward(
        tick, tok, mixed, cot, ffn_gain, final_gain, out_pieces, gated_pieces, down_pieces
    )

    chunk = functools.partial(Chunk, groups)
    down_sum = chunk(pair)
    tick = after(tick, down_sum.keep)
    down_sum.core(tick)
    gate_sum = chunk(gate_grads(tick, n2t, gate_grad))
    tick = after(tick, gate_sum.keep, down_sum.from_core)
    down_sum.x(tick)
    gate_sum.core(tick)
    *pair, hidden_grad, attn_in = up_grads(
        tick, ffn_gain, n2t, gate_grad, up_grad, hidden, after_grad, gated_pieces
    )
    up_sum = chunk(pair)
    tick = after(tick, up_sum.keep, gate_sum.from_core)
    gate_sum.x(tick)
    up_sum.core(tick)
    *pair, mixed_grad = out_grads(tick, ot, fnt, attn_in, cot, out_pieces)
    out_sum = chunk(pair)
    tick = after(tick, out_sum.keep, up_sum.from_core, down_sum.from_x)
    down_sum.first(tick)
    up_sum.x(tick)
    out_sum.core(tick)
    held = attention_back(tick, qkv, et, linv, ot, mixed_grad, 0, pairs // 2, ())
    tick = after(tick, held[0], out_sum.from_core, down_sum.from_first)
    down_sum.second(tick)
    out_sum.x(tick)
    dq, dk, dv, bias_part = attention_back(
        tick, qkv, et, linv, ot, mixed_grad, pairs // 2, pairs - pairs // 2, held
    )
    tick = after(tick, dq, gate_sum.from_x, down_sum.from_second)
    gate_sum.first(tick)
    down_sum.rest(tick)
    *pair, value_send, value_keep = qkv_grads(tick, bias_part, n1t, dq, dk, dv)
    first_sum, value_sum = chunk(pair), chunk((value_send, value_keep))
    tick = after(
        tick,
        first_sum.keep,
        gate_sum.from_first,
        up_sum.from_x,
        down_sum.from_rest,
        out_sum.from_x,
    )
    first_sum.core(tick)
    value_sum.core(tick)
    gate_sum.second(tick)
    up_sum.first(tick)
    down_sum.back_second(tick)
    blocks = token_grads(
        tick, attn_gain, embedded, dq, dk, dv, hidden_grad, tok, qkv_pieces
    )
    tick = after(
        tick,
        blocks[0],
        first_sum.from_core,
        value_sum.from_core,
        gate_sum.from_second,
        up_sum.from_first,
        down_sum.other_second,
    )
    first_sum.x(tick)
    gate_sum.rest(tick)
    up_sum.second(tick)
    down_sum.back_first(tick)
    tick = after(tick, marker(tick), up_sum.from_second)
    up_sum.rest(tick)
    value_sum.x(tick)
    tick = after(tick, marker(tick), gate_sum.from_rest, down_sum.other)
    out_sum.first(tick)
    tick = after(tick, marker(tick), up_sum.from_rest)
    gated_sum = Group(gate_sum, up_sum)
    gated_sum.back_second(tick)
    tick = after(tick, marker(tick), first_sum.from_x)
    first_sum.first(tick)
    block_x = across_x(blocks[2])
    block_far = across_far(blocks[3])
    tick = after(tick, marker(tick), out_sum.from_first, value_sum.from_x)
    value_sum.first(tick)
    out_sum.second(tick)
    tick = after(tick, marker(tick), first_sum.from_first, gated_sum.other_second)
    first_sum.second(tick)
    gated_sum.back_first(tick)
    tick = after(tick, marker(tick), value_sum.from_first, out_sum.from_second)
    value_sum.second(tick)
    out_sum.rest(tick)
    tick = after(tick, marker(tick), first_sum.from_second)
    first_sum.rest(tick)
    tick = after(tick, marker(tick), value_sum.from_second)
    value_sum.rest(tick)
    tick = after(
        tick, marker(tick), first_sum.from_rest, value_sum.from_rest, out_sum.from_rest, gated_sum.other, block_x, block_far
    )
    attn_sum = Group(out_sum, first_sum, value_sum)
    attn_sum.back_second(tick)
    block_core = across_core(blocks[1])
    tick = after(tick, marker(tick), attn_sum.other_second, block_core)
    attn_sum.back_first(tick)
    down_grad, = assemble(down_sum, (D,))
    gate_weight_grad, up_weight_grad, ffn_gain_grad = assemble(
        gated_sum, (FF, FF), ((0, 0, 0), (1, 1, 0)), (gate_weight, up_weight), (ffn_gain,)
    )
    embedded, tokens_grad = unpack((blocks[0], block_core, block_x, block_far))
    (
        out_grad,
        proj_grad,
        query_grad,
        key_grad,
        value_grad,
        final_gain_grad,
        attn_gain_grad,
        table_grad,
    ) = assemble(
        attn_sum,
        (D, PROJ, D, D, D),
        ((1, 0, 0), (2, 1, 1), (3, 2, 1), (4, 3, 1)),
        (proj_weight, query_weight, key_weight, value_weight),
        (final_gain, attn_gain),
        table=True,
    )
    return (
        embedded,
        tokens_grad,
        query_grad,
        key_grad,
        value_grad,
        out_grad,
        gate_weight_grad,
        up_weight_grad,
        down_grad,
        proj_grad,
        attn_gain_grad,
        ffn_gain_grad,
        final_gain_grad,
        table_grad,
    )


def solution(mesh):
    placed = (
        P("dp", "seq", None),
        P("dp"),
        P("seq", None),
        P("seq", None),
        P("seq", None),
        P("seq", None),
        P("seq", None),
        P("seq", None),
        P("seq", None),
        P("seq", None),
        P(),
        P(),
        P(),
        P(),
        P("dp", "seq", None),
    )
    return jax.shard_map(
        functools.partial(per_device, mesh.shape["dp"]),
        mesh=mesh,
        in_specs=placed,
        out_specs=(
            P("dp", "seq", None),
            P("dp", "seq", None),
            P("seq", None),
            P("seq", None),
            P("seq", None),
            P("seq", None),
            P("seq", None),
            P("seq", None),
            P("seq", None),
            P("seq", None),
            P("seq"),
            P("seq"),
            P("seq"),
            P("seq", None),
        ),
        check_vma=False,
    )
```

```python
import functools

import jax
import jax.numpy as jnp
import numpy as np
from jax import lax
from jax.experimental import pallas as pl
from jax.experimental.pallas import tpu as pltpu
from jax.sharding import PartitionSpec as P

D = 768
H = 12
HEAD = 64
FF = 2048
PROJ = 128
BUCKETS = 32
SLOT = 512
BLOCK = 128
SEQ = 4
SHARD = D // SEQ
HALF_FF = FF // 2
WIDE = D + PROJ
EPSILON = 1e-06
BIG_NEGATIVE = -1e30
GELU_A = 0.7978845608028654
GELU_B = 0.044715

F32 = jnp.float32
BF16 = jnp.bfloat16
VMEM = pl.BlockSpec(memory_space=pltpu.VMEM)
SMEM = pl.BlockSpec(memory_space=pltpu.SMEM)
ANY = pl.BlockSpec(memory_space=pl.ANY)
MIB = 1 << 20


def shape(dims, kind):
    return jax.ShapeDtypeStruct(dims, kind)


def params(wide=False):
    return pltpu.CompilerParams(vmem_limit_bytes=(58 if wide else 20) * MIB)


COST = pl.CostEstimate(flops=90000000000, bytes_accessed=300000000, transcendentals=0)
SMALL_COST = pl.CostEstimate(flops=1, bytes_accessed=1, transcendentals=0)


def bucket_of(relative):
    distance = np.abs(relative)
    scaled = np.log(np.maximum(distance, 1) / 8.0) / np.log(16.0) * 8.0
    far_bucket = np.minimum(8 + scaled.astype(np.int64), 15)
    return (relative > 0) * 16 + np.where(distance < 8, distance, far_bucket)


def skew_buckets():
    lanes = (np.arange(SLOT) + SLOT // 2) % SLOT - SLOT // 2
    relative = np.arange(8)[:, None] - lanes[None, :]
    return bucket_of(relative).astype(np.int32)


def table_indicator():
    lanes = (np.arange(SLOT) + SLOT // 2) % SLOT - SLOT // 2
    buckets = np.concatenate([bucket_of(-lanes), np.full(BLOCK, 15), np.full(BLOCK, 31)])
    here = BUCKETS // SEQ
    place = (buckets // here) * SHARD + buckets % here
    return (place[:, None] == np.arange(D)[None, :]).astype(np.float32)


def dot(left, right):
    return jnp.dot(left, right, preferred_element_type=F32)


def dot_t(left, right):
    return lax.dot_general(left, right, (((1,), (1,)), ((), ())), preferred_element_type=F32)


def place():
    return lax.axis_index("seq"), lax.rem(lax.axis_index("dp"), 2)


def relative_starts(rows, natural=False):
    me, y = place()
    z = lax.rem(lax.axis_index("dp") // 2, 2)
    bits = (me & 1, me >> 1, y, z)
    block = rows // 16
    starts = []
    for number in range(16):
        own = [(number >> shift) & 1 for shift in (3, 2, 1, 0)]
        core, x, first, second = (b if o else 1 - b for b, o in zip(bits, own))
        if natural:
            second = own[3]
        place_of = ((x * 2 + core) * 2 + first) * 2 + second
        starts.append(pl.multiple_of(place_of * block, 16))
    return block, starts


def begin(copies):
    for copy in copies:
        copy.start()
    return copies


def finish(copies):
    for copy in copies:
        copy.wait()


def run_all(copies):
    finish(begin(copies))


class Copies:
    def __init__(self, sems):
        self.sems, self.used = sems, 0

    def __call__(self, source, target):
        copy = pltpu.make_async_copy(source, target, self.sems.at[self.used])
        self.used += 1
        copy.start()
        return copy


def pieces_of(rows, plan, refs, target, sems, first=0):
    me, y = place()
    half = rows // 2
    starts = (
        me * rows,
        (me ^ 1) * rows,
        (me ^ 2) * rows + y * half,
        (me ^ 2) * rows + (1 - y) * half,
        (me ^ 3) * rows + y * half,
        (me ^ 3) * rows + (1 - y) * half,
        (me ^ 2) * rows,
        (me ^ 3) * rows,
    )
    copies = []
    for number, (ref, piece, source, to, width, *some) in enumerate(plan):
        first_row, skip, size = some or (0, 0, half if 2 <= piece < 6 else rows)
        copies.append(
            pltpu.make_async_copy(
                refs[ref].at[pl.ds(first_row, size), pl.ds(source, width)],
                target.at[
                    pl.ds(pl.multiple_of(starts[piece] + skip, 16), size), pl.ds(to, width)
                ],
                sems.at[first + number],
            )
        )
    return copies


QKV_PLANS = tuple(
    ((number, 0, 0, number * D, D),)
    + tuple((2 + piece, piece, number * D, number * D, D) for piece in range(1, 6))
    for number in range(3)
)
OUT_PLAN = tuple((ref, piece, 0, 0, WIDE) for ref, piece in enumerate((0, 1, 6, 7)))
DOWN_SHARD = FF // SEQ
EARLY = 64
DOWN_PLAN = (
    (0, 0, 0, 0, D),
    (1, 1, 0, 0, D),
    (2, 6, 0, 0, D, SHARD, 0, EARLY),
    (3, 6, 0, 0, D, 0, EARLY, DOWN_SHARD - EARLY),
    (4, 7, 0, 0, D, SHARD, 0, EARLY),
    (5, 7, 0, 0, D, 0, EARLY, DOWN_SHARD - EARLY),
)


def gated_plan(part):
    column = part * HALF_FF
    parts = [(4 + 4 * part + number, piece) for number, piece in enumerate((2, 3, 4, 5))]
    return (
        (0, 0, column, column, HALF_FF),
        (1, 0, column, FF + column, HALF_FF),
        (2, 1, column, column, HALF_FF),
        (3, 1, column, FF + column, HALF_FF),
    ) + tuple(
        (ref, piece, number * HALF_FF, number * FF + column, HALF_FF)
        for ref, piece in parts
        for number in range(2)
    )


GATED_PLANS = (gated_plan(0), gated_plan(1))


def relative_copies(source, target, sems, natural=False):
    block, starts = relative_starts(source.shape[0], natural)
    return [
        pltpu.make_async_copy(
            source.at[pl.ds(begin, block), :],
            target.at[pl.ds(number * block, block), :],
            sems.at[number],
        )
        for number, begin in enumerate(starts)
    ]


def inverse_rms(values):
    return lax.rsqrt(jnp.mean(values * values, axis=-1, keepdims=True) + EPSILON)


def norm_backward(values, gain, incoming):
    r = inverse_rms(values)
    weighted = gain * incoming
    inner = jnp.mean(weighted * values, axis=-1, keepdims=True)
    return r * weighted - values * (r * r * r * inner)


def pack_first_kernel(lens, q, k, v, qkv_half, sems):
    _, y = place()
    half = SHARD // 2
    rows = pl.ds(pl.multiple_of(y * half, 16), half)
    run_all(
        [
            pltpu.make_async_copy(
                weight.at[rows, :], qkv_half.at[:, pl.ds(number * D, D)], sems.at[number]
            )
            for number, weight in enumerate((q, k, v))
        ]
    )


def pack_first(lens, q, k, v):
    return pl.pallas_call(
        pack_first_kernel,
        out_shape=shape((SHARD // 2, 3 * D), BF16),
        in_specs=[SMEM] + [ANY] * 3,
        out_specs=VMEM,
        scratch_shapes=[pltpu.SemaphoreType.DMA((3,))],
        compiler_params=params(wide=True),
        cost_estimate=COST,
        name="pack_first",
    )(lens, q, k, v)


def pack_tokens_kernel(lens, tokens, cot, *refs):
    blocks, sems = refs[:4], refs[4]
    me, _ = place()
    pairs = []
    for flip, block in enumerate(blocks):
        pairs.append((tokens.at[me ^ flip], block.at[:, pl.ds(0, D)]))
        pairs.append((cot.at[me ^ flip], block.at[:, pl.ds(D, PROJ)]))
    run_all([pltpu.make_async_copy(a, b, sems.at[i]) for i, (a, b) in enumerate(pairs)])


def pack_tokens(lens, tokens, cot):
    return pl.pallas_call(
        pack_tokens_kernel,
        out_shape=(shape((BLOCK, WIDE), BF16),) * 4,
        in_specs=[SMEM] + [ANY] * 2,
        out_specs=(VMEM,) * 4,
        scratch_shapes=[pltpu.SemaphoreType.DMA((8,))],
        compiler_params=params(wide=True),
        cost_estimate=COST,
        name="pack_tokens",
    )(lens, tokens, cot)


def pack_rest_kernel(
    lens, q, k, v, out, proj, gate, up, down, qkv, out_own, part_0, part_1, down_rest, sems
):
    _, y = place()
    half = SHARD // 2
    rows = pl.ds(pl.multiple_of(y * half, 16), half)
    pairs = [(w, qkv.at[:, pl.ds(number * D, D)]) for number, w in enumerate((q, k, v))]
    pairs.append((out, out_own.at[pl.ds(0, SHARD), pl.ds(0, D)]))
    pairs.append((proj, out_own.at[pl.ds(0, SHARD), pl.ds(D, PROJ)]))
    pairs.append((down.at[pl.ds(0, EARLY), :], out_own.at[pl.ds(SHARD, EARLY), pl.ds(0, D)]))
    pairs.append((down.at[pl.ds(EARLY, DOWN_SHARD - EARLY), :], down_rest))
    for number, part in enumerate((part_0, part_1)):
        columns = pl.ds(number * HALF_FF, HALF_FF)
        pairs.append((gate.at[rows, columns], part.at[:, pl.ds(0, HALF_FF)]))
        pairs.append((up.at[rows, columns], part.at[:, pl.ds(HALF_FF, HALF_FF)]))
    run_all([pltpu.make_async_copy(a, b, sems.at[i]) for i, (a, b) in enumerate(pairs)])


def pack_rest(lens, q, k, v, out, proj, gate, up, down):
    half = SHARD // 2
    return pl.pallas_call(
        pack_rest_kernel,
        out_shape=(shape((SHARD, 3 * D), BF16), shape((SHARD + EARLY, WIDE), BF16))
        + (shape((half, FF), BF16),) * 2
        + (shape((DOWN_SHARD - EARLY, D), BF16),),
        in_specs=[SMEM] + [ANY] * 8,
        out_specs=(VMEM,) * 5,
        scratch_shapes=[pltpu.SemaphoreType.DMA((11,))],
        compiler_params=params(wide=True),
        cost_estimate=COST,
        name="pack_rest",
    )(lens, q, k, v, out, proj, gate, up, down)


def first_norm_kernel(lens, own, from_core, from_x, from_far, gain, tok, cot, n1, n1t, held, sems):
    me, _ = place()
    run_all(
        [
            pltpu.make_async_copy(
                piece,
                held.at[pl.ds(pl.multiple_of((me ^ flip) * BLOCK, BLOCK), BLOCK), :],
                sems.at[flip],
            )
            for flip, piece in enumerate((own, from_core, from_x, from_far))
        ]
    )
    scale = gain[...].reshape(1, D)
    for block in range(SLOT // BLOCK):
        rows = pl.ds(block * BLOCK, BLOCK)
        here = held[rows, 0:D]
        tok[rows, :] = here
        cot[rows, :] = held[rows, D : D + PROJ]
        values = here.astype(F32)
        normed = (values * inverse_rms(values) * scale).astype(BF16)
        n1[rows, :] = normed
        n1t[:, rows] = normed.T


def first_norm(lens, blocks, gain):
    return pl.pallas_call(
        first_norm_kernel,
        out_shape=(
            shape((SLOT, D), BF16),
            shape((SLOT, PROJ), BF16),
            shape((SLOT, D), BF16),
            shape((D, SLOT), BF16),
        ),
        in_specs=[SMEM, ANY, ANY, ANY, ANY, VMEM],
        out_specs=(VMEM,) * 4,
        scratch_shapes=[pltpu.VMEM((SLOT, WIDE), BF16), pltpu.SemaphoreType.DMA((4,))],
        compiler_params=params(wide=True),
        cost_estimate=COST,
        name="first_norm",
    )(lens, *blocks, gain)


def qkv_kernel(lens, n1, *refs):
    pieces, (out, weight, sems) = refs[:8], refs[8:]
    group = pl.program_id(0)

    def copies(number):
        return pieces_of(SHARD, QKV_PLANS[number], pieces, weight, sems, 6 * number)

    @pl.when(group == 0)
    def start():
        for number in range(3):
            begin(copies(number))

    for number in range(3):

        @pl.when(group == number)
        def ready():
            finish(copies(number))

    for tile in range(D // 256):
        columns = pl.ds(pl.multiple_of(group * D + tile * 256, 256), 256)
        out[:, tile * 256 : (tile + 1) * 256] = dot(n1[...], weight[:, columns]).astype(BF16)


def qkv_project(lens, n1, pieces):
    return pl.pallas_call(
        qkv_kernel,
        grid=(3,),
        out_shape=shape((SLOT, 3 * D), BF16),
        in_specs=[SMEM, VMEM] + [ANY] * 8,
        out_specs=pl.BlockSpec((SLOT, D), lambda i: (0, i)),
        scratch_shapes=[pltpu.VMEM((D, 3 * D), BF16), pltpu.SemaphoreType.DMA((18,))],
        compiler_params=params(wide=True),
        cost_estimate=COST,
        name="qkv_project",
    )(lens, n1, *pieces)


HALF_Q = 512


def attention_kernel(first, lens, q, k, v, rows_of_bias, buckets, *refs):
    et, linv, ot, o, bias = refs[-5:]
    me, _ = place()
    length = lens[me]
    pair = pl.program_id(0) + first
    k_pair = k[...]
    vt = v[...].T
    qt = q[...].T
    row_in_pair = lax.broadcasted_iota(jnp.int32, (2 * HEAD, SLOT), 0)
    key_index = lax.broadcasted_iota(jnp.int32, (SLOT, HALF_Q), 0)
    for head in range(2):
        base = jnp.zeros((8, SLOT), F32)
        for bucket in range(BUCKETS):
            base = jnp.where(buckets[...] == bucket, rows_of_bias[bucket, 2 * pair + head], base)
        for group in range(BLOCK // 8):
            bias[pl.ds(group * 8, 8), :] = pltpu.roll(base, 8 * group, 1) if group else base
        below = rows_of_bias[15, 2 * pair + head]
        above = rows_of_bias[31, 2 * pair + head]
        in_head = (row_in_pair >= HEAD * head) & (row_in_pair < HEAD * (head + 1))
        qt_head = jnp.where(in_head, qt, jnp.zeros_like(qt))
        for part in range(SLOT // HALF_Q):
            raw = dot(k_pair, qt_head[:, part * HALF_Q : (part + 1) * HALF_Q])
            rows = []
            for key_block in range(4):
                cells = []
                for sub in range(HALF_Q // BLOCK):
                    query_block = part * (HALF_Q // BLOCK) + sub
                    cell = raw[
                        key_block * BLOCK : (key_block + 1) * BLOCK,
                        sub * BLOCK : (sub + 1) * BLOCK,
                    ]
                    apart = key_block - query_block
                    if apart >= 2:
                        cell = cell + above
                    elif apart <= -2:
                        cell = cell + below
                    else:
                        lane = (-apart * BLOCK) % SLOT
                        cell = cell + bias[:, lane : lane + BLOCK]
                    cells.append(cell)
                rows.append(jnp.concatenate(cells, axis=1))
            scores = jnp.concatenate(rows, axis=0)
            scores = jnp.where(key_index < length, scores, BIG_NEGATIVE)
            top = jnp.max(scores, axis=0, keepdims=True)
            weights = jnp.exp(scores - top)
            inverse = 1.0 / jnp.sum(weights, axis=0, keepdims=True)
            low = weights.astype(BF16)
            columns = pl.ds(part * HALF_Q, HALF_Q)
            et[head, :, columns] = low
            linv[head, :, columns] = inverse
            mixed = dot(vt[head * HEAD : (head + 1) * HEAD, :], low) * inverse
            ot[pl.ds(head * HEAD, HEAD), columns] = mixed.astype(BF16)
    o[...] = ot[...].T


def attention(lens, qkv, rows_of_bias, first, count, held):
    pair = 2 * HEAD
    pairs = H // 2
    return pl.pallas_call(
        functools.partial(attention_kernel, first),
        grid=(count,),
        out_shape=(
            shape((H, SLOT, SLOT), BF16),
            shape((H, 1, SLOT), F32),
            shape((D, SLOT), BF16),
            shape((SLOT, D), BF16),
        ),
        in_specs=[
            SMEM,
            pl.BlockSpec((SLOT, pair), lambda i: (0, first + i)),
            pl.BlockSpec((SLOT, pair), lambda i: (0, pairs + first + i)),
            pl.BlockSpec((SLOT, pair), lambda i: (0, 2 * pairs + first + i)),
            SMEM,
            pl.BlockSpec((8, SLOT), lambda i: (0, 0)),
        ]
        + [ANY] * len(held),
        out_specs=(
            pl.BlockSpec((2, SLOT, SLOT), lambda i: (first + i, 0, 0)),
            pl.BlockSpec((2, 1, SLOT), lambda i: (first + i, 0, 0)),
            pl.BlockSpec((pair, SLOT), lambda i: (first + i, 0)),
            pl.BlockSpec((SLOT, pair), lambda i: (0, first + i)),
        ),
        input_output_aliases={6 + i: i for i in range(len(held))},
        scratch_shapes=[pltpu.VMEM((BLOCK, SLOT), F32)],
        compiler_params=params(wide=True),
        cost_estimate=COST,
        name="attention",
    )(lens, qkv, qkv, qkv, rows_of_bias, jnp.asarray(skew_buckets()), *held)


def feed_forward_kernel(lens, ffn_gain, final_gain, tok, mixed, cot, *refs):
    out_pieces, gated_pieces, down_pieces, refs = refs[:4], refs[4:16], refs[16:22], refs[22:]
    hidden_out, n2t_out, gate_out, up_out, embedded_out, after_out, fnt_out = refs[:7]
    send_out, keep_out = refs[7:9]
    w_out, w_gated, w_down, tok_v, mixed_v, cot_v, hidden, n2, n2t, inner, innert = refs[9:20]
    slope, level, embedded, after_grad, down_in, fnt, send, keep = refs[20:28]
    out_sems, gated_sems, down_sems, in_sems, done_sems = refs[28:]
    load, store = Copies(in_sems), Copies(done_sems)

    loads = begin(pieces_of(SHARD, OUT_PLAN, out_pieces, w_out, out_sems))
    loads += [load(mixed, mixed_v), load(tok, tok_v), load(cot, cot_v)]
    gated_loads = [
        begin(pieces_of(SHARD, plan, gated_pieces, w_gated, gated_sems, 12 * number))
        for number, plan in enumerate(GATED_PLANS)
    ]
    down_loads = begin(pieces_of(FF // SEQ, DOWN_PLAN, down_pieces, w_down, down_sems))
    stores = []

    finish(loads)
    scale = ffn_gain[...].reshape(1, D)
    for block in range(2):
        rows = pl.ds(block * 256, 256)
        values = tok_v[rows, :].astype(F32) + dot(mixed_v[rows, :], w_out[:, 0:D])
        hidden[rows, :] = values
        normed = (values * inverse_rms(values) * scale).astype(BF16)
        n2[rows, :] = normed
        n2t[:, rows] = normed.T
    stores.append(store(hidden, hidden_out))
    size, starts = relative_starts(D)
    for number, begin_row in enumerate(starts):
        stores.append(
            store(n2t.at[pl.ds(begin_row, size), :], n2t_out.at[pl.ds(number * size, size), :])
        )

    me, y = place()
    z = lax.rem(lax.axis_index("dp") // 2, 2)

    def step(tile, carry):
        columns = pl.ds(pl.multiple_of(tile * 512, 512), 512)
        g = dot(n2[...], w_gated[:, columns])
        u = dot(n2[...], w_gated[:, pl.ds(pl.multiple_of(FF + tile * 512, 512), 512)])
        square = g * g
        t = jnp.tanh(GELU_A * g * (1.0 + GELU_B * square))
        half_up = 0.5 * (1.0 + t)
        activated = g * half_up
        derivative = half_up + 0.5 * g * (1.0 - t * t) * (GELU_A * (1.0 + 3 * GELU_B * square))
        value = (activated * u).astype(BF16)
        inner[:, columns] = value
        slope[:, columns] = (derivative * u).astype(BF16)
        level[:, columns] = activated.astype(BF16)
        core_own = (lax.rem(tile, 2) == lax.rem(me, 2)).astype(jnp.int32)
        x_own = (tile // 2 == me // 2).astype(jnp.int32)
        target = (core_own * 2 + x_own) * 512
        turned = value.T
        for number in range(4):
            y_own = (number >> 1 == y).astype(jnp.int32)
            z_own = ((number & 1) == z).astype(jnp.int32)
            row = pl.multiple_of(target + y_own * 256 + z_own * BLOCK, BLOCK)
            innert[pl.ds(row, BLOCK), :] = turned[number * BLOCK : (number + 1) * BLOCK, :]
        return carry

    for part in range(2):
        finish(gated_loads[part])
        lax.fori_loop(2 * part, 2 * part + 2, step, 0)

    finish(down_loads)
    scale = final_gain[...].reshape(1, D)
    for block in range(2):
        rows = pl.ds(block * 256, 256)
        values = hidden[rows, :] + dot(inner[rows, :], w_down[...])
        normed = (values * inverse_rms(values) * scale).astype(BF16)
        fnt[:, rows] = normed.T
        embedded[rows, :] = dot(normed, w_out[:, D:WIDE]).astype(BF16)
        gradient = norm_backward(values, scale, dot_t(cot_v[rows, :], w_out[:, D:WIDE]))
        after_grad[rows, :] = gradient
        down_in[rows, :] = gradient.astype(BF16)
    for source, target in ((after_grad, after_out), (embedded, embedded_out), (fnt, fnt_out)):
        stores.append(store(source, target))

    for number, (part, target) in enumerate(((send, send_out), (keep, keep_out))):

        def grad(tile, carry):
            rows = pl.ds(pl.multiple_of(tile * 256, 256), 256)
            source = pl.ds(pl.multiple_of(number * (FF // 2) + tile * 256, 256), 256)
            part[rows, :] = dot(innert[source, :], down_in[...]).astype(BF16)
            return carry

        lax.fori_loop(0, FF // 2 // 256, grad, 0)
        stores.append(store(part, target))

    def back(tile, carry):
        columns = pl.ds(pl.multiple_of(tile * 512, 512), 512)
        incoming = dot_t(down_in[...], w_down[columns, :])
        slope[:, columns] = (incoming * slope[:, columns].astype(F32)).astype(BF16)
        level[:, columns] = (incoming * level[:, columns].astype(F32)).astype(BF16)
        return carry

    lax.fori_loop(0, FF // 512, back, 0)
    stores += [store(slope, gate_out), store(level, up_out)]
    finish(stores)


def feed_forward(lens, tok, mixed, cot, ffn_gain, final_gain, out_pieces, gated_pieces, down_pieces):
    wide, tall, full = (SLOT, D), (D, SLOT), (SLOT, FF)
    pieces = tuple(out_pieces) + tuple(gated_pieces) + tuple(down_pieces)
    return pl.pallas_call(
        feed_forward_kernel,
        out_shape=(
            shape(wide, F32),
            shape(tall, BF16),
            shape(full, BF16),
            shape(full, BF16),
            shape((SLOT, PROJ), BF16),
            shape(wide, F32),
            shape(tall, BF16),
            shape((FF // 2, D), BF16),
            shape((FF // 2, D), BF16),
        ),
        in_specs=[SMEM, VMEM, VMEM] + [ANY] * (3 + len(pieces)),
        out_specs=(ANY,) * 9,
        scratch_shapes=[
            pltpu.VMEM((D, WIDE), BF16),
            pltpu.VMEM((D, 2 * FF), BF16),
            pltpu.VMEM((FF, D), BF16),
            pltpu.VMEM(wide, BF16),
            pltpu.VMEM(wide, BF16),
            pltpu.VMEM((SLOT, PROJ), BF16),
            pltpu.VMEM(wide, F32),
            pltpu.VMEM(wide, BF16),
            pltpu.VMEM(tall, BF16),
            pltpu.VMEM(full, BF16),
            pltpu.VMEM((FF, SLOT), BF16),
            pltpu.VMEM(full, BF16),
            pltpu.VMEM(full, BF16),
            pltpu.VMEM((SLOT, PROJ), BF16),
            pltpu.VMEM(wide, F32),
            pltpu.VMEM(wide, BF16),
            pltpu.VMEM(tall, BF16),
            pltpu.VMEM((FF // 2, D), BF16),
            pltpu.VMEM((FF // 2, D), BF16),
            pltpu.SemaphoreType.DMA((4,)),
            pltpu.SemaphoreType.DMA((24,)),
            pltpu.SemaphoreType.DMA((6,)),
            pltpu.SemaphoreType.DMA((3,)),
            pltpu.SemaphoreType.DMA((24,)),
        ],
        compiler_params=params(wide=True),
        cost_estimate=COST,
        name="feed_forward",
    )(lens, ffn_gain, final_gain, tok, mixed, cot, *pieces)


def row_grads(left, right, halves, column=0, loads=(), store=None, outs=()):
    half = left.shape[0] // 2
    width = right.shape[1]
    size = 1024 if width % 1024 == 0 else width
    stores = []
    for tile in range(width // size):
        if loads:
            loads[tile].wait()
        target = slice(column + tile * size, column + (tile + 1) * size)
        both = dot(left[...], right[:, tile * size : (tile + 1) * size]).astype(BF16)
        for number, part in enumerate(halves):
            part[:, target] = both[number * half : (number + 1) * half, :]
            stores.append(store(part.at[:, target], outs[number].at[:, target]))
    return stores


def tile_loads(load, source, target, size=1024):
    return [
        load(source.at[:, pl.ds(begin_at, size)], target.at[:, pl.ds(begin_at, size)])
        for begin_at in range(0, source.shape[1], size)
    ]


def gate_grad_kernel(lens, n2t, gate_grad, send_out, keep_out, n2t_v, gate_v, send, keep, *sems):
    load, store = Copies(sems[0]), Copies(sems[1])
    first = load(n2t, n2t_v)
    loads = tile_loads(load, gate_grad, gate_v)
    first.wait()
    finish(row_grads(n2t_v, gate_v, (send, keep), 0, loads, store, (send_out, keep_out)))


def gate_grads(lens, n2t, gate_grad):
    part = (D // 2, FF)
    return pl.pallas_call(
        gate_grad_kernel,
        out_shape=(shape(part, BF16),) * 2,
        in_specs=[SMEM] + [ANY] * 2,
        out_specs=(ANY,) * 2,
        scratch_shapes=[
            pltpu.VMEM((D, SLOT), BF16),
            pltpu.VMEM((SLOT, FF), BF16),
            pltpu.VMEM(part, BF16),
            pltpu.VMEM(part, BF16),
            pltpu.SemaphoreType.DMA((3,)),
            pltpu.SemaphoreType.DMA((4,)),
        ],
        compiler_params=params(wide=True),
        cost_estimate=COST,
        name="gate_grads",
    )(lens, n2t, gate_grad)


def up_grad_kernel(lens, gain, n2t, gate_grad, up_grad, hidden, after_grad, *refs):
    pieces, outs, refs = refs[:12], refs[12:16], refs[16:]
    weight, n2t_v, gate_v, up_v, hidden_v, after_v, send, keep, grad, attn_in = refs[:10]
    sems, in_sems, done_sems = refs[10:]
    load, store = Copies(in_sems), Copies(done_sems)
    first = load(n2t, n2t_v)
    loads = tile_loads(load, up_grad, up_v)
    gate_load = load(gate_grad, gate_v)
    plan = sum(GATED_PLANS, ())
    gate_plan = tuple(entry for entry in plan if entry[3] < FF)
    up_plan = tuple(entry for entry in plan if entry[3] >= FF)
    gate_pieces = begin(pieces_of(SHARD, gate_plan, pieces, weight, sems))
    up_pieces = begin(pieces_of(SHARD, up_plan, pieces, weight, sems, len(gate_plan)))
    later = [load(hidden, hidden_v), load(after_grad, after_v)]
    first.wait()
    stores = row_grads(n2t_v, up_v, (send, keep), 0, loads, store, outs[0:2])
    gate_load.wait()
    finish(gate_pieces)
    for block in range(2):
        rows = pl.ds(block * 256, 256)
        grad[rows, :] = dot_t(gate_v[rows, :], weight[:, 0:FF])
    finish(up_pieces)
    finish(later)
    scale = gain[...].reshape(1, D)
    for block in range(2):
        rows = pl.ds(block * 256, 256)
        incoming = grad[rows, :] + dot_t(up_v[rows, :], weight[:, FF:])
        gradient = norm_backward(hidden_v[rows, :], scale, incoming) + after_v[rows, :]
        grad[rows, :] = gradient
        attn_in[rows, :] = gradient.astype(BF16)
    stores += [store(attn_in, outs[3]), store(grad, outs[2])]
    finish(stores)


def up_grads(lens, gain, n2t, gate_grad, up_grad, hidden, after_grad, pieces):
    full, part, wide = (SLOT, FF), (D // 2, FF), (SLOT, D)
    return pl.pallas_call(
        up_grad_kernel,
        out_shape=(shape(part, BF16),) * 2 + (shape(wide, F32), shape(wide, BF16)),
        in_specs=[SMEM, VMEM] + [ANY] * 17,
        out_specs=(ANY,) * 4,
        scratch_shapes=[
            pltpu.VMEM((D, 2 * FF), BF16),
            pltpu.VMEM((D, SLOT), BF16),
            pltpu.VMEM(full, BF16),
            pltpu.VMEM(full, BF16),
            pltpu.VMEM(wide, F32),
            pltpu.VMEM(wide, F32),
            pltpu.VMEM(part, BF16),
            pltpu.VMEM(part, BF16),
            pltpu.VMEM(wide, F32),
            pltpu.VMEM(wide, BF16),
            pltpu.SemaphoreType.DMA((24,)),
            pltpu.SemaphoreType.DMA((6,)),
            pltpu.SemaphoreType.DMA((6,)),
        ],
        compiler_params=params(wide=True),
        cost_estimate=COST,
        name="up_grads",
    )(lens, gain, n2t, gate_grad, up_grad, hidden, after_grad, *pieces)


def out_grad_kernel(lens, ot, fnt, attn_in, cot, *refs):
    pieces, outs, refs = refs[:4], refs[4:7], refs[7:]
    weight, left, proj_left, attn_v, cot_v, send, keep, mixed = refs[:8]
    sems, left_sems, proj_sems, in_sems, done_sems = refs[8:]
    load, store = Copies(in_sems), Copies(done_sems)
    loads = [load(attn_in, attn_v)]
    loads += begin(relative_copies(ot, left, left_sems))
    pieces = begin(pieces_of(SHARD, OUT_PLAN, pieces, weight, sems))
    later = [load(cot, cot_v)]
    later += begin(relative_copies(fnt, proj_left, proj_sems))
    finish(loads)
    stores = row_grads(left, attn_v, (send, keep), 0, (), store, outs[0:2])
    finish(later)
    stores += row_grads(proj_left, cot_v, (send, keep), D, (), store, outs[0:2])
    finish(pieces)
    mixed[...] = dot_t(attn_v[...], weight[:, 0:D]).astype(BF16)
    stores.append(store(mixed, outs[2]))
    finish(stores)


def out_grads(lens, ot, fnt, attn_in, cot, pieces):
    return pl.pallas_call(
        out_grad_kernel,
        out_shape=(shape((D // 2, WIDE), BF16),) * 2 + (shape((SLOT, D), BF16),),
        in_specs=[SMEM] + [ANY] * 8,
        out_specs=(ANY,) * 3,
        scratch_shapes=[
            pltpu.VMEM((D, WIDE), BF16),
            pltpu.VMEM((D, SLOT), BF16),
            pltpu.VMEM((D, SLOT), BF16),
            pltpu.VMEM((SLOT, D), BF16),
            pltpu.VMEM((SLOT, PROJ), BF16),
            pltpu.VMEM((D // 2, WIDE), BF16),
            pltpu.VMEM((D // 2, WIDE), BF16),
            pltpu.VMEM((SLOT, D), BF16),
            pltpu.SemaphoreType.DMA((4,)),
            pltpu.SemaphoreType.DMA((16,)),
            pltpu.SemaphoreType.DMA((16,)),
            pltpu.SemaphoreType.DMA((2,)),
            pltpu.SemaphoreType.DMA((5,)),
        ],
        compiler_params=params(wide=True),
        cost_estimate=COST,
        name="out_grads",
    )(lens, ot, fnt, attn_in, cot, *pieces)


def qkv_grad_kernel(lens, table, indicator, n1t, dq, dk, dv, *refs):
    outs, left, dq_v, dk_v, dv_v = refs[:4], refs[4], refs[5], refs[6], refs[7]
    send, keep, value_send, value_keep, small, left_sems, in_sems, done_sems = refs[8:]
    load, store = Copies(in_sems), Copies(done_sems)
    first = [load(dq, dq_v)] + begin(relative_copies(n1t, left, left_sems))
    second, third = load(dk, dk_v), load(dv, dv_v)
    finish(first)
    stores = row_grads(left, dq_v, (send, keep), 0, (), store, outs[0:2])
    stores += row_grads(left, dk_v, (send, keep), D, (second,), store, outs[0:2])
    by_lane = jnp.concatenate([table[pair] for pair in range(H // 2)], axis=0)
    high = by_lane.astype(BF16)
    low = (by_lane - high.astype(F32)).astype(BF16)
    by_bucket = dot(high, indicator[...]) + dot(low, indicator[...])
    small[...] = jnp.concatenate([by_bucket, jnp.zeros((PROJ - H, D), F32)], axis=0).T
    block, starts = relative_starts(D)
    for number, row in enumerate(starts):
        target = value_keep if number >= 8 else value_send
        target[pl.ds((number & 7) * block, block), D:WIDE] = small[pl.ds(row, block), :].astype(
            BF16
        )
    columns = pl.ds(D, PROJ)
    for number, part in enumerate((value_send, value_keep)):
        stores.append(store(part.at[:, columns], outs[2 + number].at[:, columns]))
    stores += row_grads(left, dv_v, (value_send, value_keep), 0, (third,), store, outs[2:4])
    finish(stores)


def qkv_grads(lens, table, n1t, dq, dk, dv):
    pair, single = (D // 2, 2 * D), (D // 2, WIDE)
    return pl.pallas_call(
        qkv_grad_kernel,
        out_shape=(shape(pair, BF16),) * 2 + (shape(single, BF16),) * 2,
        in_specs=[SMEM, VMEM, VMEM] + [ANY] * 4,
        out_specs=(ANY,) * 4,
        scratch_shapes=[pltpu.VMEM((D, SLOT), BF16)]
        + [pltpu.VMEM((SLOT, D), BF16)] * 3
        + [pltpu.VMEM(pair, BF16)] * 2
        + [pltpu.VMEM(single, BF16)] * 2
        + [
            pltpu.VMEM((D, PROJ), F32),
            pltpu.SemaphoreType.DMA((16,)),
            pltpu.SemaphoreType.DMA((3,)),
            pltpu.SemaphoreType.DMA((8,)),
        ],
        compiler_params=params(wide=True),
        cost_estimate=COST,
        name="qkv_grads",
    )(lens, table, jnp.asarray(table_indicator(), dtype=BF16), n1t, dq, dk, dv)


def attention_back_kernel(lens, q, k, v, et, linv, ot, do, *refs):
    dq, dk, dv, bias_grad, dqt, near = refs[-6:]
    lane_in_pair = lax.broadcasted_iota(jnp.int32, (SLOT, 2 * HEAD), 1)
    q_pair, v_pair = q[...], v[...]
    kt = k[...].T
    out_gradt = do[...].astype(F32).T
    scaled = []
    deltas = []
    for head in range(2):
        rows = slice(head * HEAD, (head + 1) * HEAD)
        low = (out_gradt[rows, :] * linv[head]).astype(BF16)
        scaled.append(low)
        deltas.append(
            jnp.sum(low.astype(F32) * ot[rows, :].astype(F32), axis=0, keepdims=True)
        )
    scaled_pair = jnp.concatenate(scaled, axis=0).T
    zeros = jnp.zeros((HEAD, SLOT), BF16)
    key_total = jnp.zeros((SLOT, 2 * HEAD), F32)
    value_total = jnp.zeros((SLOT, 2 * HEAD), F32)
    row_of_eight = lax.broadcasted_iota(jnp.int32, (8, SLOT), 0)
    for head in range(2):
        in_head = (lane_in_pair >= head * HEAD) & (lane_in_pair < (head + 1) * HEAD)
        q_head = jnp.where(in_head, q_pair, jnp.zeros_like(q_pair))
        do_head = jnp.where(in_head, scaled_pair, jnp.zeros_like(scaled_pair))
        dot_head = jnp.concatenate(
            [scaled[head], zeros] if head == 0 else [zeros, scaled[head]], axis=0
        )
        near_sums = {-1: None, 0: None, 1: None}
        far_sums = {-1: None, 1: None}
        for part in range(SLOT // HALF_Q):
            columns = slice(part * HALF_Q, (part + 1) * HALF_Q)
            prob_grad = dot(v_pair, dot_head[:, columns])
            low_weights = et[head, :, columns]
            score_grad = low_weights.astype(F32) * (prob_grad - deltas[head][:, columns])
            low = score_grad.astype(BF16)
            key_total = key_total + dot(low, q_head[columns, :])
            value_total = value_total + dot(low_weights, do_head[columns, :])
            dqt[pl.ds(head * HEAD, HEAD), columns] = dot(
                kt[head * HEAD : (head + 1) * HEAD, :], low
            ).astype(BF16)
            for key_block in range(4):
                for sub in range(HALF_Q // BLOCK):
                    apart = key_block - part * (HALF_Q // BLOCK) - sub
                    cell = score_grad[
                        key_block * BLOCK : (key_block + 1) * BLOCK,
                        sub * BLOCK : (sub + 1) * BLOCK,
                    ]
                    if abs(apart) >= 2:
                        side = 1 if apart > 0 else -1
                        folded = jnp.sum(cell.reshape(BLOCK // 8, 8, BLOCK), axis=0)
                        old = far_sums[side]
                        far_sums[side] = folded if old is None else old + folded
                    else:
                        old = near_sums[apart]
                        near_sums[apart] = cell if old is None else old + cell
        near[...] = jnp.zeros_like(near)
        for apart in (-1, 0, 1):
            lane = (-apart * BLOCK) % SLOT
            near[:, lane : lane + BLOCK] = near_sums[apart]
        folded = near[0:8, :]
        for group in range(1, BLOCK // 8):
            folded = folded + pltpu.roll(near[group * 8 : group * 8 + 8, :], SLOT - 8 * group, 1)
        for bit in (1, 2, 4):
            folded = jnp.where(
                (row_of_eight & bit) != 0, pltpu.roll(folded, SLOT - bit, 1), folded
            )
        here = slice(head, head + 1)
        bias_grad[0, here, 0:SLOT] = jnp.sum(folded, axis=0, keepdims=True)
        for number, side in enumerate((-1, 1)):
            lane = SLOT + number * BLOCK
            bias_grad[0, here, lane : lane + BLOCK] = jnp.sum(
                far_sums[side], axis=0, keepdims=True
            )
    dk[...] = key_total.astype(BF16)
    dv[...] = value_total.astype(BF16)
    dq[...] = dqt[...].T


def attention_back(lens, qkv, et, linv, ot, do, first, count, held):
    pair = 2 * HEAD
    pairs = H // 2
    wide = pl.BlockSpec((SLOT, pair), lambda i: (0, first + i))
    return pl.pallas_call(
        attention_back_kernel,
        grid=(count,),
        out_shape=(shape((SLOT, D), BF16),) * 3 + (shape((pairs, 2, D), F32),),
        in_specs=[
            SMEM,
            wide,
            pl.BlockSpec((SLOT, pair), lambda i: (0, pairs + first + i)),
            pl.BlockSpec((SLOT, pair), lambda i: (0, 2 * pairs + first + i)),
            pl.BlockSpec((2, SLOT, SLOT), lambda i: (first + i, 0, 0)),
            pl.BlockSpec((2, 1, SLOT), lambda i: (first + i, 0, 0)),
            pl.BlockSpec((pair, SLOT), lambda i: (first + i, 0)),
            wide,
        ]
        + [ANY] * len(held),
        out_specs=(wide,) * 3 + (pl.BlockSpec((1, 2, D), lambda i: (first + i, 0, 0)),),
        input_output_aliases={8 + i: i for i in range(len(held))},
        scratch_shapes=[pltpu.VMEM((pair, SLOT), BF16), pltpu.VMEM((BLOCK, SLOT), F32)],
        compiler_params=params(wide=True),
        cost_estimate=COST,
        name="attention_back",
    )(lens, qkv, qkv, qkv, et, linv, ot, do, *held)


def token_grad_kernel(lens, gain, embedded, dq, dk, dv, hidden_grad, tok, *refs):
    pieces, outs, refs = refs[:8], refs[8:12], refs[12:]
    weight, embedded_v, dq_v, dk_v, dv_v, hidden_v, tok_v, total = refs[:8]
    packed, (sems, in_sems, done_sems) = refs[8:12], refs[12:]
    load, store = Copies(in_sems), Copies(done_sems)
    me, _ = place()
    loads = []
    for number, (source, target) in enumerate(((dq, dq_v), (dk, dk_v), (dv, dv_v))):
        plan = QKV_PLANS[number]
        loads.append(
            [load(source, target)]
            + begin(pieces_of(SHARD, plan, pieces, weight, sems, 6 * number))
        )
    later = [load(hidden_grad, hidden_v), load(tok, tok_v), load(embedded, embedded_v)]
    for number, source in enumerate((dq_v, dk_v, dv_v)):
        finish(loads[number])
        for block in range(2):
            rows = pl.ds(block * 256, 256)
            term = dot_t(source[rows, :], weight[:, number * D : (number + 1) * D])
            total[rows, :] = term if number == 0 else total[rows, :] + term
    finish(later)
    scale = gain[...].reshape(1, D)
    stores = []
    for flip, target in enumerate(packed):
        rows = pl.ds(pl.multiple_of((me ^ flip) * BLOCK, BLOCK), BLOCK)
        gradient = norm_backward(tok_v[rows, :].astype(F32), scale, total[rows, :])
        target[:, 0:D] = (hidden_v[rows, :] + gradient).astype(BF16)
        target[:, D:WIDE] = embedded_v[rows, :]
        stores.append(store(target, outs[flip]))
    finish(stores)


def token_grads(lens, gain, embedded, dq, dk, dv, hidden_grad, tok, pieces):
    wide = (SLOT, D)
    return pl.pallas_call(
        token_grad_kernel,
        out_shape=(shape((BLOCK, WIDE), BF16),) * 4,
        in_specs=[SMEM, VMEM] + [ANY] * 14,
        out_specs=(ANY,) * 4,
        scratch_shapes=[
            pltpu.VMEM((D, 3 * D), BF16),
            pltpu.VMEM((SLOT, PROJ), BF16),
            pltpu.VMEM(wide, BF16),
            pltpu.VMEM(wide, BF16),
            pltpu.VMEM(wide, BF16),
            pltpu.VMEM(wide, F32),
            pltpu.VMEM(wide, BF16),
            pltpu.VMEM(wide, F32),
        ]
        + [pltpu.VMEM((BLOCK, WIDE), BF16)] * 4
        + [
            pltpu.SemaphoreType.DMA((18,)),
            pltpu.SemaphoreType.DMA((6,)),
            pltpu.SemaphoreType.DMA((4,)),
        ],
        compiler_params=params(wide=True),
        cost_estimate=COST,
        name="token_grads",
    )(lens, gain, embedded, dq, dk, dv, hidden_grad, tok, *pieces)


def unpack_kernel(block_0, block_1, block_2, block_3, embedded, tokens_grad):
    me, _ = place()
    for flip, block in enumerate((block_0, block_1, block_2, block_3)):
        tokens_grad[me ^ flip] = block[:, 0:D].astype(F32)
        embedded[me ^ flip] = block[:, D:WIDE]


def unpack(blocks):
    return pl.pallas_call(
        unpack_kernel,
        out_shape=(shape((SEQ, BLOCK, PROJ), BF16), shape((SEQ, BLOCK, D), F32)),
        in_specs=[VMEM] * 4,
        out_specs=(VMEM,) * 2,
        compiler_params=params(),
        cost_estimate=SMALL_COST,
        name="unpack",
    )(*blocks)


def exchange(value, axis, flip, size):
    return lax.ppermute(value, axis, [(i, i ^ flip) for i in range(size)])


def after(value, *others):
    return lax.optimization_barrier((value,) + others)[0]


def add(*terms):
    total = terms[0].astype(F32)
    for term in terms[1:]:
        total = total + term.astype(F32)
    return total.astype(BF16)


def marker_kernel(tick, mark):
    pass


def marker(tick):
    return pl.pallas_call(
        marker_kernel,
        out_shape=shape((8, 128), F32),
        in_specs=[ANY],
        out_specs=ANY,
        compiler_params=params(),
        cost_estimate=COST,
        name="marker",
    )(tick)


def halves_kernel(skip, *refs):
    terms, (to_send, own, held, sems) = refs[:-4], refs[-4:]
    rows = own.shape[0]
    finish(
        begin(
            [
                pltpu.make_async_copy(
                    source.at[pl.ds(first, 2 * rows), :], held.at[number], sems.at[number]
                )
                for number, (source, first) in enumerate(zip(terms, skip))
            ]
        )
    )
    for number, target in enumerate((to_send, own)):

        def body(index, carry):
            here = pl.ds(pl.multiple_of(number * rows + index * 16, 16), 16)
            total = held[0, here, :].astype(F32)
            for term in range(1, len(terms)):
                total = total + held[term, here, :].astype(F32)
            target[pl.ds(pl.multiple_of(index * 16, 16), 16), :] = total.astype(BF16)
            return carry

        lax.fori_loop(0, rows // 16, body, 0)


def halves(rows, *terms):
    width = terms[0][0].shape[1]
    return pl.pallas_call(
        functools.partial(halves_kernel, tuple(first for _, first in terms)),
        out_shape=(shape((rows, width), BF16),) * 2,
        in_specs=[ANY] * len(terms),
        out_specs=(VMEM,) * 2,
        scratch_shapes=[
            pltpu.VMEM((len(terms), 2 * rows, width), BF16),
            pltpu.SemaphoreType.DMA((len(terms),)),
        ],
        compiler_params=params(),
        cost_estimate=SMALL_COST,
        name="halves",
    )(*(term for term, _ in terms))


class Chunk:
    def __init__(self, groups, pair, thin=False):
        self.groups, self.thin = groups, thin
        self.send, self.keep = pair
        self.rows = self.send.shape[0] // 4

    def along(self, flip, value):
        return exchange(value, "dp", flip, self.groups)

    def core(self, tick):
        self.send = after(self.send, tick)
        self.from_core = exchange(self.send, "seq", 1, SEQ)

    def x(self, tick):
        both = 2 * self.rows
        self.from_core = after(self.from_core, tick)
        mine = add(self.keep[:both], self.from_core[:both])
        self.from_x = exchange(mine, "seq", 2, SEQ)

    def first(self, tick):
        self.from_x = after(self.from_x, tick)
        rows = self.rows
        mine, self.base = halves(
            rows, (self.keep, 2 * rows), (self.from_core, 2 * rows), (self.from_x, 0)
        )
        self.from_first = self.along(1, mine)

    def _summed(self, begin, end):
        return add(self.base[begin:end], self.from_first[begin:end])

    def second(self, tick):
        self.from_first = after(self.from_first, tick)
        self.total = self._summed(0, self.rows if self.thin else self.rows // 2)
        self.from_second = self.along(2, self.total)

    def rest(self, tick):
        self.from_second = after(self.from_second, tick)
        if not self.thin:
            self.total = self._summed(self.rows // 2, self.rows)
        self.total = add(self.total, self.from_second)
        step = 4
        while step < self.groups:
            if step > 4:
                self.total = add(self.total, self.from_rest)
            self.from_rest = self.along(step, self.total)
            step *= 2

    def back_second(self, tick):
        self.from_rest = after(self.from_rest, tick)
        self.total = add(self.total, self.from_rest)
        self.other_second = self.along(2, self.total)

    def back_first(self, tick):
        if self.thin:
            self.from_rest = after(self.from_rest, tick)
            self.total = add(self.total, self.from_rest)
        else:
            self.other_second = after(self.other_second, tick)
            self.total = jnp.concatenate([self.other_second, self.total], axis=0)
        self.other = self.along(1, self.total)


def join_kernel(*refs):
    terms, out = refs[:-1], refs[-1]
    column = 0
    for left, right in zip(terms[0::2], terms[1::2]):
        width = left.shape[1]
        out[:, column : column + width] = (
            left[...].astype(F32) + right[...].astype(F32)
        ).astype(BF16)
        column += width


class Group:
    thin = False

    def __init__(self, *chunks):
        self.chunks, self.rows, self.along = chunks, chunks[0].rows, chunks[0].along

    def back_second(self, tick):
        terms = []
        for chunk in self.chunks:
            terms += [chunk.total, after(chunk.from_rest, tick)]
        width = sum(chunk.total.shape[1] for chunk in self.chunks)
        self.total = pl.pallas_call(
            join_kernel,
            out_shape=shape((self.rows // 2, width), BF16),
            in_specs=[VMEM] * len(terms),
            out_specs=VMEM,
            compiler_params=params(),
            cost_estimate=SMALL_COST,
            name="join",
        )(*terms)
        self.other_second = self.along(2, self.total)

    def back_first(self, tick):
        self.other_second = after(self.other_second, tick)
        self.total = jnp.concatenate([self.other_second, self.total], axis=0)
        self.other = self.along(1, self.total)


def assemble_kernel(rows, widths, marks, counts, table, natural, total, other, *refs):
    weights, refs = refs[: counts[0]], refs[counts[0] :]
    gains, outs = refs[: counts[1]], refs[counts[1] :]
    me, y = place()
    z = lax.rem(lax.axis_index("dp") // 2, 2)
    half = rows // 2
    column = 0
    sums = [None] * counts[1]

    def blocks():
        for source, first in ((total, 1), (other, 0)):
            for second in range(2):
                y_of = y if first else 1 - y
                z_of = second if natural else (z if second else 1 - z)
                yield source, second * half, y_of, z_of

    for number, width in enumerate(widths):
        columns = slice(column, column + width)
        out = outs[number]
        for source, row, y_of, z_of in blocks():
            begin_row = pl.multiple_of(y_of * rows + z_of * half, 16)
            out[pl.ds(begin_row, half), :] = source[row : row + half, columns].astype(F32)
        column += width
        for which, weight, target in marks:
            if which == number:
                part = jnp.sum(
                    weights[weight][...].astype(F32) * out[...], axis=1, keepdims=True
                )
                sums[target] = part if sums[target] is None else sums[target] + part
    for number, (summed, gain) in enumerate(zip(sums, gains)):
        total_rows = jnp.broadcast_to(summed, (2 * rows, BLOCK)).T[0:1, :]
        whole = gain[...].reshape(1, D)
        mine = whole[:, 0:SHARD]
        for shard in range(1, SEQ):
            mine = jnp.where(me == shard, whole[:, shard * SHARD : (shard + 1) * SHARD], mine)
        outs[len(widths) + number][...] = (total_rows / mine).reshape(2 * rows)
    if table:
        for source, row, y_of, z_of in blocks():
            if natural and z_of:
                continue

            @pl.when((y_of == 0) if natural else (y_of == 0) & (z_of == 0))
            def store():
                outs[-1][...] = source[
                    row : row + BUCKETS // SEQ, column : column + H
                ].astype(F32)


def assemble(chunk, widths, marks=(), weights=(), gains=(), table=False):
    rows = chunk.rows
    out_shape = [shape((2 * rows, width), F32) for width in widths]
    out_shape += [shape((2 * rows,), F32) for _ in gains]
    if table:
        out_shape.append(shape((BUCKETS // SEQ, H), F32))
    operands = tuple(weights) + tuple(gains)
    return pl.pallas_call(
        functools.partial(
            assemble_kernel,
            rows,
            widths,
            marks,
            (len(weights), len(gains)),
            table,
            chunk.thin,
        ),
        out_shape=tuple(out_shape),
        in_specs=[VMEM] * (2 + len(operands)),
        out_specs=(VMEM,) * len(out_shape),
        compiler_params=params(),
        cost_estimate=SMALL_COST,
        name="assemble",
    )(chunk.total, chunk.other, *operands)


def per_device(
    groups,
    tokens,
    doc_lengths,
    query_weight,
    key_weight,
    value_weight,
    out_weight,
    gate_weight,
    up_weight,
    down_weight,
    proj_weight,
    attn_gain,
    ffn_gain,
    final_gain,
    bucket_bias_rows,
    embed_cotangent,
):
    tick = doc_lengths

    def across_x(mine):
        return exchange(after(mine, tick), "seq", 2, SEQ)

    def across_y(mine):
        return exchange(after(mine, tick), "dp", 1, groups)

    def across_core(mine):
        return exchange(after(mine, tick), "seq", 1, SEQ)

    def across_far(mine):
        return exchange(after(mine, tick), "seq", 3, SEQ)

    qkv_half = pack_first(tick, query_weight, key_weight, value_weight)
    qkv_x = across_x(qkv_half)
    tick = after(tick, qkv_half)
    blocks = pack_tokens(tick, tokens, embed_cotangent)
    block_x = across_x(blocks[2])
    block_far = across_far(blocks[3])
    block_core = across_core(blocks[1])
    tick = after(tick, blocks[0])
    qkv_own, out_own, gated_half_0, gated_half_1, down_rest = pack_rest(
        tick,
        query_weight,
        key_weight,
        value_weight,
        out_weight,
        proj_weight,
        gate_weight,
        up_weight,
        down_weight,
    )
    tick = after(tick, qkv_x, gated_half_0)
    qkv_y = across_y(qkv_x)
    qkv_cx = across_core(qkv_x)
    tick = after(tick, block_x, block_far, block_core)
    qkv_core = across_core(qkv_own)
    out_x = across_x(out_own)
    tok, cot, n1, n1t = first_norm(tick, (blocks[0], block_core, block_x, block_far), attn_gain)
    tick = after(tick, n1, qkv_y, qkv_cx)
    qkv_cy = across_core(qkv_y)
    tick = after(tick, qkv_cy, qkv_core, out_x)
    out_core = across_core(out_own)
    gated_x_0 = across_x(gated_half_0)
    gated_x_1 = across_x(gated_half_1)
    gate_core = across_core(gate_weight)
    qkv_pieces = (
        query_weight, key_weight, value_weight, qkv_core, qkv_x, qkv_y, qkv_cx, qkv_cy
    )
    qkv = qkv_project(tick, n1, qkv_pieces)
    pairs = H // 2
    third = pairs // 3
    tick = after(tick, qkv, gated_x_0, out_core, gate_core)
    gated_y_0 = across_y(gated_x_0)
    gated_cx_0 = across_core(gated_x_0)
    out_cx = across_core(out_x)
    down_x = across_x(down_rest)
    held = attention(tick, qkv, bucket_bias_rows, 0, third, ())
    tick = after(tick, held[0], gated_x_1, gated_cx_0, out_cx)
    gated_y_1 = across_y(gated_x_1)
    gated_cx_1 = across_core(gated_x_1)
    up_core = across_core(up_weight)
    held = attention(tick, qkv, bucket_bias_rows, third, third, held)
    tick = after(tick, held[0], gated_y_0, gated_cx_1, up_core)
    gated_cy_0 = across_core(gated_y_0)
    down_core = across_core(down_weight)
    et, linv, ot, mixed = attention(
        tick, qkv, bucket_bias_rows, 2 * third, pairs - 2 * third, held
    )
    tick = after(tick, mixed, gated_y_1, gated_cy_0, down_core)
    gated_cy_1 = across_core(gated_y_1)
    tick = after(tick, down_x)
    down_cx = across_core(down_x)
    tick = after(tick, gated_cy_1, down_cx)
    out_pieces = (out_own, out_core, out_x, out_cx)
    down_pieces = (down_weight, down_core, out_x, down_x, out_cx, down_cx)
    gated_pieces = (
        gate_weight, up_weight, gate_core, up_core,
        gated_x_0, gated_y_0, gated_cx_0, gated_cy_0,
        gated_x_1, gated_y_1, gated_cx_1, gated_cy_1,
    )
    hidden, n2t, gate_grad, up_grad, embedded, after_grad, fnt, *pair = feed_forward(
        tick, tok, mixed, cot, ffn_gain, final_gain, out_pieces, gated_pieces, down_pieces
    )

    chunk = functools.partial(Chunk, groups)
    down_sum = chunk(pair)
    tick = after(tick, down_sum.keep)
    down_sum.core(tick)
    gate_sum = chunk(gate_grads(tick, n2t, gate_grad))
    tick = after(tick, gate_sum.keep, down_sum.from_core)
    down_sum.x(tick)
    gate_sum.core(tick)
    *pair, hidden_grad, attn_in = up_grads(
        tick, ffn_gain, n2t, gate_grad, up_grad, hidden, after_grad, gated_pieces
    )
    up_sum = chunk(pair)
    tick = after(tick, up_sum.keep, gate_sum.from_core)
    gate_sum.x(tick)
    up_sum.core(tick)
    *pair, mixed_grad = out_grads(tick, ot, fnt, attn_in, cot, out_pieces)
    out_sum = chunk(pair)
    tick = after(tick, out_sum.keep, up_sum.from_core, down_sum.from_x)
    down_sum.first(tick)
    up_sum.x(tick)
    out_sum.core(tick)
    held = attention_back(tick, qkv, et, linv, ot, mixed_grad, 0, pairs // 2, ())
    tick = after(tick, held[0], out_sum.from_core, down_sum.from_first)
    down_sum.second(tick)
    out_sum.x(tick)
    dq, dk, dv, bias_part = attention_back(
        tick, qkv, et, linv, ot, mixed_grad, pairs // 2, pairs - pairs // 2, held
    )
    tick = after(tick, dq, gate_sum.from_x, down_sum.from_second)
    gate_sum.first(tick)
    down_sum.rest(tick)
    *pair, value_send, value_keep = qkv_grads(tick, bias_part, n1t, dq, dk, dv)
    first_sum, value_sum = chunk(pair), chunk((value_send, value_keep))
    tick = after(
        tick,
        first_sum.keep,
        gate_sum.from_first,
        up_sum.from_x,
        down_sum.from_rest,
        out_sum.from_x,
    )
    first_sum.core(tick)
    value_sum.core(tick)
    gate_sum.second(tick)
    up_sum.first(tick)
    down_sum.back_second(tick)
    blocks = token_grads(
        tick, attn_gain, embedded, dq, dk, dv, hidden_grad, tok, qkv_pieces
    )
    tick = after(
        tick,
        blocks[0],
        first_sum.from_core,
        value_sum.from_core,
        gate_sum.from_second,
        up_sum.from_first,
        down_sum.other_second,
    )
    first_sum.x(tick)
    gate_sum.rest(tick)
    up_sum.second(tick)
    down_sum.back_first(tick)
    tick = after(tick, marker(tick), up_sum.from_second)
    up_sum.rest(tick)
    value_sum.x(tick)
    tick = after(tick, marker(tick), gate_sum.from_rest, down_sum.other)
    out_sum.first(tick)
    tick = after(tick, marker(tick), up_sum.from_rest)
    gated_sum = Group(gate_sum, up_sum)
    gated_sum.back_second(tick)
    tick = after(tick, marker(tick), first_sum.from_x)
    first_sum.first(tick)
    block_x = across_x(blocks[2])
    block_far = across_far(blocks[3])
    block_core = across_core(blocks[1])
    tick = after(tick, marker(tick), out_sum.from_first, value_sum.from_x)
    value_sum.first(tick)
    out_sum.second(tick)
    tick = after(tick, marker(tick), first_sum.from_first, gated_sum.other_second)
    first_sum.second(tick)
    gated_sum.back_first(tick)
    tick = after(tick, marker(tick), value_sum.from_first, out_sum.from_second)
    value_sum.second(tick)
    out_sum.rest(tick)
    tick = after(tick, marker(tick), first_sum.from_second)
    first_sum.rest(tick)
    tick = after(tick, marker(tick), value_sum.from_second)
    value_sum.rest(tick)
    tick = after(
        tick, marker(tick), first_sum.from_rest, value_sum.from_rest, out_sum.from_rest, gated_sum.other, block_x, block_far
    )
    attn_sum = Group(out_sum, first_sum, value_sum)
    attn_sum.back_second(tick)
    tick = after(tick, marker(tick), attn_sum.other_second, block_core)
    attn_sum.back_first(tick)
    down_grad, = assemble(down_sum, (D,))
    gate_weight_grad, up_weight_grad, ffn_gain_grad = assemble(
        gated_sum, (FF, FF), ((0, 0, 0), (1, 1, 0)), (gate_weight, up_weight), (ffn_gain,)
    )
    embedded, tokens_grad = unpack((blocks[0], block_core, block_x, block_far))
    (
        out_grad,
        proj_grad,
        query_grad,
        key_grad,
        value_grad,
        final_gain_grad,
        attn_gain_grad,
        table_grad,
    ) = assemble(
        attn_sum,
        (D, PROJ, D, D, D),
        ((1, 0, 0), (2, 1, 1), (3, 2, 1), (4, 3, 1)),
        (proj_weight, query_weight, key_weight, value_weight),
        (final_gain, attn_gain),
        table=True,
    )
    return (
        embedded,
        tokens_grad,
        query_grad,
        key_grad,
        value_grad,
        out_grad,
        gate_weight_grad,
        up_weight_grad,
        down_grad,
        proj_grad,
        attn_gain_grad,
        ffn_gain_grad,
        final_gain_grad,
        table_grad,
    )


def solution(mesh):
    placed = (
        P("dp", "seq", None),
        P("dp"),
        P("seq", None),
        P("seq", None),
        P("seq", None),
        P("seq", None),
        P("seq", None),
        P("seq", None),
        P("seq", None),
        P("seq", None),
        P(),
        P(),
        P(),
        P(),
        P("dp", "seq", None),
    )
    return jax.shard_map(
        functools.partial(per_device, mesh.shape["dp"]),
        mesh=mesh,
        in_specs=placed,
        out_specs=(
            P("dp", "seq", None),
            P("dp", "seq", None),
            P("seq", None),
            P("seq", None),
            P("seq", None),
            P("seq", None),
            P("seq", None),
            P("seq", None),
            P("seq", None),
            P("seq", None),
            P("seq"),
            P("seq"),
            P("seq"),
            P("seq", None),
        ),
        check_vma=False,
    )
```
